32 devices in a mesh: dp: 8 (over y, x, core), mp: 4 (over z).
Axes of the slice: x: 2, y: 2, z: 4, core: 2. Of those that a mesh axis runs over, the one named last changes fastest.
Arguments:
- tokens_in: bfloat16 [16384, 768], P('dp'), may hold values from -6 to 6
- cotangent: bfloat16 [16384, 768], P('dp'), may hold values from -6 to 6
- patch_counts: int32 [16, 10], P('dp'), may hold values from 0 to 100, as said below
- w_qkv: float32 [768, 3, 768], P('dp', None, 'mp'), may hold values from -1 to 1
- w_out: float32 [768, 768], P('mp', 'dp'), may hold values from -0.4375 to 0.4375
- w_up: float32 [768, 3072], P('dp', 'mp'), may hold values from -0.21875 to 0.21875
- w_down: float32 [3072, 768], P('mp', 'dp'), may hold values from -0.109375 to 0.109375
- layer_vector_rows: float32 [8, 768], replicated, may hold values from -1.2 to 2.4
- inner_biases: float32 [6, 768], replicated, may hold values from -3 to 3
- qkvrows_prior: float32 [768], P('dp'), may hold values from 1638 to 6553
- qkvcols_prior: float32 [3, 768], P(None, 'mp'), may hold values from 1638 to 6553
- outrows_prior: float32 [768], P('mp'), may hold values from 2293 to 9175
- outcols_prior: float32 [768], P('dp'), may hold values from 2293 to 9175
- uprows_prior: float32 [768], P('dp'), may hold values from 819 to 3276
- upcols_prior: float32 [3072], P('mp'), may hold values from 819 to 3276
- downrows_prior: float32 [3072], P('mp'), may hold values from 2293 to 9175
- downcols_prior: float32 [768], P('dp'), may hold values from 2293 to 9175
- vector_moment: float32 [8, 768], replicated, may hold values from 1638 to 8192
- bias_moment: float32 [6, 768], replicated, may hold values from 292 to 4681
Outputs:
- stream_out: bfloat16 [16384, 768], P('dp')
- input_grad: float32 [16384, 768], P('dp', 'mp')
- qkv_grad: float32 [768, 3, 768], P('dp', None, 'mp')
- out_grad: float32 [768, 768], P('mp', 'dp')
- up_grad: float32 [768, 3072], P('dp', 'mp')
- down_grad: float32 [3072, 768], P('mp', 'dp')
- qkv_after: float32 [768, 3, 768], P('dp', None, 'mp')
- out_after: float32 [768, 768], P('mp', 'dp')
- up_after: float32 [768, 3072], P('dp', 'mp')
- down_after: float32 [3072, 768], P('mp', 'dp')
- qkv_bfloat: bfloat16 [768, 3, 768], P('dp', None, 'mp')
- out_bfloat: bfloat16 [768, 768], P('mp', 'dp')
- up_bfloat: bfloat16 [768, 3072], P('dp', 'mp')
- down_bfloat: bfloat16 [3072, 768], P('mp', 'dp')
- qkvrows_after: float32 [768], P('dp')
- qkvcols_after: float32 [3, 768], P(None, 'mp')
- outrows_after: float32 [768], P('mp')
- outcols_after: float32 [768], P('dp')
- uprows_after: float32 [768], P('dp')
- upcols_after: float32 [3072], P('mp')
- downrows_after: float32 [3072], P('mp')
- downcols_after: float32 [768], P('dp')
- vector_grad: float32 [8, 768], replicated
- bias_grad: float32 [6, 768], replicated
- moment_vectors: float32 [8, 768], replicated
- moment_biases: float32 [6, 768], replicated
- vectors_after: float32 [8, 768], replicated
- biases_after: float32 [6, 768], replicated
- update_scale: float32 [4], replicated
- token_spread: float32 [3], replicated
The draws below stay inside these ranges and needn't reach their ends.
Inputs may be any that keep to these rules, and one draw needn't show every extreme that they name: `patch_counts`: every set holds at least one image; used slots come first and hold 60 to 100 patches, the first slot of every set exactly 100; later slots hold 0.
All inputs are finite; a program needn't handle non-finite values.
Results may differ from the reference program's by a relative error of at most 0.018.
Values may be sent and summed in bfloat16 or wider, within the bound.
A program may use at most 192 MiB of HBM per device.

```python
import math
import jax
import jax.numpy as jnp
from jax import lax

D = 768
HEADS = 12
HD = 64
FF = 3072
ROWS = 1024
IMGS = 10
MOST = 100
LEAST = 60
STEP = 3
SETS = 16
TOKENS = 16384
N_MP = 4


def draw_patch_counts(key, part):
    key = jax.random.fold_in(key, 11)
    set_index = jnp.arange(SETS, dtype=jnp.int32)
    used_slots = jnp.maximum(1, (IMGS * (SETS - 1) + 2 * IMGS * set_index) // (3 * (SETS - 1)))
    drawn = jax.random.randint(key, (SETS, IMGS), LEAST, MOST + 1, dtype=jnp.int32)
    slot_index = jnp.arange(IMGS, dtype=jnp.int32)
    drawn = jnp.where(slot_index[None, :] == 0, MOST, drawn)
    return jnp.where(slot_index[None, :] < used_slots[:, None], drawn, 0).astype(jnp.int32)


def draw_layer_vector_rows(key, part):
    key = jax.random.fold_in(key, 23)
    key_list = jax.random.split(key, 3)
    ramp = jnp.arange(D, dtype=jnp.float32) / (D - 1)
    base_gain = 0.6 + 1.2 * ramp
    rough = 1.0 + jnp.clip(0.1 * jax.random.normal(key_list[0], (8, D), jnp.float32), -0.3, 0.3)
    noise = jnp.clip(0.3 * jax.random.normal(key_list[1], (8, D), jnp.float32), -1.2, 1.2)
    layer_scales = jnp.exp(jax.random.uniform(key_list[2], (8, D), jnp.float32, math.log(0.6), math.log(1.5)))
    row_index = jnp.arange(8)[:, None]
    gains = base_gain[None, :] * rough
    chosen = jnp.where((row_index == 0) | (row_index == 2), gains, jnp.where((row_index == 4) | (row_index == 5), layer_scales, noise))
    return chosen.astype(jnp.float32)


def draw_w_qkv(key, part):
    key = jax.random.fold_in(key, 37)
    key_list = jax.random.split(key, 2)
    noise = jnp.clip(jax.random.normal(key_list[0], (D, 3, D), jnp.float32), -6.0, 6.0)
    offset = jnp.clip(0.8 * jax.random.normal(key_list[1], (1, 3, D), jnp.float32), -3.0, 3.0)
    return ((noise + offset) * D ** (-0.5)).astype(jnp.float32)


def block_scale(rng, shape, shards, least, top_value):
    factor_of = 1.0
    for position, parts in shards:
        steps = jax.random.uniform(jax.random.fold_in(jax.random.fold_in(rng, 6), position), (parts,), jnp.float32, least / len(shards), top_value / len(shards))
        factor_of = factor_of * jnp.repeat(jnp.exp(steps), shape[position] // parts).reshape((-1,) + (1,) * (len(shape) - 1 - position))
    return factor_of


def gaussian(stream_key, dims, scale, limit, shards=(), kind=jnp.bfloat16):
    entries = scale * jax.random.normal(stream_key, dims, jnp.float32)
    if shards:
        entries = entries * block_scale(stream_key, dims, shards, -0.22, 0.18)
    return jnp.clip(entries, -limit, limit).astype(kind)


def setup_inputs(seed: int = 0) -> dict:
    keys = jax.random.split(jax.random.key(seed), 20)
    return {
        "tokens_in": gaussian(keys[0], (TOKENS, D), 1.0, 6.0, ((0, 8),)),
        "cotangent": gaussian(keys[1], (TOKENS, D), 1.0, 6.0, ((0, 8),)),
        "patch_counts": draw_patch_counts(jax.random.fold_in(keys[19], 71), 0),
        "w_qkv": draw_w_qkv(jax.random.fold_in(keys[19], 71), 0),
        "w_out": gaussian(keys[4], (D, D), (D // 4) ** -0.5, 0.4375, ((0, 4), (1, 8)), jnp.float32),
        "w_up": gaussian(keys[5], (D, FF), D ** -0.5, 0.21875, ((0, 8), (1, 4)), jnp.float32),
        "w_down": gaussian(keys[6], (FF, D), FF ** -0.5, 0.109375, ((0, 4), (1, 8)), jnp.float32),
        "layer_vector_rows": draw_layer_vector_rows(jax.random.fold_in(keys[19], 71), 0),
        "inner_biases": gaussian(keys[8], (2 + FF // D, D), 0.5, 3.0, (), jnp.float32),
        "qkvrows_prior": jnp.clip(jnp.exp(math.log(6553.0) - 1.386447 * jax.random.uniform(keys[9], (D,), jnp.float32) ** block_scale(keys[9], (D,), ((0, 8),), -0.2, 0.2)), 1638.0, 6553.0),
        "qkvcols_prior": jnp.clip(jnp.exp(math.log(6553.0) - 1.386447 * jax.random.uniform(keys[10], (3, D), jnp.float32) ** block_scale(keys[10], (3, D), ((1, 4),), -0.2, 0.2)), 1638.0, 6553.0),
        "outrows_prior": jnp.clip(jnp.exp(math.log(9175.0) - 1.3866214 * jax.random.uniform(keys[11], (D,), jnp.float32) ** block_scale(keys[11], (D,), ((0, 4),), -0.2, 0.2)), 2293.0, 9175.0),
        "outcols_prior": jnp.clip(jnp.exp(math.log(9175.0) - 1.3866214 * jax.random.uniform(keys[12], (D,), jnp.float32) ** block_scale(keys[12], (D,), ((0, 8),), -0.2, 0.2)), 2293.0, 9175.0),
        "uprows_prior": jnp.clip(jnp.exp(math.log(3276.0) - 1.3862944 * jax.random.uniform(keys[13], (D,), jnp.float32) ** block_scale(keys[13], (D,), ((0, 8),), -0.2, 0.2)), 819.0, 3276.0),
        "upcols_prior": jnp.clip(jnp.exp(math.log(3276.0) - 1.3862944 * jax.random.uniform(keys[14], (FF,), jnp.float32) ** block_scale(keys[14], (FF,), ((0, 4),), -0.2, 0.2)), 819.0, 3276.0),
        "downrows_prior": jnp.clip(jnp.exp(math.log(9175.0) - 1.3866214 * jax.random.uniform(keys[15], (FF,), jnp.float32) ** block_scale(keys[15], (FF,), ((0, 4),), -0.2, 0.2)), 2293.0, 9175.0),
        "downcols_prior": jnp.clip(jnp.exp(math.log(9175.0) - 1.3866214 * jax.random.uniform(keys[16], (D,), jnp.float32) ** block_scale(keys[16], (D,), ((0, 8),), -0.2, 0.2)), 2293.0, 9175.0),
        "vector_moment": jnp.clip(jnp.exp(jax.random.uniform(keys[17], (8, D), jnp.float32, math.log(1638.0), math.log(8192.0))), 1638.0, 8192.0),
        "bias_moment": jnp.clip(jnp.exp(jax.random.uniform(keys[18], (2 + FF // D, D), jnp.float32, math.log(292.0), math.log(4681.0))), 292.0, 4681.0),
    }


@jax.custom_vjp
def low(v):
    return lax.optimization_barrier(v.astype(jnp.bfloat16)).astype(jnp.float32)

@jax.custom_vjp
def low_back(v):
    return v

def low_keep(v):
    return (low(v), None)

def low_pass(kept, grad):
    return (grad,)

def back_keep(v):
    return (v, None)

def back_low(kept, grad):
    return (low(grad),)
low.defvjp(low_keep, low_pass)
low_back.defvjp(back_keep, back_low)
norm_eps = 1e-06
square_eps = 1e-30
clip_limit = 0.5
step_rate = 0.6
mask_fill = -1000000000.0
highest = lax.Precision.HIGHEST

def rounded_both(values):
    return low(low_back(values))

def normalize(stream, gain_row, shift_row):
    center = stream - lax.optimization_barrier(jnp.mean(stream, axis=-1, keepdims=True))
    spread = lax.optimization_barrier(jnp.mean(center * center, axis=-1, keepdims=True))
    return center * lax.rsqrt(spread + norm_eps) * gain_row + shift_row

def segment_ids(counts):
    image_ends = jnp.cumsum(counts)
    places = jnp.arange(ROWS, dtype=jnp.int32)
    return lax.optimization_barrier(jnp.sum((places[:, None] >= image_ends[None, :]).astype(jnp.int32), axis=1))

def block_sum(left_side, right_side, block_width):
    running = jnp.zeros((left_side.shape[0], right_side.shape[1]), jnp.float32)
    for block_index in range(N_MP):
        lower = block_index * block_width
        running = running + low(jnp.dot(left_side[:, lower:lower + block_width], right_side[lower:lower + block_width], precision=highest))
    return running

def one_set(params, stream, counts):
    w_qkv, w_out, w_up, w_down, layer_vector_rows, inner_biases = params
    segment = segment_ids(counts)
    same_image = segment[:, None] == segment[None, :]
    normalized_rows = low(normalize(stream, layer_vector_rows[0], layer_vector_rows[1]))
    query_rows = rounded_both(jnp.dot(normalized_rows, w_qkv[:, 0, :], precision=highest) + inner_biases[0])
    key_rows = rounded_both(jnp.dot(normalized_rows, w_qkv[:, 1, :], precision=highest))
    value_rows = rounded_both(jnp.dot(normalized_rows, w_qkv[:, 2, :], precision=highest) + inner_biases[1])
    query_heads = query_rows.reshape(ROWS, HEADS, HD)
    key_heads = key_rows.reshape(ROWS, HEADS, HD)
    value_heads = value_rows.reshape(ROWS, HEADS, HD)
    scores = jnp.einsum('qhd,khd->hqk', query_heads, key_heads, precision=highest) * HD ** (-0.5)
    scores = low_back(jnp.where(same_image[None], scores, mask_fill))
    weights = jax.nn.softmax(scores, axis=-1)
    mixed_heads = rounded_both(jnp.einsum('hqk,khd->qhd', low(weights), value_heads, precision=highest).reshape(ROWS, D))
    proj = low_back(block_sum(mixed_heads, w_out, D // N_MP) + layer_vector_rows[6])
    middle = stream + layer_vector_rows[4] * proj
    normed_two = low(normalize(middle, layer_vector_rows[2], layer_vector_rows[3]))
    up_bias = inner_biases[2:].T.reshape(FF)
    hidden = low_back(jnp.dot(normed_two, w_up, precision=highest) + up_bias)
    active = low(jax.nn.gelu(hidden, approximate=False))
    branch = low_back(block_sum(active, w_down, FF // N_MP) + layer_vector_rows[7])
    return (middle + layer_vector_rows[5] * branch, layer_vector_rows[4] * proj, layer_vector_rows[5] * branch)

def forward(stream_all, w_qkv, w_out, w_up, w_down, layer_vector_rows, inner_biases, counts):
    params = (low(w_qkv), low(w_out), low(w_up), low(w_down), layer_vector_rows, inner_biases)
    set_step = jax.checkpoint(lambda set_item: one_set(params, set_item[0], set_item[1]))
    outputs, attn_part, mlp_part = lax.map(set_step, (stream_all.reshape(SETS, ROWS, D), counts))
    return (outputs.reshape(TOKENS, D), (attn_part, mlp_part))

def factored(weight, gradient, rows_old, cols_old):
    decay_rate = 1.0 - STEP ** (-0.8)
    square = gradient * gradient
    rows_new = decay_rate * rows_old + (1.0 - decay_rate) * (lax.optimization_barrier(jnp.mean(square, axis=1)) + square_eps)
    cols_new = decay_rate * cols_old + (1.0 - decay_rate) * (lax.optimization_barrier(jnp.mean(square, axis=0)) + square_eps)
    estimate = rows_new[:, None] * cols_new[None, :] / jnp.mean(rows_new)
    update = gradient * lax.rsqrt(estimate)
    update_rms = jnp.sqrt(jnp.mean(update * update))
    rate_here = step_rate * jnp.sqrt(jnp.mean(weight * weight))
    renewed = weight - rate_here * update / jnp.maximum(1.0, update_rms / clip_limit)
    return (renewed, rows_new, cols_new, update_rms)

def plain(weight, gradient, moment_old):
    decay_rate = 1.0 - STEP ** (-0.8)
    moment = decay_rate * moment_old + (1.0 - decay_rate) * (gradient * gradient + square_eps)
    update = gradient * lax.rsqrt(moment)
    update_rms = jnp.sqrt(jnp.mean(update * update))
    rate_here = step_rate * jnp.sqrt(jnp.mean(weight * weight))
    return (weight - rate_here * update / jnp.maximum(1.0, update_rms / clip_limit), moment)

def reference(tokens_in, cotangent, patch_counts, w_qkv, w_out, w_up, w_down, layer_vector_rows, inner_biases, qkvrows_prior, qkvcols_prior, outrows_prior, outcols_prior, uprows_prior, upcols_prior, downrows_prior, downcols_prior, vector_moment, bias_moment):
    stream = tokens_in.astype(jnp.float32)
    segment = jax.vmap(segment_ids)(patch_counts)
    valid_rows = (segment < IMGS).astype(jnp.float32).reshape(TOKENS)

    def wrapped(stream_in, weight_qkv, weight_out, weight_up, weight_down, vectors_in, biases_in):
        return forward(stream_in, weight_qkv, weight_out, weight_up, weight_down, vectors_in, biases_in, patch_counts)
    result, pull, aux_parts = jax.vjp(wrapped, stream, w_qkv, w_out, w_up, w_down, layer_vector_rows, inner_biases, has_aux=True)
    attn_part, mlp_part = aux_parts
    back_grad = cotangent.astype(jnp.float32) * valid_rows[:, None]
    grad_stream, grad_qkv, grad_out, grad_up, grad_down, grad_vectors, grad_biases = pull(back_grad)
    row_weight = valid_rows.reshape(SETS, ROWS, 1)
    valid_total = jnp.sum(valid_rows)

    def spread_of(field_in):
        return jnp.sqrt(jnp.sum(row_weight * field_in * field_in) / (valid_total * D))
    token_spread = jnp.stack([spread_of(result.reshape(SETS, ROWS, D)), spread_of(attn_part), spread_of(mlp_part)])
    qkv_after, qkvrows_after, qkvcols_flat, scale_qkv = factored(w_qkv.reshape(D, 3 * D), grad_qkv.reshape(D, 3 * D), qkvrows_prior, qkvcols_prior.reshape(3 * D))
    out_after, outrows_after, outcols_after, scale_out = factored(w_out, grad_out, outrows_prior, outcols_prior)
    up_after, uprows_after, upcols_after, scale_up = factored(w_up, grad_up, uprows_prior, upcols_prior)
    down_after, downrows_after, downcols_after, scale_down = factored(w_down, grad_down, downrows_prior, downcols_prior)
    qkv_after = qkv_after.reshape(D, 3, D)
    vectors_after, moment_vectors = jax.vmap(plain)(layer_vector_rows, grad_vectors, vector_moment)
    heads_after, heads_moment = jax.vmap(plain)(inner_biases[:2], grad_biases[:2], bias_moment[:2])
    upper_after, upper_moment = plain(inner_biases[2:].reshape(FF), grad_biases[2:].reshape(FF), bias_moment[2:].reshape(FF))
    biases_after = jnp.concatenate([heads_after, upper_after.reshape(FF // D, D)], axis=0)
    moment_biases = jnp.concatenate([heads_moment, upper_moment.reshape(FF // D, D)], axis=0)
    update_scale = jnp.stack([scale_qkv, scale_out, scale_up, scale_down])
    return (result.astype(jnp.bfloat16), grad_stream, grad_qkv, grad_out, grad_up, grad_down, qkv_after, out_after, up_after, down_after, qkv_after.astype(jnp.bfloat16), out_after.astype(jnp.bfloat16), up_after.astype(jnp.bfloat16), down_after.astype(jnp.bfloat16), qkvrows_after, qkvcols_flat.reshape(3, D), outrows_after, outcols_after, uprows_after, upcols_after, downrows_after, downcols_after, grad_vectors, grad_biases, moment_vectors, moment_biases, vectors_after, biases_after, update_scale, token_spread)
```

```python
import functools

import jax
import jax.numpy as jnp
from jax import lax
from jax.experimental import pallas as pl
from jax.experimental.pallas import tpu as pltpu
from jax.sharding import PartitionSpec as P

HD = 64
FF = 3072
STEP = 3


norm_eps = 1e-06
square_eps = 1e-30
clip_limit = 0.5
step_rate = 0.6
mask_fill = -1000000000.0


MESH = pl.DeviceIdType.MESH
HALO = 128
GROUPS = 3
CHUNKS = (0, 1, 3, 4, 6, 7, 2, 9, 5, 10, 8, 11)
BACK = tuple(CHUNKS.index(i) for i in range(12))


def moments_of(stream):
    center = stream - jnp.mean(stream, axis=-1, keepdims=True)
    spread = jnp.mean(center * center, axis=-1, keepdims=True)
    return (center, lax.rsqrt(spread + norm_eps))


def normalize(stream, gain_row, shift_row):
    center, inverse = moments_of(stream)
    return center * inverse * gain_row + shift_row


def segment_ids(counts, set_rows):
    image_ends = jnp.cumsum(counts)
    places = jnp.arange(set_rows, dtype=jnp.int32)
    return jnp.sum((places[:, None] >= image_ends[None, :]).astype(jnp.int32), axis=1)


def permute_chunks(block, order):
    parts = [block[..., HD * i : HD * (i + 1)] for i in order]
    return jnp.concatenate(parts, axis=-1)


def pack(qkv, out, up, down):
    first = jnp.concatenate([qkv[:, 0], qkv[:, 1], qkv[:, 2], out.T], axis=1)
    return jnp.stack([permute_chunks(first, CHUNKS), up, down.T])


def unpack(blocks):
    first = permute_chunks(blocks[0], BACK)
    width = first.shape[-1] // 4
    qkv = first[:, : 3 * width].reshape(first.shape[0], 3, width)
    return qkv, first[:, 3 * width :].T, blocks[1], blocks[2].T


def neighbours(dp):
    core = dp % 2
    return dp + 1 - 2 * core, dp + 2 - 4 * ((dp // 2) % 2), (dp + 4) % 8, (dp + 4) % 8 + 2 - 4 * ((dp // 2) % 2)


OFFSETS = 7


def offset_of(step):
    half = (step + 1) // 2
    return half * (1 - 2 * (step % 2))


def flip(dp):
    return dp + 1 - 2 * (dp % 2)


def greet(devices, extra):
    barrier = pltpu.get_barrier_semaphore()
    for device in devices:
        pl.semaphore_signal(barrier, inc=1, device_id=device, device_id_type=MESH)
    for condition, device in extra:

        @pl.when(condition)
        def _():
            pl.semaphore_signal(barrier, inc=1, device_id=device, device_id_type=MESH)

    peers = len(devices)
    for condition, _ in extra:
        peers = peers + jnp.where(condition, 1, 0)
    pl.semaphore_wait(barrier, peers)


A_Z, A_X, A_Y, A_D0, A_D1, A_S, A_SX, A_SY, A_SD0, A_SD1 = range(10)
KINDS = 10


def gather_kernel(n_mp, src, out, send_sems, recv_sems, up_sems, local_sem):
    dp, mp = lax.axis_index("dp"), lax.axis_index("mp")
    sib, xn, yn, dn = neighbours(dp)
    rows = src.shape[1]
    half = rows // 2
    up, down = jnp.minimum(mp + 1, n_mp - 1), jnp.maximum(mp - 1, 0)
    greet(
        [(sib, mp), (xn, mp), (yn, mp)], [(mp < n_mp - 1, (dp, up)), (mp > 0, (dp, down))]
    )
    top, low_half, high_half = pl.ds(0, rows), pl.ds(0, half), pl.ds(half, half)

    def message(kind, group, plane, slot, part, device, sems=None):
        where = out.at[group, plane, slot, part]
        return pltpu.make_async_remote_copy(
            src_ref=where,
            dst_ref=where,
            send_sem=(send_sems if sems is None else sems).at[group, plane, kind],
            recv_sem=recv_sems.at[group, plane, kind],
            device_id=device,
            device_id_type=MESH,
        )

    def z_message(group, plane, device, way):
        where = out.at[group, plane, dp]
        return pltpu.make_async_remote_copy(
            src_ref=where,
            dst_ref=where,
            send_sem=up_sems.at[group, plane, way],
            recv_sem=recv_sems.at[group, plane, A_Z],
            device_id=device,
            device_id_type=MESH,
        )

    own = pltpu.make_async_copy(src, out.at[:, mp, dp], local_sem)
    own.start()
    own.wait()

    def sends(stage, group, plane):
        if stage == 0:
            return [
                message(A_X, group, plane, dp, top, (xn, mp)),
                message(A_Y, group, plane, dp, top, (yn, mp)),
                message(A_S, group, plane, dp, top, (sib, mp)),
            ]
        if stage == 1:
            return [
                message(A_D0, group, plane, xn, low_half, (yn, mp)),
                message(A_SX, group, plane, xn, top, (sib, mp)),
            ]
        if stage == 2:
            return [
                message(A_D1, group, plane, yn, high_half, (xn, mp)),
                message(A_SY, group, plane, yn, top, (sib, mp)),
            ]
        if stage == 3:
            return [message(A_SD0, group, plane, dn, low_half, (sib, mp))]
        return [message(A_SD1, group, plane, dn, high_half, (sib, mp))]

    awaited = {
        1: (A_X, xn, top),
        2: (A_Y, yn, top),
        3: (A_D0, dn, low_half),
        4: (A_D1, dn, high_half),
    }

    def run(stage, step):
        group, offset = step // OFFSETS, offset_of(step % OFFSETS)
        plane = mp + offset

        @pl.when((step >= 0) & (step < GROUPS * OFFSETS) & (plane >= 0) & (plane < n_mp))
        def _():
            if stage == 0:

                @pl.when(offset != 0)
                def _():
                    z_message(group, plane, (dp, mp), 0).wait_recv()

                @pl.when((offset <= 0) & (mp < n_mp - 1))
                def _():
                    z_message(group, plane, (dp, up), 0).start()

                @pl.when((offset >= 0) & (mp > 0))
                def _():
                    z_message(group, plane, (dp, down), 1).start()
            else:
                kind, slot, part = awaited[stage]
                message(kind, group, plane, slot, part, (sib, mp)).wait_recv()
            for copy in sends(stage, group, plane):
                copy.start()

    lags = (0, 1, 1, 2, 2)

    def body(step, _):
        for stage in range(5):
            run(stage, step - lags[stage])
        return 0

    lax.fori_loop(0, GROUPS * OFFSETS + 2, body, 0)

    def finish(step, _):
        group, plane = step // n_mp, step % n_mp
        for kind, slot, part in (
            (A_S, sib, top),
            (A_SX, flip(xn), top),
            (A_SY, flip(yn), top),
            (A_SD0, flip(dn), low_half),
            (A_SD1, flip(dn), high_half),
        ):
            message(kind, group, plane, slot, part, (sib, mp)).wait_recv()
        for stage in range(5):
            for copy in sends(stage, group, plane):
                copy.wait_send()

        @pl.when((plane <= mp) & (mp < n_mp - 1))
        def _():
            z_message(group, plane, (dp, up), 0).wait_send()

        @pl.when((plane >= mp) & (mp > 0))
        def _():
            z_message(group, plane, (dp, down), 1).wait_send()

        return 0

    lax.fori_loop(0, GROUPS * n_mp, finish, 0)


def gather_all(blocks, n_dp, n_mp):
    groups, rows, width = blocks.shape
    if n_dp != 8 or rows % 32:
        wide = lax.all_gather(blocks, "dp", axis=1, tiled=True)
        return lax.all_gather(wide, "mp", axis=1)
    out = pl.pallas_call(
        functools.partial(gather_kernel, n_mp),
        out_shape=jax.ShapeDtypeStruct((groups, n_mp, n_dp, rows, width), blocks.dtype),
        in_specs=[pl.BlockSpec(memory_space=pl.ANY)],
        out_specs=pl.BlockSpec(memory_space=pl.ANY),
        scratch_shapes=[
            pltpu.SemaphoreType.DMA((groups, n_mp, KINDS)),
            pltpu.SemaphoreType.DMA((groups, n_mp, KINDS)),
            pltpu.SemaphoreType.DMA((groups, n_mp, 2)),
            pltpu.SemaphoreType.DMA,
        ],
        compiler_params=pltpu.CompilerParams(collective_id=1, has_side_effects=True),
    )(blocks)
    return out.reshape(groups, n_mp, n_dp * rows, width)


R_S, R_D0, R_D1, R_X, R_Y, R_UP, R_DOWN = range(7)


def scatter_kernel(
    n_mp, grads, out, pair_in, halves_in, x_in, y_in, z_in, mine, summed, load_sems, send_sems, recv_sems
):
    dp, mp = lax.axis_index("dp"), lax.axis_index("mp")
    sib, xn, yn, dn = neighbours(dp)
    core = dp % 2
    rows = out.shape[1]
    half = rows // 2
    here, at_x, at_y, at_d = dp // 2, xn // 2, yn // 2, dn // 2
    up, down = jnp.minimum(mp + 1, n_mp - 1), jnp.maximum(mp - 1, 0)
    greet(
        [(sib, mp), (xn, mp), (yn, mp)], [(mp < n_mp - 1, (dp, up)), (mp > 0, (dp, down))]
    )
    low_half, high_half = pl.ds(0, half), pl.ds(half, half)

    def remote(kind, group, plane, src, dst, device):
        return pltpu.make_async_remote_copy(
            src_ref=src,
            dst_ref=dst,
            send_sem=send_sems.at[group, plane, kind],
            recv_sem=recv_sems.at[group, plane, kind],
            device_id=device,
            device_id_type=MESH,
        )

    def messages(kind, group, plane):
        if kind == R_S:
            return remote(
                kind, group, plane, grads.at[group, plane, :, 1 - core], pair_in.at[group, plane], (sib, mp)
            )
        if kind == R_D0:
            return remote(
                kind, group, plane, mine.at[group, plane, at_d, low_half], halves_in.at[group, plane, 0], (xn, mp)
            )
        if kind == R_D1:
            return remote(
                kind, group, plane, mine.at[group, plane, at_d, high_half], halves_in.at[group, plane, 1], (yn, mp)
            )
        if kind == R_X:
            return remote(kind, group, plane, mine.at[group, plane, at_x], x_in.at[group, plane], (xn, mp))
        if kind == R_Y:
            return remote(kind, group, plane, mine.at[group, plane, at_y], y_in.at[group, plane], (yn, mp))
        if kind == R_UP:
            return remote(kind, group, plane, summed.at[group, plane], z_in.at[group, plane, 0], (dp, up))
        return remote(kind, group, plane, summed.at[group, plane], z_in.at[group, plane, 1], (dp, down))

    def load(group, plane):
        return pltpu.make_async_copy(
            grads.at[group, plane, :, core], mine.at[group, plane], load_sems.at[group, plane]
        )

    def run(stage, step):
        group, position = step // OFFSETS, step % OFFSETS
        offset = offset_of(OFFSETS - 1 - position)
        plane = mp + offset

        @pl.when((step >= 0) & (step < GROUPS * OFFSETS) & (plane >= 0) & (plane < n_mp))
        def _():
            if stage == 0:
                messages(R_S, group, plane).start()
                load(group, plane).start()
            elif stage == 1:
                messages(R_S, group, plane).wait_recv()
                load(group, plane).wait()
                mine[group, plane] = mine[group, plane] + pair_in[group, plane]
                messages(R_D0, group, plane).start()
                messages(R_D1, group, plane).start()
            elif stage == 2:
                messages(R_D0, group, plane).wait_recv()
                messages(R_D1, group, plane).wait_recv()
                mine[group, plane, at_y, low_half] = (
                    mine[group, plane, at_y, low_half] + halves_in[group, plane, 0]
                )
                mine[group, plane, at_x, high_half] = (
                    mine[group, plane, at_x, high_half] + halves_in[group, plane, 1]
                )
                messages(R_X, group, plane).start()
                messages(R_Y, group, plane).start()
            else:
                messages(R_X, group, plane).wait_recv()
                messages(R_Y, group, plane).wait_recv()
                total = (
                    mine[group, plane, here].astype(jnp.float32)
                    + x_in[group, plane].astype(jnp.float32)
                    + y_in[group, plane].astype(jnp.float32)
                )

                @pl.when(offset == 0)
                def _():
                    out[group] = total

                    @pl.when(mp > 0)
                    def _():
                        messages(R_UP, group, plane).wait_recv()
                        out[group] += z_in[group, plane, 0].astype(jnp.float32)

                    @pl.when(mp < n_mp - 1)
                    def _():
                        messages(R_DOWN, group, plane).wait_recv()
                        out[group] += z_in[group, plane, 1].astype(jnp.float32)

                @pl.when(offset > 0)
                def _():
                    @pl.when(mp > 0)
                    def _():
                        messages(R_UP, group, plane).wait_recv()
                        summed[group, plane] = (
                            total + z_in[group, plane, 0].astype(jnp.float32)
                        ).astype(jnp.bfloat16)

                    @pl.when(mp == 0)
                    def _():
                        summed[group, plane] = total.astype(jnp.bfloat16)

                    messages(R_UP, group, plane).start()

                @pl.when(offset < 0)
                def _():
                    @pl.when(mp < n_mp - 1)
                    def _():
                        messages(R_DOWN, group, plane).wait_recv()
                        summed[group, plane] = (
                            total + z_in[group, plane, 1].astype(jnp.float32)
                        ).astype(jnp.bfloat16)

                    @pl.when(mp == n_mp - 1)
                    def _():
                        summed[group, plane] = total.astype(jnp.bfloat16)

                    messages(R_DOWN, group, plane).start()

    lags = (0, 2, 4, 6)

    def body(step, _):
        for stage in range(4):
            run(stage, step - lags[stage])
        return 0

    lax.fori_loop(0, GROUPS * OFFSETS + lags[-1], body, 0)

    def finish(step, _):
        group, plane = step // n_mp, step % n_mp
        for kind in (R_S, R_D0, R_D1, R_X, R_Y):
            messages(kind, group, plane).wait_send()

        @pl.when(plane > mp)
        def _():
            messages(R_UP, group, plane).wait_send()

        @pl.when(plane < mp)
        def _():
            messages(R_DOWN, group, plane).wait_send()

        return 0

    lax.fori_loop(0, GROUPS * n_mp, finish, 0)


def scatter_sum(grads, n_dp, n_mp):
    groups, _, whole, width = grads.shape
    rows = whole // n_dp
    if n_dp != 8 or rows % 32:
        own = lax.psum_scatter(grads, "mp", scatter_dimension=1)
        return lax.psum_scatter(own, "dp", scatter_dimension=1, tiled=True).astype(jnp.float32)
    low = jnp.bfloat16
    return pl.pallas_call(
        functools.partial(scatter_kernel, n_mp),
        out_shape=jax.ShapeDtypeStruct((groups, rows, width), jnp.float32),
        in_specs=[pl.BlockSpec(memory_space=pl.ANY)],
        out_specs=pl.BlockSpec(memory_space=pltpu.VMEM),
        scratch_shapes=[
            pltpu.VMEM((groups, n_mp, 4, rows, width), low),
            pltpu.VMEM((groups, n_mp, 2, rows // 2, width), low),
            pltpu.VMEM((groups, n_mp, rows, width), low),
            pltpu.VMEM((groups, n_mp, rows, width), low),
            pltpu.VMEM((groups, n_mp, 2, rows, width), low),
            pltpu.VMEM((groups, n_mp, 4, rows, width), low),
            pltpu.VMEM((groups, n_mp, rows, width), low),
            pltpu.SemaphoreType.DMA((groups, n_mp)),
            pltpu.SemaphoreType.DMA((groups, n_mp, 7)),
            pltpu.SemaphoreType.DMA((groups, n_mp, 7)),
        ],
        compiler_params=pltpu.CompilerParams(
            collective_id=2, has_side_effects=True, vmem_limit_bytes=60 * 2**20
        ),
    )(grads.reshape(groups, n_mp, n_dp // 2, 2, rows, width))

def shard_offset(shard_piece, block_index, whole_length, axis_at):
    shape_list = list(shard_piece.shape)
    shape_list[axis_at] = whole_length
    empty = jnp.zeros(tuple(shape_list), jnp.float32)
    return lax.dynamic_update_slice_in_dim(
        empty, shard_piece, block_index * shard_piece.shape[axis_at], axis_at
    )


def select_slice(whole_array, block_index, block_width, axis_at):
    return lax.dynamic_slice_in_dim(whole_array, block_index * block_width, block_width, axis_at)


def factor_step(
    gradient,
    rows_old,
    cols_old,
    rows_mine,
    cols_mine,
    rows_total,
    count_rows,
    count_cols,
    prior_total,
):
    decay_rate = 1.0 - STEP ** (-0.8)
    rows_new = decay_rate * rows_old + (1.0 - decay_rate) * (rows_mine / count_cols + square_eps)
    cols_new = decay_rate * cols_old + (1.0 - decay_rate) * (cols_mine / count_rows + square_eps)
    rows_average = (
        decay_rate * prior_total
        + (1.0 - decay_rate) * (rows_total / count_cols + count_rows * square_eps)
    ) / count_rows
    update = gradient * lax.rsqrt(rows_new[:, None] * cols_new[None, :] / rows_average)
    return (rows_new, cols_new, update, jnp.sum(update * update))


def plain_step(weight, gradient, moment_old):
    decay_rate = 1.0 - STEP ** (-0.8)
    moment = decay_rate * moment_old + (1.0 - decay_rate) * (gradient * gradient + square_eps)
    update = gradient * lax.rsqrt(moment)
    update_rms = jnp.sqrt(jnp.mean(update * update))
    rate_here = step_rate * jnp.sqrt(jnp.mean(weight * weight))
    return (weight - rate_here * update / jnp.maximum(1.0, update_rms / clip_limit), moment)


def shards(
    tokens_in,
    cotangent,
    patch_counts,
    w_qkv,
    w_out,
    w_up,
    w_down,
    layer_vector_rows,
    inner_biases,
    qkvrows_prior,
    qkvcols_prior,
    outrows_prior,
    outcols_prior,
    uprows_prior,
    upcols_prior,
    downrows_prior,
    downcols_prior,
    vector_moment,
    bias_moment,
):
    data_index = lax.axis_index("dp")
    parallel_model_index = lax.axis_index("mp")
    n_dp, n_mp = lax.axis_size("dp"), lax.axis_size("mp")
    row_count, parallel_model_width = tokens_in.shape
    set_count, slot_count = patch_counts.shape
    set_rows = row_count // set_count
    own_rows = row_count // n_mp
    shard_width_local = w_qkv.shape[2]
    local_hidden = w_up.shape[1]
    heads = parallel_model_width // HD
    score_scale = HD ** (-0.5)
    f32, low = jnp.float32, jnp.bfloat16
    blocks = pack(w_qkv, w_out, w_up, w_down)
    gathered = gather_all(blocks.astype(low), n_dp, n_mp)

    per_set = set_rows // own_rows
    set_index, part_index = parallel_model_index // per_set, parallel_model_index % per_set
    window = own_rows + HALO
    window_start = part_index * (set_rows - window)
    own_start = part_index * (window - own_rows)

    def of_set(rows_in):
        return lax.dynamic_slice_in_dim(rows_in, set_index * set_rows, set_rows, 0)

    def of_window(rows_in):
        return lax.dynamic_slice_in_dim(rows_in, window_start, window, 0)

    def own(rows_in):
        return lax.dynamic_slice_in_dim(rows_in, own_start, own_rows, 0)

    vec = layer_vector_rows
    segment_set = segment_ids(
        lax.dynamic_slice_in_dim(patch_counts, set_index, 1, 0)[0], set_rows
    )
    segment = of_window(segment_set)
    valid = (segment < slot_count).astype(f32)[:, None]
    stream_set = of_set(tokens_in).astype(f32)
    stream = of_window(stream_set)
    cot = of_window(of_set(cotangent)).astype(f32)

    first = permute_chunks(gathered[0], BACK)
    width = shard_width_local
    w_q, w_k, w_v, w_ot = [
        first[:, :, i * width : (i + 1) * width].transpose(1, 0, 2).reshape(parallel_model_width, -1)
        for i in range(4)
    ]
    w_u = gathered[1].transpose(1, 0, 2).reshape(parallel_model_width, -1)
    w_dt = gathered[2].transpose(1, 0, 2).reshape(parallel_model_width, -1)

    def mm(a, b, dims):
        return lax.dot_general(a, b, (dims, ((), ())), preferred_element_type=f32)

    nn, nt, tn = ((1,), (0,)), ((1,), (1,)), ((0,), (0,))
    normed_set = normalize(stream_set, vec[0], vec[1]).astype(low)
    normed = of_window(normed_set)
    query = (mm(normed, w_q, nn) + inner_biases[0]).astype(low)
    key = mm(normed_set, w_k, nn).astype(low)
    value = (mm(normed_set, w_v, nn) + inner_biases[1]).astype(low)

    def split(rows_in):
        return rows_in.reshape(rows_in.shape[0], heads, HD)

    def scores_of(query_rows, key_rows, same):
        raw = jnp.einsum("qhd,khd->hqk", split(query_rows), split(key_rows), preferred_element_type=f32)
        return jnp.where(same[None], raw * score_scale, mask_fill)

    scores = scores_of(query, key, segment[:, None] == segment_set[None, :])
    weights = jax.nn.softmax(scores, axis=-1).astype(low)
    mixed = jnp.einsum("hqk,khd->qhd", weights, split(value), preferred_element_type=f32)
    mixed = mixed.astype(low).reshape(window, parallel_model_width)
    proj = mm(mixed, w_ot, nt) + vec[6]
    middle = stream + vec[4] * proj
    normed_two = normalize(middle, vec[2], vec[3]).astype(low)
    up_bias = inner_biases[2:].T.reshape(-1)
    hidden = mm(normed_two, w_u, nn) + up_bias
    active, gelu_pull = jax.vjp(lambda t: jax.nn.gelu(t, approximate=False), hidden)
    active = active.astype(low)
    active_own = own(active)
    branch = mm(active_own, w_dt, nt) + vec[7]
    proj_own, middle_own = own(proj), own(middle)
    result = middle_own + vec[5] * branch

    back = cot * valid
    d_branch = (back * vec[5]).astype(low)
    d_active = mm(d_branch, w_dt, nn)
    d_hidden = gelu_pull(d_active)[0].astype(low)
    d_normed_two = mm(d_hidden, w_u, nt)

    def norm_back(stream_in, gain, grad):
        center, inverse = moments_of(stream_in)
        unit = center * inverse
        e = grad * gain
        dv = inverse * (
            e - jnp.mean(e, axis=-1, keepdims=True) - unit * jnp.mean(e * unit, axis=-1, keepdims=True)
        )
        return dv, unit

    dv_two, unit_two = norm_back(middle, vec[2], d_normed_two)
    d_middle = back + dv_two
    d_proj = (d_middle * vec[4]).astype(low)
    d_mixed = mm(d_proj, w_ot, nn).astype(low)

    key_w, value_w = of_window(key), of_window(value)
    scores = scores_of(query, key_w, segment[:, None] == segment[None, :])
    attn = jax.nn.softmax(scores, axis=-1)
    d_value = jnp.einsum("hqk,qhd->khd", attn.astype(low), split(d_mixed), preferred_element_type=f32)
    d_attn = jnp.einsum("qhd,khd->hqk", split(d_mixed), split(value_w), preferred_element_type=f32)
    d_scores = (attn * (d_attn - jnp.sum(d_attn * attn, axis=-1, keepdims=True))).astype(low)
    d_query = jnp.einsum("hqk,khd->qhd", d_scores, split(key_w), preferred_element_type=f32) * score_scale
    d_key = jnp.einsum("hqk,qhd->khd", d_scores, split(query), preferred_element_type=f32) * score_scale

    def joined(heads_in):
        return own(heads_in.astype(low).reshape(window, parallel_model_width))

    d_query, d_key, d_value = joined(d_query), joined(d_key), joined(d_value)
    d_normed = mm(d_query, w_q, nt) + mm(d_key, w_k, nt) + mm(d_value, w_v, nt)
    normed_own, normed_two_own = own(normed), own(normed_two)
    d_branch_own, d_hidden_own, d_proj_own = own(d_branch), own(d_hidden), own(d_proj)
    d_middle_own, back_own = own(d_middle), own(back)
    dv_one, unit_one = norm_back(own(stream), vec[0], d_normed)
    input_rows = d_middle_own + dv_one

    def by_mp(columns):
        return columns.reshape(parallel_model_width, n_mp, -1).transpose(1, 0, 2)

    mixed_own = own(mixed)
    grads = jnp.stack(
        [
            permute_chunks(
                jnp.concatenate(
                    [
                        by_mp(mm(normed_own, d_query, tn)),
                        by_mp(mm(normed_own, d_key, tn)),
                        by_mp(mm(normed_own, d_value, tn)),
                        by_mp(mm(d_proj_own, mixed_own, tn)),
                    ],
                    axis=2,
                ),
                CHUNKS,
            ),
            by_mp(mm(normed_two_own, d_hidden_own, tn)),
            by_mp(mm(d_branch_own, active_own, tn)),
        ]
    ).astype(low)
    reduced = scatter_sum(grads, n_dp, n_mp)

    result_low = lax.all_gather(result.astype(low), "mp", axis=0, tiled=True)
    input_grad = lax.all_to_all(input_rows.astype(low), "mp", 1, 0, tiled=True).astype(f32)

    def sums(rows_in):
        return jnp.sum(rows_in.astype(f32), axis=0)

    d_normed_two_own = own(d_normed_two)
    vector_part = jnp.stack(
        [
            sums(d_normed * unit_one),
            sums(d_normed),
            sums(d_normed_two_own * own(unit_two)),
            sums(d_normed_two_own),
            sums(d_middle_own * proj_own),
            sums(back_own * branch),
            sums(d_proj_own),
            sums(d_branch_own),
        ]
    )
    hidden_sums = sums(d_hidden_own).reshape(parallel_model_width, -1).T
    bias_part = jnp.concatenate([sums(d_query)[None], sums(d_value)[None], hidden_sums], axis=0)
    valid_own = own(valid)
    squares = jnp.stack(
        [
            jnp.sum(valid_own * field_in * field_in)
            for field_in in (result, vec[4] * proj_own, vec[5] * branch)
        ]
    )
    vector_grad, bias_grad, squares_all, counted_all = lax.psum(
        (vector_part, bias_part, squares, jnp.sum(valid_own)), ("dp", "mp")
    )
    token_spread = jnp.sqrt(squares_all / (counted_all * parallel_model_width))
    qkv_grad, out_grad, up_grad, down_grad = unpack(reduced)
    square_qkv = qkv_grad * qkv_grad
    square_out = out_grad * out_grad
    square_up = up_grad * up_grad
    square_down = down_grad * down_grad
    scalars = jnp.stack(
        [
            jnp.sum(w_qkv * w_qkv),
            jnp.sum(w_out * w_out),
            jnp.sum(w_up * w_up),
            jnp.sum(w_down * w_down),
            jnp.where(parallel_model_index == 0, jnp.sum(qkvrows_prior), 0.0),
            jnp.where(data_index == 0, jnp.sum(outrows_prior), 0.0),
            jnp.where(parallel_model_index == 0, jnp.sum(uprows_prior), 0.0),
            jnp.where(data_index == 0, jnp.sum(downrows_prior), 0.0),
        ]
    )
    factor_totals = lax.psum(
        (
            shard_offset(jnp.sum(square_qkv, axis=(1, 2)), data_index, parallel_model_width, 0),
            shard_offset(
                jnp.sum(square_qkv, axis=0), parallel_model_index, parallel_model_width, 1
            ),
            shard_offset(
                jnp.sum(square_out, axis=1), parallel_model_index, parallel_model_width, 0
            ),
            shard_offset(jnp.sum(square_out, axis=0), data_index, parallel_model_width, 0),
            shard_offset(jnp.sum(square_up, axis=1), data_index, parallel_model_width, 0),
            shard_offset(jnp.sum(square_up, axis=0), parallel_model_index, FF, 0),
            shard_offset(jnp.sum(square_down, axis=1), parallel_model_index, FF, 0),
            shard_offset(jnp.sum(square_down, axis=0), data_index, parallel_model_width, 0),
            scalars,
        ),
        ("dp", "mp"),
    )
    (
        rows_qkv,
        cols_qkv,
        rows_out,
        cols_out,
        rows_up,
        cols_up,
        rows_down,
        cols_down,
        scalar_totals,
    ) = factor_totals
    local_rows = w_qkv.shape[0]
    local_cols = w_out.shape[1]
    qkvrows_after, qkvcols_flat, update_qkv, usq_qkv = factor_step(
        qkv_grad.reshape(local_rows, 3 * shard_width_local),
        qkvrows_prior,
        qkvcols_prior.reshape(3 * shard_width_local),
        select_slice(rows_qkv, data_index, local_rows, 0),
        select_slice(cols_qkv, parallel_model_index, shard_width_local, 1).reshape(
            3 * shard_width_local
        ),
        jnp.sum(rows_qkv),
        parallel_model_width,
        3 * parallel_model_width,
        scalar_totals[4],
    )
    outrows_after, outcols_after, update_out, usq_out = factor_step(
        out_grad,
        outrows_prior,
        outcols_prior,
        select_slice(rows_out, parallel_model_index, shard_width_local, 0),
        select_slice(cols_out, data_index, local_cols, 0),
        jnp.sum(rows_out),
        parallel_model_width,
        parallel_model_width,
        scalar_totals[5],
    )
    uprows_after, upcols_after, update_up, usq_up = factor_step(
        up_grad,
        uprows_prior,
        upcols_prior,
        select_slice(rows_up, data_index, local_rows, 0),
        select_slice(cols_up, parallel_model_index, local_hidden, 0),
        jnp.sum(rows_up),
        parallel_model_width,
        FF,
        scalar_totals[6],
    )
    downrows_after, downcols_after, update_down, usq_down = factor_step(
        down_grad,
        downrows_prior,
        downcols_prior,
        select_slice(rows_down, parallel_model_index, local_hidden, 0),
        select_slice(cols_down, data_index, local_cols, 0),
        jnp.sum(rows_down),
        FF,
        parallel_model_width,
        scalar_totals[7],
    )
    usq_totals = lax.psum(jnp.stack([usq_qkv, usq_out, usq_up, usq_down]), ("dp", "mp"))
    entry_counts = jnp.array(
        [
            3.0 * parallel_model_width * parallel_model_width,
            1.0 * parallel_model_width * parallel_model_width,
            1.0 * parallel_model_width * FF,
            1.0 * FF * parallel_model_width,
        ],
        jnp.float32,
    )
    update_scale = jnp.sqrt(usq_totals / entry_counts)
    weight_rms = jnp.sqrt(scalar_totals[:4] / entry_counts)
    limits = jnp.maximum(1.0, update_scale / clip_limit)
    qkv_after = (
        w_qkv.reshape(local_rows, 3 * shard_width_local)
        - step_rate * weight_rms[0] * update_qkv / limits[0]
    ).reshape(w_qkv.shape)
    out_after = w_out - step_rate * weight_rms[1] * update_out / limits[1]
    up_after = w_up - step_rate * weight_rms[2] * update_up / limits[2]
    down_after = w_down - step_rate * weight_rms[3] * update_down / limits[3]
    vectors_after, moment_vectors = jax.vmap(plain_step)(
        layer_vector_rows, vector_grad, vector_moment
    )
    heads_after, heads_moment = jax.vmap(plain_step)(
        inner_biases[:2], bias_grad[:2], bias_moment[:2]
    )
    upper_after, upper_moment = plain_step(
        inner_biases[2:].reshape(FF), bias_grad[2:].reshape(FF), bias_moment[2:].reshape(FF)
    )
    biases_after = jnp.concatenate(
        [heads_after, upper_after.reshape(FF // parallel_model_width, parallel_model_width)], axis=0
    )
    moment_biases = jnp.concatenate(
        [heads_moment, upper_moment.reshape(FF // parallel_model_width, parallel_model_width)],
        axis=0,
    )
    return (
        result_low,
        input_grad,
        qkv_grad,
        out_grad,
        up_grad,
        down_grad,
        qkv_after,
        out_after,
        up_after,
        down_after,
        qkv_after.astype(jnp.bfloat16),
        out_after.astype(jnp.bfloat16),
        up_after.astype(jnp.bfloat16),
        down_after.astype(jnp.bfloat16),
        qkvrows_after,
        qkvcols_flat.reshape(3, shard_width_local),
        outrows_after,
        outcols_after,
        uprows_after,
        upcols_after,
        downrows_after,
        downcols_after,
        vector_grad,
        bias_grad,
        moment_vectors,
        moment_biases,
        vectors_after,
        biases_after,
        update_scale,
        token_spread,
    )


def solution(mesh):
    in_specs = (
        P("dp", None),
        P("dp", None),
        P("dp", None),
        P("dp", None, "mp"),
        P("mp", "dp"),
        P("dp", "mp"),
        P("mp", "dp"),
        P(),
        P(),
        P("dp"),
        P(None, "mp"),
        P("mp"),
        P("dp"),
        P("dp"),
        P("mp"),
        P("mp"),
        P("dp"),
        P(),
        P(),
    )
    out_specs = (
        P("dp", None),
        P("dp", "mp"),
        P("dp", None, "mp"),
        P("mp", "dp"),
        P("dp", "mp"),
        P("mp", "dp"),
        P("dp", None, "mp"),
        P("mp", "dp"),
        P("dp", "mp"),
        P("mp", "dp"),
        P("dp", None, "mp"),
        P("mp", "dp"),
        P("dp", "mp"),
        P("mp", "dp"),
        P("dp"),
        P(None, "mp"),
        P("mp"),
        P("dp"),
        P("dp"),
        P("mp"),
        P("mp"),
        P("dp"),
        P(),
        P(),
        P(),
        P(),
        P(),
        P(),
        P(),
        P(),
    )
    return jax.shard_map(shards, mesh=mesh, in_specs=in_specs, out_specs=out_specs, check_vma=False)
```

```python
import functools

import jax
import jax.numpy as jnp
from jax import lax
from jax.experimental import pallas as pl
from jax.experimental.pallas import tpu as pltpu
from jax.sharding import PartitionSpec as P

HD = 64
FF = 3072
STEP = 3


norm_eps = 1e-06
square_eps = 1e-30
clip_limit = 0.5
step_rate = 0.6
mask_fill = -1000000000.0


MESH = pl.DeviceIdType.MESH
HALO = 128
GROUPS = 3
CHUNKS = (0, 1, 3, 4, 6, 7, 9, 10, 2, 11, 5, 8)
BACK = tuple(CHUNKS.index(i) for i in range(12))


def moments_of(stream):
    center = stream - jnp.mean(stream, axis=-1, keepdims=True)
    spread = jnp.mean(center * center, axis=-1, keepdims=True)
    return (center, lax.rsqrt(spread + norm_eps))


def normalize(stream, gain_row, shift_row):
    center, inverse = moments_of(stream)
    return center * inverse * gain_row + shift_row


def segment_ids(counts, set_rows):
    image_ends = jnp.cumsum(counts)
    places = jnp.arange(set_rows, dtype=jnp.int32)
    return jnp.sum((places[:, None] >= image_ends[None, :]).astype(jnp.int32), axis=1)


def permute_chunks(block, order):
    parts = [block[..., HD * i : HD * (i + 1)] for i in order]
    return jnp.concatenate(parts, axis=-1)


def pack(qkv, out, up, down):
    first = jnp.concatenate([qkv[:, 0], qkv[:, 1], qkv[:, 2], out.T], axis=1)
    return jnp.stack([permute_chunks(first, CHUNKS), up, down.T])


def unpack(blocks):
    first = permute_chunks(blocks[0], BACK)
    width = first.shape[-1] // 4
    qkv = first[:, : 3 * width].reshape(first.shape[0], 3, width)
    return qkv, first[:, 3 * width :].T, blocks[1], blocks[2].T


def neighbours(dp):
    core = dp % 2
    return dp + 1 - 2 * core, dp + 2 - 4 * ((dp // 2) % 2), (dp + 4) % 8, (dp + 4) % 8 + 2 - 4 * ((dp // 2) % 2)


OFFSETS = 7


def offset_of(step):
    half = (step + 1) // 2
    return half * (1 - 2 * (step % 2))


def flip(dp):
    return dp + 1 - 2 * (dp % 2)


def greet(devices, extra):
    barrier = pltpu.get_barrier_semaphore()
    for device in devices:
        pl.semaphore_signal(barrier, inc=1, device_id=device, device_id_type=MESH)
    for condition, device in extra:

        @pl.when(condition)
        def _():
            pl.semaphore_signal(barrier, inc=1, device_id=device, device_id_type=MESH)

    peers = len(devices)
    for condition, _ in extra:
        peers = peers + jnp.where(condition, 1, 0)
    pl.semaphore_wait(barrier, peers)


A_Z, A_X, A_Y, A_D0, A_D1, A_S, A_SX, A_SY, A_SD0, A_SD1 = range(10)
KINDS = 10


def gather_kernel(n_mp, src, out, send_sems, recv_sems, up_sems, local_sem):
    dp, mp = lax.axis_index("dp"), lax.axis_index("mp")
    sib, xn, yn, dn = neighbours(dp)
    rows = src.shape[1]
    half = rows // 2
    up, down = jnp.minimum(mp + 1, n_mp - 1), jnp.maximum(mp - 1, 0)
    greet(
        [(sib, mp), (xn, mp), (yn, mp)], [(mp < n_mp - 1, (dp, up)), (mp > 0, (dp, down))]
    )
    top, low_half, high_half = pl.ds(0, rows), pl.ds(0, half), pl.ds(half, half)

    def message(kind, group, plane, slot, part, device, sems=None):
        where = out.at[group, plane, slot, part]
        return pltpu.make_async_remote_copy(
            src_ref=where,
            dst_ref=where,
            send_sem=(send_sems if sems is None else sems).at[group, plane, kind],
            recv_sem=recv_sems.at[group, plane, kind],
            device_id=device,
            device_id_type=MESH,
        )

    def z_message(group, plane, device, way):
        where = out.at[group, plane, dp]
        return pltpu.make_async_remote_copy(
            src_ref=where,
            dst_ref=where,
            send_sem=up_sems.at[group, plane, way],
            recv_sem=recv_sems.at[group, plane, A_Z],
            device_id=device,
            device_id_type=MESH,
        )

    own = pltpu.make_async_copy(src, out.at[:, mp, dp], local_sem)
    own.start()
    own.wait()

    def sends(stage, group, plane):
        if stage == 0:
            return [
                message(A_X, group, plane, dp, top, (xn, mp)),
                message(A_Y, group, plane, dp, top, (yn, mp)),
                message(A_S, group, plane, dp, top, (sib, mp)),
            ]
        if stage == 1:
            return [
                message(A_D0, group, plane, xn, low_half, (yn, mp)),
                message(A_SX, group, plane, xn, top, (sib, mp)),
            ]
        if stage == 2:
            return [
                message(A_D1, group, plane, yn, high_half, (xn, mp)),
                message(A_SY, group, plane, yn, top, (sib, mp)),
            ]
        if stage == 3:
            return [message(A_SD0, group, plane, dn, low_half, (sib, mp))]
        return [message(A_SD1, group, plane, dn, high_half, (sib, mp))]

    awaited = {
        1: (A_X, xn, top),
        2: (A_Y, yn, top),
        3: (A_D0, dn, low_half),
        4: (A_D1, dn, high_half),
    }

    def run(stage, step):
        group, offset = step // OFFSETS, offset_of(step % OFFSETS)
        plane = mp + offset

        @pl.when((step >= 0) & (step < GROUPS * OFFSETS) & (plane >= 0) & (plane < n_mp))
        def _():
            if stage == 0:

                @pl.when(offset != 0)
                def _():
                    z_message(group, plane, (dp, mp), 0).wait_recv()

                @pl.when((offset <= 0) & (mp < n_mp - 1))
                def _():
                    z_message(group, plane, (dp, up), 0).start()

                @pl.when((offset >= 0) & (mp > 0))
                def _():
                    z_message(group, plane, (dp, down), 1).start()
            else:
                kind, slot, part = awaited[stage]
                message(kind, group, plane, slot, part, (sib, mp)).wait_recv()
            for copy in sends(stage, group, plane):
                copy.start()

    lags = (0, 1, 1, 2, 2)

    def body(step, _):
        for stage in range(5):
            run(stage, step - lags[stage])
        return 0

    lax.fori_loop(0, GROUPS * OFFSETS + 2, body, 0)

    def finish(step, _):
        group, plane = step // n_mp, step % n_mp
        for kind, slot, part in (
            (A_S, sib, top),
            (A_SX, flip(xn), top),
            (A_SY, flip(yn), top),
            (A_SD0, flip(dn), low_half),
            (A_SD1, flip(dn), high_half),
        ):
            message(kind, group, plane, slot, part, (sib, mp)).wait_recv()
        for stage in range(5):
            for copy in sends(stage, group, plane):
                copy.wait_send()

        @pl.when((plane <= mp) & (mp < n_mp - 1))
        def _():
            z_message(group, plane, (dp, up), 0).wait_send()

        @pl.when((plane >= mp) & (mp > 0))
        def _():
            z_message(group, plane, (dp, down), 1).wait_send()

        return 0

    lax.fori_loop(0, GROUPS * n_mp, finish, 0)


def gather_all(blocks, n_dp, n_mp):
    groups, rows, width = blocks.shape
    if n_dp != 8 or rows % 32:
        wide = lax.all_gather(blocks, "dp", axis=1, tiled=True)
        return lax.all_gather(wide, "mp", axis=1)
    out = pl.pallas_call(
        functools.partial(gather_kernel, n_mp),
        out_shape=jax.ShapeDtypeStruct((groups, n_mp, n_dp, rows, width), blocks.dtype),
        in_specs=[pl.BlockSpec(memory_space=pl.ANY)],
        out_specs=pl.BlockSpec(memory_space=pl.ANY),
        scratch_shapes=[
            pltpu.SemaphoreType.DMA((groups, n_mp, KINDS)),
            pltpu.SemaphoreType.DMA((groups, n_mp, KINDS)),
            pltpu.SemaphoreType.DMA((groups, n_mp, 2)),
            pltpu.SemaphoreType.DMA,
        ],
        compiler_params=pltpu.CompilerParams(collective_id=1, has_side_effects=True),
    )(blocks)
    return out.reshape(groups, n_mp, n_dp * rows, width)


R_S, R_D0, R_D1, R_X, R_Y, R_UP, R_DOWN = range(7)


def scatter_kernel(
    n_mp, grads, out, pair_in, halves_in, x_in, y_in, z_in, mine, summed, load_sems, send_sems, recv_sems
):
    dp, mp = lax.axis_index("dp"), lax.axis_index("mp")
    sib, xn, yn, dn = neighbours(dp)
    core = dp % 2
    rows = out.shape[1]
    half = rows // 2
    here, at_x, at_y, at_d = dp // 2, xn // 2, yn // 2, dn // 2
    up, down = jnp.minimum(mp + 1, n_mp - 1), jnp.maximum(mp - 1, 0)
    greet(
        [(sib, mp), (xn, mp), (yn, mp)], [(mp < n_mp - 1, (dp, up)), (mp > 0, (dp, down))]
    )
    low_half, high_half = pl.ds(0, half), pl.ds(half, half)

    def remote(kind, group, plane, src, dst, device):
        return pltpu.make_async_remote_copy(
            src_ref=src,
            dst_ref=dst,
            send_sem=send_sems.at[group, plane, kind],
            recv_sem=recv_sems.at[group, plane, kind],
            device_id=device,
            device_id_type=MESH,
        )

    def messages(kind, group, plane):
        if kind == R_S:
            return remote(
                kind, group, plane, grads.at[group, plane, :, 1 - core], pair_in.at[group, plane], (sib, mp)
            )
        if kind == R_D0:
            return remote(
                kind, group, plane, mine.at[group, plane, at_d, low_half], halves_in.at[group, plane, 0], (xn, mp)
            )
        if kind == R_D1:
            return remote(
                kind, group, plane, mine.at[group, plane, at_d, high_half], halves_in.at[group, plane, 1], (yn, mp)
            )
        if kind == R_X:
            return remote(kind, group, plane, mine.at[group, plane, at_x], x_in.at[group, plane], (xn, mp))
        if kind == R_Y:
            return remote(kind, group, plane, mine.at[group, plane, at_y], y_in.at[group, plane], (yn, mp))
        if kind == R_UP:
            return remote(kind, group, plane, summed.at[group, plane], z_in.at[group, plane, 0], (dp, up))
        return remote(kind, group, plane, summed.at[group, plane], z_in.at[group, plane, 1], (dp, down))

    def load(group, plane):
        return pltpu.make_async_copy(
            grads.at[group, plane, :, core], mine.at[group, plane], load_sems.at[group, plane]
        )

    def run(stage, step):
        group, position = step // OFFSETS, step % OFFSETS
        offset = offset_of(OFFSETS - 1 - position)
        plane = mp + offset

        @pl.when((step >= 0) & (step < GROUPS * OFFSETS) & (plane >= 0) & (plane < n_mp))
        def _():
            if stage == 0:
                messages(R_S, group, plane).start()
                load(group, plane).start()
            elif stage == 1:
                messages(R_S, group, plane).wait_recv()
                load(group, plane).wait()
                mine[group, plane] = mine[group, plane] + pair_in[group, plane]
                messages(R_D0, group, plane).start()
                messages(R_D1, group, plane).start()
            elif stage == 2:
                messages(R_D0, group, plane).wait_recv()
                messages(R_D1, group, plane).wait_recv()
                mine[group, plane, at_y, low_half] = (
                    mine[group, plane, at_y, low_half] + halves_in[group, plane, 0]
                )
                mine[group, plane, at_x, high_half] = (
                    mine[group, plane, at_x, high_half] + halves_in[group, plane, 1]
                )
                messages(R_X, group, plane).start()
                messages(R_Y, group, plane).start()
            else:
                messages(R_X, group, plane).wait_recv()
                messages(R_Y, group, plane).wait_recv()
                total = (
                    mine[group, plane, here].astype(jnp.float32)
                    + x_in[group, plane].astype(jnp.float32)
                    + y_in[group, plane].astype(jnp.float32)
                )

                @pl.when(offset == 0)
                def _():
                    out[group] = total

                    @pl.when(mp > 0)
                    def _():
                        messages(R_UP, group, plane).wait_recv()
                        out[group] += z_in[group, plane, 0].astype(jnp.float32)

                    @pl.when(mp < n_mp - 1)
                    def _():
                        messages(R_DOWN, group, plane).wait_recv()
                        out[group] += z_in[group, plane, 1].astype(jnp.float32)

                @pl.when(offset > 0)
                def _():
                    @pl.when(mp > 0)
                    def _():
                        messages(R_UP, group, plane).wait_recv()
                        summed[group, plane] = (
                            total + z_in[group, plane, 0].astype(jnp.float32)
                        ).astype(jnp.bfloat16)

                    @pl.when(mp == 0)
                    def _():
                        summed[group, plane] = total.astype(jnp.bfloat16)

                    messages(R_UP, group, plane).start()

                @pl.when(offset < 0)
                def _():
                    @pl.when(mp < n_mp - 1)
                    def _():
                        messages(R_DOWN, group, plane).wait_recv()
                        summed[group, plane] = (
                            total + z_in[group, plane, 1].astype(jnp.float32)
                        ).astype(jnp.bfloat16)

                    @pl.when(mp == n_mp - 1)
                    def _():
                        summed[group, plane] = total.astype(jnp.bfloat16)

                    messages(R_DOWN, group, plane).start()

    lags = (0, 2, 4, 6)

    def body(step, _):
        for stage in range(4):
            run(stage, step - lags[stage])
        return 0

    lax.fori_loop(0, GROUPS * OFFSETS + lags[-1], body, 0)

    def finish(step, _):
        group, plane = step // n_mp, step % n_mp
        for kind in (R_S, R_D0, R_D1, R_X, R_Y):
            messages(kind, group, plane).wait_send()

        @pl.when(plane > mp)
        def _():
            messages(R_UP, group, plane).wait_send()

        @pl.when(plane < mp)
        def _():
            messages(R_DOWN, group, plane).wait_send()

        return 0

    lax.fori_loop(0, GROUPS * n_mp, finish, 0)


def scatter_sum(grads, n_dp, n_mp):
    groups, _, whole, width = grads.shape
    rows = whole // n_dp
    if n_dp != 8 or rows % 32:
        own = lax.psum_scatter(grads, "mp", scatter_dimension=1)
        return lax.psum_scatter(own, "dp", scatter_dimension=1, tiled=True).astype(jnp.float32)
    low = jnp.bfloat16
    return pl.pallas_call(
        functools.partial(scatter_kernel, n_mp),
        out_shape=jax.ShapeDtypeStruct((groups, rows, width), jnp.float32),
        in_specs=[pl.BlockSpec(memory_space=pl.ANY)],
        out_specs=pl.BlockSpec(memory_space=pltpu.VMEM),
        scratch_shapes=[
            pltpu.VMEM((groups, n_mp, 4, rows, width), low),
            pltpu.VMEM((groups, n_mp, 2, rows // 2, width), low),
            pltpu.VMEM((groups, n_mp, rows, width), low),
            pltpu.VMEM((groups, n_mp, rows, width), low),
            pltpu.VMEM((groups, n_mp, 2, rows, width), low),
            pltpu.VMEM((groups, n_mp, 4, rows, width), low),
            pltpu.VMEM((groups, n_mp, rows, width), low),
            pltpu.SemaphoreType.DMA((groups, n_mp)),
            pltpu.SemaphoreType.DMA((groups, n_mp, 7)),
            pltpu.SemaphoreType.DMA((groups, n_mp, 7)),
        ],
        compiler_params=pltpu.CompilerParams(
            collective_id=2, has_side_effects=True, vmem_limit_bytes=60 * 2**20
        ),
    )(grads.reshape(groups, n_mp, n_dp // 2, 2, rows, width))

LANES = 128
NN = (((1,), (0,)), ((), ()))
NT = (((1,), (1,)), ((), ()))
BIG = 2.0**36


def mm(left, right, dims=NN):
    return lax.dot_general(left, right, dims, preferred_element_type=jnp.float32)


def gelu_parts(t):
    k = 1.0 / (1.0 + 0.2316419 * jnp.abs(t))
    series = k * (
        0.319381530 + k * (-0.356563782 + k * (1.781477937 + k * (-1.821255978 + k * 1.330274429)))
    )
    density = 0.3989422804014327 * jnp.exp(-0.5 * t * t)
    tail = density * series
    phi = jnp.where(t >= 0.0, 1.0 - tail, tail)
    return t * phi, phi + t * density


def row_stats(x):
    width = x.shape[1]
    center = x - jnp.sum(x, axis=1, keepdims=True) * (1.0 / width)
    spread = jnp.sum(center * center, axis=1, keepdims=True) * (1.0 / width)
    inverse = lax.rsqrt(spread + norm_eps)
    return center * inverse, inverse


def image_ends(counts_ref, set_index, slots):
    lane = lax.broadcasted_iota(jnp.int32, (8, LANES), 1) % (LANES // 2)
    low = jnp.zeros((8, LANES), jnp.int32)
    high = jnp.zeros((8, LANES), jnp.int32)
    edge = jnp.int32(0)
    for slot in range(slots + 1):
        after = jnp.int32(1 << 20) if slot == slots else edge + counts_ref[set_index, slot]
        low = jnp.where(lane == slot, edge, low)
        high = jnp.where(lane == slot, after, high)
        edge = after if slot < slots else edge
    return low[0:1], high[0:1], edge


def own_row(hidden_half, tile):
    lane = lax.broadcasted_iota(jnp.int32, tile.shape, 1)
    return (lane < LANES // 2) if hidden_half == 0 else (lane >= LANES // 2)


def keep_half(half, tile, other):
    return jnp.where(own_row(half, tile), tile, other)


HEAD_TILES = ((0, 128, 256, 0, 0), (0, 128, 256, 1, 1), (512, 640, 640, 0, 1))
MIX = 384
CHUNKS_DOC = "q0 q1 k0 k1 v0 v1 o0 o1 q2 o2 k2 v2"


def make_features(counts_ref, set_index, slots, set_rows, feat_q, feat_k):
    low, high, total = image_ends(counts_ref, set_index, slots)
    step = 256

    def body(i, _):
        at = pl.ds(pl.multiple_of(i * step, step), step)
        row = lax.broadcasted_iota(jnp.int32, (step, LANES), 0) + i * step
        same = (row >= low) & (row < high)
        lane = lax.broadcasted_iota(jnp.int32, (step, LANES), 1) % (LANES // 2)
        feat_k[at] = jnp.where(same, 1.0, 0.0).astype(jnp.bfloat16)
        feat_q[at] = jnp.where(same | (lane > slots), 0.0, -BIG).astype(jnp.bfloat16)
        return 0

    lax.fori_loop(0, set_rows // step, body, 0)
    return total


def attend(m, qkv, mixed, feat_q, feat_k, window_start, window, step):
    keys, values = [], []
    for q_at, k_at, v_at, half, v_half in HEAD_TILES:
        keys.append(keep_half(half, qkv[m, :, k_at : k_at + LANES], feat_k[...]))
        tile = qkv[m, :, v_at : v_at + LANES]
        values.append(keep_half(v_half, tile, jnp.ones_like(tile)))

    def block(i, _):
        at = pl.ds(pl.multiple_of(window_start + i * step, LANES), step)
        outs = []
        for head, (q_at, k_at, v_at, half, v_half) in enumerate(HEAD_TILES):
            query = keep_half(half, qkv[m, at, q_at : q_at + LANES], feat_q[at])
            scores = mm(query, keys[head], NT)
            top = jnp.max(scores, axis=1, keepdims=True)
            weights = jnp.exp((scores - top) * HD ** (-0.5)).astype(jnp.bfloat16)
            out = mm(weights, values[head])
            outs.append(out / pltpu.roll(out, LANES // 2, 1))
        here = pl.ds(pl.multiple_of(i * step, LANES), step)
        low = jnp.bfloat16
        mixed[m, here, 0:LANES] = keep_half(0, outs[0], outs[1]).astype(low)
        mixed[m, here, LANES : 2 * LANES] = keep_half(1, outs[2], jnp.zeros_like(outs[2])).astype(low)
        return 0

    lax.fori_loop(0, window // step, block, 0)


def forward_kernel(
    n_mp, slots, tokens, cot, weights, counts, vec, bias,
    qkv, mixed, proj, middle, normed_t, normed_two_t, active, slope, result, spread,
    w, normed, normed_two, branch, feat_q, feat_k, sems,
):
    set_rows, width = tokens.shape
    own_rows = result.shape[0]
    window = proj.shape[0]
    mp = lax.axis_index("mp")
    per_set = set_rows // own_rows
    set_index, part = mp // per_set, mp % per_set
    window_start = pl.multiple_of(part * (set_rows - window), LANES)
    own_start = pl.multiple_of(part * (window - own_rows), LANES)
    low, f32 = jnp.bfloat16, jnp.float32

    def load(group, m):
        return pltpu.make_async_copy(weights.at[group, m], w.at[group, m], sems.at[group, m])

    for group in range(GROUPS):
        for m in range(n_mp):
            load(group, m).start()

    total = make_features(counts, set_index, slots, set_rows, feat_q, feat_k)

    def norm_one(i, _):
        at = pl.ds(pl.multiple_of(i * LANES, LANES), LANES)
        unit, _inv = row_stats(tokens[at].astype(f32))
        normed[at] = (unit * vec[0:1] + vec[1:2]).astype(low)
        return 0

    lax.fori_loop(0, set_rows // LANES, norm_one, 0)

    def project(m, _):
        load(0, m).wait()
        qkv[m] = (mm(normed[...], w[0, m]) + bias[pl.ds(m, 1)]).astype(low)
        return 0

    lax.fori_loop(0, n_mp, project, 0)

    def heads(m, _):
        attend(m, qkv, mixed, feat_q, feat_k, window_start, window, window // 2)
        return 0

    lax.fori_loop(0, n_mp, heads, 0)

    own_set = pl.ds(pl.multiple_of(window_start + own_start, LANES), own_rows)
    own = pl.ds(own_start, own_rows)
    normed_t[...] = normed[own_set].T

    def out_part(m):
        return mm(mixed[m], w[0, m, :, MIX : MIX + 2 * LANES], NT)

    proj[...] = sum((out_part(m) for m in range(n_mp)), vec[6:7])

    def norm_two(i, _):
        at = pl.ds(pl.multiple_of(i * LANES, LANES), LANES)
        x = tokens[pl.ds(pl.multiple_of(window_start + i * LANES, LANES), LANES)].astype(f32)
        mid = x + vec[4:5] * proj[at]
        middle[at] = mid
        unit, _inv = row_stats(mid)
        normed_two[at] = (unit * vec[2:3] + vec[3:4]).astype(low)
        return 0

    lax.fori_loop(0, window // LANES, norm_two, 0)
    normed_two_t[...] = normed_two[own].T

    def feed(m, _):
        load(1, m).wait()

        def rows(i, _):
            at = pl.ds(pl.multiple_of(i * LANES, LANES), LANES)
            hidden = mm(normed_two[at], w[1, m]) + bias[pl.ds(n_mp + m, 1)]
            act, slp = gelu_parts(hidden)
            active[m, at] = act.astype(low)
            slope[m, at] = slp.astype(low)
            return 0

        lax.fori_loop(0, window // LANES, rows, 0)
        load(2, m).wait()
        part_sum = mm(active[m, own], w[2, m], NT)

        @pl.when(m == 0)
        def _():
            branch[...] = part_sum

        @pl.when(m > 0)
        def _():
            branch[...] += part_sum

        return 0

    lax.fori_loop(0, n_mp, feed, 0)

    def final(i, carry):
        at = pl.ds(pl.multiple_of(i * LANES, LANES), LANES)
        there = pl.ds(pl.multiple_of(own_start + i * LANES, LANES), LANES)
        row = lax.broadcasted_iota(jnp.int32, (LANES, 1), 0) + (window_start + own_start + i * LANES)
        valid = jnp.where(row < total, 1.0, 0.0)
        br = branch[at] + vec[7:8]
        branch[at] = br
        scaled = vec[5:6] * br
        res = middle[there] + scaled
        result[at] = res.astype(low)
        attn = vec[4:5] * proj[there]
        sums = [jnp.sum(valid * v * v, axis=0, keepdims=True) for v in (res, attn, scaled)]
        in_set = pl.ds(pl.multiple_of(window_start + own_start + i * LANES, LANES), LANES)
        back = cot[in_set].astype(f32) * valid
        sums.append(jnp.sum(back * br, axis=0, keepdims=True))
        return tuple(c + s for c, s in zip(carry, sums))

    zero = jnp.zeros((1, width), f32)
    sums = lax.fori_loop(0, own_rows // LANES, final, (zero,) * 4)
    for i in range(4):
        spread[i : i + 1] = sums[i]
    spread[4:8] = jnp.zeros((4, width), f32)


TN = (((0,), (0,)), ((), ()))


def norm_grad(x, gain, grad):
    width = x.shape[1]
    unit, inverse = row_stats(x)
    e = grad * gain
    mean_e = jnp.sum(e, axis=1, keepdims=True) * (1.0 / width)
    mean_eu = jnp.sum(e * unit, axis=1, keepdims=True) * (1.0 / width)
    return inverse * (e - mean_e - unit * mean_eu), grad * unit


def attend_back(m, qkv, d_mixed, feat_q, feat_k, window_start, window, acc, d_query):
    band = 3 * LANES
    acc[...] = jnp.zeros_like(acc)
    low = jnp.bfloat16
    scale = HD ** (-0.5)

    def block(b, _):
        start = jnp.clip(b - 1, 0, window // LANES - 3) * LANES
        keys_at = pl.ds(pl.multiple_of(start, LANES), band)
        keys_in = pl.ds(pl.multiple_of(window_start + start, LANES), band)
        here = pl.ds(pl.multiple_of(b * LANES, LANES), LANES)
        rows_in = pl.ds(pl.multiple_of(window_start + b * LANES, LANES), LANES)
        f_q, f_k = feat_q[rows_in], feat_k[keys_in]
        got = []
        for head, (q_at, k_at, v_at, half, v_half) in enumerate(HEAD_TILES):
            q_tile = qkv[m, rows_in, q_at : q_at + LANES]
            k_tile = qkv[m, keys_in, k_at : k_at + LANES]
            v_tile = qkv[m, keys_in, v_at : v_at + LANES]
            mix_at = 0 if head < 2 else LANES
            d_tile = d_mixed[m, here, mix_at : mix_at + LANES]
            d_out = keep_half(v_half, d_tile, jnp.zeros_like(d_tile))
            scores = mm(keep_half(half, k_tile, f_k), keep_half(half, q_tile, f_q), NT)
            top = jnp.max(scores, axis=0, keepdims=True)
            weights = jnp.exp((scores - top) * scale)
            weights = weights * (1.0 / jnp.sum(weights, axis=0, keepdims=True))
            d_weights = mm(v_tile, d_out, NT)
            delta = jnp.sum(d_weights * weights, axis=0, keepdims=True)
            d_scores = (weights * (d_weights - delta)).astype(low)
            d_key = mm(d_scores, keep_half(half, q_tile * scale, jnp.zeros_like(q_tile)))
            d_value = mm(weights.astype(low), d_out)
            d_q = mm(d_scores, keep_half(half, k_tile * scale, jnp.zeros_like(k_tile)), TN)
            got.append((d_q, d_key, d_value))
        acc[keys_at, 0:LANES] += got[0][1] + got[1][1]
        acc[keys_at, LANES : 2 * LANES] += got[0][2] + got[1][2]
        acc[keys_at, 2 * LANES : 3 * LANES] += got[2][1] + got[2][2]
        d_query[here, 0:LANES] = (got[0][0] + got[1][0]).astype(low)
        d_query[here, LANES : 2 * LANES] = got[2][0].astype(low)
        return 0

    lax.fori_loop(0, window // LANES, block, 0)


def backward_kernel(
    n_mp, slots, tokens, cot, weights, counts, vec, qkv, mixed, proj, middle, normed_t, normed_two_t, active, slope, spread,
    grads, input_rows, vector_sums, bias_sums,
    w, d_branch, d_branch_t, d_two, d_proj, d_proj_t, d_mixed, acc, d_query, d_qkv, d_normed, stage, feat_q, feat_k, sems, out_sems,
):
    set_rows, width = tokens.shape
    own_rows = input_rows.shape[0]
    window = proj.shape[0]
    mp = lax.axis_index("mp")
    per_set = set_rows // own_rows
    set_index, part = mp // per_set, mp % per_set
    window_start = pl.multiple_of(part * (set_rows - window), LANES)
    own_start = pl.multiple_of(part * (window - own_rows), LANES)
    low, f32 = jnp.bfloat16, jnp.float32

    def load(group, m):
        return pltpu.make_async_copy(weights.at[group, m], w.at[group, m], sems.at[group, m])

    for group in (2, 1, 0):
        for m in range(n_mp):
            load(group, m).start()

    total = make_features(counts, set_index, slots, set_rows, feat_q, feat_k)
    own = pl.ds(own_start, own_rows)
    tiles = window // LANES

    def tile_at(i):
        return pl.ds(pl.multiple_of(i * LANES, LANES), LANES), pl.ds(
            pl.multiple_of(window_start + i * LANES, LANES), LANES
        )

    def is_own(i):
        first = i * LANES
        return jnp.where((first >= own_start) & (first < own_start + own_rows), 1.0, 0.0)

    def back_of(i):
        row = lax.broadcasted_iota(jnp.int32, (LANES, 1), 0) + (window_start + i * LANES)
        valid = jnp.where(row < total, 1.0, 0.0)
        return cot[tile_at(i)[1]].astype(f32) * valid

    def column_sum(v):
        return jnp.sum(v, axis=0, keepdims=True)

    zero_row = jnp.zeros((1, width), f32)

    def first(i, total_row):
        at, _ = tile_at(i)
        db = (back_of(i) * vec[5:6]).astype(low)
        d_branch[at] = db
        return total_row + is_own(i) * column_sum(db.astype(f32))

    branch_sum = lax.fori_loop(0, tiles, first, zero_row)
    d_branch_t[...] = d_branch[own].T

    def put(group, m, slot, value):
        stage[slot] = value.astype(low)
        pltpu.make_async_copy(stage.at[slot], grads.at[group, m], out_sems.at[slot]).start()

    def put_done(slot):
        pltpu.make_async_copy(stage.at[slot], grads.at[0, 0], out_sems.at[slot]).wait()

    def feed(m, _):
        load(2, m).wait()

        def rows(i, total_row):
            at, _ = tile_at(i)
            dh = (mm(d_branch[at], w[2, m]) * slope[m, at].astype(f32)).astype(low)
            slope[m, at] = dh
            return total_row + is_own(i) * column_sum(dh.astype(f32))

        bias_sums[pl.ds(n_mp + m, 1)] = lax.fori_loop(0, tiles, rows, zero_row)

        @pl.when(m > 0)
        def _():
            put_done(0)
            put_done(1)

        put(2, m, 0, mm(d_branch_t[...], active[m, own]))
        put(1, m, 1, mm(normed_two_t[...], slope[m, own]))
        load(1, m).wait()
        part_sum = mm(slope[m], w[1, m], NT)

        @pl.when(m == 0)
        def _():
            d_two[...] = part_sum

        @pl.when(m > 0)
        def _():
            d_two[...] += part_sum

        return 0

    lax.fori_loop(0, n_mp, feed, 0)

    def norm_two(i, carry):
        at, _ = tile_at(i)
        grad = d_two[at]
        dv, grad_unit = norm_grad(middle[at], vec[2:3], grad)
        d_mid = back_of(i) + dv
        d_two[at] = d_mid
        dp = (d_mid * vec[4:5]).astype(low)
        d_proj[at] = dp
        mine = is_own(i)
        new = (grad_unit, grad, d_mid * proj[at], dp.astype(f32))
        return tuple(c + mine * column_sum(n) for c, n in zip(carry, new))

    gain_sum, shift_sum, scale_sum, proj_sum = lax.fori_loop(0, tiles, norm_two, (zero_row,) * 4)
    d_proj_t[...] = d_proj[own].T

    def attention(m, _):
        @pl.when(m == 0)
        def _():
            put_done(0)
            put_done(1)

        load(0, m).wait()
        dm = mm(d_proj[...], w[0, m, :, MIX : MIX + 2 * LANES]).astype(low)
        d_mixed[m, :, 0:LANES] = dm[:, 0:LANES]
        d_mixed[m, :, LANES:] = keep_half(1, dm[:, LANES:], jnp.zeros_like(dm[:, LANES:]))
        attend_back(m, qkv, d_mixed, feat_q, feat_k, window_start, window, acc, d_query)
        d_qkv[m, :, 0:128] = d_query[own, 0:128]
        d_qkv[m, :, 128:256] = acc[own, 0:128].astype(low)
        d_qkv[m, :, 256:384] = acc[own, 128:256].astype(low)
        d_qkv[m, :, 384:512] = jnp.zeros((own_rows, LANES), low)
        d_qkv[m, :, 512:640] = d_query[own, 128:256]
        d_qkv[m, :, 640:768] = acc[own, 256:384].astype(low)
        bias_sums[pl.ds(m, 1)] = column_sum(d_qkv[m].astype(f32))

        @pl.when(m > 0)
        def _():
            put_done(0)

        block = mm(normed_t[...], d_qkv[m])
        extra = mm(d_proj_t[...], mixed[m, own])
        stage[0, :, 0:MIX] = block[:, 0:MIX].astype(low)
        stage[0, :, MIX : MIX + 2 * LANES] = (block[:, MIX : MIX + 2 * LANES] + extra).astype(low)
        stage[0, :, MIX + 2 * LANES :] = block[:, MIX + 2 * LANES :].astype(low)
        pltpu.make_async_copy(stage.at[0], grads.at[0, m], out_sems.at[0]).start()
        part_sum = mm(d_qkv[m], w[0, m], NT)

        @pl.when(m == 0)
        def _():
            d_normed[...] = part_sum

        @pl.when(m > 0)
        def _():
            d_normed[...] += part_sum

        return 0

    lax.fori_loop(0, n_mp, attention, 0)

    def norm_one(i, carry):
        at, _ = tile_at(i)
        there = pl.ds(pl.multiple_of(own_start + i * LANES, LANES), LANES)
        in_set = pl.ds(pl.multiple_of(window_start + own_start + i * LANES, LANES), LANES)
        grad = d_normed[at]
        dv, grad_unit = norm_grad(tokens[in_set].astype(f32), vec[0:1], grad)
        input_rows[at] = (d_two[there] + dv).astype(low)
        return tuple(c + column_sum(n) for c, n in zip(carry, (grad_unit, grad)))

    gain_one, shift_one = lax.fori_loop(0, own_rows // LANES, norm_one, (zero_row, zero_row))
    for i, row in enumerate(
        (gain_one, shift_one, gain_sum, shift_sum, scale_sum, spread[3:4], proj_sum, branch_sum)
    ):
        vector_sums[i : i + 1] = row
    put_done(0)


def shard_offset(shard_piece, block_index, whole_length, axis_at):
    shape_list = list(shard_piece.shape)
    shape_list[axis_at] = whole_length
    empty = jnp.zeros(tuple(shape_list), jnp.float32)
    return lax.dynamic_update_slice_in_dim(
        empty, shard_piece, block_index * shard_piece.shape[axis_at], axis_at
    )


def select_slice(whole_array, block_index, block_width, axis_at):
    return lax.dynamic_slice_in_dim(whole_array, block_index * block_width, block_width, axis_at)


def factor_step(
    gradient,
    rows_old,
    cols_old,
    rows_mine,
    cols_mine,
    rows_total,
    count_rows,
    count_cols,
    prior_total,
):
    decay_rate = 1.0 - STEP ** (-0.8)
    rows_new = decay_rate * rows_old + (1.0 - decay_rate) * (rows_mine / count_cols + square_eps)
    cols_new = decay_rate * cols_old + (1.0 - decay_rate) * (cols_mine / count_rows + square_eps)
    rows_average = (
        decay_rate * prior_total
        + (1.0 - decay_rate) * (rows_total / count_cols + count_rows * square_eps)
    ) / count_rows
    update = gradient * lax.rsqrt(rows_new[:, None] * cols_new[None, :] / rows_average)
    return (rows_new, cols_new, update, jnp.sum(update * update))


def plain_step(weight, gradient, moment_old):
    decay_rate = 1.0 - STEP ** (-0.8)
    moment = decay_rate * moment_old + (1.0 - decay_rate) * (gradient * gradient + square_eps)
    update = gradient * lax.rsqrt(moment)
    update_rms = jnp.sqrt(jnp.mean(update * update))
    rate_here = step_rate * jnp.sqrt(jnp.mean(weight * weight))
    return (weight - rate_here * update / jnp.maximum(1.0, update_rms / clip_limit), moment)


def shards(
    tokens_in,
    cotangent,
    patch_counts,
    w_qkv,
    w_out,
    w_up,
    w_down,
    layer_vector_rows,
    inner_biases,
    qkvrows_prior,
    qkvcols_prior,
    outrows_prior,
    outcols_prior,
    uprows_prior,
    upcols_prior,
    downrows_prior,
    downcols_prior,
    vector_moment,
    bias_moment,
):
    n_dp, n_mp = lax.axis_size("dp"), lax.axis_size("mp")
    data_index = lax.axis_index("dp")
    parallel_model_index = lax.axis_index("mp")
    row_count, parallel_model_width = tokens_in.shape
    set_count, slot_count = patch_counts.shape
    set_rows = row_count // set_count
    own_rows = row_count // n_mp
    shard_width_local = w_qkv.shape[2]
    local_hidden = w_up.shape[1]
    f32, low = jnp.float32, jnp.bfloat16
    width, hidden_width = parallel_model_width, local_hidden
    blocks = pack(w_qkv, w_out, w_up, w_down)
    gathered = gather_all(blocks.astype(low), n_dp, n_mp)
    set_index = parallel_model_index // (set_rows // own_rows)

    def of_set(rows_in):
        return lax.dynamic_slice_in_dim(rows_in, set_index * set_rows, set_rows, 0)

    tokens_set, cot_set = of_set(tokens_in), of_set(cotangent)
    window = own_rows + HALO
    by_mp = inner_biases.reshape(6, n_mp, shard_width_local)
    none = jnp.zeros((n_mp, shard_width_local), f32)
    bias_rows = jnp.concatenate(
        [
            permute_chunks(jnp.concatenate([by_mp[0], none, by_mp[1], none], axis=1), CHUNKS),
            by_mp[2:].transpose(1, 2, 0).reshape(n_mp, hidden_width),
        ]
    )
    vmem = pl.BlockSpec(memory_space=pltpu.VMEM)
    anywhere = pl.BlockSpec(memory_space=pl.ANY)
    scalars_in = pl.BlockSpec(memory_space=pltpu.SMEM)

    def shape(*dims, dtype=low):
        return jax.ShapeDtypeStruct(dims, dtype)

    qkv, mixed, proj, middle, normed_t, normed_two_t, active, slope, result, spread = pl.pallas_call(
        functools.partial(forward_kernel, n_mp, slot_count),
        out_shape=(
            shape(n_mp, set_rows, width),
            shape(n_mp, window, 2 * LANES),
            shape(window, width, dtype=f32),
            shape(window, width, dtype=f32),
            shape(width, own_rows),
            shape(width, own_rows),
            shape(n_mp, window, hidden_width),
            shape(n_mp, window, hidden_width),
            shape(own_rows, width),
            shape(8, width, dtype=f32),
        ),
        in_specs=[vmem, vmem, anywhere, scalars_in, vmem, vmem],
        out_specs=(vmem,) * 10,
        scratch_shapes=[
            pltpu.VMEM((GROUPS, n_mp, width, width), low),
            pltpu.VMEM((set_rows, width), low),
            pltpu.VMEM((window, width), low),
            pltpu.VMEM((own_rows, width), f32),
            pltpu.VMEM((set_rows, LANES), low),
            pltpu.VMEM((set_rows, LANES), low),
            pltpu.SemaphoreType.DMA((GROUPS, n_mp)),
        ],
        compiler_params=pltpu.CompilerParams(vmem_limit_bytes=62 * 2**20),
    )(tokens_set, cot_set, gathered, patch_counts, layer_vector_rows, bias_rows)
    grads, input_rows, vector_part, bias_sums = pl.pallas_call(
        functools.partial(backward_kernel, n_mp, slot_count),
        out_shape=(
            shape(GROUPS, n_mp, width, width),
            shape(own_rows, width),
            shape(8, width, dtype=f32),
            shape(2 * n_mp, width, dtype=f32),
        ),
        in_specs=[vmem, vmem, anywhere, scalars_in] + [vmem] * 10,
        out_specs=(anywhere, vmem, vmem, vmem),
        scratch_shapes=[
            pltpu.VMEM((GROUPS, n_mp, width, width), low),
            pltpu.VMEM((window, width), low),
            pltpu.VMEM((width, own_rows), low),
            pltpu.VMEM((window, width), f32),
            pltpu.VMEM((window, width), low),
            pltpu.VMEM((width, own_rows), low),
            pltpu.VMEM((n_mp, window, 2 * LANES), low),
            pltpu.VMEM((window, 3 * LANES), f32),
            pltpu.VMEM((window, 2 * LANES), low),
            pltpu.VMEM((n_mp, own_rows, width), low),
            pltpu.VMEM((own_rows, width), f32),
            pltpu.VMEM((2, width, width), low),
            pltpu.VMEM((set_rows, LANES), low),
            pltpu.VMEM((set_rows, LANES), low),
            pltpu.SemaphoreType.DMA((GROUPS, n_mp)),
            pltpu.SemaphoreType.DMA((2,)),
        ],
        compiler_params=pltpu.CompilerParams(vmem_limit_bytes=62 * 2**20),
    )(
        tokens_set, cot_set, gathered, patch_counts, layer_vector_rows,
        qkv, mixed, proj, middle, normed_t, normed_two_t, active, slope, spread,
    )
    reduced = scatter_sum(grads, n_dp, n_mp)
    result_low = lax.all_gather(result, "mp", axis=0, tiled=True)
    input_grad = lax.all_to_all(input_rows, "mp", 1, 0, tiled=True).astype(f32)

    bias_qkv = permute_chunks(bias_sums[:n_mp], BACK).reshape(n_mp, 4, shard_width_local)
    hidden_sums = bias_sums[n_mp:].reshape(n_mp, shard_width_local, -1).transpose(2, 0, 1)
    bias_part = jnp.concatenate(
        [
            bias_qkv[:, 0].reshape(1, width),
            bias_qkv[:, 2].reshape(1, width),
            hidden_sums.reshape(-1, width),
        ]
    )
    own_first = parallel_model_index % (set_rows // own_rows) * own_rows
    held = jnp.sum(lax.dynamic_index_in_dim(patch_counts, set_index, 0, keepdims=False))
    counted = jnp.clip(held - own_first, 0, own_rows).astype(f32)
    vector_grad, bias_grad, squares_all, counted_all = lax.psum(
        (vector_part, bias_part, jnp.sum(spread[:3], axis=1), counted), ("dp", "mp")
    )
    token_spread = jnp.sqrt(squares_all / (counted_all * parallel_model_width))
    qkv_grad, out_grad, up_grad, down_grad = unpack(reduced)
    square_qkv = qkv_grad * qkv_grad
    square_out = out_grad * out_grad
    square_up = up_grad * up_grad
    square_down = down_grad * down_grad
    scalars = jnp.stack(
        [
            jnp.sum(w_qkv * w_qkv),
            jnp.sum(w_out * w_out),
            jnp.sum(w_up * w_up),
            jnp.sum(w_down * w_down),
            jnp.where(parallel_model_index == 0, jnp.sum(qkvrows_prior), 0.0),
            jnp.where(data_index == 0, jnp.sum(outrows_prior), 0.0),
            jnp.where(parallel_model_index == 0, jnp.sum(uprows_prior), 0.0),
            jnp.where(data_index == 0, jnp.sum(downrows_prior), 0.0),
        ]
    )
    factor_totals = lax.psum(
        (
            shard_offset(jnp.sum(square_qkv, axis=(1, 2)), data_index, parallel_model_width, 0),
            shard_offset(
                jnp.sum(square_qkv, axis=0), parallel_model_index, parallel_model_width, 1
            ),
            shard_offset(
                jnp.sum(square_out, axis=1), parallel_model_index, parallel_model_width, 0
            ),
            shard_offset(jnp.sum(square_out, axis=0), data_index, parallel_model_width, 0),
            shard_offset(jnp.sum(square_up, axis=1), data_index, parallel_model_width, 0),
            shard_offset(jnp.sum(square_up, axis=0), parallel_model_index, FF, 0),
            shard_offset(jnp.sum(square_down, axis=1), parallel_model_index, FF, 0),
            shard_offset(jnp.sum(square_down, axis=0), data_index, parallel_model_width, 0),
            scalars,
        ),
        ("dp", "mp"),
    )
    (
        rows_qkv,
        cols_qkv,
        rows_out,
        cols_out,
        rows_up,
        cols_up,
        rows_down,
        cols_down,
        scalar_totals,
    ) = factor_totals
    local_rows = w_qkv.shape[0]
    local_cols = w_out.shape[1]
    qkvrows_after, qkvcols_flat, update_qkv, usq_qkv = factor_step(
        qkv_grad.reshape(local_rows, 3 * shard_width_local),
        qkvrows_prior,
        qkvcols_prior.reshape(3 * shard_width_local),
        select_slice(rows_qkv, data_index, local_rows, 0),
        select_slice(cols_qkv, parallel_model_index, shard_width_local, 1).reshape(
            3 * shard_width_local
        ),
        jnp.sum(rows_qkv),
        parallel_model_width,
        3 * parallel_model_width,
        scalar_totals[4],
    )
    outrows_after, outcols_after, update_out, usq_out = factor_step(
        out_grad,
        outrows_prior,
        outcols_prior,
        select_slice(rows_out, parallel_model_index, shard_width_local, 0),
        select_slice(cols_out, data_index, local_cols, 0),
        jnp.sum(rows_out),
        parallel_model_width,
        parallel_model_width,
        scalar_totals[5],
    )
    uprows_after, upcols_after, update_up, usq_up = factor_step(
        up_grad,
        uprows_prior,
        upcols_prior,
        select_slice(rows_up, data_index, local_rows, 0),
        select_slice(cols_up, parallel_model_index, local_hidden, 0),
        jnp.sum(rows_up),
        parallel_model_width,
        FF,
        scalar_totals[6],
    )
    downrows_after, downcols_after, update_down, usq_down = factor_step(
        down_grad,
        downrows_prior,
        downcols_prior,
        select_slice(rows_down, parallel_model_index, local_hidden, 0),
        select_slice(cols_down, data_index, local_cols, 0),
        jnp.sum(rows_down),
        FF,
        parallel_model_width,
        scalar_totals[7],
    )
    usq_totals = lax.psum(jnp.stack([usq_qkv, usq_out, usq_up, usq_down]), ("dp", "mp"))
    entry_counts = jnp.array(
        [
            3.0 * parallel_model_width * parallel_model_width,
            1.0 * parallel_model_width * parallel_model_width,
            1.0 * parallel_model_width * FF,
            1.0 * FF * parallel_model_width,
        ],
        jnp.float32,
    )
    update_scale = jnp.sqrt(usq_totals / entry_counts)
    weight_rms = jnp.sqrt(scalar_totals[:4] / entry_counts)
    limits = jnp.maximum(1.0, update_scale / clip_limit)
    qkv_after = (
        w_qkv.reshape(local_rows, 3 * shard_width_local)
        - step_rate * weight_rms[0] * update_qkv / limits[0]
    ).reshape(w_qkv.shape)
    out_after = w_out - step_rate * weight_rms[1] * update_out / limits[1]
    up_after = w_up - step_rate * weight_rms[2] * update_up / limits[2]
    down_after = w_down - step_rate * weight_rms[3] * update_down / limits[3]
    vectors_after, moment_vectors = jax.vmap(plain_step)(
        layer_vector_rows, vector_grad, vector_moment
    )
    heads_after, heads_moment = jax.vmap(plain_step)(
        inner_biases[:2], bias_grad[:2], bias_moment[:2]
    )
    upper_after, upper_moment = plain_step(
        inner_biases[2:].reshape(FF), bias_grad[2:].reshape(FF), bias_moment[2:].reshape(FF)
    )
    biases_after = jnp.concatenate(
        [heads_after, upper_after.reshape(FF // parallel_model_width, parallel_model_width)], axis=0
    )
    moment_biases = jnp.concatenate(
        [heads_moment, upper_moment.reshape(FF // parallel_model_width, parallel_model_width)],
        axis=0,
    )
    return (
        result_low,
        input_grad,
        qkv_grad,
        out_grad,
        up_grad,
        down_grad,
        qkv_after,
        out_after,
        up_after,
        down_after,
        qkv_after.astype(jnp.bfloat16),
        out_after.astype(jnp.bfloat16),
        up_after.astype(jnp.bfloat16),
        down_after.astype(jnp.bfloat16),
        qkvrows_after,
        qkvcols_flat.reshape(3, shard_width_local),
        outrows_after,
        outcols_after,
        uprows_after,
        upcols_after,
        downrows_after,
        downcols_after,
        vector_grad,
        bias_grad,
        moment_vectors,
        moment_biases,
        vectors_after,
        biases_after,
        update_scale,
        token_spread,
    )


def solution(mesh):
    in_specs = (
        P("dp", None),
        P("dp", None),
        P("dp", None),
        P("dp", None, "mp"),
        P("mp", "dp"),
        P("dp", "mp"),
        P("mp", "dp"),
        P(),
        P(),
        P("dp"),
        P(None, "mp"),
        P("mp"),
        P("dp"),
        P("dp"),
        P("mp"),
        P("mp"),
        P("dp"),
        P(),
        P(),
    )
    out_specs = (
        P("dp", None),
        P("dp", "mp"),
        P("dp", None, "mp"),
        P("mp", "dp"),
        P("dp", "mp"),
        P("mp", "dp"),
        P("dp", None, "mp"),
        P("mp", "dp"),
        P("dp", "mp"),
        P("mp", "dp"),
        P("dp", None, "mp"),
        P("mp", "dp"),
        P("dp", "mp"),
        P("mp", "dp"),
        P("dp"),
        P(None, "mp"),
        P("mp"),
        P("dp"),
        P("dp"),
        P("mp"),
        P("mp"),
        P("dp"),
        P(),
        P(),
        P(),
        P(),
        P(),
        P(),
        P(),
        P(),
    )
    return jax.shard_map(shards, mesh=mesh, in_specs=in_specs, out_specs=out_specs, check_vma=False)
```

```python
import functools

import jax
import jax.numpy as jnp
from jax import lax
from jax.experimental import pallas as pl
from jax.experimental.pallas import tpu as pltpu
from jax.sharding import PartitionSpec as P

HD = 64
FF = 3072
STEP = 3


norm_eps = 1e-06
square_eps = 1e-30
clip_limit = 0.5
step_rate = 0.6
mask_fill = -1000000000.0


MESH = pl.DeviceIdType.MESH
HALO = 128
GROUPS = 3
CHUNKS = (0, 1, 3, 4, 6, 7, 9, 10, 2, 11, 5, 8)
BACK = tuple(CHUNKS.index(i) for i in range(12))


def moments_of(stream):
    center = stream - jnp.mean(stream, axis=-1, keepdims=True)
    spread = jnp.mean(center * center, axis=-1, keepdims=True)
    return (center, lax.rsqrt(spread + norm_eps))


def normalize(stream, gain_row, shift_row):
    center, inverse = moments_of(stream)
    return center * inverse * gain_row + shift_row


def segment_ids(counts, set_rows):
    image_ends = jnp.cumsum(counts)
    places = jnp.arange(set_rows, dtype=jnp.int32)
    return jnp.sum((places[:, None] >= image_ends[None, :]).astype(jnp.int32), axis=1)


def permute_chunks(block, order):
    parts = [block[..., HD * i : HD * (i + 1)] for i in order]
    return jnp.concatenate(parts, axis=-1)


def pack(qkv, out, up, down):
    first = jnp.concatenate([qkv[:, 0], qkv[:, 1], qkv[:, 2], out.T], axis=1)
    return jnp.stack([permute_chunks(first, CHUNKS), up, down.T])


def unpack(blocks):
    first = permute_chunks(blocks[0], BACK)
    width = first.shape[-1] // 4
    qkv = first[:, : 3 * width].reshape(first.shape[0], 3, width)
    return qkv, first[:, 3 * width :].T, blocks[1], blocks[2].T


def neighbours(dp):
    core = dp % 2
    return dp + 1 - 2 * core, dp + 2 - 4 * ((dp // 2) % 2), (dp + 4) % 8, (dp + 4) % 8 + 2 - 4 * ((dp // 2) % 2)


def flip(dp):
    return dp + 1 - 2 * (dp % 2)


def greet(devices, extra):
    barrier = pltpu.get_barrier_semaphore()
    for device in devices:
        pl.semaphore_signal(barrier, inc=1, device_id=device, device_id_type=MESH)
    for condition, device in extra:

        @pl.when(condition)
        def _():
            pl.semaphore_signal(barrier, inc=1, device_id=device, device_id_type=MESH)

    peers = len(devices)
    for condition, _ in extra:
        peers = peers + jnp.where(condition, 1, 0)
    pl.semaphore_wait(barrier, peers)


A_Z, A_X, A_Y, A_D0, A_D1, A_S, A_SX, A_SY, A_SD0, A_SD1 = range(10)
KINDS = 10
ORDERS = ((0, 1, 2, 3), (1, 0, 2, 3), (2, 3, 1, 0), (3, 2, 1, 0))


def plane_at(mp, unit):
    codes = [sum(plane * 4**i for i, plane in enumerate(order)) for order in ORDERS]
    code = jnp.where(mp == 0, codes[0], jnp.where(mp == 1, codes[1], jnp.where(mp == 2, codes[2], codes[3])))
    power = jnp.where(unit == 0, 1, jnp.where(unit == 1, 4, jnp.where(unit == 2, 16, 64)))
    return (code // power) % 4


class Gather:
    def __init__(self, n_mp, out, send_sems, recv_sems, way_sems):
        self.dp, self.mp, self.n_mp = lax.axis_index("dp"), lax.axis_index("mp"), n_mp
        self.out, self.send_sems, self.recv_sems, self.way_sems = out, send_sems, recv_sems, way_sems
        self.sib, self.xn, self.yn, self.dn = neighbours(self.dp)
        self.rows = out.shape[3]
        self.up, self.down = jnp.minimum(self.mp + 1, n_mp - 1), jnp.maximum(self.mp - 1, 0)
        half = self.rows // 2
        self.all, self.low, self.high = pl.ds(0, self.rows), pl.ds(0, half), pl.ds(half, half)

    def greet(self):
        dp, mp = self.dp, self.mp
        greet(
            [(self.sib, mp), (self.xn, mp), (self.yn, mp)],
            [(mp < self.n_mp - 1, (dp, self.up)), (mp > 0, (dp, self.down))],
        )

    def message(self, kind, group, plane, slot, part, device):
        where = self.out.at[group, plane, slot, part]
        return pltpu.make_async_remote_copy(
            src_ref=where,
            dst_ref=where,
            send_sem=self.send_sems.at[group, plane, kind],
            recv_sem=self.recv_sems.at[group, plane, kind],
            device_id=(device, self.mp),
            device_id_type=MESH,
        )

    def along(self, group, plane, way):
        where = self.out.at[group, plane, self.dp]
        return pltpu.make_async_remote_copy(
            src_ref=where,
            dst_ref=where,
            send_sem=self.way_sems.at[group, plane, way],
            recv_sem=self.recv_sems.at[group, plane, A_Z],
            device_id=(self.dp, self.down if way else self.up),
            device_id_type=MESH,
        )

    def sends(self, group, plane):
        dp, xn, yn, dn, sib = self.dp, self.xn, self.yn, self.dn, self.sib
        first = [(A_X, dp, self.all, xn), (A_Y, dp, self.all, yn), (A_S, dp, self.all, sib)]
        second = [(A_D0, xn, self.low, yn), (A_SX, xn, self.all, sib), (A_D1, yn, self.high, xn), (A_SY, yn, self.all, sib)]
        third = [(A_SD0, dn, self.low, sib), (A_SD1, dn, self.high, sib)]
        return [
            [functools.partial(self.message, kind, group, plane, *rest) for kind, *rest in part]
            for part in (first, second, third)
        ]

    def unit(self, t):
        group = t // self.n_mp
        return group, plane_at(self.mp, t % self.n_mp)

    def guarded(self, t, action):
        if isinstance(t, int):
            if 0 <= t < GROUPS * self.n_mp:
                action(*self.unit(t))
            return

        @pl.when((t >= 0) & (t < GROUPS * self.n_mp))
        def _():
            action(*self.unit(t))

    def stage_z(self, t):
        def action(group, plane):
            @pl.when(plane != self.mp)
            def _():
                self.along(group, plane, 0).wait_recv()

            @pl.when((plane <= self.mp) & (self.mp < self.n_mp - 1))
            def _():
                self.along(group, plane, 0).start()

            @pl.when((plane >= self.mp) & (self.mp > 0))
            def _():
                self.along(group, plane, 1).start()

        self.guarded(t, action)

    def stage_a(self, t):
        def action(group, plane):
            for copy in self.sends(group, plane)[0]:
                copy().start()

        self.guarded(t, action)

    def stage_b(self, t):
        def action(group, plane):
            out = self.sends(group, plane)[1]
            self.message(A_X, group, plane, self.xn, self.all, self.xn).wait_recv()
            out[0]().start()
            out[1]().start()
            self.message(A_Y, group, plane, self.yn, self.all, self.yn).wait_recv()
            out[2]().start()
            out[3]().start()

        self.guarded(t, action)

    def stage_c(self, t):
        def action(group, plane):
            out = self.sends(group, plane)[2]
            self.message(A_D0, group, plane, self.dn, self.low, self.yn).wait_recv()
            out[0]().start()
            self.message(A_D1, group, plane, self.dn, self.high, self.xn).wait_recv()
            out[1]().start()

        self.guarded(t, action)

    def stage_d(self, t):
        def action(group, plane):
            for kind, slot, part in (
                (A_S, self.sib, self.all),
                (A_SX, flip(self.xn), self.all),
                (A_SY, flip(self.yn), self.all),
                (A_SD0, flip(self.dn), self.low),
                (A_SD1, flip(self.dn), self.high),
            ):
                self.message(kind, group, plane, slot, part, self.sib).wait_recv()

        self.guarded(t, action)

    def plane(self, u):
        return plane_at(self.mp, u)

    def begin(self):
        for t in (0, 1):
            self.stage_z(t)
            self.stage_a(t)

    def step(self, s):
        self.stage_b(s)
        ahead = (2,) if isinstance(s, int) and s < 2 else (2, 3) if isinstance(s, int) and s == 2 else (3,)
        for more in ahead:
            self.stage_z(s + more)
            self.stage_a(s + more)
        self.stage_c(s - 1)

    def finish(self):
        def body(t, _):
            group, plane = self.unit(t)
            for part in self.sends(group, plane):
                for copy in part:
                    copy().wait_send()

            @pl.when((plane <= self.mp) & (self.mp < self.n_mp - 1))
            def _():
                self.along(group, plane, 0).wait_send()

            @pl.when((plane >= self.mp) & (self.mp > 0))
            def _():
                self.along(group, plane, 1).wait_send()

            return 0

        lax.fori_loop(0, GROUPS * self.n_mp, body, 0)


R_S, R_D0, R_D1, R_X, R_Y, R_UP, R_DOWN = range(7)
R_KINDS = 7


class Scatter:
    def __init__(self, n_mp, grads, fresh, out, bufs, load_sems, send_sems, recv_sems):
        self.dp, self.mp, self.n_mp = lax.axis_index("dp"), lax.axis_index("mp"), n_mp
        self.grads, self.fresh, self.out = grads, fresh, out
        self.pair_in, self.halves_in, self.x_in, self.y_in, self.z_in, self.mine, self.summed = bufs
        self.load_sems, self.send_sems, self.recv_sems = load_sems, send_sems, recv_sems
        self.sib, self.xn, self.yn, self.dn = neighbours(self.dp)
        self.core = self.dp % 2
        self.rows = out.shape[1]
        self.here, self.at_x, self.at_y, self.at_d = self.dp // 2, self.xn // 2, self.yn // 2, self.dn // 2
        self.up, self.down = jnp.minimum(self.mp + 1, n_mp - 1), jnp.maximum(self.mp - 1, 0)
        half = self.rows // 2
        self.low, self.high = pl.ds(0, half), pl.ds(half, half)
        self.units = GROUPS * n_mp

    def greet(self):
        dp, mp = self.dp, self.mp
        greet(
            [(self.sib, mp), (self.xn, mp), (self.yn, mp)],
            [(mp < self.n_mp - 1, (dp, self.up)), (mp > 0, (dp, self.down))],
        )

    def plane(self, u):
        return plane_at(self.mp, self.n_mp - 1 - u)

    def unit(self, t):
        return t // self.n_mp, self.plane(t % self.n_mp)

    def remote(self, kind, group, plane, src, dst, device):
        return pltpu.make_async_remote_copy(
            src_ref=src,
            dst_ref=dst,
            send_sem=self.send_sems.at[group, plane, kind],
            recv_sem=self.recv_sems.at[group, plane, kind],
            device_id=device,
            device_id_type=MESH,
        )

    def pair(self, group, plane, fresh):
        src = (
            self.fresh.at[plane, :, 1 - self.core] if fresh else self.grads.at[group, plane, :, 1 - self.core]
        )
        return self.remote(R_S, group, plane, src, self.pair_in.at[group, plane], (self.sib, self.mp))

    def message(self, kind, group, plane):
        mp, mine = self.mp, self.mine
        if kind == R_D0:
            src, dst = mine.at[group, plane, self.at_d, self.low], self.halves_in.at[group, plane, 0]
            device = (self.xn, mp)
        elif kind == R_D1:
            src, dst = mine.at[group, plane, self.at_d, self.high], self.halves_in.at[group, plane, 1]
            device = (self.yn, mp)
        elif kind == R_X:
            src, dst, device = mine.at[group, plane, self.at_x], self.x_in.at[group, plane], (self.xn, mp)
        elif kind == R_Y:
            src, dst, device = mine.at[group, plane, self.at_y], self.y_in.at[group, plane], (self.yn, mp)
        elif kind == R_UP:
            src, dst = self.summed.at[group, plane], self.z_in.at[group, plane, 0]
            device = (self.dp, self.up)
        else:
            src, dst = self.summed.at[group, plane], self.z_in.at[group, plane, 1]
            device = (self.dp, self.down)
        return self.remote(kind, group, plane, src, dst, device)

    def load(self, group, plane):
        return pltpu.make_async_copy(
            self.grads.at[group, plane, :, self.core],
            self.mine.at[group, plane],
            self.load_sems.at[group, plane],
        )

    def guarded(self, t, first, last, action):
        if isinstance(t, int):
            if first <= t < last:
                action(*self.unit(t))
            return

        @pl.when((t >= first) & (t < last))
        def _():
            action(*self.unit(t))

    def offer(self, t):
        def action(group, plane):
            self.pair(group, plane, False).start()
            self.load(group, plane).start()

        self.guarded(t, 0, 2 * self.n_mp, action)

    def offer_fresh(self, u):
        plane = self.plane(u)
        self.pair(2, plane, True).start()

    def add_pair(self, t):
        def action(group, plane, fresh):
            self.pair(group, plane, fresh).wait_recv()
            if fresh:
                self.mine[group, plane] = self.fresh[plane, :, self.core] + self.pair_in[group, plane]
            else:
                self.load(group, plane).wait()
                self.mine[group, plane] = self.mine[group, plane] + self.pair_in[group, plane]
            self.message(R_D0, group, plane).start()
            self.message(R_D1, group, plane).start()

        self.guarded(t, 0, 2 * self.n_mp, lambda g, p: action(g, p, False))
        self.guarded(t, 2 * self.n_mp, self.units, lambda g, p: action(2, p, True))

    def add_halves(self, t):
        def action(group, plane):
            mine, halves = self.mine, self.halves_in
            self.message(R_D0, group, plane).wait_recv()
            mine[group, plane, self.at_y, self.low] = (
                mine[group, plane, self.at_y, self.low] + halves[group, plane, 0]
            )
            self.message(R_D1, group, plane).wait_recv()
            mine[group, plane, self.at_x, self.high] = (
                mine[group, plane, self.at_x, self.high] + halves[group, plane, 1]
            )
            self.message(R_X, group, plane).start()
            self.message(R_Y, group, plane).start()

        self.guarded(t, 0, self.units, action)

    def add_plane(self, t):
        def action(group, plane):
            f32, mp, last = jnp.float32, self.mp, self.n_mp - 1
            self.message(R_X, group, plane).wait_recv()
            self.message(R_Y, group, plane).wait_recv()
            total = (
                self.mine[group, plane, self.here].astype(f32)
                + self.x_in[group, plane].astype(f32)
                + self.y_in[group, plane].astype(f32)
            )

            @pl.when(plane == mp)
            def _():
                self.out[group] = total

            @pl.when(plane != mp)
            def _():
                self.summed[group, plane] = total.astype(jnp.bfloat16)

            @pl.when((plane > mp) & (mp == 0))
            def _():
                self.message(R_UP, group, plane).start()

            @pl.when((plane < mp) & (mp == last))
            def _():
                self.message(R_DOWN, group, plane).start()

        self.guarded(t, 0, self.units, action)

    def add_along(self, t):
        def action(group, plane):
            f32, mp, last = jnp.float32, self.mp, self.n_mp - 1

            def add(way):
                self.summed[group, plane] = (
                    self.summed[group, plane].astype(f32) + self.z_in[group, plane, way].astype(f32)
                ).astype(jnp.bfloat16)

            @pl.when((plane > mp) & (mp > 0))
            def _():
                self.message(R_UP, group, plane).wait_recv()
                add(0)
                self.message(R_UP, group, plane).start()

            @pl.when((plane < mp) & (mp < last))
            def _():
                self.message(R_DOWN, group, plane).wait_recv()
                add(1)
                self.message(R_DOWN, group, plane).start()

            @pl.when((plane == mp) & (mp > 0))
            def _():
                self.message(R_UP, group, plane).wait_recv()
                self.out[group] += self.z_in[group, plane, 0].astype(f32)

            @pl.when((plane == mp) & (mp < last))
            def _():
                self.message(R_DOWN, group, plane).wait_recv()
                self.out[group] += self.z_in[group, plane, 1].astype(f32)

        self.guarded(t, 0, self.units, action)

    STEPS = 3

    def step(self, s):
        self.offer(s + 2)
        self.add_pair(s)
        self.add_halves(s - 1)
        self.add_plane(s - 2)
        self.add_along(s - 3)

    def finish(self):
        def body(t, _):
            group, plane = self.unit(t)

            @pl.when(group < 2)
            def _():
                self.pair(group, plane, False).wait_send()

            @pl.when(group == 2)
            def _():
                self.pair(2, plane, True).wait_send()

            for kind in (R_D0, R_D1, R_X, R_Y):
                self.message(kind, group, plane).wait_send()

            @pl.when(plane > self.mp)
            def _():
                self.message(R_UP, group, plane).wait_send()

            @pl.when(plane < self.mp)
            def _():
                self.message(R_DOWN, group, plane).wait_send()

            return 0

        lax.fori_loop(0, self.units, body, 0)


LANES = 128
NN = (((1,), (0,)), ((), ()))
NT = (((1,), (1,)), ((), ()))
BIG = 2.0**36


def mm(left, right, dims=NN):
    return lax.dot_general(left, right, dims, preferred_element_type=jnp.float32)


def gelu_parts(t):
    k = 1.0 / (1.0 + 0.2316419 * jnp.abs(t))
    series = k * (
        0.319381530 + k * (-0.356563782 + k * (1.781477937 + k * (-1.821255978 + k * 1.330274429)))
    )
    density = 0.3989422804014327 * jnp.exp(-0.5 * t * t)
    tail = density * series
    phi = jnp.where(t >= 0.0, 1.0 - tail, tail)
    return t * phi, phi + t * density


def row_stats(x):
    width = x.shape[1]
    center = x - jnp.sum(x, axis=1, keepdims=True) * (1.0 / width)
    spread = jnp.sum(center * center, axis=1, keepdims=True) * (1.0 / width)
    inverse = lax.rsqrt(spread + norm_eps)
    return center * inverse, inverse


def image_ends(counts_ref, set_index, slots):
    lane = lax.broadcasted_iota(jnp.int32, (8, LANES), 1) % (LANES // 2)
    low = jnp.zeros((8, LANES), jnp.int32)
    high = jnp.zeros((8, LANES), jnp.int32)
    edge = jnp.int32(0)
    for slot in range(slots + 1):
        after = jnp.int32(1 << 20) if slot == slots else edge + counts_ref[set_index, slot]
        low = jnp.where(lane == slot, edge, low)
        high = jnp.where(lane == slot, after, high)
        edge = after if slot < slots else edge
    return low[0:1], high[0:1], edge


def own_row(hidden_half, tile):
    lane = lax.broadcasted_iota(jnp.int32, tile.shape, 1)
    return (lane < LANES // 2) if hidden_half == 0 else (lane >= LANES // 2)


def keep_half(half, tile, other):
    return jnp.where(own_row(half, tile), tile, other)


HEAD_TILES = ((0, 128, 256, 0, 0), (0, 128, 256, 1, 1), (512, 640, 640, 0, 1))
MIX = 384


def make_features(counts_ref, set_index, slots, set_rows, feat_q, feat_k):
    low, high, total = image_ends(counts_ref, set_index, slots)
    step = 256

    def body(i, _):
        at = pl.ds(pl.multiple_of(i * step, step), step)
        row = lax.broadcasted_iota(jnp.int32, (step, LANES), 0) + i * step
        same = (row >= low) & (row < high)
        lane = lax.broadcasted_iota(jnp.int32, (step, LANES), 1) % (LANES // 2)
        feat_k[at] = jnp.where(same, 1.0, 0.0).astype(jnp.bfloat16)
        feat_q[at] = jnp.where(same | (lane > slots), 0.0, -BIG).astype(jnp.bfloat16)
        return 0

    lax.fori_loop(0, set_rows // step, body, 0)
    return total


def attend(m, qkv, mixed, feat_q, feat_k, window_start, window, step):
    keys, values = [], []
    for q_at, k_at, v_at, half, v_half in HEAD_TILES:
        keys.append(keep_half(half, qkv[m, :, k_at : k_at + LANES], feat_k[...]))
        tile = qkv[m, :, v_at : v_at + LANES]
        values.append(keep_half(v_half, tile, jnp.ones_like(tile)))

    def block(i, _):
        at = pl.ds(pl.multiple_of(window_start + i * step, LANES // 2), step)
        outs = []
        for head, (q_at, k_at, v_at, half, v_half) in enumerate(HEAD_TILES):
            query = keep_half(half, qkv[m, at, q_at : q_at + LANES], feat_q[at])
            scores = mm(query, keys[head], NT)
            top = jnp.max(scores, axis=1, keepdims=True)
            weights = jnp.exp((scores - top) * HD ** (-0.5)).astype(jnp.bfloat16)
            out = mm(weights, values[head])
            outs.append(out / pltpu.roll(out, LANES // 2, 1))
        here = pl.ds(pl.multiple_of(i * step, LANES // 2), step)
        low = jnp.bfloat16
        mixed[m, here, 0:LANES] = keep_half(0, outs[0], outs[1]).astype(low)
        mixed[m, here, LANES : 2 * LANES] = keep_half(1, outs[2], jnp.zeros_like(outs[2])).astype(low)
        return 0

    lax.fori_loop(0, window // step, block, 0)


TN = (((0,), (0,)), ((), ()))


def norm_grad(x, gain, grad):
    width = x.shape[1]
    unit, inverse = row_stats(x)
    e = grad * gain
    mean_e = jnp.sum(e, axis=1, keepdims=True) * (1.0 / width)
    mean_eu = jnp.sum(e * unit, axis=1, keepdims=True) * (1.0 / width)
    return inverse * (e - mean_e - unit * mean_eu), grad * unit


def attend_back(m, qkv, d_mixed, feat_q, feat_k, window_start, window, acc, d_query):
    band = 3 * LANES
    acc[...] = jnp.zeros_like(acc)
    low = jnp.bfloat16
    scale = HD ** (-0.5)

    def block(b, _):
        start = jnp.clip(b - 1, 0, window // LANES - 3) * LANES
        keys_at = pl.ds(pl.multiple_of(start, LANES), band)
        keys_in = pl.ds(pl.multiple_of(window_start + start, LANES), band)
        keys_w = pl.ds(pl.multiple_of(start, LANES), band)
        here = pl.ds(pl.multiple_of(b * LANES, LANES), LANES)
        rows_in = pl.ds(pl.multiple_of(window_start + b * LANES, LANES), LANES)
        f_q, f_k = feat_q[rows_in], feat_k[keys_in]
        got = []
        for head, (q_at, k_at, v_at, half, v_half) in enumerate(HEAD_TILES):
            q_tile = qkv[m, here, q_at : q_at + LANES]
            k_tile = qkv[m, keys_w, k_at : k_at + LANES]
            v_tile = qkv[m, keys_w, v_at : v_at + LANES]
            mix_at = 0 if head < 2 else LANES
            d_tile = d_mixed[m, here, mix_at : mix_at + LANES]
            d_out = keep_half(v_half, d_tile, jnp.zeros_like(d_tile))
            scores = mm(keep_half(half, k_tile, f_k), keep_half(half, q_tile, f_q), NT)
            top = jnp.max(scores, axis=0, keepdims=True)
            weights = jnp.exp((scores - top) * scale)
            weights = weights * (1.0 / jnp.sum(weights, axis=0, keepdims=True))
            d_weights = mm(v_tile, d_out, NT)
            delta = jnp.sum(d_weights * weights, axis=0, keepdims=True)
            d_scores = (weights * (d_weights - delta)).astype(low)
            d_key = mm(d_scores, keep_half(half, q_tile * scale, jnp.zeros_like(q_tile)))
            d_value = mm(weights.astype(low), d_out)
            d_q = mm(d_scores, keep_half(half, k_tile * scale, jnp.zeros_like(k_tile)), TN)
            got.append((d_q, d_key, d_value))
        acc[keys_at, 0:LANES] += got[0][1] + got[1][1]
        acc[keys_at, LANES : 2 * LANES] += got[0][2] + got[1][2]
        acc[keys_at, 2 * LANES : 3 * LANES] += got[2][1] + got[2][2]
        d_query[here, 0:LANES] = (got[0][0] + got[1][0]).astype(low)
        d_query[here, LANES : 2 * LANES] = got[2][0].astype(low)
        return 0

    lax.fori_loop(0, window // LANES, block, 0)


class Loader:
    def __init__(self, n_mp, weights, out, sems):
        self.n_mp, self.weights, self.out, self.sems = n_mp, weights, out, sems
        self.mp = lax.axis_index("mp")

    def copy(self, t):
        group, plane = t // self.n_mp, t % self.n_mp
        return pltpu.make_async_copy(
            self.weights.at[group, plane], self.out.at[group, plane], self.sems.at[group, plane]
        )

    def plane(self, u):
        return u

    def begin(self):
        for t in range(GROUPS * self.n_mp):
            self.copy(t).start()

    def step(self, s):
        pass

    def stage_d(self, t):
        self.copy(t).wait()

    def finish(self):
        pass


def tile_rows(i, first=0):
    return pl.ds(pl.multiple_of(first + i * LANES, LANES), LANES)


def column_sum(v):
    return jnp.sum(v, axis=0, keepdims=True)


class Place:
    def __init__(self, set_rows, own_rows):
        self.set_rows, self.own_rows, self.window = set_rows, own_rows, own_rows + HALO
        mp = lax.axis_index("mp")
        per_set = set_rows // own_rows
        self.set_index, part = mp // per_set, mp % per_set
        self.window_start = pl.multiple_of(part * (set_rows - self.window), LANES)
        self.own_start = pl.multiple_of(part * (self.window - own_rows), LANES)
        self.own = pl.ds(self.own_start, own_rows)
        self.own_set = pl.ds(pl.multiple_of(self.window_start + self.own_start, LANES), own_rows)
        self.tiles = self.window // LANES

    def is_own(self, i):
        first = i * LANES
        return jnp.where((first >= self.own_start) & (first < self.own_start + self.own_rows), 1.0, 0.0)

    def valid(self, i, total):
        row = lax.broadcasted_iota(jnp.int32, (LANES, 1), 0) + (self.window_start + i * LANES)
        return jnp.where(row < total, 1.0, 0.0)


def layer_kernel(
    n_mp, slots, own_rows, remote, tokens_in, cot_in, blocks, counts, vec, bias,
    w0_out, qkv_out, mixed_out, normed_t_out, d_mid_out, d_proj_out, d_proj_t_out, grads_out, result_out, sums_out,
    w, tokens, cot, normed, normed_t, qkv, mixed, proj, middle, normed_two, normed_two_t, active, slope, branch,
    d_branch, d_branch_t, d_two, d_proj, stage, result, feat_q, feat_k,
    send_sems, recv_sems, way_sems, local_sems, out_sems, stage_sems,
):
    set_rows, width = tokens.shape
    place = Place(set_rows, own_rows)
    window, own, own_start, window_start, tiles = (
        place.window, place.own, place.own_start, place.window_start, place.tiles
    )
    low, f32 = jnp.bfloat16, jnp.float32
    in_set = pl.ds(pl.multiple_of(place.set_index * set_rows, LANES), set_rows)
    token_copy = pltpu.make_async_copy(tokens_in.at[in_set], tokens, local_sems.at[0])
    cot_copy = pltpu.make_async_copy(cot_in.at[in_set], cot, local_sems.at[1])
    token_copy.start()
    cot_copy.start()
    if remote:
        net = Gather(n_mp, w, send_sems, recv_sems, way_sems)
        own_copy = pltpu.make_async_copy(blocks, w.at[:, net.mp, net.dp], local_sems.at[2])
        own_copy.start()
        net.greet()
        own_copy.wait()
    else:
        net = Loader(n_mp, blocks, w, recv_sems)
    net.begin()

    def weight(group, m, lanes=None):
        block = w[group, m] if lanes is None else w[group, m, :, :, lanes]
        return block.reshape(width, block.shape[-1])

    total = make_features(counts, place.set_index, slots, set_rows, feat_q, feat_k)
    token_copy.wait()

    def norm_one(i, _):
        at = tile_rows(i)
        unit, _inv = row_stats(tokens[at].astype(f32))
        normed[at] = (unit * vec[0:1] + vec[1:2]).astype(low)
        return 0

    lax.fori_loop(0, set_rows // LANES, norm_one, 0)
    net.step(0)
    cot_copy.wait()
    zero_row = jnp.zeros((1, width), f32)

    def back_of(i):
        return cot[tile_rows(i, window_start)].astype(f32) * place.valid(i, total)

    def first_grad(i, total_row):
        db = (back_of(i) * vec[5:6]).astype(low)
        d_branch[tile_rows(i)] = db
        return total_row + place.is_own(i) * column_sum(db.astype(f32))

    branch_sum = lax.fori_loop(0, tiles, first_grad, zero_row)
    d_branch_t[...] = d_branch[own].T
    net.step(1)
    normed_t[...] = normed[place.own_set].T

    def project(u, _):
        net.step(u + 2)
        net.stage_d(u)
        m = net.plane(u)
        qkv[m] = (mm(normed[...], weight(0, m)) + bias[pl.ds(m, 1)]).astype(low)
        attend(m, qkv, mixed, feat_q, feat_k, window_start, window, window // 2)
        return 0

    project(0, 0)
    lax.fori_loop(1, n_mp, project, 0)
    outs = [
        pltpu.make_async_copy(w.at[0], w0_out, out_sems.at[0]),
        pltpu.make_async_copy(
            qkv.at[:, pl.ds(window_start, window)], qkv_out, out_sems.at[1]
        ),
        pltpu.make_async_copy(mixed.at[:, own], mixed_out, out_sems.at[2]),
        pltpu.make_async_copy(normed_t, normed_t_out, out_sems.at[3]),
    ]
    for copy in outs:
        copy.start()
    net.step(n_mp + 2)

    def out_part(m):
        return mm(mixed[m], weight(0, m, pl.ds(MIX, 2 * LANES)), NT)

    proj[...] = sum((out_part(m) for m in range(n_mp)), vec[6:7])

    def norm_two(i, _):
        at = tile_rows(i)
        mid = tokens[tile_rows(i, window_start)].astype(f32) + vec[4:5] * proj[at]
        middle[at] = mid
        unit, _inv = row_stats(mid)
        normed_two[at] = (unit * vec[2:3] + vec[3:4]).astype(low)
        return 0

    lax.fori_loop(0, tiles, norm_two, 0)
    normed_two_t[...] = normed_two[own].T

    def feed_up(u, _):
        net.step(u + 3 + n_mp)
        net.stage_d(u + n_mp)
        m = net.plane(u)

        def rows(i, _):
            at = tile_rows(i)
            hidden = mm(normed_two[at], weight(1, m)) + bias[pl.ds(n_mp + m, 1)]
            act, slp = gelu_parts(hidden)
            active[m, at] = act.astype(low)
            slope[m, at] = slp.astype(low)
            return 0

        lax.fori_loop(0, tiles, rows, 0)
        return 0

    lax.fori_loop(0, n_mp, feed_up, 0)

    def put(slot, group, m, value):
        stage[slot] = value.astype(low)
        pltpu.make_async_copy(stage.at[slot], grads_out.at[group, m], stage_sems.at[slot]).start()

    def put_done(slot):
        pltpu.make_async_copy(stage.at[slot], grads_out.at[0, 0], stage_sems.at[slot]).wait()

    def feed_down(u, _):
        net.step(u + 3 + 2 * n_mp)
        net.stage_d(u + 2 * n_mp)
        m = net.plane(u)
        down = weight(2, m)
        part_sum = mm(active[m, own], down, NT)

        @pl.when(u == 0)
        def _():
            branch[...] = part_sum

        @pl.when(u > 0)
        def _():
            branch[...] += part_sum

        def rows(i, total_row):
            at = tile_rows(i)
            dh = (mm(d_branch[at], weight(2, m)) * slope[m, at].astype(f32)).astype(low)
            slope[m, at] = dh
            return total_row + place.is_own(i) * column_sum(dh.astype(f32))

        sums_out[pl.ds(8 + m, 1)] = lax.fori_loop(0, tiles, rows, zero_row)

        @pl.when(u > 0)
        def _():
            put_done(0)
            put_done(1)

        put(0, 1, m, mm(d_branch_t[...], active[m, own]))
        put(1, 0, m, mm(normed_two_t[...], slope[m, own]))
        two_sum = mm(slope[m], weight(1, m), NT)

        @pl.when(u == 0)
        def _():
            d_two[...] = two_sum

        @pl.when(u > 0)
        def _():
            d_two[...] += two_sum

        return 0

    lax.fori_loop(0, n_mp, feed_down, 0)

    def final(i, carry):
        at, there = tile_rows(i), tile_rows(i, own_start)
        block = own_start // LANES + i
        br = branch[at] + vec[7:8]
        scaled = vec[5:6] * br
        res = middle[there] + scaled
        result[at] = res.astype(low)
        attn = vec[4:5] * proj[there]
        valid = place.valid(block, total)
        sums = [column_sum(valid * v * v) for v in (res, attn, scaled)] + [column_sum(back_of(block) * br)]
        return tuple(c + s for c, s in zip(carry, sums))

    res_sq, attn_sq, scaled_sq, back_branch = lax.fori_loop(0, own_rows // LANES, final, (zero_row,) * 4)
    result_copy = pltpu.make_async_copy(result, result_out, out_sems.at[4])
    result_copy.start()

    def norm_two_back(i, carry):
        at = tile_rows(i)
        grad = d_two[at]
        dv, grad_unit = norm_grad(middle[at], vec[2:3], grad)
        d_mid = back_of(i) + dv
        d_two[at] = d_mid
        dp = (d_mid * vec[4:5]).astype(low)
        d_proj[at] = dp
        mine = place.is_own(i)
        new = (grad_unit, grad, d_mid * proj[at], dp.astype(f32))
        return tuple(c + mine * column_sum(n) for c, n in zip(carry, new))

    gain_sum, shift_sum, scale_sum, proj_sum = lax.fori_loop(0, tiles, norm_two_back, (zero_row,) * 4)
    d_branch_t[...] = d_proj[own].T
    more = [
        pltpu.make_async_copy(d_two, d_mid_out, out_sems.at[5]),
        pltpu.make_async_copy(d_proj, d_proj_out, out_sems.at[6]),
        pltpu.make_async_copy(d_branch_t, d_proj_t_out, out_sems.at[7]),
    ]
    for copy in more:
        copy.start()
    rows_out = (zero_row, zero_row, gain_sum, shift_sum, scale_sum, back_branch, proj_sum, branch_sum)
    for i, row in enumerate(rows_out):
        sums_out[i : i + 1] = row
    for i, row in enumerate((res_sq, attn_sq, scaled_sq, zero_row)):
        sums_out[12 + i : 13 + i] = row
    put_done(0)
    put_done(1)
    for copy in outs + [result_copy] + more:
        copy.wait()
    net.finish()


class Stream:
    CUTS = 4

    def __init__(self, n_mp, src, out, send_sems, recv_sems):
        self.dp, self.mp, self.n_mp = lax.axis_index("dp"), lax.axis_index("mp"), n_mp
        self.src, self.out, self.send_sems, self.recv_sems = src, out, send_sems, recv_sems
        self.rows = out.shape[1] // self.CUTS
        self.up, self.down = jnp.minimum(self.mp + 1, n_mp - 1), jnp.maximum(self.mp - 1, 0)

    def message(self, plane, cut, way, own):
        part = pl.ds(pl.multiple_of(cut * self.rows, self.rows), self.rows)
        where = self.out.at[plane, part]
        return pltpu.make_async_remote_copy(
            src_ref=self.src.at[part] if own else where,
            dst_ref=where,
            send_sem=self.send_sems.at[way, plane, cut],
            recv_sem=self.recv_sems.at[plane, cut],
            device_id=(self.dp, self.down if way else self.up),
            device_id_type=MESH,
        )

    def pass_on(self, distance, cut, ways, action):
        mp, last = self.mp, self.n_mp - 1
        below, above = mp - distance, mp + distance

        def one(plane, way, there):
            @pl.when(there)
            def _():
                action(plane, way, True)

        one(below, 0, below >= 0)
        one(above, 1, above <= last)

    def step(self, s):
        distance, cut = s // self.CUTS, s % self.CUTS
        mp, last = self.mp, self.n_mp - 1

        @pl.when((distance == 0) & (mp < last))
        def _():
            self.message(mp, cut, 0, True).start()

        @pl.when((distance == 0) & (mp > 0))
        def _():
            self.message(mp, cut, 1, True).start()

        below, above = mp - distance, mp + distance

        @pl.when((distance > 0) & (below >= 0))
        def _():
            self.message(below, cut, 0, False).wait_recv()

            @pl.when(mp < last)
            def _():
                self.message(below, cut, 0, False).start()

        @pl.when((distance > 0) & (above <= last))
        def _():
            self.message(above, cut, 1, False).wait_recv()

            @pl.when(mp > 0)
            def _():
                self.message(above, cut, 1, False).start()

    STEPS = 16

    def finish(self):
        mp, last = self.mp, self.n_mp - 1

        def body(t, _):
            plane, cut = t // self.CUTS, t % self.CUTS

            @pl.when((plane <= mp) & (mp < last))
            def _():
                self.message(plane, cut, 0, False).wait_send()

            @pl.when((plane >= mp) & (mp > 0))
            def _():
                self.message(plane, cut, 1, False).wait_send()

            return 0

        lax.fori_loop(0, self.n_mp * self.CUTS, body, 0)


def back_kernel(
    n_mp, slots, own_rows, set_rows, remote, tokens_in, counts, vec, w0_in, qkv_in, mixed_in, normed_t_in, d_mid_in,
    d_proj_in, d_proj_t_in, grads_in, result_in,
    reduced, input_out, sums_out, stream_out, *rest,
):
    if remote:
        rest, scatter_refs = rest[:-12], rest[-12:]
    (
        tokens, w0, qkv, mixed, normed_t, d_mid, d_proj, d_proj_t, d_mixed, acc, d_query, d_qkv, d_normed, fresh,
        feat_q, feat_k, local_sems,
    ) = rest
    width = d_mid.shape[1]
    place = Place(set_rows, own_rows)
    window, own, own_start = place.window, place.own, place.own_start
    low, f32 = jnp.bfloat16, jnp.float32
    mp = lax.axis_index("mp")
    first = pl.multiple_of(place.set_index * set_rows + place.window_start + own_start, LANES)
    loads = [
        pltpu.make_async_copy(src, dst, local_sems.at[i])
        for i, (src, dst) in enumerate(
            (
                (d_proj_in, d_proj), (w0_in, w0), (qkv_in, qkv), (normed_t_in, normed_t), (d_proj_t_in, d_proj_t),
                (mixed_in, mixed), (tokens_in.at[pl.ds(first, own_rows)], tokens), (d_mid_in, d_mid),
            )
        )
    ]
    for copy in loads:
        copy.start()
    if remote:
        bufs, load_sems, send_sems, recv_sems, stream_send, stream_recv = (
            scatter_refs[:7], *scatter_refs[7:]
        )
        net = Scatter(n_mp, grads_in, fresh, reduced, bufs, load_sems, send_sems, recv_sems)
        stream = Stream(n_mp, result_in, stream_out, stream_send, stream_recv)
        net.greet()
        net.offer(0)
        net.offer(1)
        own_result = pltpu.make_async_copy(result_in, stream_out.at[mp], local_sems.at[8])
        own_result.start()

    def step(s):
        if remote:
            net.step(s)
            stream.step(s)

    make_features(counts, place.set_index, slots, set_rows, feat_q, feat_k)
    zero_row = jnp.zeros((1, width), f32)

    def weight(m, lanes=None):
        block = w0[m] if lanes is None else w0[m, :, :, lanes]
        return block.reshape(width, block.shape[-1])

    for copy in loads:
        copy.wait()

    def attention(u, _):
        m = net.plane(u) if remote else u
        dm = mm(d_proj[...], weight(m, pl.ds(MIX, 2 * LANES))).astype(low)
        d_mixed[m, :, 0:LANES] = dm[:, 0:LANES]
        d_mixed[m, :, LANES:] = keep_half(1, dm[:, LANES:], jnp.zeros_like(dm[:, LANES:]))
        step(2 * u)
        attend_back(m, qkv, d_mixed, feat_q, feat_k, place.window_start, window, acc, d_query)
        d_qkv[m, :, 0:128] = d_query[own, 0:128]
        d_qkv[m, :, 128:256] = acc[own, 0:128].astype(low)
        d_qkv[m, :, 256:384] = acc[own, 128:256].astype(low)
        d_qkv[m, :, 384:512] = jnp.zeros((own_rows, LANES), low)
        d_qkv[m, :, 512:640] = d_query[own, 128:256]
        d_qkv[m, :, 640:768] = acc[own, 256:384].astype(low)
        sums_out[pl.ds(8 + m, 1)] = column_sum(d_qkv[m].astype(f32))
        step(2 * u + 1)
        block = mm(normed_t[...], d_qkv[m])
        extra = mm(d_proj_t[...], mixed[m])
        shape = fresh.shape[1:4]

        def keep(lanes, value):
            fresh[m, :, :, :, lanes] = value.astype(low).reshape(*shape, value.shape[1])

        keep(pl.ds(0, MIX), block[:, 0:MIX])
        keep(pl.ds(MIX, 2 * LANES), block[:, MIX : MIX + 2 * LANES] + extra)
        keep(pl.ds(MIX + 2 * LANES, LANES), block[:, MIX + 2 * LANES :])
        if remote:
            net.offer_fresh(u)
        part_sum = mm(d_qkv[m], weight(m), NT)

        @pl.when(u == 0)
        def _():
            d_normed[...] = part_sum

        @pl.when(u > 0)
        def _():
            d_normed[...] += part_sum

        return 0

    lax.fori_loop(0, n_mp, attention, 0)

    def norm_one(i, carry):
        at = tile_rows(i)
        grad = d_normed[at]
        dv, grad_unit = norm_grad(tokens[at].astype(f32), vec[0:1], grad)
        input_out[at] = (d_mid[tile_rows(i, own_start)] + dv).astype(low)
        return tuple(c + column_sum(n) for c, n in zip(carry, (grad_unit, grad)))

    gain_one, shift_one = lax.fori_loop(0, own_rows // LANES, norm_one, (zero_row, zero_row))
    sums_out[0:1] = gain_one
    sums_out[1:2] = shift_one
    sums_out[2:8] = jnp.zeros((6, width), f32)
    if remote:

        def more(s, _):
            step(s)
            return 0

        lax.fori_loop(2 * n_mp, GROUPS * n_mp + net.STEPS, more, 0)

        def rest_of_stream(s, _):
            stream.step(s)
            return 0

        lax.fori_loop(GROUPS * n_mp + net.STEPS, stream.STEPS, rest_of_stream, 0)
        net.finish()
        stream.finish()
        own_result.wait()
    else:
        reduced[...] = jnp.zeros_like(reduced)
        fresh_copy = pltpu.make_async_copy(fresh, stream_out, local_sems.at[8])
        fresh_copy.start()
        fresh_copy.wait()


def shard_offset(shard_piece, block_index, whole_length, axis_at):
    shape_list = list(shard_piece.shape)
    shape_list[axis_at] = whole_length
    empty = jnp.zeros(tuple(shape_list), jnp.float32)
    return lax.dynamic_update_slice_in_dim(
        empty, shard_piece, block_index * shard_piece.shape[axis_at], axis_at
    )


def select_slice(whole_array, block_index, block_width, axis_at):
    return lax.dynamic_slice_in_dim(whole_array, block_index * block_width, block_width, axis_at)


def factor_step(
    gradient,
    rows_old,
    cols_old,
    rows_mine,
    cols_mine,
    rows_total,
    count_rows,
    count_cols,
    prior_total,
):
    decay_rate = 1.0 - STEP ** (-0.8)
    rows_new = decay_rate * rows_old + (1.0 - decay_rate) * (rows_mine / count_cols + square_eps)
    cols_new = decay_rate * cols_old + (1.0 - decay_rate) * (cols_mine / count_rows + square_eps)
    rows_average = (
        decay_rate * prior_total
        + (1.0 - decay_rate) * (rows_total / count_cols + count_rows * square_eps)
    ) / count_rows
    update = gradient * lax.rsqrt(rows_new[:, None] * cols_new[None, :] / rows_average)
    return (rows_new, cols_new, update, jnp.sum(update * update))


def plain_step(weight, gradient, moment_old):
    decay_rate = 1.0 - STEP ** (-0.8)
    moment = decay_rate * moment_old + (1.0 - decay_rate) * (gradient * gradient + square_eps)
    update = gradient * lax.rsqrt(moment)
    update_rms = jnp.sqrt(jnp.mean(update * update))
    rate_here = step_rate * jnp.sqrt(jnp.mean(weight * weight))
    return (weight - rate_here * update / jnp.maximum(1.0, update_rms / clip_limit), moment)


def shards(
    tokens_in,
    cotangent,
    patch_counts,
    w_qkv,
    w_out,
    w_up,
    w_down,
    layer_vector_rows,
    inner_biases,
    qkvrows_prior,
    qkvcols_prior,
    outrows_prior,
    outcols_prior,
    uprows_prior,
    upcols_prior,
    downrows_prior,
    downcols_prior,
    vector_moment,
    bias_moment,
):
    n_dp, n_mp = lax.axis_size("dp"), lax.axis_size("mp")
    data_index = lax.axis_index("dp")
    parallel_model_index = lax.axis_index("mp")
    row_count, parallel_model_width = tokens_in.shape
    set_count, slot_count = patch_counts.shape
    set_rows = row_count // set_count
    own_rows = row_count // n_mp
    shard_width_local = w_qkv.shape[2]
    local_hidden = w_up.shape[1]
    f32, low = jnp.float32, jnp.bfloat16
    width, hidden_width = parallel_model_width, local_hidden
    blocks = pack(w_qkv, w_out, w_up, w_down).astype(low)
    set_index = parallel_model_index // (set_rows // own_rows)
    window = own_rows + HALO
    by_mp = inner_biases.reshape(6, n_mp, shard_width_local)
    none = jnp.zeros((n_mp, shard_width_local), f32)
    bias_rows = jnp.concatenate(
        [
            permute_chunks(jnp.concatenate([by_mp[0], none, by_mp[1], none], axis=1), CHUNKS),
            by_mp[2:].transpose(1, 2, 0).reshape(n_mp, hidden_width),
        ]
    )
    vmem = pl.BlockSpec(memory_space=pltpu.VMEM)
    anywhere = pl.BlockSpec(memory_space=pl.ANY)
    scalars_in = pl.BlockSpec(memory_space=pltpu.SMEM)
    dma = pltpu.SemaphoreType.DMA

    def shape(*dims, dtype=low):
        return jax.ShapeDtypeStruct(dims, dtype)

    block_rows = blocks.shape[1]
    remote = n_dp == 8 and n_mp == 4 and block_rows % 32 == 0
    split_dp = (n_dp, block_rows)
    if not remote:
        blocks = lax.all_gather(lax.all_gather(blocks, "dp", axis=1, tiled=True), "mp", axis=1)
        split_dp = (1, width)
        blocks = blocks.reshape(GROUPS, n_mp, 1, width, width)
    w0, qkv, mixed, normed_t, d_mid, d_proj, d_proj_t, grads_ffn, result, sums_a = pl.pallas_call(
        functools.partial(layer_kernel, n_mp, slot_count, own_rows, remote),
        out_shape=(
            shape(n_mp, *split_dp, width),
            shape(n_mp, window, width),
            shape(n_mp, own_rows, 2 * LANES),
            shape(width, own_rows),
            shape(window, width, dtype=f32),
            shape(window, width),
            shape(width, own_rows),
            shape(2, n_mp, width, width),
            shape(own_rows, width),
            shape(16, width, dtype=f32),
        ),
        in_specs=[anywhere, anywhere, anywhere, scalars_in, vmem, vmem],
        out_specs=(anywhere,) * 9 + (vmem,),
        scratch_shapes=[
            pltpu.VMEM((GROUPS, n_mp, *split_dp, width), low),
            pltpu.VMEM((set_rows, width), low),
            pltpu.VMEM((set_rows, width), low),
            pltpu.VMEM((set_rows, width), low),
            pltpu.VMEM((width, own_rows), low),
            pltpu.VMEM((n_mp, set_rows, width), low),
            pltpu.VMEM((n_mp, window, 2 * LANES), low),
            pltpu.VMEM((window, width), f32),
            pltpu.VMEM((window, width), f32),
            pltpu.VMEM((window, width), low),
            pltpu.VMEM((width, own_rows), low),
            pltpu.VMEM((n_mp, window, hidden_width), low),
            pltpu.VMEM((n_mp, window, hidden_width), low),
            pltpu.VMEM((own_rows, width), f32),
            pltpu.VMEM((window, width), low),
            pltpu.VMEM((width, own_rows), low),
            pltpu.VMEM((window, width), f32),
            pltpu.VMEM((window, width), low),
            pltpu.VMEM((2, width, width), low),
            pltpu.VMEM((own_rows, width), low),
            pltpu.VMEM((set_rows, LANES), low),
            pltpu.VMEM((set_rows, LANES), low),
            dma((GROUPS, n_mp, KINDS)),
            dma((GROUPS, n_mp, KINDS) if remote else (GROUPS, n_mp)),
            dma((GROUPS, n_mp, 2)),
            dma((3,)),
            dma((8,)),
            dma((2,)),
        ],
        compiler_params=pltpu.CompilerParams(
            vmem_limit_bytes=63 * 2**20,
            **(dict(collective_id=1, has_side_effects=True) if remote else {}),
        ),
    )(tokens_in, cotangent, blocks, patch_counts, layer_vector_rows, bias_rows)
    block = (n_mp, block_rows, width)
    scatter_scratch = [
        pltpu.VMEM((GROUPS, n_mp, 4, block_rows, width), low),
        pltpu.VMEM((GROUPS, n_mp, 2, block_rows // 2, width), low),
        pltpu.VMEM((GROUPS, *block), low),
        pltpu.VMEM((GROUPS, *block), low),
        pltpu.VMEM((GROUPS, n_mp, 2, block_rows, width), low),
        pltpu.VMEM((GROUPS, n_mp, 4, block_rows, width), low),
        pltpu.VMEM((GROUPS, *block), low),
        dma((GROUPS, n_mp)),
        dma((GROUPS, n_mp, R_KINDS)),
        dma((GROUPS, n_mp, R_KINDS)),
        dma((2, n_mp, Stream.CUTS)),
        dma((n_mp, Stream.CUTS)),
    ]
    reduced, input_rows, sums_b, stream = pl.pallas_call(
        functools.partial(back_kernel, n_mp, slot_count, own_rows, set_rows, remote),
        out_shape=(
            shape(GROUPS, block_rows, width, dtype=f32),
            shape(own_rows, width),
            shape(16, width, dtype=f32),
            shape(n_mp, own_rows, width) if remote else shape(n_mp, 1, 1, width, width),
        ),
        in_specs=[anywhere, scalars_in, vmem] + [anywhere] * 9,
        out_specs=(vmem, vmem, vmem, anywhere),
        scratch_shapes=[
            pltpu.VMEM((own_rows, width), low),
            pltpu.VMEM((n_mp, *split_dp, width), low),
            pltpu.VMEM((n_mp, window, width), low),
            pltpu.VMEM((n_mp, own_rows, 2 * LANES), low),
            pltpu.VMEM((width, own_rows), low),
            pltpu.VMEM((window, width), f32),
            pltpu.VMEM((window, width), low),
            pltpu.VMEM((width, own_rows), low),
            pltpu.VMEM((n_mp, window, 2 * LANES), low),
            pltpu.VMEM((window, 3 * LANES), f32),
            pltpu.VMEM((window, 2 * LANES), low),
            pltpu.VMEM((n_mp, own_rows, width), low),
            pltpu.VMEM((own_rows, width), f32),
            pltpu.VMEM((n_mp, n_dp // 2, 2, block_rows, width) if remote else (n_mp, 1, 1, width, width), low),
            pltpu.VMEM((set_rows, LANES), low),
            pltpu.VMEM((set_rows, LANES), low),
            dma((9,)),
        ]
        + (scatter_scratch if remote else []),
        compiler_params=pltpu.CompilerParams(
            vmem_limit_bytes=63 * 2**20,
            **(dict(collective_id=2, has_side_effects=True) if remote else {}),
        ),
    )(
        tokens_in, patch_counts, layer_vector_rows, w0, qkv, mixed, normed_t, d_mid, d_proj, d_proj_t,
        grads_ffn.reshape(2, n_mp, n_dp // 2, 2, block_rows, width), result,
    )
    vector_part = sums_a[:8] + sums_b[:8]
    bias_sums = jnp.concatenate([sums_b[8 : 8 + n_mp], sums_a[8 : 8 + n_mp]])
    if remote:
        result_low = stream.reshape(row_count, width)
        reduced = jnp.concatenate([reduced[2:], reduced[:2]])
    else:
        result_low = lax.all_gather(result, "mp", axis=0, tiled=True)
        grads = jnp.concatenate([stream.reshape(1, n_mp, width, width), grads_ffn])
        own = lax.psum_scatter(grads, "mp", scatter_dimension=1)
        reduced = lax.psum_scatter(own, "dp", scatter_dimension=1, tiled=True).astype(f32)
    input_grad = lax.all_to_all(input_rows, "mp", 1, 0, tiled=True).astype(f32)

    bias_qkv = permute_chunks(bias_sums[:n_mp], BACK).reshape(n_mp, 4, shard_width_local)
    hidden_sums = bias_sums[n_mp:].reshape(n_mp, shard_width_local, -1).transpose(2, 0, 1)
    bias_part = jnp.concatenate(
        [
            bias_qkv[:, 0].reshape(1, width),
            bias_qkv[:, 2].reshape(1, width),
            hidden_sums.reshape(-1, width),
        ]
    )
    own_first = parallel_model_index % (set_rows // own_rows) * own_rows
    held = jnp.sum(lax.dynamic_index_in_dim(patch_counts, set_index, 0, keepdims=False))
    counted = jnp.clip(held - own_first, 0, own_rows).astype(f32)
    vector_grad, bias_grad, squares_all, counted_all = lax.psum(
        (vector_part, bias_part, jnp.sum(sums_a[12:15], axis=1), counted), ("dp", "mp")
    )
    token_spread = jnp.sqrt(squares_all / (counted_all * parallel_model_width))
    qkv_grad, out_grad, up_grad, down_grad = unpack(reduced)
    square_qkv = qkv_grad * qkv_grad
    square_out = out_grad * out_grad
    square_up = up_grad * up_grad
    square_down = down_grad * down_grad
    scalars = jnp.stack(
        [
            jnp.sum(w_qkv * w_qkv),
            jnp.sum(w_out * w_out),
            jnp.sum(w_up * w_up),
            jnp.sum(w_down * w_down),
            jnp.where(parallel_model_index == 0, jnp.sum(qkvrows_prior), 0.0),
            jnp.where(data_index == 0, jnp.sum(outrows_prior), 0.0),
            jnp.where(parallel_model_index == 0, jnp.sum(uprows_prior), 0.0),
            jnp.where(data_index == 0, jnp.sum(downrows_prior), 0.0),
        ]
    )
    factor_totals = lax.psum(
        (
            shard_offset(jnp.sum(square_qkv, axis=(1, 2)), data_index, parallel_model_width, 0),
            shard_offset(
                jnp.sum(square_qkv, axis=0), parallel_model_index, parallel_model_width, 1
            ),
            shard_offset(
                jnp.sum(square_out, axis=1), parallel_model_index, parallel_model_width, 0
            ),
            shard_offset(jnp.sum(square_out, axis=0), data_index, parallel_model_width, 0),
            shard_offset(jnp.sum(square_up, axis=1), data_index, parallel_model_width, 0),
            shard_offset(jnp.sum(square_up, axis=0), parallel_model_index, FF, 0),
            shard_offset(jnp.sum(square_down, axis=1), parallel_model_index, FF, 0),
            shard_offset(jnp.sum(square_down, axis=0), data_index, parallel_model_width, 0),
            scalars,
        ),
        ("dp", "mp"),
    )
    (
        rows_qkv,
        cols_qkv,
        rows_out,
        cols_out,
        rows_up,
        cols_up,
        rows_down,
        cols_down,
        scalar_totals,
    ) = factor_totals
    local_rows = w_qkv.shape[0]
    local_cols = w_out.shape[1]
    qkvrows_after, qkvcols_flat, update_qkv, usq_qkv = factor_step(
        qkv_grad.reshape(local_rows, 3 * shard_width_local),
        qkvrows_prior,
        qkvcols_prior.reshape(3 * shard_width_local),
        select_slice(rows_qkv, data_index, local_rows, 0),
        select_slice(cols_qkv, parallel_model_index, shard_width_local, 1).reshape(
            3 * shard_width_local
        ),
        jnp.sum(rows_qkv),
        parallel_model_width,
        3 * parallel_model_width,
        scalar_totals[4],
    )
    outrows_after, outcols_after, update_out, usq_out = factor_step(
        out_grad,
        outrows_prior,
        outcols_prior,
        select_slice(rows_out, parallel_model_index, shard_width_local, 0),
        select_slice(cols_out, data_index, local_cols, 0),
        jnp.sum(rows_out),
        parallel_model_width,
        parallel_model_width,
        scalar_totals[5],
    )
    uprows_after, upcols_after, update_up, usq_up = factor_step(
        up_grad,
        uprows_prior,
        upcols_prior,
        select_slice(rows_up, data_index, local_rows, 0),
        select_slice(cols_up, parallel_model_index, local_hidden, 0),
        jnp.sum(rows_up),
        parallel_model_width,
        FF,
        scalar_totals[6],
    )
    downrows_after, downcols_after, update_down, usq_down = factor_step(
        down_grad,
        downrows_prior,
        downcols_prior,
        select_slice(rows_down, parallel_model_index, local_hidden, 0),
        select_slice(cols_down, data_index, local_cols, 0),
        jnp.sum(rows_down),
        FF,
        parallel_model_width,
        scalar_totals[7],
    )
    usq_totals = lax.psum(jnp.stack([usq_qkv, usq_out, usq_up, usq_down]), ("dp", "mp"))
    entry_counts = jnp.array(
        [
            3.0 * parallel_model_width * parallel_model_width,
            1.0 * parallel_model_width * parallel_model_width,
            1.0 * parallel_model_width * FF,
            1.0 * FF * parallel_model_width,
        ],
        jnp.float32,
    )
    update_scale = jnp.sqrt(usq_totals / entry_counts)
    weight_rms = jnp.sqrt(scalar_totals[:4] / entry_counts)
    limits = jnp.maximum(1.0, update_scale / clip_limit)
    qkv_after = (
        w_qkv.reshape(local_rows, 3 * shard_width_local)
        - step_rate * weight_rms[0] * update_qkv / limits[0]
    ).reshape(w_qkv.shape)
    out_after = w_out - step_rate * weight_rms[1] * update_out / limits[1]
    up_after = w_up - step_rate * weight_rms[2] * update_up / limits[2]
    down_after = w_down - step_rate * weight_rms[3] * update_down / limits[3]
    vectors_after, moment_vectors = jax.vmap(plain_step)(
        layer_vector_rows, vector_grad, vector_moment
    )
    heads_after, heads_moment = jax.vmap(plain_step)(
        inner_biases[:2], bias_grad[:2], bias_moment[:2]
    )
    upper_after, upper_moment = plain_step(
        inner_biases[2:].reshape(FF), bias_grad[2:].reshape(FF), bias_moment[2:].reshape(FF)
    )
    biases_after = jnp.concatenate(
        [heads_after, upper_after.reshape(FF // parallel_model_width, parallel_model_width)], axis=0
    )
    moment_biases = jnp.concatenate(
        [heads_moment, upper_moment.reshape(FF // parallel_model_width, parallel_model_width)],
        axis=0,
    )
    return (
        result_low,
        input_grad,
        qkv_grad,
        out_grad,
        up_grad,
        down_grad,
        qkv_after,
        out_after,
        up_after,
        down_after,
        qkv_after.astype(jnp.bfloat16),
        out_after.astype(jnp.bfloat16),
        up_after.astype(jnp.bfloat16),
        down_after.astype(jnp.bfloat16),
        qkvrows_after,
        qkvcols_flat.reshape(3, shard_width_local),
        outrows_after,
        outcols_after,
        uprows_after,
        upcols_after,
        downrows_after,
        downcols_after,
        vector_grad,
        bias_grad,
        moment_vectors,
        moment_biases,
        vectors_after,
        biases_after,
        update_scale,
        token_spread,
    )


def solution(mesh):
    in_specs = (
        P("dp", None),
        P("dp", None),
        P("dp", None),
        P("dp", None, "mp"),
        P("mp", "dp"),
        P("dp", "mp"),
        P("mp", "dp"),
        P(),
        P(),
        P("dp"),
        P(None, "mp"),
        P("mp"),
        P("dp"),
        P("dp"),
        P("mp"),
        P("mp"),
        P("dp"),
        P(),
        P(),
    )
    out_specs = (
        P("dp", None),
        P("dp", "mp"),
        P("dp", None, "mp"),
        P("mp", "dp"),
        P("dp", "mp"),
        P("mp", "dp"),
        P("dp", None, "mp"),
        P("mp", "dp"),
        P("dp", "mp"),
        P("mp", "dp"),
        P("dp", None, "mp"),
        P("mp", "dp"),
        P("dp", "mp"),
        P("mp", "dp"),
        P("dp"),
        P(None, "mp"),
        P("mp"),
        P("dp"),
        P("dp"),
        P("mp"),
        P("mp"),
        P("dp"),
        P(),
        P(),
        P(),
        P(),
        P(),
        P(),
        P(),
        P(),
    )
    return jax.shard_map(shards, mesh=mesh, in_specs=in_specs, out_specs=out_specs, check_vma=False)
```

```python
import functools

import jax
import jax.numpy as jnp
from jax import lax
from jax.experimental import pallas as pl
from jax.experimental.pallas import tpu as pltpu
from jax.sharding import PartitionSpec as P

HD = 64
FF = 3072
STEP = 3


norm_eps = 1e-06
square_eps = 1e-30
clip_limit = 0.5
step_rate = 0.6
mask_fill = -1000000000.0


MESH = pl.DeviceIdType.MESH
HALO = 128
GROUPS = 3
CHUNKS = (0, 1, 3, 4, 6, 7, 9, 10, 2, 11, 5, 8)
BACK = tuple(CHUNKS.index(i) for i in range(12))


def moments_of(stream):
    center = stream - jnp.mean(stream, axis=-1, keepdims=True)
    spread = jnp.mean(center * center, axis=-1, keepdims=True)
    return (center, lax.rsqrt(spread + norm_eps))


def normalize(stream, gain_row, shift_row):
    center, inverse = moments_of(stream)
    return center * inverse * gain_row + shift_row


def segment_ids(counts, set_rows):
    image_ends = jnp.cumsum(counts)
    places = jnp.arange(set_rows, dtype=jnp.int32)
    return jnp.sum((places[:, None] >= image_ends[None, :]).astype(jnp.int32), axis=1)


def permute_chunks(block, order):
    parts = [block[..., HD * i : HD * (i + 1)] for i in order]
    return jnp.concatenate(parts, axis=-1)


def pack(qkv, out, up, down):
    first = jnp.concatenate([qkv[:, 0], qkv[:, 1], qkv[:, 2], out.T], axis=1)
    return jnp.stack([permute_chunks(first, CHUNKS), up, down.T])


def unpack(blocks):
    first = permute_chunks(blocks[0], BACK)
    width = first.shape[-1] // 4
    qkv = first[:, : 3 * width].reshape(first.shape[0], 3, width)
    return qkv, first[:, 3 * width :].T, blocks[1], blocks[2].T


def neighbours(dp):
    core = dp % 2
    return dp + 1 - 2 * core, dp + 2 - 4 * ((dp // 2) % 2), (dp + 4) % 8, (dp + 4) % 8 + 2 - 4 * ((dp // 2) % 2)


def flip(dp):
    return dp + 1 - 2 * (dp % 2)


def greet(devices, extra):
    barrier = pltpu.get_barrier_semaphore()
    for device in devices:
        pl.semaphore_signal(barrier, inc=1, device_id=device, device_id_type=MESH)
    for condition, device in extra:

        @pl.when(condition)
        def _():
            pl.semaphore_signal(barrier, inc=1, device_id=device, device_id_type=MESH)

    peers = len(devices)
    for condition, _ in extra:
        peers = peers + jnp.where(condition, 1, 0)
    pl.semaphore_wait(barrier, peers)


A_Z, A_X, A_Y, A_D0, A_D1, A_S, A_SX, A_SY, A_SD0, A_SD1 = range(10)
KINDS = 10
ORDERS = ((0, 1, 2, 3), (1, 0, 2, 3), (2, 3, 1, 0), (3, 2, 1, 0))


def plane_at(mp, unit):
    codes = [sum(plane * 4**i for i, plane in enumerate(order)) for order in ORDERS]
    code = jnp.where(mp == 0, codes[0], jnp.where(mp == 1, codes[1], jnp.where(mp == 2, codes[2], codes[3])))
    power = jnp.where(unit == 0, 1, jnp.where(unit == 1, 4, jnp.where(unit == 2, 16, 64)))
    return (code // power) % 4


class Gather:
    def __init__(self, n_mp, out, send_sems, recv_sems, way_sems):
        self.dp, self.mp, self.n_mp = lax.axis_index("dp"), lax.axis_index("mp"), n_mp
        self.out, self.send_sems, self.recv_sems, self.way_sems = out, send_sems, recv_sems, way_sems
        self.sib, self.xn, self.yn, self.dn = neighbours(self.dp)
        self.rows = out.shape[3]
        self.up, self.down = jnp.minimum(self.mp + 1, n_mp - 1), jnp.maximum(self.mp - 1, 0)
        half = self.rows // 2
        self.all, self.low, self.high = pl.ds(0, self.rows), pl.ds(0, half), pl.ds(half, half)

    def greet(self):
        dp, mp = self.dp, self.mp
        greet(
            [(self.sib, mp), (self.xn, mp), (self.yn, mp)],
            [(mp < self.n_mp - 1, (dp, self.up)), (mp > 0, (dp, self.down))],
        )

    def message(self, kind, group, plane, slot, part, device):
        where = self.out.at[group, plane, slot, part]
        return pltpu.make_async_remote_copy(
            src_ref=where,
            dst_ref=where,
            send_sem=self.send_sems.at[group, plane, kind],
            recv_sem=self.recv_sems.at[group, plane, kind],
            device_id=(device, self.mp),
            device_id_type=MESH,
        )

    def along(self, group, plane, way):
        where = self.out.at[group, plane, self.dp]
        return pltpu.make_async_remote_copy(
            src_ref=where,
            dst_ref=where,
            send_sem=self.way_sems.at[group, plane, way],
            recv_sem=self.recv_sems.at[group, plane, A_Z],
            device_id=(self.dp, self.down if way else self.up),
            device_id_type=MESH,
        )

    def sends(self, group, plane):
        dp, xn, yn, dn, sib = self.dp, self.xn, self.yn, self.dn, self.sib
        first = [(A_X, dp, self.all, xn), (A_Y, dp, self.all, yn), (A_S, dp, self.all, sib)]
        second = [(A_D0, xn, self.low, yn), (A_SX, xn, self.all, sib), (A_D1, yn, self.high, xn), (A_SY, yn, self.all, sib)]
        third = [(A_SD0, dn, self.low, sib), (A_SD1, dn, self.high, sib)]
        return [
            [functools.partial(self.message, kind, group, plane, *rest) for kind, *rest in part]
            for part in (first, second, third)
        ]

    def unit(self, t):
        group = t // self.n_mp
        return group, plane_at(self.mp, t % self.n_mp)

    def guarded(self, t, action):
        if isinstance(t, int):
            if 0 <= t < GROUPS * self.n_mp:
                action(*self.unit(t))
            return

        @pl.when((t >= 0) & (t < GROUPS * self.n_mp))
        def _():
            action(*self.unit(t))

    def stage_z(self, t):
        def action(group, plane):
            @pl.when(plane != self.mp)
            def _():
                self.along(group, plane, 0).wait_recv()

            @pl.when((plane <= self.mp) & (self.mp < self.n_mp - 1))
            def _():
                self.along(group, plane, 0).start()

            @pl.when((plane >= self.mp) & (self.mp > 0))
            def _():
                self.along(group, plane, 1).start()

        self.guarded(t, action)

    def stage_a(self, t):
        def action(group, plane):
            for copy in self.sends(group, plane)[0]:
                copy().start()

        self.guarded(t, action)

    def stage_b(self, t):
        def action(group, plane):
            out = self.sends(group, plane)[1]
            self.message(A_X, group, plane, self.xn, self.all, self.xn).wait_recv()
            out[0]().start()
            out[1]().start()
            self.message(A_Y, group, plane, self.yn, self.all, self.yn).wait_recv()
            out[2]().start()
            out[3]().start()

        self.guarded(t, action)

    def stage_c(self, t):
        def action(group, plane):
            out = self.sends(group, plane)[2]
            self.message(A_D0, group, plane, self.dn, self.low, self.yn).wait_recv()
            out[0]().start()
            self.message(A_D1, group, plane, self.dn, self.high, self.xn).wait_recv()
            out[1]().start()

        self.guarded(t, action)

    def stage_d(self, t):
        def action(group, plane):
            for kind, slot, part in (
                (A_S, self.sib, self.all),
                (A_SX, flip(self.xn), self.all),
                (A_SY, flip(self.yn), self.all),
                (A_SD0, flip(self.dn), self.low),
                (A_SD1, flip(self.dn), self.high),
            ):
                self.message(kind, group, plane, slot, part, self.sib).wait_recv()

        self.guarded(t, action)

    def plane(self, u):
        return plane_at(self.mp, u)

    def begin(self):
        for t in (0, 1):
            self.stage_z(t)
            self.stage_a(t)

    def step(self, s):
        self.stage_b(s)
        ahead = (2,) if isinstance(s, int) and s < 2 else (2, 3) if isinstance(s, int) and s == 2 else (3,)
        for more in ahead:
            self.stage_z(s + more)
            self.stage_a(s + more)
        self.stage_c(s - 1)

    def finish(self):
        def body(t, _):
            group, plane = self.unit(t)
            for part in self.sends(group, plane):
                for copy in part:
                    copy().wait_send()

            @pl.when((plane <= self.mp) & (self.mp < self.n_mp - 1))
            def _():
                self.along(group, plane, 0).wait_send()

            @pl.when((plane >= self.mp) & (self.mp > 0))
            def _():
                self.along(group, plane, 1).wait_send()

            return 0

        lax.fori_loop(0, GROUPS * self.n_mp, body, 0)


R_S, R_D0, R_D1, R_X, R_Y, R_UP, R_DOWN = range(7)
R_KINDS = 7


class Scatter:
    def __init__(self, n_mp, grads, fresh, out, bufs, load_sems, send_sems, recv_sems):
        self.dp, self.mp, self.n_mp = lax.axis_index("dp"), lax.axis_index("mp"), n_mp
        self.grads, self.fresh, self.out = grads, fresh, out
        self.pair_in, self.halves_in, self.x_in, self.y_in, self.z_in, self.mine, self.summed = bufs
        self.load_sems, self.send_sems, self.recv_sems = load_sems, send_sems, recv_sems
        self.sib, self.xn, self.yn, self.dn = neighbours(self.dp)
        self.core = self.dp % 2
        self.rows = out.shape[1]
        self.here, self.at_x, self.at_y, self.at_d = self.dp // 2, self.xn // 2, self.yn // 2, self.dn // 2
        self.up, self.down = jnp.minimum(self.mp + 1, n_mp - 1), jnp.maximum(self.mp - 1, 0)
        half = self.rows // 2
        self.low, self.high = pl.ds(0, half), pl.ds(half, half)
        self.units = GROUPS * n_mp

    def greet(self):
        dp, mp = self.dp, self.mp
        greet(
            [(self.sib, mp), (self.xn, mp), (self.yn, mp)],
            [(mp < self.n_mp - 1, (dp, self.up)), (mp > 0, (dp, self.down))],
        )

    def plane(self, u):
        return plane_at(self.mp, self.n_mp - 1 - u)

    def unit(self, t):
        return t // self.n_mp, self.plane(t % self.n_mp)

    def remote(self, kind, group, plane, src, dst, device):
        return pltpu.make_async_remote_copy(
            src_ref=src,
            dst_ref=dst,
            send_sem=self.send_sems.at[group, plane, kind],
            recv_sem=self.recv_sems.at[group, plane, kind],
            device_id=device,
            device_id_type=MESH,
        )

    def pair(self, group, plane, fresh):
        src = (
            self.fresh.at[plane, :, 1 - self.core] if fresh else self.grads.at[group, plane, :, 1 - self.core]
        )
        return self.remote(R_S, group, plane, src, self.pair_in.at[group, plane], (self.sib, self.mp))

    def message(self, kind, group, plane):
        mp, mine = self.mp, self.mine
        if kind == R_D0:
            src, dst = mine.at[group, plane, self.at_d, self.low], self.halves_in.at[group, plane, 0]
            device = (self.xn, mp)
        elif kind == R_D1:
            src, dst = mine.at[group, plane, self.at_d, self.high], self.halves_in.at[group, plane, 1]
            device = (self.yn, mp)
        elif kind == R_X:
            src, dst, device = mine.at[group, plane, self.at_x], self.x_in.at[group, plane], (self.xn, mp)
        elif kind == R_Y:
            src, dst, device = mine.at[group, plane, self.at_y], self.y_in.at[group, plane], (self.yn, mp)
        elif kind == R_UP:
            src, dst = self.summed.at[group, plane], self.z_in.at[group, plane, 0]
            device = (self.dp, self.up)
        else:
            src, dst = self.summed.at[group, plane], self.z_in.at[group, plane, 1]
            device = (self.dp, self.down)
        return self.remote(kind, group, plane, src, dst, device)

    def load(self, group, plane):
        return pltpu.make_async_copy(
            self.grads.at[group, plane, :, self.core],
            self.mine.at[group, plane],
            self.load_sems.at[group, plane],
        )

    def guarded(self, t, first, last, action):
        if isinstance(t, int):
            if first <= t < last:
                action(*self.unit(t))
            return

        @pl.when((t >= first) & (t < last))
        def _():
            action(*self.unit(t))

    def offer(self, t):
        def action(group, plane):
            self.pair(group, plane, False).start()
            self.load(group, plane).start()

        self.guarded(t, 0, 2 * self.n_mp, action)

    def offer_fresh(self, u):
        plane = self.plane(u)
        self.pair(2, plane, True).start()

    def add_pair(self, t):
        def action(group, plane, fresh):
            self.pair(group, plane, fresh).wait_recv()
            if fresh:
                self.mine[group, plane] = self.fresh[plane, :, self.core] + self.pair_in[group, plane]
            else:
                self.load(group, plane).wait()
                self.mine[group, plane] = self.mine[group, plane] + self.pair_in[group, plane]
            self.message(R_D0, group, plane).start()
            self.message(R_D1, group, plane).start()

        self.guarded(t, 0, 2 * self.n_mp, lambda g, p: action(g, p, False))
        self.guarded(t, 2 * self.n_mp, self.units, lambda g, p: action(2, p, True))

    def add_halves(self, t):
        def action(group, plane):
            mine, halves = self.mine, self.halves_in
            self.message(R_D0, group, plane).wait_recv()
            mine[group, plane, self.at_y, self.low] = (
                mine[group, plane, self.at_y, self.low] + halves[group, plane, 0]
            )
            self.message(R_D1, group, plane).wait_recv()
            mine[group, plane, self.at_x, self.high] = (
                mine[group, plane, self.at_x, self.high] + halves[group, plane, 1]
            )
            self.message(R_X, group, plane).start()
            self.message(R_Y, group, plane).start()

        self.guarded(t, 0, self.units, action)

    def add_plane(self, t):
        def action(group, plane):
            f32, mp, last = jnp.float32, self.mp, self.n_mp - 1
            self.message(R_X, group, plane).wait_recv()
            self.message(R_Y, group, plane).wait_recv()
            total = (
                self.mine[group, plane, self.here].astype(f32)
                + self.x_in[group, plane].astype(f32)
                + self.y_in[group, plane].astype(f32)
            )

            @pl.when(plane == mp)
            def _():
                self.out[group] = total

            @pl.when(plane != mp)
            def _():
                self.summed[group, plane] = total.astype(jnp.bfloat16)

            @pl.when((plane > mp) & (mp == 0))
            def _():
                self.message(R_UP, group, plane).start()

            @pl.when((plane < mp) & (mp == last))
            def _():
                self.message(R_DOWN, group, plane).start()

        self.guarded(t, 0, self.units, action)

    def add_along(self, t):
        def action(group, plane):
            f32, mp, last = jnp.float32, self.mp, self.n_mp - 1

            def add(way):
                self.summed[group, plane] = (
                    self.summed[group, plane].astype(f32) + self.z_in[group, plane, way].astype(f32)
                ).astype(jnp.bfloat16)

            @pl.when((plane > mp) & (mp > 0))
            def _():
                self.message(R_UP, group, plane).wait_recv()
                add(0)
                self.message(R_UP, group, plane).start()

            @pl.when((plane < mp) & (mp < last))
            def _():
                self.message(R_DOWN, group, plane).wait_recv()
                add(1)
                self.message(R_DOWN, group, plane).start()

            @pl.when((plane == mp) & (mp > 0))
            def _():
                self.message(R_UP, group, plane).wait_recv()
                self.out[group] += self.z_in[group, plane, 0].astype(f32)

            @pl.when((plane == mp) & (mp < last))
            def _():
                self.message(R_DOWN, group, plane).wait_recv()
                self.out[group] += self.z_in[group, plane, 1].astype(f32)

        self.guarded(t, 0, self.units, action)

    STEPS = 3

    def step(self, s):
        self.offer(s + 2)
        self.add_pair(s)
        self.add_halves(s - 1)
        self.add_plane(s - 2)
        self.add_along(s - 3)

    def finish(self):
        def body(t, _):
            group, plane = self.unit(t)

            @pl.when(group < 2)
            def _():
                self.pair(group, plane, False).wait_send()

            @pl.when(group == 2)
            def _():
                self.pair(2, plane, True).wait_send()

            for kind in (R_D0, R_D1, R_X, R_Y):
                self.message(kind, group, plane).wait_send()

            @pl.when(plane > self.mp)
            def _():
                self.message(R_UP, group, plane).wait_send()

            @pl.when(plane < self.mp)
            def _():
                self.message(R_DOWN, group, plane).wait_send()

            return 0

        lax.fori_loop(0, self.units, body, 0)


LANES = 128
NN = (((1,), (0,)), ((), ()))
NT = (((1,), (1,)), ((), ()))
BIG = 2.0**36


def mm(left, right, dims=NN):
    return lax.dot_general(left, right, dims, preferred_element_type=jnp.float32)


def gelu_parts(t):
    k = 1.0 / (1.0 + 0.2316419 * jnp.abs(t))
    series = k * (
        0.319381530 + k * (-0.356563782 + k * (1.781477937 + k * (-1.821255978 + k * 1.330274429)))
    )
    density = 0.3989422804014327 * jnp.exp(-0.5 * t * t)
    tail = density * series
    phi = jnp.where(t >= 0.0, 1.0 - tail, tail)
    return t * phi, phi + t * density


def row_stats(x):
    width = x.shape[1]
    center = x - jnp.sum(x, axis=1, keepdims=True) * (1.0 / width)
    spread = jnp.sum(center * center, axis=1, keepdims=True) * (1.0 / width)
    inverse = lax.rsqrt(spread + norm_eps)
    return center * inverse, inverse


def image_ends(counts_ref, set_index, slots):
    lane = lax.broadcasted_iota(jnp.int32, (8, LANES), 1) % (LANES // 2)
    low = jnp.zeros((8, LANES), jnp.int32)
    high = jnp.zeros((8, LANES), jnp.int32)
    edge = jnp.int32(0)
    for slot in range(slots + 1):
        after = jnp.int32(1 << 20) if slot == slots else edge + counts_ref[set_index, slot]
        low = jnp.where(lane == slot, edge, low)
        high = jnp.where(lane == slot, after, high)
        edge = after if slot < slots else edge
    return low[0:1], high[0:1], edge


def own_row(hidden_half, tile):
    lane = lax.broadcasted_iota(jnp.int32, tile.shape, 1)
    return (lane < LANES // 2) if hidden_half == 0 else (lane >= LANES // 2)


def keep_half(half, tile, other):
    return jnp.where(own_row(half, tile), tile, other)


HEAD_TILES = ((0, 128, 256, 0, 0), (0, 128, 256, 1, 1), (512, 640, 640, 0, 1))
MIX = 384


def make_features(counts_ref, set_index, slots, set_rows, feat_q, feat_k):
    low, high, total = image_ends(counts_ref, set_index, slots)
    step = 256

    def body(i, _):
        at = pl.ds(pl.multiple_of(i * step, step), step)
        row = lax.broadcasted_iota(jnp.int32, (step, LANES), 0) + i * step
        same = (row >= low) & (row < high)
        lane = lax.broadcasted_iota(jnp.int32, (step, LANES), 1) % (LANES // 2)
        feat_k[at] = jnp.where(same, 1.0, 0.0).astype(jnp.bfloat16)
        feat_q[at] = jnp.where(same | (lane > slots), 0.0, -BIG).astype(jnp.bfloat16)
        return 0

    lax.fori_loop(0, set_rows // step, body, 0)
    return total


def attend(m, qkv, mixed, feat_q, feat_k, window_start, window, step):
    keys, values = [], []
    for q_at, k_at, v_at, half, v_half in HEAD_TILES:
        keys.append(keep_half(half, qkv[m, :, k_at : k_at + LANES], feat_k[...]))
        tile = qkv[m, :, v_at : v_at + LANES]
        values.append(keep_half(v_half, tile, jnp.ones_like(tile)))

    def block(i, _):
        at = pl.ds(pl.multiple_of(window_start + i * step, LANES // 2), step)
        outs = []
        for head, (q_at, k_at, v_at, half, v_half) in enumerate(HEAD_TILES):
            query = keep_half(half, qkv[m, at, q_at : q_at + LANES], feat_q[at])
            scores = mm(query, keys[head], NT)
            top = jnp.max(scores, axis=1, keepdims=True)
            weights = jnp.exp((scores - top) * HD ** (-0.5)).astype(jnp.bfloat16)
            out = mm(weights, values[head])
            outs.append(out / pltpu.roll(out, LANES // 2, 1))
        here = pl.ds(pl.multiple_of(i * step, LANES // 2), step)
        low = jnp.bfloat16
        mixed[m, here, 0:LANES] = keep_half(0, outs[0], outs[1]).astype(low)
        mixed[m, here, LANES : 2 * LANES] = keep_half(1, outs[2], jnp.zeros_like(outs[2])).astype(low)
        return 0

    lax.fori_loop(0, window // step, block, 0)


TN = (((0,), (0,)), ((), ()))


def norm_grad(x, gain, grad):
    width = x.shape[1]
    unit, inverse = row_stats(x)
    e = grad * gain
    mean_e = jnp.sum(e, axis=1, keepdims=True) * (1.0 / width)
    mean_eu = jnp.sum(e * unit, axis=1, keepdims=True) * (1.0 / width)
    return inverse * (e - mean_e - unit * mean_eu), grad * unit


def attend_back(m, qkv, d_mixed, feat_q, feat_k, window_start, window, acc, d_query):
    band = 3 * LANES
    acc[...] = jnp.zeros_like(acc)
    low = jnp.bfloat16
    scale = HD ** (-0.5)

    def block(b, _):
        start = jnp.clip(b - 1, 0, window // LANES - 3) * LANES
        keys_at = pl.ds(pl.multiple_of(start, LANES), band)
        keys_in = pl.ds(pl.multiple_of(window_start + start, LANES), band)
        keys_w = pl.ds(pl.multiple_of(start, LANES), band)
        here = pl.ds(pl.multiple_of(b * LANES, LANES), LANES)
        rows_in = pl.ds(pl.multiple_of(window_start + b * LANES, LANES), LANES)
        f_q, f_k = feat_q[rows_in], feat_k[keys_in]
        got = []
        for head, (q_at, k_at, v_at, half, v_half) in enumerate(HEAD_TILES):
            q_tile = qkv[m, here, q_at : q_at + LANES]
            k_tile = qkv[m, keys_w, k_at : k_at + LANES]
            v_tile = qkv[m, keys_w, v_at : v_at + LANES]
            mix_at = 0 if head < 2 else LANES
            d_tile = d_mixed[m, here, mix_at : mix_at + LANES]
            d_out = keep_half(v_half, d_tile, jnp.zeros_like(d_tile))
            scores = mm(keep_half(half, k_tile, f_k), keep_half(half, q_tile, f_q), NT)
            top = jnp.max(scores, axis=0, keepdims=True)
            weights = jnp.exp((scores - top) * scale)
            weights = weights * (1.0 / jnp.sum(weights, axis=0, keepdims=True))
            d_weights = mm(v_tile, d_out, NT)
            delta = jnp.sum(d_weights * weights, axis=0, keepdims=True)
            d_scores = (weights * (d_weights - delta)).astype(low)
            d_key = mm(d_scores, keep_half(half, q_tile * scale, jnp.zeros_like(q_tile)))
            d_value = mm(weights.astype(low), d_out)
            d_q = mm(d_scores, keep_half(half, k_tile * scale, jnp.zeros_like(k_tile)), TN)
            got.append((d_q, d_key, d_value))
        acc[keys_at, 0:LANES] += got[0][1] + got[1][1]
        acc[keys_at, LANES : 2 * LANES] += got[0][2] + got[1][2]
        acc[keys_at, 2 * LANES : 3 * LANES] += got[2][1] + got[2][2]
        d_query[here, 0:LANES] = (got[0][0] + got[1][0]).astype(low)
        d_query[here, LANES : 2 * LANES] = got[2][0].astype(low)
        return 0

    lax.fori_loop(0, window // LANES, block, 0)


class Loader:
    def __init__(self, n_mp, weights, out, sems):
        self.n_mp, self.weights, self.out, self.sems = n_mp, weights, out, sems
        self.mp = lax.axis_index("mp")

    def copy(self, t):
        group, plane = t // self.n_mp, t % self.n_mp
        return pltpu.make_async_copy(
            self.weights.at[group, plane], self.out.at[group, plane], self.sems.at[group, plane]
        )

    def plane(self, u):
        return u

    def begin(self):
        for t in range(GROUPS * self.n_mp):
            self.copy(t).start()

    def step(self, s):
        pass

    def stage_d(self, t):
        self.copy(t).wait()

    def finish(self):
        pass


def tile_rows(i, first=0):
    return pl.ds(pl.multiple_of(first + i * LANES, LANES), LANES)


def column_sum(v):
    return jnp.sum(v, axis=0, keepdims=True)


class Place:
    def __init__(self, set_rows, own_rows):
        self.set_rows, self.own_rows, self.window = set_rows, own_rows, own_rows + HALO
        mp = lax.axis_index("mp")
        per_set = set_rows // own_rows
        self.set_index, part = mp // per_set, mp % per_set
        self.window_start = pl.multiple_of(part * (set_rows - self.window), LANES)
        self.own_start = pl.multiple_of(part * (self.window - own_rows), LANES)
        self.own = pl.ds(self.own_start, own_rows)
        self.own_set = pl.ds(pl.multiple_of(self.window_start + self.own_start, LANES), own_rows)
        self.tiles = self.window // LANES

    def is_own(self, i):
        first = i * LANES
        return jnp.where((first >= self.own_start) & (first < self.own_start + self.own_rows), 1.0, 0.0)

    def valid(self, i, total):
        row = lax.broadcasted_iota(jnp.int32, (LANES, 1), 0) + (self.window_start + i * LANES)
        return jnp.where(row < total, 1.0, 0.0)


def layer_kernel(
    n_mp, slots, own_rows, remote, tokens_in, cot_in, blocks, counts, vec, bias,
    w0_out, qkv_out, mixed_out, normed_t_out, d_mid_out, d_proj_out, d_proj_t_out, grads_out, result_out, sums_out,
    w, tokens, cot, normed, normed_t, qkv, mixed, proj, middle, normed_two, normed_two_t, active, slope, branch,
    d_branch, d_branch_t, d_two, d_proj, stage, result, feat_q, feat_k,
    send_sems, recv_sems, way_sems, local_sems, out_sems, stage_sems,
):
    set_rows, width = tokens.shape
    place = Place(set_rows, own_rows)
    window, own, own_start, window_start, tiles = (
        place.window, place.own, place.own_start, place.window_start, place.tiles
    )
    low, f32 = jnp.bfloat16, jnp.float32
    in_set = pl.ds(pl.multiple_of(place.set_index * set_rows, LANES), set_rows)
    token_copy = pltpu.make_async_copy(tokens_in.at[in_set], tokens, local_sems.at[0])
    cot_copy = pltpu.make_async_copy(cot_in.at[in_set], cot, local_sems.at[1])
    token_copy.start()
    cot_copy.start()
    if remote:
        net = Gather(n_mp, w, send_sems, recv_sems, way_sems)
        own_copy = pltpu.make_async_copy(blocks, w.at[:, net.mp, net.dp], local_sems.at[2])
        own_copy.start()
        net.greet()
        own_copy.wait()
    else:
        net = Loader(n_mp, blocks, w, recv_sems)
    net.begin()

    def weight(group, m, lanes=None):
        block = w[group, m] if lanes is None else w[group, m, :, :, lanes]
        return block.reshape(width, block.shape[-1])

    total = make_features(counts, place.set_index, slots, set_rows, feat_q, feat_k)
    token_copy.wait()

    def norm_one(i, _):
        at = tile_rows(i)
        unit, _inv = row_stats(tokens[at].astype(f32))
        normed[at] = (unit * vec[0:1] + vec[1:2]).astype(low)
        return 0

    lax.fori_loop(0, set_rows // LANES, norm_one, 0)
    net.step(0)
    cot_copy.wait()
    zero_row = jnp.zeros((1, width), f32)

    def back_of(i):
        return cot[tile_rows(i, window_start)].astype(f32) * place.valid(i, total)

    def first_grad(i, total_row):
        db = (back_of(i) * vec[5:6]).astype(low)
        d_branch[tile_rows(i)] = db
        return total_row + place.is_own(i) * column_sum(db.astype(f32))

    branch_sum = lax.fori_loop(0, tiles, first_grad, zero_row)
    d_branch_t[...] = d_branch[own].T
    net.step(1)
    normed_t[...] = normed[place.own_set].T

    def project(u, _):
        net.step(u + 2)
        net.stage_d(u)
        m = net.plane(u)
        qkv[m] = (mm(normed[...], weight(0, m)) + bias[pl.ds(m, 1)]).astype(low)
        attend(m, qkv, mixed, feat_q, feat_k, window_start, window, window // 2)
        return 0

    project(0, 0)
    lax.fori_loop(1, n_mp, project, 0)
    outs = [
        pltpu.make_async_copy(w.at[0], w0_out, out_sems.at[0]),
        pltpu.make_async_copy(
            qkv.at[:, pl.ds(window_start, window)], qkv_out, out_sems.at[1]
        ),
        pltpu.make_async_copy(mixed.at[:, own], mixed_out, out_sems.at[2]),
        pltpu.make_async_copy(normed_t, normed_t_out, out_sems.at[3]),
    ]
    for copy in outs:
        copy.start()
    net.step(n_mp + 2)

    def out_part(m):
        return mm(mixed[m], weight(0, m, pl.ds(MIX, 2 * LANES)), NT)

    proj[...] = sum((out_part(m) for m in range(n_mp)), vec[6:7])

    def norm_two(i, _):
        at = tile_rows(i)
        mid = tokens[tile_rows(i, window_start)].astype(f32) + vec[4:5] * proj[at]
        middle[at] = mid
        unit, _inv = row_stats(mid)
        normed_two[at] = (unit * vec[2:3] + vec[3:4]).astype(low)
        return 0

    lax.fori_loop(0, tiles, norm_two, 0)
    normed_two_t[...] = normed_two[own].T

    def feed_up(u, _):
        net.step(u + 3 + n_mp)
        net.stage_d(u + n_mp)
        m = net.plane(u)

        def rows(i, _):
            at = tile_rows(i)
            hidden = mm(normed_two[at], weight(1, m)) + bias[pl.ds(n_mp + m, 1)]
            act, slp = gelu_parts(hidden)
            active[m, at] = act.astype(low)
            slope[m, at] = slp.astype(low)
            return 0

        lax.fori_loop(0, tiles, rows, 0)
        return 0

    lax.fori_loop(0, n_mp, feed_up, 0)

    def put(slot, group, m, value):
        stage[slot] = value.astype(low)
        pltpu.make_async_copy(stage.at[slot], grads_out.at[group, m], stage_sems.at[slot]).start()

    def put_done(slot):
        pltpu.make_async_copy(stage.at[slot], grads_out.at[0, 0], stage_sems.at[slot]).wait()

    def feed_down(u, _):
        net.step(u + 3 + 2 * n_mp)
        net.stage_d(u + 2 * n_mp)
        m = net.plane(u)
        down = weight(2, m)
        part_sum = mm(active[m, own], down, NT)

        @pl.when(u == 0)
        def _():
            branch[...] = part_sum

        @pl.when(u > 0)
        def _():
            branch[...] += part_sum

        def rows(i, total_row):
            at = tile_rows(i)
            dh = (mm(d_branch[at], weight(2, m)) * slope[m, at].astype(f32)).astype(low)
            slope[m, at] = dh
            return total_row + place.is_own(i) * column_sum(dh.astype(f32))

        sums_out[pl.ds(8 + m, 1)] = lax.fori_loop(0, tiles, rows, zero_row)

        @pl.when(u > 0)
        def _():
            put_done(0)
            put_done(1)

        put(0, 1, m, mm(d_branch_t[...], active[m, own]))
        put(1, 0, m, mm(normed_two_t[...], slope[m, own]))
        two_sum = mm(slope[m], weight(1, m), NT)

        @pl.when(u == 0)
        def _():
            d_two[...] = two_sum

        @pl.when(u > 0)
        def _():
            d_two[...] += two_sum

        return 0

    lax.fori_loop(0, n_mp, feed_down, 0)

    def final(i, carry):
        at, there = tile_rows(i), tile_rows(i, own_start)
        block = own_start // LANES + i
        br = branch[at] + vec[7:8]
        scaled = vec[5:6] * br
        res = middle[there] + scaled
        result[at] = res.astype(low)
        attn = vec[4:5] * proj[there]
        valid = place.valid(block, total)
        sums = [column_sum(valid * v * v) for v in (res, attn, scaled)] + [column_sum(back_of(block) * br)]
        return tuple(c + s for c, s in zip(carry, sums))

    res_sq, attn_sq, scaled_sq, back_branch = lax.fori_loop(0, own_rows // LANES, final, (zero_row,) * 4)
    result_copy = pltpu.make_async_copy(result, result_out, out_sems.at[4])
    result_copy.start()

    def norm_two_back(i, carry):
        at = tile_rows(i)
        grad = d_two[at]
        dv, grad_unit = norm_grad(middle[at], vec[2:3], grad)
        d_mid = back_of(i) + dv
        d_two[at] = d_mid
        dp = (d_mid * vec[4:5]).astype(low)
        d_proj[at] = dp
        mine = place.is_own(i)
        new = (grad_unit, grad, d_mid * proj[at], dp.astype(f32))
        return tuple(c + mine * column_sum(n) for c, n in zip(carry, new))

    gain_sum, shift_sum, scale_sum, proj_sum = lax.fori_loop(0, tiles, norm_two_back, (zero_row,) * 4)
    d_branch_t[...] = d_proj[own].T
    more = [
        pltpu.make_async_copy(d_two, d_mid_out, out_sems.at[5]),
        pltpu.make_async_copy(d_proj, d_proj_out, out_sems.at[6]),
        pltpu.make_async_copy(d_branch_t, d_proj_t_out, out_sems.at[7]),
    ]
    for copy in more:
        copy.start()
    rows_out = (zero_row, zero_row, gain_sum, shift_sum, scale_sum, back_branch, proj_sum, branch_sum)
    for i, row in enumerate(rows_out):
        sums_out[i : i + 1] = row
    for i, row in enumerate((res_sq, attn_sq, scaled_sq, zero_row)):
        sums_out[12 + i : 13 + i] = row
    put_done(0)
    put_done(1)
    for copy in outs + [result_copy] + more:
        copy.wait()
    net.finish()


DECAY = 1.0 - STEP ** (-0.8)
EXACT = lax.Precision.HIGHEST
SUB_QKV, SUB_OUT, SUB_UP, SUB_DOWN = range(4)


class Exchange:
    def __init__(self, axis, size, bufs, send_sems, recv_sems):
        self.axis, self.size, self.bufs = axis, size, bufs
        self.send_sems, self.recv_sems = send_sems, recv_sems
        self.me = lax.axis_index(axis)

    def copy(self, away):
        peer = (self.me + away) % self.size
        return pltpu.make_async_remote_copy(
            src_ref=self.bufs.at[0],
            dst_ref=self.bufs.at[away],
            send_sem=self.send_sems.at[away],
            recv_sem=self.recv_sems.at[away],
            device_id={self.axis: peer},
            device_id_type=MESH,
        )

    def total(self, value):
        self.bufs[0] = value
        for away in range(1, self.size):
            self.copy(away).start()
        for away in range(1, self.size):
            self.copy(away).wait_recv()
        total = jnp.zeros_like(value)
        for index in range(self.size):
            away = (self.me - index + self.size) % self.size
            total = total + self.bufs[away]
        for away in range(1, self.size):
            self.copy(away).wait_send()
        return total


class Doubling:
    def __init__(self, value, bufs, send_sems, recv_sems):
        self.value, self.bufs, self.send_sems, self.recv_sems = value, bufs, send_sems, recv_sems
        dp, mp = lax.axis_index("dp"), lax.axis_index("mp")
        sib, xn, yn, _ = neighbours(dp)
        self.peers = (
            {"dp": sib}, {"dp": xn}, {"dp": yn}, {"mp": mp + 1 - 2 * (mp % 2)}, {"mp": (mp + 2) % 4}
        )

    def copy(self, i):
        return pltpu.make_async_remote_copy(
            src_ref=self.value.at[i],
            dst_ref=self.bufs.at[i],
            send_sem=self.send_sems.at[i],
            recv_sem=self.recv_sems.at[i],
            device_id=self.peers[i],
            device_id_type=MESH,
        )

    def send(self, i):
        self.copy(i).start()

    def add(self, i):
        self.copy(i).wait_recv()
        self.value[i + 1] = self.value[i] + self.bufs[i]

    def finish(self):
        for i in range(5):
            self.copy(i).wait_send()


def lane_sums(mask, squares):
    return lax.dot_general(mask, squares, NT, precision=EXACT, preferred_element_type=jnp.float32)


def o_lanes(width):
    lane = lax.broadcasted_iota(jnp.int32, (1, width), 1)
    return jnp.where(((lane >= MIX) & (lane < MIX + 128)) | ((lane >= 576) & (lane < 640)), 1.0, 0.0)


def masks_of(width, scale_rows):
    row = lax.broadcasted_iota(jnp.int32, (8, width), 0)
    is_o = o_lanes(width)
    up = jnp.where(row == SUB_UP, scale_rows[0:1], 0.0)
    down = jnp.where(row == SUB_DOWN, scale_rows[1:2], 0.0)
    first = scale_rows[2:3]
    mixed = jnp.where(row == SUB_QKV, first * (1.0 - is_o), jnp.where(row == SUB_OUT, first * is_o, 0.0))
    return up, down, mixed


def factor_sums(reduced, sub_prior, lane_prior, masters, n_dp, n_mp, along_mp, along_dp, along_mp2, along_dp2, outs):
    sub_out, lane_out, scalar_out = outs
    f32 = jnp.float32
    groups, rows, width = reduced.shape
    ones = jnp.ones((3, width), f32)
    sub_mine = jnp.zeros((8, rows), f32)
    weight_sums = jnp.zeros((8, 1), f32)
    lanes = []
    for group, mask in enumerate(masks_of(width, ones)):
        squares = reduced[group] * reduced[group]
        sub_mine = sub_mine + lane_sums(mask, squares)
        lanes.append(column_sum(squares))
        by_lane = column_sum(masters[group] * masters[group])
        weight_sums = weight_sums + jnp.sum(mask * by_lane, axis=1, keepdims=True)
    is_o = o_lanes(width)
    lane8 = lax.broadcasted_iota(jnp.int32, (8, LANES), 1)
    row8 = lax.broadcasted_iota(jnp.int32, (8, LANES), 0)

    def spot(row, lane, value):
        return jnp.where((row8 == row) & (lane8 == lane), value, 0.0)

    out_prior = jnp.sum(lane_prior[2:3] * is_o, axis=1, keepdims=True)
    down_prior = jnp.sum(lane_prior[1:2], axis=1, keepdims=True)
    first = jnp.concatenate([sub_mine, jnp.zeros((8, LANES - rows), f32)], axis=1)
    for i in range(4):
        first = first + spot(4, i, weight_sums[i : i + 1])
    first = first + spot(4, 4, out_prior) + spot(4, 5, down_prior)
    first = along_mp.total(first)
    sub_sum = jnp.where(lane8 < rows, first, 0.0)
    second = jnp.zeros((8, width), f32)
    row_w = lax.broadcasted_iota(jnp.int32, (8, width), 0)
    lane_w = lax.broadcasted_iota(jnp.int32, (8, width), 1)
    for i in range(3):
        second = second + jnp.where(row_w == i, lanes[i], 0.0)
    sub_total = jnp.sum(sub_sum, axis=1, keepdims=True)
    prior_total = jnp.sum(jnp.where(lane8 < rows, sub_prior[...], 0.0), axis=1, keepdims=True)

    def put(value, lane):
        return jnp.where((row_w == 3) & (lane_w == lane), value, 0.0)

    for i in range(4):
        second = second + put(sub_total[i : i + 1], i) + put(first[4:5, i : i + 1], 4 + i)
    second = second + put(prior_total[SUB_QKV : SUB_QKV + 1], 8) + put(prior_total[SUB_UP : SUB_UP + 1], 9)
    second = along_dp.total(second)
    whole = float(rows * n_dp)
    counts = (3.0 * whole, whole, 4.0 * whole, 4.0 * whole)
    count = jnp.where(row8 == SUB_QKV, counts[0], jnp.where(row8 == SUB_OUT, counts[1], counts[2]))
    sub_new = DECAY * sub_prior[...] + (1.0 - DECAY) * (sub_sum / count + square_eps)
    lane_new = DECAY * lane_prior[...] + (1.0 - DECAY) * (second[0:3] / whole + square_eps)
    sub_out[...] = sub_new
    lane_out[0:3] = lane_new
    lane_out[3:8] = jnp.zeros((5, width), f32)

    def average(index, prior, prior_length):
        entries = counts[index] * whole
        return DECAY * prior / prior_length + (1.0 - DECAY) * (second[3:4, index : index + 1] / entries + square_eps)

    means = (
        average(0, second[3:4, 8:9], whole),
        average(1, first[4:5, 4:5], whole),
        average(2, second[3:4, 9:10], whole),
        average(3, first[4:5, 5:6], 4.0 * whole),
    )
    shares = jnp.zeros((8, rows), f32)
    for group, mask in enumerate(masks_of(width, 1.0 / lane_new)):
        shares = shares + lane_sums(mask, reduced[group] * reduced[group])
    mean_rows = jnp.zeros((8, 1), f32)
    row1 = lax.broadcasted_iota(jnp.int32, (8, 1), 0)
    for i in range(4):
        mean_rows = mean_rows + jnp.where(row1 == i, means[i], 0.0)
    update_squares = jnp.sum(shares / sub_new[:, 0:rows], axis=1, keepdims=True) * mean_rows
    update_squares = jnp.where(row1 < 4, update_squares, 0.0)
    third = along_mp2.total(update_squares + jnp.zeros((8, LANES), f32))
    fourth = along_dp2.total(third)
    weight_total = jnp.zeros((8, 1), f32)
    for i in range(4):
        weight_total = weight_total + jnp.where(row1 == i, second[3:4, 4 + i : 5 + i], 0.0)
    scalar_out[...] = jnp.where(lane8 == 0, fourth, jnp.where(lane8 == 1, weight_total, mean_rows))


def update_kernel(
    n_dp, n_mp, reduced, masters, sub_new, lane_new, scalars, sums, vec, bias, vec_moment, bias_moment, input_in, stream_in,
    stream_out, input_out, qkv_g, out_g, up_g, down_g, qkv_a, out_a, up_a, down_a, qkv_b, out_b, up_b, down_b,
    vec_g, bias_g, vec_m, bias_m, vec_a, bias_a, small, held, sems,
):
    f32 = jnp.float32
    groups, rows, width = reduced.shape
    load = pltpu.make_async_copy(stream_in, held, sems.at[0])
    load.start()
    span = input_in.shape[2]
    for i in range(n_mp):
        input_out[:, i * span : (i + 1) * span] = input_in[i].astype(f32)
    load.wait()
    store = pltpu.make_async_copy(held, stream_out, sems.at[1])
    store.start()
    whole = float(rows * n_dp)
    entries = (3.0 * whole * whole, whole * whole, 4.0 * whole * whole, 4.0 * whole * whole)
    row1 = lax.broadcasted_iota(jnp.int32, (8, 1), 0)
    size = jnp.where(row1 == 0, entries[0], jnp.where(row1 == 1, entries[1], entries[2]))
    scale = jnp.sqrt(scalars[:, 0:1] / size)
    rms = jnp.sqrt(scalars[:, 1:2] / size)
    rate = step_rate * rms / jnp.maximum(1.0, scale / clip_limit)
    mean_rows = scalars[:, 2:3]
    sub = lax.dot_general(
        jnp.where(
            lax.broadcasted_iota(jnp.int32, (rows, LANES), 0) == lax.broadcasted_iota(jnp.int32, (rows, LANES), 1), 1.0, 0.0
        ),
        sub_new[...], NT, precision=EXACT, preferred_element_type=f32,
    )
    is_o = o_lanes(width)

    def renewed(group, index):
        gradient = reduced[group]
        product = sub[:, index : index + 1] * lane_new[group : group + 1] / mean_rows[index : index + 1]
        return masters[group] - rate[index : index + 1] * (gradient * lax.rsqrt(product))

    def spread(value, qkv, out):
        half = LANES // 2
        tails = (value[:, 512:576], value[:, 640:704], value[:, 704:768])
        for i in range(3):
            qkv[i, :, 0:LANES] = value[:, i * LANES : (i + 1) * LANES].astype(qkv.dtype)
            qkv[i, :, LANES : LANES + half] = tails[i].astype(qkv.dtype)
        out[:, 0:LANES] = value[:, MIX : MIX + LANES].astype(out.dtype)
        out[:, LANES : LANES + half] = value[:, 576:640].astype(out.dtype)

    first = jnp.where(is_o > 0.0, renewed(2, 1), renewed(2, 0))
    spread(reduced[2], qkv_g, out_g)
    spread(first, qkv_a, out_a)
    spread(first, qkv_b, out_b)
    for group, index, grad, after, short in ((0, 2, up_g, up_a, up_b), (1, 3, down_g, down_a, down_b)):
        new = renewed(group, index)
        grad[...] = reduced[group]
        after[...] = new
        short[...] = new.astype(short.dtype)

    def plain(weight, gradient, moment_old, together):
        moment = DECAY * moment_old + (1.0 - DECAY) * (gradient * gradient + square_eps)
        update = gradient * lax.rsqrt(moment)
        update_mean = jnp.mean(update * update, axis=1, keepdims=True)
        weight_mean = jnp.mean(weight * weight, axis=1, keepdims=True)
        if together is not None:
            row = lax.broadcasted_iota(jnp.int32, update_mean.shape, 0)
            number = float(weight.shape[0] - together)

            def join(mean):
                shared = jnp.sum(jnp.where(row >= together, mean, 0.0), axis=0, keepdims=True) / number
                return jnp.where(row >= together, shared, mean)

            update_mean, weight_mean = join(update_mean), join(weight_mean)
        rate_here = step_rate * jnp.sqrt(weight_mean)
        return weight - rate_here * update / jnp.maximum(1.0, jnp.sqrt(update_mean) / clip_limit), moment

    vec_g[...] = sums[0:8]
    bias_g[...] = sums[8:14]
    vec_a[...], vec_m[...] = plain(vec[...], sums[0:8], vec_moment[...], None)
    bias_a[...], bias_m[...] = plain(bias[...], sums[8:14], bias_moment[...], 2)
    lane8 = lax.broadcasted_iota(jnp.int32, (8, LANES), 1)
    row8 = lax.broadcasted_iota(jnp.int32, (8, LANES), 0)
    spreads = jnp.sqrt(sums[14:15, 0:LANES] / (sums[14:15, 3:4] * width))
    scales = jnp.zeros((1, LANES), f32)
    lane1 = lax.broadcasted_iota(jnp.int32, (1, LANES), 1)
    for i in range(4):
        scales = scales + jnp.where(lane1 == i, scale[i : i + 1], 0.0)
    small[...] = jnp.where(row8 == 0, scales, spreads)
    store.wait()


def bias_rows_natural(qkv_sums, hidden_sums, n_mp, width):
    f32 = jnp.float32
    share = width // n_mp
    half = LANES // 2
    query = [qkv_sums[m : m + 1, a:b] for m in range(n_mp) for a, b in ((0, LANES), (512, 512 + half))]
    value = [qkv_sums[m : m + 1, a:b] for m in range(n_mp) for a, b in ((256, 256 + LANES), (704, 704 + half))]
    source = lax.broadcasted_iota(jnp.int32, (width, width), 0)
    target = lax.broadcasted_iota(jnp.int32, (width, width), 1)
    move = jnp.where(source == 4 * (target % share) + target // share, 1.0, 0.0)
    moved = lax.dot_general(hidden_sums, move, NN, precision=EXACT, preferred_element_type=f32)
    rows = [jnp.concatenate(query, axis=1), jnp.concatenate(value, axis=1)]
    for r in range(width // share):
        rows.append(
            jnp.concatenate([moved[m : m + 1, r * share : (r + 1) * share] for m in range(n_mp)], axis=1)
        )
    return rows


class Stream:
    CUTS = 4

    def __init__(self, n_mp, src, out, send_sems, recv_sems):
        self.dp, self.mp, self.n_mp = lax.axis_index("dp"), lax.axis_index("mp"), n_mp
        self.src, self.out, self.send_sems, self.recv_sems = src, out, send_sems, recv_sems
        self.rows = out.shape[1] // self.CUTS
        self.up, self.down = jnp.minimum(self.mp + 1, n_mp - 1), jnp.maximum(self.mp - 1, 0)

    def message(self, plane, cut, way, own):
        part = pl.ds(pl.multiple_of(cut * self.rows, self.rows), self.rows)
        where = self.out.at[plane, part]
        return pltpu.make_async_remote_copy(
            src_ref=self.src.at[part] if own else where,
            dst_ref=where,
            send_sem=self.send_sems.at[way, plane, cut],
            recv_sem=self.recv_sems.at[plane, cut],
            device_id=(self.dp, self.down if way else self.up),
            device_id_type=MESH,
        )

    def pass_on(self, distance, cut, ways, action):
        mp, last = self.mp, self.n_mp - 1
        below, above = mp - distance, mp + distance

        def one(plane, way, there):
            @pl.when(there)
            def _():
                action(plane, way, True)

        one(below, 0, below >= 0)
        one(above, 1, above <= last)

    def step(self, s):
        distance, cut = s // self.CUTS, s % self.CUTS
        mp, last = self.mp, self.n_mp - 1

        @pl.when((distance == 0) & (mp < last))
        def _():
            self.message(mp, cut, 0, True).start()

        @pl.when((distance == 0) & (mp > 0))
        def _():
            self.message(mp, cut, 1, True).start()

        below, above = mp - distance, mp + distance

        @pl.when((distance > 0) & (below >= 0))
        def _():
            self.message(below, cut, 0, False).wait_recv()

            @pl.when(mp < last)
            def _():
                self.message(below, cut, 0, False).start()

        @pl.when((distance > 0) & (above <= last))
        def _():
            self.message(above, cut, 1, False).wait_recv()

            @pl.when(mp > 0)
            def _():
                self.message(above, cut, 1, False).start()

    STEPS = 16

    def finish(self):
        mp, last = self.mp, self.n_mp - 1

        def body(t, _):
            plane, cut = t // self.CUTS, t % self.CUTS

            @pl.when((plane <= mp) & (mp < last))
            def _():
                self.message(plane, cut, 0, False).wait_send()

            @pl.when((plane >= mp) & (mp > 0))
            def _():
                self.message(plane, cut, 1, False).wait_send()

            return 0

        lax.fori_loop(0, self.n_mp * self.CUTS, body, 0)


def back_kernel(
    n_dp, n_mp, slots, own_rows, set_rows, remote, tokens_in, counts, vec, w0_in, qkv_in, mixed_in, normed_t_in, d_mid_in,
    d_proj_in, d_proj_t_in, grads_in, result_in, sums_in, sub_prior, lane_prior, masters,
    reduced, input_out, sums_out, stream_out, sub_out, lane_out, scalar_out, *rest,
):
    if remote:
        rest, scatter_refs = rest[:-27], rest[-27:]
    (
        tokens, w0, qkv, mixed, normed_t, d_mid, d_proj, d_proj_t, d_mixed, acc, d_query, d_qkv, d_normed, fresh,
        feat_q, feat_k, local_sems,
    ) = rest
    width = d_mid.shape[1]
    place = Place(set_rows, own_rows)
    window, own, own_start = place.window, place.own, place.own_start
    low, f32 = jnp.bfloat16, jnp.float32
    mp = lax.axis_index("mp")
    first = pl.multiple_of(place.set_index * set_rows + place.window_start + own_start, LANES)
    loads = [
        pltpu.make_async_copy(src, dst, local_sems.at[i])
        for i, (src, dst) in enumerate(
            (
                (d_proj_in, d_proj), (w0_in, w0), (qkv_in, qkv), (normed_t_in, normed_t), (d_proj_t_in, d_proj_t),
                (mixed_in, mixed), (tokens_in.at[pl.ds(first, own_rows)], tokens), (d_mid_in, d_mid),
            )
        )
    ]
    for copy in loads:
        copy.start()
    if remote:
        bufs, load_sems, send_sems, recv_sems, stream_send, stream_recv = (
            scatter_refs[:7], *scatter_refs[7:12]
        )
        (
            input_t, turn_send, turn_recv, value, swap_in, swap_send, swap_recv, mp_buf, dp_buf, mp_buf2, dp_buf2,
            small_send, small_recv, sums_mine, result,
        ) = scatter_refs[12:]
        swaps = Doubling(value, swap_in, swap_send, swap_recv)
        exchanges = [
            Exchange(axis, size, buf, small_send.at[i], small_recv.at[i])
            for i, (axis, size, buf) in enumerate(
                (("mp", n_mp, mp_buf), ("dp", n_dp, dp_buf), ("mp", n_mp, mp_buf2), ("dp", n_dp, dp_buf2))
            )
        ]
        net = Scatter(n_mp, grads_in, fresh, reduced, bufs, load_sems, send_sems, recv_sems)
        stream = Stream(n_mp, result, stream_out, stream_send, stream_recv)
        dp = lax.axis_index("dp")
        greet(
            [((dp + away) % n_dp, mp) for away in range(1, n_dp)] + [(dp, (mp + away) % n_mp) for away in range(1, n_mp)], []
        )
        net.offer(0)
        net.offer(1)
        result_load = pltpu.make_async_copy(result_in, result, local_sems.at[8])
        result_load.start()

    def step(s):
        if remote:
            net.step(s)
            stream.step(s)

    total = make_features(counts, place.set_index, slots, set_rows, feat_q, feat_k)
    zero_row = jnp.zeros((1, width), f32)

    def weight(m, lanes=None):
        block = w0[m] if lanes is None else w0[m, :, :, lanes]
        return block.reshape(width, block.shape[-1])

    for copy in loads:
        copy.wait()
    if remote:
        result_load.wait()
        own_result = pltpu.make_async_copy(result, stream_out.at[mp], local_sems.at[8])
        own_result.start()

    def attention(u, _):
        m = net.plane(u) if remote else u
        dm = mm(d_proj[...], weight(m, pl.ds(MIX, 2 * LANES))).astype(low)
        d_mixed[m, :, 0:LANES] = dm[:, 0:LANES]
        d_mixed[m, :, LANES:] = keep_half(1, dm[:, LANES:], jnp.zeros_like(dm[:, LANES:]))
        step(2 * u)
        attend_back(m, qkv, d_mixed, feat_q, feat_k, place.window_start, window, acc, d_query)
        d_qkv[m, :, 0:128] = d_query[own, 0:128]
        d_qkv[m, :, 128:256] = acc[own, 0:128].astype(low)
        d_qkv[m, :, 256:384] = acc[own, 128:256].astype(low)
        d_qkv[m, :, 384:512] = jnp.zeros((own_rows, LANES), low)
        d_qkv[m, :, 512:640] = d_query[own, 128:256]
        d_qkv[m, :, 640:768] = acc[own, 256:384].astype(low)
        (sums_mine if remote else sums_out)[pl.ds(8 + m, 1)] = column_sum(d_qkv[m].astype(f32))
        step(2 * u + 1)
        block = mm(normed_t[...], d_qkv[m])
        extra = mm(d_proj_t[...], mixed[m])
        shape = fresh.shape[1:4]

        def keep(lanes, value):
            fresh[m, :, :, :, lanes] = value.astype(low).reshape(*shape, value.shape[1])

        keep(pl.ds(0, MIX), block[:, 0:MIX])
        keep(pl.ds(MIX, 2 * LANES), block[:, MIX : MIX + 2 * LANES] + extra)
        keep(pl.ds(MIX + 2 * LANES, LANES), block[:, MIX + 2 * LANES :])
        if remote:
            net.offer_fresh(u)
        part_sum = mm(d_qkv[m], weight(m), NT)

        @pl.when(u == 0)
        def _():
            d_normed[...] = part_sum

        @pl.when(u > 0)
        def _():
            d_normed[...] += part_sum

        return 0

    lax.fori_loop(0, n_mp, attention, 0)

    def norm_one(i, carry):
        at = tile_rows(i)
        grad = d_normed[at]
        dv, grad_unit = norm_grad(tokens[at].astype(f32), vec[0:1], grad)
        rows_out = (d_mid[tile_rows(i, own_start)] + dv).astype(low)
        if remote:
            input_t[:, at] = rows_out.T
        else:
            input_out[at] = rows_out
        return tuple(c + column_sum(n) for c, n in zip(carry, (grad_unit, grad)))

    gain_one, shift_one = lax.fori_loop(0, own_rows // LANES, norm_one, (zero_row, zero_row))
    if not remote:
        sums_out[0:1] = gain_one
        sums_out[1:2] = shift_one
        sums_out[2:8] = jnp.zeros((6, width), f32)
        reduced[...] = jnp.zeros_like(reduced)
        fresh_copy = pltpu.make_async_copy(fresh, stream_out, local_sems.at[8])
        fresh_copy.start()
        fresh_copy.wait()
        return

    share = width // n_mp

    def turn(away):
        peer = (mp + away) % n_mp
        return pltpu.make_async_remote_copy(
            src_ref=input_t.at[pl.ds(pl.multiple_of(peer * share, HD), share)],
            dst_ref=input_out.at[mp],
            send_sem=turn_send.at[away],
            recv_sem=turn_recv.at[away],
            device_id={"mp": peer},
            device_id_type=MESH,
        )

    def turned(away):
        source = (mp - away + n_mp) % n_mp
        return pltpu.make_async_remote_copy(
            src_ref=input_t.at[pl.ds(0, share)],
            dst_ref=input_out.at[source],
            send_sem=turn_send.at[away],
            recv_sem=turn_recv.at[away],
            device_id={"mp": source},
            device_id_type=MESH,
        )

    for away in range(1, n_mp):
        turn(away).start()
    own_turn = pltpu.make_async_copy(
        input_t.at[pl.ds(pl.multiple_of(mp * share, HD), share)], input_out.at[mp], local_sems.at[9]
    )
    own_turn.start()
    first_row = place.window_start + own_start
    held = jnp.clip(total - first_row, 0, own_rows).astype(f32)
    lane_w = lax.broadcasted_iota(jnp.int32, (1, width), 1)
    scalar_row = jnp.where(lane_w == 3, held, 0.0)
    for i in range(3):
        part = jnp.sum(sums_in[12 + i : 13 + i], axis=1, keepdims=True)
        scalar_row = scalar_row + jnp.where(lane_w == i, part, 0.0)
    value[0, 0:1] = gain_one
    value[0, 1:2] = shift_one
    value[0, 2:8] = sums_in[2:8]
    natural = bias_rows_natural(sums_mine[8 : 8 + n_mp], sums_in[8 : 8 + n_mp], n_mp, width)
    for i, row in enumerate(natural + [scalar_row, zero_row]):
        value[0, 8 + i : 9 + i] = row
    swaps.send(0)
    steps = GROUPS * n_mp + net.STEPS
    for i in range(5):
        step(2 * n_mp + i)
        swaps.add(i)
        if i < 4:
            swaps.send(i + 1)
    sums_out[...] = value[5]

    def more(s, _):
        step(s)
        return 0

    lax.fori_loop(2 * n_mp + 5, steps, more, 0)
    factor_sums(
        reduced, sub_prior, lane_prior, masters, n_dp, n_mp, *exchanges, (sub_out, lane_out, scalar_out)
    )

    def rest_of_stream(s, _):
        stream.step(s)
        return 0

    lax.fori_loop(steps, stream.STEPS, rest_of_stream, 0)
    for away in range(1, n_mp):
        turned(away).wait_recv()
        turn(away).wait_send()
    own_turn.wait()
    net.finish()
    stream.finish()
    swaps.finish()
    own_result.wait()


def shard_offset(shard_piece, block_index, whole_length, axis_at):
    shape_list = list(shard_piece.shape)
    shape_list[axis_at] = whole_length
    empty = jnp.zeros(tuple(shape_list), jnp.float32)
    return lax.dynamic_update_slice_in_dim(
        empty, shard_piece, block_index * shard_piece.shape[axis_at], axis_at
    )


def select_slice(whole_array, block_index, block_width, axis_at):
    return lax.dynamic_slice_in_dim(whole_array, block_index * block_width, block_width, axis_at)


def factor_step(
    gradient,
    rows_old,
    cols_old,
    rows_mine,
    cols_mine,
    rows_total,
    count_rows,
    count_cols,
    prior_total,
):
    decay_rate = 1.0 - STEP ** (-0.8)
    rows_new = decay_rate * rows_old + (1.0 - decay_rate) * (rows_mine / count_cols + square_eps)
    cols_new = decay_rate * cols_old + (1.0 - decay_rate) * (cols_mine / count_rows + square_eps)
    rows_average = (
        decay_rate * prior_total
        + (1.0 - decay_rate) * (rows_total / count_cols + count_rows * square_eps)
    ) / count_rows
    update = gradient * lax.rsqrt(rows_new[:, None] * cols_new[None, :] / rows_average)
    return (rows_new, cols_new, update, jnp.sum(update * update))


def plain_step(weight, gradient, moment_old):
    decay_rate = 1.0 - STEP ** (-0.8)
    moment = decay_rate * moment_old + (1.0 - decay_rate) * (gradient * gradient + square_eps)
    update = gradient * lax.rsqrt(moment)
    update_rms = jnp.sqrt(jnp.mean(update * update))
    rate_here = step_rate * jnp.sqrt(jnp.mean(weight * weight))
    return (weight - rate_here * update / jnp.maximum(1.0, update_rms / clip_limit), moment)


def shards(
    tokens_in,
    cotangent,
    patch_counts,
    w_qkv,
    w_out,
    w_up,
    w_down,
    layer_vector_rows,
    inner_biases,
    qkvrows_prior,
    qkvcols_prior,
    outrows_prior,
    outcols_prior,
    uprows_prior,
    upcols_prior,
    downrows_prior,
    downcols_prior,
    vector_moment,
    bias_moment,
):
    n_dp, n_mp = lax.axis_size("dp"), lax.axis_size("mp")
    data_index = lax.axis_index("dp")
    parallel_model_index = lax.axis_index("mp")
    row_count, parallel_model_width = tokens_in.shape
    set_count, slot_count = patch_counts.shape
    set_rows = row_count // set_count
    own_rows = row_count // n_mp
    shard_width_local = w_qkv.shape[2]
    local_hidden = w_up.shape[1]
    f32, low = jnp.float32, jnp.bfloat16
    width, hidden_width = parallel_model_width, local_hidden
    blocks = pack(w_qkv, w_out, w_up, w_down).astype(low)
    set_index = parallel_model_index // (set_rows // own_rows)
    window = own_rows + HALO
    by_mp = inner_biases.reshape(6, n_mp, shard_width_local)
    none = jnp.zeros((n_mp, shard_width_local), f32)
    bias_rows = jnp.concatenate(
        [
            permute_chunks(jnp.concatenate([by_mp[0], none, by_mp[1], none], axis=1), CHUNKS),
            by_mp[2:].transpose(1, 2, 0).reshape(n_mp, hidden_width),
        ]
    )
    vmem = pl.BlockSpec(memory_space=pltpu.VMEM)
    anywhere = pl.BlockSpec(memory_space=pl.ANY)
    scalars_in = pl.BlockSpec(memory_space=pltpu.SMEM)
    dma = pltpu.SemaphoreType.DMA

    def shape(*dims, dtype=low):
        return jax.ShapeDtypeStruct(dims, dtype)

    block_rows = blocks.shape[1]
    remote = n_dp == 8 and n_mp == 4 and block_rows % 32 == 0
    split_dp = (n_dp, block_rows)
    if not remote:
        blocks = lax.all_gather(lax.all_gather(blocks, "dp", axis=1, tiled=True), "mp", axis=1)
        split_dp = (1, width)
        blocks = blocks.reshape(GROUPS, n_mp, 1, width, width)
    w0, qkv, mixed, normed_t, d_mid, d_proj, d_proj_t, grads_ffn, result, sums_a = pl.pallas_call(
        functools.partial(layer_kernel, n_mp, slot_count, own_rows, remote),
        out_shape=(
            shape(n_mp, *split_dp, width),
            shape(n_mp, window, width),
            shape(n_mp, own_rows, 2 * LANES),
            shape(width, own_rows),
            shape(window, width, dtype=f32),
            shape(window, width),
            shape(width, own_rows),
            shape(2, n_mp, width, width),
            shape(own_rows, width),
            shape(16, width, dtype=f32),
        ),
        in_specs=[anywhere, anywhere, anywhere, scalars_in, vmem, vmem],
        out_specs=(anywhere,) * 9 + (vmem,),
        scratch_shapes=[
            pltpu.VMEM((GROUPS, n_mp, *split_dp, width), low),
            pltpu.VMEM((set_rows, width), low),
            pltpu.VMEM((set_rows, width), low),
            pltpu.VMEM((set_rows, width), low),
            pltpu.VMEM((width, own_rows), low),
            pltpu.VMEM((n_mp, set_rows, width), low),
            pltpu.VMEM((n_mp, window, 2 * LANES), low),
            pltpu.VMEM((window, width), f32),
            pltpu.VMEM((window, width), f32),
            pltpu.VMEM((window, width), low),
            pltpu.VMEM((width, own_rows), low),
            pltpu.VMEM((n_mp, window, hidden_width), low),
            pltpu.VMEM((n_mp, window, hidden_width), low),
            pltpu.VMEM((own_rows, width), f32),
            pltpu.VMEM((window, width), low),
            pltpu.VMEM((width, own_rows), low),
            pltpu.VMEM((window, width), f32),
            pltpu.VMEM((window, width), low),
            pltpu.VMEM((2, width, width), low),
            pltpu.VMEM((own_rows, width), low),
            pltpu.VMEM((set_rows, LANES), low),
            pltpu.VMEM((set_rows, LANES), low),
            dma((GROUPS, n_mp, KINDS)),
            dma((GROUPS, n_mp, KINDS) if remote else (GROUPS, n_mp)),
            dma((GROUPS, n_mp, 2)),
            dma((3,)),
            dma((8,)),
            dma((2,)),
        ],
        compiler_params=pltpu.CompilerParams(
            vmem_limit_bytes=63 * 2**20,
            **(dict(collective_id=1, has_side_effects=True) if remote else {}),
        ),
    )(tokens_in, cotangent, blocks, patch_counts, layer_vector_rows, bias_rows)
    block = (n_mp, block_rows, width)
    scatter_scratch = [
        pltpu.VMEM((GROUPS, n_mp, 4, block_rows, width), low),
        pltpu.VMEM((GROUPS, n_mp, 2, block_rows // 2, width), low),
        pltpu.VMEM((GROUPS, *block), low),
        pltpu.VMEM((GROUPS, *block), low),
        pltpu.VMEM((GROUPS, n_mp, 2, block_rows, width), low),
        pltpu.VMEM((GROUPS, n_mp, 4, block_rows, width), low),
        pltpu.VMEM((GROUPS, *block), low),
        dma((GROUPS, n_mp)),
        dma((GROUPS, n_mp, R_KINDS)),
        dma((GROUPS, n_mp, R_KINDS)),
        dma((2, n_mp, Stream.CUTS)),
        dma((n_mp, Stream.CUTS)),
        pltpu.VMEM((width, own_rows), low),
        dma((n_mp,)),
        dma((n_mp,)),
        pltpu.VMEM((6, 16, width), f32),
        pltpu.VMEM((5, 16, width), f32),
        dma((5,)),
        dma((5,)),
        pltpu.VMEM((n_mp, 8, LANES), f32),
        pltpu.VMEM((n_dp, 8, width), f32),
        pltpu.VMEM((n_mp, 8, LANES), f32),
        pltpu.VMEM((n_dp, 8, LANES), f32),
        dma((4, max(n_dp, n_mp))),
        dma((4, max(n_dp, n_mp))),
        pltpu.VMEM((16, width), f32),
        pltpu.VMEM((own_rows, width), low),
    ]
    first_block = permute_chunks(
        jnp.concatenate([w_qkv[:, 0], w_qkv[:, 1], w_qkv[:, 2], w_out.T], axis=1), CHUNKS
    )
    masters = jnp.stack([w_up, w_down.T, first_block])
    sub_prior = jnp.pad(
        jnp.stack([qkvrows_prior, outcols_prior, uprows_prior, downcols_prior]), ((0, 4), (0, LANES - block_rows))
    )
    lane_prior = jnp.stack(
        [
            upcols_prior,
            downrows_prior,
            permute_chunks(jnp.concatenate([qkvcols_prior.reshape(-1), outrows_prior]), CHUNKS),
        ]
    )
    reduced, input_rows, sums_b, stream, sub_new, lane_new, scalar_rows = pl.pallas_call(
        functools.partial(back_kernel, n_dp, n_mp, slot_count, own_rows, set_rows, remote),
        out_shape=(
            shape(GROUPS, block_rows, width, dtype=f32),
            shape(n_mp, width // n_mp, own_rows) if remote else shape(own_rows, width),
            shape(16, width, dtype=f32),
            shape(n_mp, own_rows, width) if remote else shape(n_mp, 1, 1, width, width),
            shape(8, LANES, dtype=f32),
            shape(8, width, dtype=f32),
            shape(8, LANES, dtype=f32),
        ),
        in_specs=[anywhere, scalars_in, vmem] + [anywhere] * 9 + [vmem] * 4,
        out_specs=(vmem, anywhere if remote else vmem, vmem, anywhere, vmem, vmem, vmem),
        scratch_shapes=[
            pltpu.VMEM((own_rows, width), low),
            pltpu.VMEM((n_mp, *split_dp, width), low),
            pltpu.VMEM((n_mp, window, width), low),
            pltpu.VMEM((n_mp, own_rows, 2 * LANES), low),
            pltpu.VMEM((width, own_rows), low),
            pltpu.VMEM((window, width), f32),
            pltpu.VMEM((window, width), low),
            pltpu.VMEM((width, own_rows), low),
            pltpu.VMEM((n_mp, window, 2 * LANES), low),
            pltpu.VMEM((window, 3 * LANES), f32),
            pltpu.VMEM((window, 2 * LANES), low),
            pltpu.VMEM((n_mp, own_rows, width), low),
            pltpu.VMEM((own_rows, width), f32),
            pltpu.VMEM((n_mp, n_dp // 2, 2, block_rows, width) if remote else (n_mp, 1, 1, width, width), low),
            pltpu.VMEM((set_rows, LANES), low),
            pltpu.VMEM((set_rows, LANES), low),
            dma((10,)),
        ]
        + (scatter_scratch if remote else []),
        compiler_params=pltpu.CompilerParams(
            vmem_limit_bytes=63 * 2**20,
            **(dict(collective_id=2, has_side_effects=True) if remote else {}),
        ),
    )(
        tokens_in, patch_counts, layer_vector_rows, w0, qkv, mixed, normed_t, d_mid, d_proj, d_proj_t,
        grads_ffn.reshape(2, n_mp, n_dp // 2, 2, block_rows, width), result,
        sums_a, sub_prior, lane_prior, masters,
    )
    if remote:
        both = lambda *dims: (shape(*dims, dtype=f32),) * 2 + (shape(*dims),)
        kinds = [
            both(3, block_rows, shard_width_local),
            both(block_rows, shard_width_local),
            both(block_rows, width),
            both(block_rows, width),
        ]
        small = [(8, width), (6, width)] * 3 + [(8, LANES)]
        outs = pl.pallas_call(
            functools.partial(update_kernel, n_dp, n_mp),
            out_shape=(
                shape(n_mp, own_rows, width),
                shape(shard_width_local, row_count, dtype=f32),
                *(kind[i] for i in range(3) for kind in kinds),
                *(shape(*dims, dtype=f32) for dims in small),
            ),
            in_specs=[vmem] * 11 + [anywhere],
            out_specs=(anywhere,) + (vmem,) * 20,
            scratch_shapes=[pltpu.VMEM((n_mp, own_rows, width), low), dma((2,))],
            compiler_params=pltpu.CompilerParams(vmem_limit_bytes=60 * 2**20),
        )(
            reduced, masters, sub_new, lane_new, scalar_rows, sums_b, layer_vector_rows, inner_biases, vector_moment,
            bias_moment, input_rows, stream,
        )
        stream_rows, input_t = outs[:2]
        weights = [
            (outs[i].transpose(1, 0, 2), outs[i + 1].T, outs[i + 2], outs[i + 3].T) for i in (2, 6, 10)
        ]
        vector_grad, bias_grad, moment_vectors, moment_biases, vectors_after, biases_after, scalars_out = outs[14:]
        lanes_first = permute_chunks(lane_new[2], BACK)
        rows_of = lambda i: sub_new[i, :block_rows]
        return (
            stream_rows.reshape(row_count, width),
            input_t.T,
            *weights[0],
            *weights[1],
            *weights[2],
            rows_of(SUB_QKV),
            lanes_first[: 3 * shard_width_local].reshape(3, shard_width_local),
            lanes_first[3 * shard_width_local :],
            rows_of(SUB_OUT),
            rows_of(SUB_UP),
            lane_new[0],
            lane_new[1],
            rows_of(SUB_DOWN),
            vector_grad,
            bias_grad,
            moment_vectors,
            moment_biases,
            vectors_after,
            biases_after,
            scalars_out[0, :4],
            scalars_out[1, :3],
        )
    vector_part = sums_a[:8] + sums_b[:8]
    bias_sums = jnp.concatenate([sums_b[8 : 8 + n_mp], sums_a[8 : 8 + n_mp]])
    result_low = lax.all_gather(result, "mp", axis=0, tiled=True)
    grads = jnp.concatenate([stream.reshape(1, n_mp, width, width), grads_ffn])
    own = lax.psum_scatter(grads, "mp", scatter_dimension=1)
    reduced = lax.psum_scatter(own, "dp", scatter_dimension=1, tiled=True).astype(f32)
    input_grad = lax.all_to_all(input_rows, "mp", 1, 0, tiled=True).astype(f32)

    bias_qkv = permute_chunks(bias_sums[:n_mp], BACK).reshape(n_mp, 4, shard_width_local)
    hidden_sums = bias_sums[n_mp:].reshape(n_mp, shard_width_local, -1).transpose(2, 0, 1)
    bias_part = jnp.concatenate(
        [
            bias_qkv[:, 0].reshape(1, width),
            bias_qkv[:, 2].reshape(1, width),
            hidden_sums.reshape(-1, width),
        ]
    )
    own_first = parallel_model_index % (set_rows // own_rows) * own_rows
    held = jnp.sum(lax.dynamic_index_in_dim(patch_counts, set_index, 0, keepdims=False))
    counted = jnp.clip(held - own_first, 0, own_rows).astype(f32)
    vector_grad, bias_grad, squares_all, counted_all = lax.psum(
        (vector_part, bias_part, jnp.sum(sums_a[12:15], axis=1), counted), ("dp", "mp")
    )
    token_spread = jnp.sqrt(squares_all / (counted_all * parallel_model_width))
    qkv_grad, out_grad, up_grad, down_grad = unpack(reduced)
    square_qkv = qkv_grad * qkv_grad
    square_out = out_grad * out_grad
    square_up = up_grad * up_grad
    square_down = down_grad * down_grad
    scalars = jnp.stack(
        [
            jnp.sum(w_qkv * w_qkv),
            jnp.sum(w_out * w_out),
            jnp.sum(w_up * w_up),
            jnp.sum(w_down * w_down),
            jnp.where(parallel_model_index == 0, jnp.sum(qkvrows_prior), 0.0),
            jnp.where(data_index == 0, jnp.sum(outrows_prior), 0.0),
            jnp.where(parallel_model_index == 0, jnp.sum(uprows_prior), 0.0),
            jnp.where(data_index == 0, jnp.sum(downrows_prior), 0.0),
        ]
    )
    factor_totals = lax.psum(
        (
            shard_offset(jnp.sum(square_qkv, axis=(1, 2)), data_index, parallel_model_width, 0),
            shard_offset(
                jnp.sum(square_qkv, axis=0), parallel_model_index, parallel_model_width, 1
            ),
            shard_offset(
                jnp.sum(square_out, axis=1), parallel_model_index, parallel_model_width, 0
            ),
            shard_offset(jnp.sum(square_out, axis=0), data_index, parallel_model_width, 0),
            shard_offset(jnp.sum(square_up, axis=1), data_index, parallel_model_width, 0),
            shard_offset(jnp.sum(square_up, axis=0), parallel_model_index, FF, 0),
            shard_offset(jnp.sum(square_down, axis=1), parallel_model_index, FF, 0),
            shard_offset(jnp.sum(square_down, axis=0), data_index, parallel_model_width, 0),
            scalars,
        ),
        ("dp", "mp"),
    )
    (
        rows_qkv,
        cols_qkv,
        rows_out,
        cols_out,
        rows_up,
        cols_up,
        rows_down,
        cols_down,
        scalar_totals,
    ) = factor_totals
    local_rows = w_qkv.shape[0]
    local_cols = w_out.shape[1]
    qkvrows_after, qkvcols_flat, update_qkv, usq_qkv = factor_step(
        qkv_grad.reshape(local_rows, 3 * shard_width_local),
        qkvrows_prior,
        qkvcols_prior.reshape(3 * shard_width_local),
        select_slice(rows_qkv, data_index, local_rows, 0),
        select_slice(cols_qkv, parallel_model_index, shard_width_local, 1).reshape(
            3 * shard_width_local
        ),
        jnp.sum(rows_qkv),
        parallel_model_width,
        3 * parallel_model_width,
        scalar_totals[4],
    )
    outrows_after, outcols_after, update_out, usq_out = factor_step(
        out_grad,
        outrows_prior,
        outcols_prior,
        select_slice(rows_out, parallel_model_index, shard_width_local, 0),
        select_slice(cols_out, data_index, local_cols, 0),
        jnp.sum(rows_out),
        parallel_model_width,
        parallel_model_width,
        scalar_totals[5],
    )
    uprows_after, upcols_after, update_up, usq_up = factor_step(
        up_grad,
        uprows_prior,
        upcols_prior,
        select_slice(rows_up, data_index, local_rows, 0),
        select_slice(cols_up, parallel_model_index, local_hidden, 0),
        jnp.sum(rows_up),
        parallel_model_width,
        FF,
        scalar_totals[6],
    )
    downrows_after, downcols_after, update_down, usq_down = factor_step(
        down_grad,
        downrows_prior,
        downcols_prior,
        select_slice(rows_down, parallel_model_index, local_hidden, 0),
        select_slice(cols_down, data_index, local_cols, 0),
        jnp.sum(rows_down),
        FF,
        parallel_model_width,
        scalar_totals[7],
    )
    usq_totals = lax.psum(jnp.stack([usq_qkv, usq_out, usq_up, usq_down]), ("dp", "mp"))
    entry_counts = jnp.array(
        [
            3.0 * parallel_model_width * parallel_model_width,
            1.0 * parallel_model_width * parallel_model_width,
            1.0 * parallel_model_width * FF,
            1.0 * FF * parallel_model_width,
        ],
        jnp.float32,
    )
    update_scale = jnp.sqrt(usq_totals / entry_counts)
    weight_rms = jnp.sqrt(scalar_totals[:4] / entry_counts)
    limits = jnp.maximum(1.0, update_scale / clip_limit)
    qkv_after = (
        w_qkv.reshape(local_rows, 3 * shard_width_local)
        - step_rate * weight_rms[0] * update_qkv / limits[0]
    ).reshape(w_qkv.shape)
    out_after = w_out - step_rate * weight_rms[1] * update_out / limits[1]
    up_after = w_up - step_rate * weight_rms[2] * update_up / limits[2]
    down_after = w_down - step_rate * weight_rms[3] * update_down / limits[3]
    vectors_after, moment_vectors = jax.vmap(plain_step)(
        layer_vector_rows, vector_grad, vector_moment
    )
    heads_after, heads_moment = jax.vmap(plain_step)(
        inner_biases[:2], bias_grad[:2], bias_moment[:2]
    )
    upper_after, upper_moment = plain_step(
        inner_biases[2:].reshape(FF), bias_grad[2:].reshape(FF), bias_moment[2:].reshape(FF)
    )
    biases_after = jnp.concatenate(
        [heads_after, upper_after.reshape(FF // parallel_model_width, parallel_model_width)], axis=0
    )
    moment_biases = jnp.concatenate(
        [heads_moment, upper_moment.reshape(FF // parallel_model_width, parallel_model_width)],
        axis=0,
    )
    return (
        result_low,
        input_grad,
        qkv_grad,
        out_grad,
        up_grad,
        down_grad,
        qkv_after,
        out_after,
        up_after,
        down_after,
        qkv_after.astype(jnp.bfloat16),
        out_after.astype(jnp.bfloat16),
        up_after.astype(jnp.bfloat16),
        down_after.astype(jnp.bfloat16),
        qkvrows_after,
        qkvcols_flat.reshape(3, shard_width_local),
        outrows_after,
        outcols_after,
        uprows_after,
        upcols_after,
        downrows_after,
        downcols_after,
        vector_grad,
        bias_grad,
        moment_vectors,
        moment_biases,
        vectors_after,
        biases_after,
        update_scale,
        token_spread,
    )


def solution(mesh):
    in_specs = (
        P("dp", None),
        P("dp", None),
        P("dp", None),
        P("dp", None, "mp"),
        P("mp", "dp"),
        P("dp", "mp"),
        P("mp", "dp"),
        P(),
        P(),
        P("dp"),
        P(None, "mp"),
        P("mp"),
        P("dp"),
        P("dp"),
        P("mp"),
        P("mp"),
        P("dp"),
        P(),
        P(),
    )
    out_specs = (
        P("dp", None),
        P("dp", "mp"),
        P("dp", None, "mp"),
        P("mp", "dp"),
        P("dp", "mp"),
        P("mp", "dp"),
        P("dp", None, "mp"),
        P("mp", "dp"),
        P("dp", "mp"),
        P("mp", "dp"),
        P("dp", None, "mp"),
        P("mp", "dp"),
        P("dp", "mp"),
        P("mp", "dp"),
        P("dp"),
        P(None, "mp"),
        P("mp"),
        P("dp"),
        P("dp"),
        P("mp"),
        P("mp"),
        P("dp"),
        P(),
        P(),
        P(),
        P(),
        P(),
        P(),
        P(),
        P(),
    )
    return jax.shard_map(shards, mesh=mesh, in_specs=in_specs, out_specs=out_specs, check_vma=False)
```

```python
import functools

import jax
import jax.numpy as jnp
from jax import lax
from jax.experimental import pallas as pl
from jax.experimental.pallas import tpu as pltpu
from jax.sharding import PartitionSpec as P

HD = 64
FF = 3072
STEP = 3


norm_eps = 1e-06
square_eps = 1e-30
clip_limit = 0.5
step_rate = 0.6
mask_fill = -1000000000.0


MESH = pl.DeviceIdType.MESH
HALO = 128
GROUPS = 3

def neighbours(dp):
    core = dp % 2
    return dp + 1 - 2 * core, dp + 2 - 4 * ((dp // 2) % 2), (dp + 4) % 8, (dp + 4) % 8 + 2 - 4 * ((dp // 2) % 2)


def flip(dp):
    return dp + 1 - 2 * (dp % 2)


def greet(devices, extra):
    barrier = pltpu.get_barrier_semaphore()
    for device in devices:
        pl.semaphore_signal(barrier, inc=1, device_id=device, device_id_type=MESH)
    for condition, device in extra:

        @pl.when(condition)
        def _():
            pl.semaphore_signal(barrier, inc=1, device_id=device, device_id_type=MESH)

    peers = len(devices)
    for condition, _ in extra:
        peers = peers + jnp.where(condition, 1, 0)
    pl.semaphore_wait(barrier, peers)


A_Z, A_X, A_Y, A_D0, A_D1, A_S, A_SX, A_SY, A_SD0, A_SD1 = range(10)
KINDS = 10
ORDERS = ((0, 1, 2, 3), (1, 0, 2, 3), (2, 3, 1, 0), (3, 2, 1, 0))


def plane_at(mp, unit):
    codes = [sum(plane * 4**i for i, plane in enumerate(order)) for order in ORDERS]
    code = jnp.where(mp == 0, codes[0], jnp.where(mp == 1, codes[1], jnp.where(mp == 2, codes[2], codes[3])))
    power = jnp.where(unit == 0, 1, jnp.where(unit == 1, 4, jnp.where(unit == 2, 16, 64)))
    return (code // power) % 4

class Gather:
    def __init__(self, n_mp, out, send_sems, recv_sems, way_sems):
        self.dp, self.mp, self.n_mp = lax.axis_index("dp"), lax.axis_index("mp"), n_mp
        self.out, self.send_sems, self.recv_sems, self.way_sems = out, send_sems, recv_sems, way_sems
        self.sib, self.xn, self.yn, self.dn = neighbours(self.dp)
        self.rows = out.shape[4]
        self.up, self.down = jnp.minimum(self.mp + 1, n_mp - 1), jnp.maximum(self.mp - 1, 0)
        self.inner = jnp.where((self.mp > 0) & (self.mp < n_mp - 1), 1, 0)
        half = self.rows // 2
        self.all, self.low, self.high = pl.ds(0, self.rows), pl.ds(0, half), pl.ds(half, half)

    def message(self, kind, group, plane, slot, part, device):
        where = self.out.at[group, plane, slot // 2, slot % 2, part]
        return pltpu.make_async_remote_copy(
            src_ref=where,
            dst_ref=where,
            send_sem=self.send_sems.at[group, plane, kind],
            recv_sem=self.recv_sems.at[group, plane, kind],
            device_id=(device, self.mp),
            device_id_type=MESH,
        )

    def along(self, group, plane, way):
        where = self.out.at[group, plane, self.dp // 2, self.dp % 2]
        return pltpu.make_async_remote_copy(
            src_ref=where,
            dst_ref=where,
            send_sem=self.way_sems.at[group, plane, way],
            recv_sem=self.recv_sems.at[group, plane, A_Z],
            device_id=(self.dp, self.down if way else self.up),
            device_id_type=MESH,
        )

    def sends(self, group, plane):
        dp, xn, yn, dn, sib = self.dp, self.xn, self.yn, self.dn, self.sib
        first = [(A_X, dp, self.all, xn), (A_Y, dp, self.all, yn), (A_S, dp, self.all, sib)]
        second = [(A_D0, xn, self.low, yn), (A_SX, xn, self.all, sib), (A_D1, yn, self.high, xn), (A_SY, yn, self.all, sib)]
        third = [(A_SD0, dn, self.low, sib), (A_SD1, dn, self.high, sib)]
        return [
            [functools.partial(self.message, kind, group, plane, *rest) for kind, *rest in part]
            for part in (first, second, third)
        ]

    def unit(self, t):
        group = t // self.n_mp
        return group, plane_at(self.mp, t % self.n_mp)

    def guarded(self, t, action):
        if isinstance(t, int):
            if 0 <= t < GROUPS * self.n_mp:
                action(*self.unit(t))
            return

        @pl.when((t >= 0) & (t < GROUPS * self.n_mp))
        def _():
            action(*self.unit(t))

    def stage_z(self, t):
        def action(group, plane):
            @pl.when(plane != self.mp)
            def _():
                self.along(group, plane, 0).wait_recv()

            @pl.when((plane <= self.mp) & (self.mp < self.n_mp - 1))
            def _():
                self.along(group, plane, 0).start()

            @pl.when((plane >= self.mp) & (self.mp > 0))
            def _():
                self.along(group, plane, 1).start()

        self.guarded(t, action)

    def stage_a(self, t):
        def action(group, plane):
            for copy in self.sends(group, plane)[0]:
                copy().start()

        self.guarded(t, action)

    def stage_b(self, t):
        def action(group, plane):
            out = self.sends(group, plane)[1]
            self.message(A_X, group, plane, self.xn, self.all, self.xn).wait_recv()
            out[0]().start()
            out[1]().start()
            self.message(A_Y, group, plane, self.yn, self.all, self.yn).wait_recv()
            out[2]().start()
            out[3]().start()

        self.guarded(t, action)

    def stage_c(self, t):
        def action(group, plane):
            out = self.sends(group, plane)[2]
            self.message(A_D0, group, plane, self.dn, self.low, self.yn).wait_recv()
            out[0]().start()
            self.message(A_D1, group, plane, self.dn, self.high, self.xn).wait_recv()
            out[1]().start()

        self.guarded(t, action)

    def stage_d(self, t):
        def action(group, plane):
            for kind, slot, part in (
                (A_S, self.sib, self.all),
                (A_SX, flip(self.xn), self.all),
                (A_SY, flip(self.yn), self.all),
                (A_SD0, flip(self.dn), self.low),
                (A_SD1, flip(self.dn), self.high),
            ):
                self.message(kind, group, plane, slot, part, self.sib).wait_recv()

        self.guarded(t, action)

    def plane(self, u):
        return plane_at(self.mp, u)

    def begin(self):
        for t in (0, 1):
            self.stage_z(t)
            self.stage_a(t)

        @pl.when(self.inner == 1)
        def _():
            self.stage_z(2)

    def step(self, s):
        self.stage_b(s)
        ahead = (2,) if isinstance(s, int) and s < 2 else (2, 3) if isinstance(s, int) and s == 2 else (3,)
        for more in ahead:
            self.stage_z(s + more + self.inner)
            self.stage_a(s + more)
        self.stage_c(s - 1)

    def finish(self, t):
        def action(group, plane):
            for part in self.sends(group, plane):
                for copy in part:
                    copy().wait_send()

            @pl.when((plane <= self.mp) & (self.mp < self.n_mp - 1))
            def _():
                self.along(group, plane, 0).wait_send()

            @pl.when((plane >= self.mp) & (self.mp > 0))
            def _():
                self.along(group, plane, 1).wait_send()

        self.guarded(t, action)

R_S, R_D0, R_D1, R_X, R_Y, R_UP, R_DOWN = range(7)
R_KINDS = 7
RING = 4


class Scatter:
    def __init__(self, n_mp, blocks, out, bufs, credit, send_sems, recv_sems):
        self.dp, self.mp, self.n_mp = lax.axis_index("dp"), lax.axis_index("mp"), n_mp
        self.blocks, self.out, self.credit = blocks, out, credit
        self.pair_in, self.halves_in, self.x_in, self.y_in, self.z_in = bufs
        self.send_sems, self.recv_sems = send_sems, recv_sems
        self.sib, self.xn, self.yn, self.dn = neighbours(self.dp)
        self.core = self.dp % 2
        self.here, self.at_x, self.at_y, self.at_d = self.dp // 2, self.xn // 2, self.yn // 2, self.dn // 2
        self.up, self.down = jnp.minimum(self.mp + 1, n_mp - 1), jnp.maximum(self.mp - 1, 0)
        rows = out.shape[1]
        self.all, self.low, self.high = pl.ds(0, rows), pl.ds(0, rows // 2), pl.ds(rows // 2, rows // 2)
        self.fed = 2 * n_mp
        self.units = GROUPS * n_mp

    def offered(self, o):
        if isinstance(o, int) and o >= self.fed:
            return 0, plane_at(self.mp, self.units - 1 - o)
        return 2 - o % 2, plane_at(self.mp, o // 2)

    def unit(self, k):
        if isinstance(k, int) and k >= self.fed:
            return 0, plane_at(self.mp, self.units - 1 - k)
        return 2 - k % 2, plane_at(self.mp, self.n_mp - 1 - k // 2)

    def remote(self, kind, group, plane, src, dst, device):
        return pltpu.make_async_remote_copy(
            src_ref=src,
            dst_ref=dst,
            send_sem=self.send_sems.at[group, plane, kind],
            recv_sem=self.recv_sems.at[group, plane, kind],
            device_id=device,
            device_id_type=MESH,
        )

    def pair(self, o, group, plane):
        return self.remote(
            R_S, group, plane, self.blocks.at[group, plane, :, 1 - self.core], self.pair_in.at[o % RING], (self.sib, self.mp)
        )

    def mine(self, group, plane, place, part=None):
        return self.blocks.at[group, plane, place, self.core, self.all if part is None else part]

    def message(self, kind, group, plane):
        mp = self.mp
        if kind == R_D0:
            src, dst = self.mine(group, plane, self.at_d, self.low), self.halves_in.at[group, plane, 0]
            device = (self.xn, mp)
        elif kind == R_D1:
            src, dst = self.mine(group, plane, self.at_d, self.high), self.halves_in.at[group, plane, 1]
            device = (self.yn, mp)
        elif kind == R_X:
            src, dst, device = self.mine(group, plane, self.at_x), self.x_in.at[group, plane], (self.xn, mp)
        elif kind == R_Y:
            src, dst, device = self.mine(group, plane, self.at_y), self.y_in.at[group, plane], (self.yn, mp)
        elif kind == R_UP:
            src, dst, device = self.mine(group, plane, self.here), self.z_in.at[group, plane], (self.dp, self.up)
        else:
            slot = jnp.where(plane == mp - 1, self.n_mp, plane)
            src, dst, device = self.mine(group, plane, self.here), self.z_in.at[group, slot], (self.dp, self.down)
        return self.remote(kind, group, plane, src, dst, device)

    def from_above(self, group, plane):
        slot = jnp.where(plane == self.mp, self.n_mp, plane)
        return slot, self.remote(
            R_DOWN, group, plane, self.mine(group, plane, self.here), self.z_in.at[group, slot], (self.dp, self.down)
        )

    def offer(self, o, group, plane):
        if isinstance(o, int):
            if o >= RING:
                pl.semaphore_wait(self.credit, 1)
        else:

            @pl.when(o >= RING)
            def _():
                pl.semaphore_wait(self.credit, 1)

        self.pair(o, group, plane).start()

    def add_pair(self, o, group, plane):
        self.pair(o, group, plane).wait_recv()
        self.blocks[group, plane, :, self.core] = self.blocks[group, plane, :, self.core] + self.pair_in[o % RING]

        @pl.when(o < self.units - RING)
        def _():
            pl.semaphore_signal(self.credit, inc=1, device_id=(self.sib, self.mp), device_id_type=MESH)

        self.message(R_D0, group, plane).start()
        self.message(R_D1, group, plane).start()

    def add_halves(self, group, plane):
        for kind, place, part, slot in ((R_D0, self.at_y, self.low, 0), (R_D1, self.at_x, self.high, 1)):
            self.message(kind, group, plane).wait_recv()
            where = self.mine(group, plane, place, part)
            where[...] = where[...] + self.halves_in[group, plane, slot]
        self.message(R_X, group, plane).start()
        self.message(R_Y, group, plane).start()

    def add_plane(self, group, plane):
        f32, mp, last = jnp.float32, self.mp, self.n_mp - 1
        self.message(R_X, group, plane).wait_recv()
        self.message(R_Y, group, plane).wait_recv()
        where = self.mine(group, plane, self.here)
        total = (
            where[...].astype(f32) + self.x_in[group, plane].astype(f32) + self.y_in[group, plane].astype(f32)
        )

        @pl.when(plane == mp)
        def _():
            self.out[(group + 2) % 3] = total

        @pl.when(plane != mp)
        def _():
            where[...] = total.astype(jnp.bfloat16)

        @pl.when((plane > mp) & (mp == 0))
        def _():
            self.message(R_UP, group, plane).start()

        @pl.when((plane < mp) & (mp == last))
        def _():
            self.message(R_DOWN, group, plane).start()

    def add_along(self, group, plane):
        f32, mp, last = jnp.float32, self.mp, self.n_mp - 1
        where = self.mine(group, plane, self.here)

        def add():
            where[...] = (where[...].astype(f32) + self.z_in[group, plane].astype(f32)).astype(jnp.bfloat16)

        @pl.when((plane > mp) & (mp > 0))
        def _():
            self.message(R_UP, group, plane).wait_recv()
            add()
            self.message(R_UP, group, plane).start()

        @pl.when((plane < mp) & (mp < last))
        def _():
            self.from_above(group, plane)[1].wait_recv()
            add()
            self.message(R_DOWN, group, plane).start()

        @pl.when((plane == mp) & (mp > 0))
        def _():
            self.message(R_UP, group, plane).wait_recv()
            self.out[(group + 2) % 3] += self.z_in[group, plane].astype(f32)

        @pl.when((plane == mp) & (mp < last))
        def _():
            slot, copy = self.from_above(group, plane)
            copy.wait_recv()
            self.out[(group + 2) % 3] += self.z_in[group, slot].astype(f32)

    def slot(self, k):
        def do(action, j):
            if isinstance(j, int):
                if 0 <= j < self.units:
                    action(*self.unit(j))
                return

            @pl.when(j >= 0)
            def _():
                action(*self.unit(j))

        do(self.add_halves, k)
        do(self.add_plane, k - 1)
        do(self.add_along, k - 2)

    def finish(self):
        def body(t, _):
            group, plane = t // self.n_mp, t % self.n_mp
            self.pair(0, group, plane).wait_send()
            for kind in (R_D0, R_D1, R_X, R_Y):
                self.message(kind, group, plane).wait_send()

            @pl.when(plane > self.mp)
            def _():
                self.message(R_UP, group, plane).wait_send()

            @pl.when(plane < self.mp)
            def _():
                self.message(R_DOWN, group, plane).wait_send()

            return 0

        lax.fori_loop(0, self.units, body, 0)

LANES = 128
NN = (((1,), (0,)), ((), ()))
NT = (((1,), (1,)), ((), ()))
BIG = 2.0**36


def mm(left, right, dims=NN):
    return lax.dot_general(left, right, dims, preferred_element_type=jnp.float32)


def gelu_parts(t):
    k = 1.0 / (1.0 + 0.2316419 * jnp.abs(t))
    series = k * (
        0.319381530 + k * (-0.356563782 + k * (1.781477937 + k * (-1.821255978 + k * 1.330274429)))
    )
    density = 0.3989422804014327 * jnp.exp(-0.5 * t * t)
    tail = density * series
    phi = jnp.where(t >= 0.0, 1.0 - tail, tail)
    return t * phi, phi + t * density


def row_stats(x):
    width = x.shape[1]
    center = x - jnp.sum(x, axis=1, keepdims=True) * (1.0 / width)
    spread = jnp.sum(center * center, axis=1, keepdims=True) * (1.0 / width)
    inverse = lax.rsqrt(spread + norm_eps)
    return center * inverse, inverse


def image_ends(counts_ref, set_index, slots):
    lane = lax.broadcasted_iota(jnp.int32, (8, LANES), 1) % (LANES // 2)
    low = jnp.zeros((8, LANES), jnp.int32)
    high = jnp.zeros((8, LANES), jnp.int32)
    edge = jnp.int32(0)
    for slot in range(slots + 1):
        after = jnp.int32(1 << 20) if slot == slots else edge + counts_ref[set_index, slot]
        low = jnp.where(lane == slot, edge, low)
        high = jnp.where(lane == slot, after, high)
        edge = after if slot < slots else edge
    return low[0:1], high[0:1], edge


def own_row(hidden_half, tile):
    lane = lax.broadcasted_iota(jnp.int32, tile.shape, 1)
    return (lane < LANES // 2) if hidden_half == 0 else (lane >= LANES // 2)


def keep_half(half, tile, other):
    return jnp.where(own_row(half, tile), tile, other)


HEAD_TILES = ((0, 128, 256, 0, 0), (0, 128, 256, 1, 1), (512, 640, 640, 0, 1))
MIX = 384


def make_features(counts_ref, set_index, slots, set_rows, feat_q, feat_k):
    low, high, total = image_ends(counts_ref, set_index, slots)
    step = 256

    def body(i, _):
        at = pl.ds(pl.multiple_of(i * step, step), step)
        row = lax.broadcasted_iota(jnp.int32, (step, LANES), 0) + i * step
        same = (row >= low) & (row < high)
        lane = lax.broadcasted_iota(jnp.int32, (step, LANES), 1) % (LANES // 2)
        feat_k[at] = jnp.where(same, 1.0, 0.0).astype(jnp.bfloat16)
        feat_q[at] = jnp.where(same | (lane > slots), 0.0, -BIG).astype(jnp.bfloat16)
        return 0

    lax.fori_loop(0, set_rows // step, body, 0)
    return total


def attend(m, qkv, mixed, feat_q, feat_k, window_start, window, step):
    keys, values = [], []
    for q_at, k_at, v_at, half, v_half in HEAD_TILES:
        keys.append(keep_half(half, qkv[m, :, k_at : k_at + LANES], feat_k[...]))
        tile = qkv[m, :, v_at : v_at + LANES]
        values.append(keep_half(v_half, tile, jnp.ones_like(tile)))

    def block(i, _):
        at = pl.ds(pl.multiple_of(window_start + i * step, LANES // 2), step)
        outs = []
        for head, (q_at, k_at, v_at, half, v_half) in enumerate(HEAD_TILES):
            query = keep_half(half, qkv[m, at, q_at : q_at + LANES], feat_q[at])
            scores = mm(query, keys[head], NT)
            top = jnp.max(scores, axis=1, keepdims=True)
            weights = jnp.exp((scores - top) * HD ** (-0.5)).astype(jnp.bfloat16)
            out = mm(weights, values[head])
            outs.append(out / pltpu.roll(out, LANES // 2, 1))
        here = pl.ds(pl.multiple_of(i * step, LANES // 2), step)
        low = jnp.bfloat16
        mixed[m, here, 0:LANES] = keep_half(0, outs[0], outs[1]).astype(low)
        mixed[m, here, LANES : 2 * LANES] = keep_half(1, outs[2], jnp.zeros_like(outs[2])).astype(low)
        return 0

    lax.fori_loop(0, window // step, block, 0)


TN = (((0,), (0,)), ((), ()))


def norm_grad(x, gain, grad):
    width = x.shape[1]
    unit, inverse = row_stats(x)
    e = grad * gain
    mean_e = jnp.sum(e, axis=1, keepdims=True) * (1.0 / width)
    mean_eu = jnp.sum(e * unit, axis=1, keepdims=True) * (1.0 / width)
    return inverse * (e - mean_e - unit * mean_eu), grad * unit


def attend_back(m, qkv, d_mixed, feat_q, feat_k, window_start, window, acc, d_query):
    band = 3 * LANES
    acc[...] = jnp.zeros_like(acc)
    low = jnp.bfloat16
    scale = HD ** (-0.5)

    def block(b, _):
        start = jnp.clip(b - 1, 0, window // LANES - 3) * LANES
        keys_at = pl.ds(pl.multiple_of(start, LANES), band)
        keys_in = pl.ds(pl.multiple_of(window_start + start, LANES), band)
        here = pl.ds(pl.multiple_of(b * LANES, LANES), LANES)
        rows_in = pl.ds(pl.multiple_of(window_start + b * LANES, LANES), LANES)
        f_q, f_k = feat_q[rows_in], feat_k[keys_in]
        got = []
        for head, (q_at, k_at, v_at, half, v_half) in enumerate(HEAD_TILES):
            q_tile = qkv[m, rows_in, q_at : q_at + LANES]
            k_tile = qkv[m, keys_in, k_at : k_at + LANES]
            v_tile = qkv[m, keys_in, v_at : v_at + LANES]
            mix_at = 0 if head < 2 else LANES
            d_tile = d_mixed[here, mix_at : mix_at + LANES]
            d_out = keep_half(v_half, d_tile, jnp.zeros_like(d_tile))
            scores = mm(keep_half(half, k_tile, f_k), keep_half(half, q_tile, f_q), NT)
            top = jnp.max(scores, axis=0, keepdims=True)
            weights = jnp.exp((scores - top) * scale)
            weights = weights * (1.0 / jnp.sum(weights, axis=0, keepdims=True))
            d_weights = mm(v_tile, d_out, NT)
            delta = jnp.sum(d_weights * weights, axis=0, keepdims=True)
            d_scores = (weights * (d_weights - delta)).astype(low)
            d_key = mm(d_scores, keep_half(half, q_tile * scale, jnp.zeros_like(q_tile)))
            d_value = mm(weights.astype(low), d_out)
            d_q = mm(d_scores, keep_half(half, k_tile * scale, jnp.zeros_like(k_tile)), TN)
            got.append((d_q, d_key, d_value))
        acc[keys_at, 0:LANES] += got[0][1] + got[1][1]
        acc[keys_at, LANES : 2 * LANES] += got[0][2] + got[1][2]
        acc[keys_at, 2 * LANES : 3 * LANES] += got[2][1] + got[2][2]
        d_query[here, 0:LANES] = (got[0][0] + got[1][0]).astype(low)
        d_query[here, LANES : 2 * LANES] = got[2][0].astype(low)
        return 0

    lax.fori_loop(0, window // LANES, block, 0)

def tile_rows(i, first=0):
    return pl.ds(pl.multiple_of(first + i * LANES, LANES), LANES)


def column_sum(v):
    return jnp.sum(v, axis=0, keepdims=True)


class Place:
    def __init__(self, set_rows, own_rows):
        self.set_rows, self.own_rows, self.window = set_rows, own_rows, own_rows + HALO
        mp = lax.axis_index("mp")
        per_set = set_rows // own_rows
        self.set_index, part = mp // per_set, mp % per_set
        self.window_start = pl.multiple_of(part * (set_rows - self.window), LANES)
        self.own_start = pl.multiple_of(part * (self.window - own_rows), LANES)
        self.own = pl.ds(self.own_start, own_rows)
        self.own_set = pl.ds(pl.multiple_of(self.window_start + self.own_start, LANES), own_rows)
        self.tiles = self.window // LANES

    def is_own(self, i):
        first = i * LANES
        return jnp.where((first >= self.own_start) & (first < self.own_start + self.own_rows), 1.0, 0.0)

    def valid(self, i, total):
        row = lax.broadcasted_iota(jnp.int32, (LANES, 1), 0) + (self.window_start + i * LANES)
        return jnp.where(row < total, 1.0, 0.0)


def pack_first(qkv, out, packed):
    out_t = out[...].T
    for i in range(3):
        packed[:, i * LANES : (i + 1) * LANES] = qkv[i, :, 0:LANES]
    packed[:, MIX : MIX + LANES] = out_t[:, 0:LANES]
    tails = [qkv[i, :, LANES:] for i in range(3)]
    packed[:, 512:640] = jnp.concatenate([tails[0], out_t[:, LANES:]], axis=1)
    packed[:, 640:768] = jnp.concatenate([tails[1], tails[2]], axis=1)


def pack_lanes(qkv_rows, out_row):
    heads = [row[:, 0:LANES] for row in (*qkv_rows, out_row)]
    q, k, v, o = [row[:, LANES:] for row in (*qkv_rows, out_row)]
    return jnp.concatenate([*heads, q, o, k, v], axis=1)


def unpack_lanes(row):
    at = ((0, 512), (128, 640), (256, 704), (MIX, 576))
    return [jnp.concatenate([row[:, a : a + LANES], row[:, b : b + LANES // 2]], axis=1) for a, b in at]


def pack_biases(biases, packed, n_mp, width):
    f32 = jnp.float32
    share = width // n_mp
    zero = jnp.zeros((1, share), f32)
    for m in range(n_mp):
        part = [biases[r : r + 1, m * share : (m + 1) * share] for r in (0, 1)]
        packed[m : m + 1] = pack_lanes((part[0], zero, part[1]), zero)
    fan = width // share
    source = lax.broadcasted_iota(jnp.int32, (share, width), 0) * fan
    target = lax.broadcasted_iota(jnp.int32, (share, width), 1)
    total = jnp.zeros((n_mp, width), f32)
    for r in range(fan):
        rows = jnp.concatenate(
            [biases[2 + r : 3 + r, m * share : (m + 1) * share] for m in range(n_mp)], axis=0
        )
        move = jnp.where(target == source + r, 1.0, 0.0)
        total = total + lax.dot_general(rows, move, NN, precision=EXACT, preferred_element_type=f32)
    packed[n_mp : 2 * n_mp] = total

DECAY = 1.0 - STEP ** (-0.8)
EXACT = lax.Precision.HIGHEST
SUB_QKV, SUB_OUT, SUB_UP, SUB_DOWN = range(4)


class Exchange:
    def __init__(self, axis, size, bufs, send_sems, recv_sems):
        self.axis, self.size, self.bufs = axis, size, bufs
        self.send_sems, self.recv_sems = send_sems, recv_sems
        self.me = lax.axis_index(axis)

    def copy(self, away):
        peer = (self.me + away) % self.size
        return pltpu.make_async_remote_copy(
            src_ref=self.bufs.at[0],
            dst_ref=self.bufs.at[away],
            send_sem=self.send_sems.at[away],
            recv_sem=self.recv_sems.at[away],
            device_id={self.axis: peer},
            device_id_type=MESH,
        )

    def send(self, value):
        self.bufs[0] = value
        for away in range(1, self.size):
            self.copy(away).start()

    def total(self):
        for away in range(1, self.size):
            self.copy(away).wait_recv()
        total = jnp.zeros(self.bufs.shape[1:], jnp.float32)
        for index in range(self.size):
            away = (self.me - index + self.size) % self.size
            total = total + self.bufs[away]
        return total

    def wait_sends(self):
        for away in range(1, self.size):
            self.copy(away).wait_send()


class Doubling:
    def __init__(self, value, bufs, send_sems, recv_sems):
        self.value, self.bufs, self.send_sems, self.recv_sems = value, bufs, send_sems, recv_sems
        dp, mp = lax.axis_index("dp"), lax.axis_index("mp")
        sib, xn, yn, _ = neighbours(dp)
        self.peers = (
            {"dp": sib}, {"dp": xn}, {"dp": yn}, {"mp": mp + 1 - 2 * (mp % 2)}, {"mp": (mp + 2) % 4}
        )

    def copy(self, i):
        return pltpu.make_async_remote_copy(
            src_ref=self.value.at[i],
            dst_ref=self.bufs.at[i],
            send_sem=self.send_sems.at[i],
            recv_sem=self.recv_sems.at[i],
            device_id=self.peers[i],
            device_id_type=MESH,
        )

    def send(self, i):
        self.copy(i).start()

    def add(self, i):
        self.copy(i).wait_recv()
        self.value[i + 1] = self.value[i] + self.bufs[i]

    def finish(self):
        for i in range(5):
            self.copy(i).wait_send()


def lane_sums(mask, squares):
    return lax.dot_general(mask, squares, NT, precision=EXACT, preferred_element_type=jnp.float32)


def o_lanes(width):
    lane = lax.broadcasted_iota(jnp.int32, (1, width), 1)
    return jnp.where(((lane >= MIX) & (lane < MIX + 128)) | ((lane >= 576) & (lane < 640)), 1.0, 0.0)


def masks_of(width, scale_rows):
    row = lax.broadcasted_iota(jnp.int32, (8, width), 0)
    is_o = o_lanes(width)
    if not isinstance(scale_rows, list):
        scale_rows = [scale_rows[i : i + 1] for i in range(3)]
    up = jnp.where(row == SUB_UP, scale_rows[0], 0.0)
    down = jnp.where(row == SUB_DOWN, scale_rows[1], 0.0)
    first = scale_rows[2]
    mixed = jnp.where(row == SUB_QKV, first * (1.0 - is_o), jnp.where(row == SUB_OUT, first * is_o, 0.0))
    return up, down, mixed


class Factors:
    def __init__(self, reduced, sub_prior, lane_prior, n_dp, swaps):
        self.reduced, self.sub_prior, self.lane_prior = reduced, sub_prior, lane_prior
        self.rows, self.width = reduced.shape[1:]
        self.whole = float(self.rows * n_dp)
        self.early_mp, self.early_dp, self.late_mp, self.late_dp, self.last_mp, self.last_dp = swaps
        self.shares = jnp.zeros((8, self.rows), jnp.float32)
        self.totals = jnp.zeros((8, 1), jnp.float32)

    def send(self, groups, along_mp, along_dp):
        masks = masks_of(self.width, jnp.ones((3, self.width), jnp.float32))
        rows = jnp.zeros((8, self.rows), jnp.float32)
        columns = []
        for group in groups:
            squares = self.reduced[group] * self.reduced[group]
            columns.append(column_sum(squares))
            rows = rows + lane_sums(masks[group], squares)
        along_dp.send(columns[0] if len(columns) == 1 else jnp.concatenate(columns, axis=0))
        along_mp.send(jnp.concatenate([rows, jnp.zeros((8, LANES - self.rows), jnp.float32)], axis=1))
        self.totals = self.totals + jnp.sum(rows, axis=1, keepdims=True)

    def collect(self, groups, along_mp, along_dp, sub_out, lane_out):
        rows, columns = along_mp.total(), along_dp.total()
        row8 = lax.broadcasted_iota(jnp.int32, (8, LANES), 0)
        count = self.whole * jnp.where(row8 == SUB_QKV, 3.0, jnp.where(row8 == SUB_OUT, 1.0, 4.0))
        sub_new = DECAY * self.sub_prior[...] + (1.0 - DECAY) * (rows / count + square_eps)
        mine = (row8 == SUB_UP) | (row8 == SUB_DOWN)
        if 2 in groups:
            mine = (row8 == SUB_QKV) | (row8 == SUB_OUT)
        sub_out[...] = jnp.where(mine, sub_new, sub_out[...])
        scale_rows = []
        for i, group in enumerate(groups):
            new = DECAY * self.lane_prior[group : group + 1] + (1.0 - DECAY) * (
                columns[i : i + 1] / self.whole + square_eps
            )
            lane_out[group : group + 1] = new
            scale_rows.append(1.0 / new)
        if len(scale_rows) == 1:
            scale_rows = [scale_rows[0]] * 3
        masks = masks_of(self.width, scale_rows + scale_rows[:1])
        shares = jnp.zeros((8, self.rows), jnp.float32)
        for group in groups:
            shares = shares + lane_sums(masks[group], self.reduced[group] * self.reduced[group])
        self.shares = self.shares + jnp.where(mine[:, 0 : self.rows], shares / sub_new[:, 0 : self.rows], 0.0)

    def finish(self, masters, scalar_out):
        f32 = jnp.float32
        masks = masks_of(self.width, jnp.ones((3, self.width), f32))
        weights = jnp.zeros((8, 1), f32)
        for group in range(GROUPS):
            by_lane = column_sum(masters[group] * masters[group])
            weights = weights + jnp.sum(masks[group] * by_lane, axis=1, keepdims=True)
        row1 = lax.broadcasted_iota(jnp.int32, (8, 1), 0)
        lane8 = lax.broadcasted_iota(jnp.int32, (8, LANES), 1)
        sub = jnp.sum(jnp.where(lane8 < self.rows, self.sub_prior[...], 0.0), axis=1, keepdims=True)
        out = jnp.sum(self.lane_prior[2:3] * o_lanes(self.width), axis=1, keepdims=True)
        down = jnp.sum(self.lane_prior[1:2], axis=1, keepdims=True)
        prior = jnp.where(row1 == SUB_OUT, out, jnp.where(row1 == SUB_DOWN, down, sub))
        shares = jnp.sum(self.shares, axis=1, keepdims=True)
        value = jnp.where(
            lane8 == 0, shares, jnp.where(lane8 == 1, weights, jnp.where(lane8 == 2, self.totals, prior))
        )
        self.last_mp.send(value)
        self.last_dp.send(self.last_mp.total())
        scalar_out[...] = self.last_dp.total()

    def wait_sends(self):
        for swap in (self.early_mp, self.early_dp, self.late_mp, self.late_dp, self.last_mp, self.last_dp):
            swap.wait_sends()


def update_kernel(
    n_dp, n_mp, reduced, masters, sub_new, lane_new, scalars, sums, vec, bias, vec_moment, bias_moment, input_in, stream_in,
    stream_out, input_out, qkv_g, out_g, up_g, down_g, qkv_a, out_a, up_a, down_a, qkv_b, out_b, up_b, down_b,
    qkvrows, qkvcols, outrows, outcols, uprows, upcols, downrows, downcols,
    vec_g, bias_g, vec_m, bias_m, vec_a, bias_a, update_scale, token_spread, held, sems,
):
    f32 = jnp.float32
    groups, rows, width = reduced.shape
    load = pltpu.make_async_copy(stream_in, held, sems.at[0])
    load.start()
    span = input_in.shape[2]
    for i in range(n_mp):
        input_out[:, i * span : (i + 1) * span] = input_in[i].astype(f32)
    load.wait()
    store = pltpu.make_async_copy(held, stream_out, sems.at[1])
    store.start()
    whole = float(rows * n_dp)
    entries = (3.0 * whole * whole, whole * whole, 4.0 * whole * whole, 4.0 * whole * whole)
    row1 = lax.broadcasted_iota(jnp.int32, (8, 1), 0)
    size = jnp.where(row1 == 0, entries[0], jnp.where(row1 == 1, entries[1], entries[2]))
    copies = jnp.where((row1 == SUB_QKV) | (row1 == SUB_UP), float(n_mp), float(n_dp))
    length = jnp.where(row1 == SUB_DOWN, 4.0 * whole, whole)
    mean_rows = DECAY * scalars[:, 3:4] / (copies * length) + (1.0 - DECAY) * (scalars[:, 2:3] / size + square_eps)
    scale = jnp.sqrt(scalars[:, 0:1] * mean_rows / size)
    rms = jnp.sqrt(scalars[:, 1:2] / size)
    rate = step_rate * rms / jnp.maximum(1.0, scale / clip_limit)
    sub = lax.dot_general(
        jnp.where(
            lax.broadcasted_iota(jnp.int32, (rows, LANES), 0) == lax.broadcasted_iota(jnp.int32, (rows, LANES), 1), 1.0, 0.0
        ),
        sub_new[...], NT, precision=EXACT, preferred_element_type=f32,
    )
    is_o = o_lanes(width)

    def renewed(group, index):
        gradient = reduced[group]
        product = sub[:, index : index + 1] * lane_new[group : group + 1] / mean_rows[index : index + 1]
        return masters[group] - rate[index : index + 1] * (gradient * lax.rsqrt(product))

    def spread(value, qkv, out):
        q, k, v, o = unpack_lanes(value)
        for i, part in enumerate((q, k, v)):
            qkv[i] = part.astype(qkv.dtype)
        out[...] = o.T.astype(out.dtype)

    first = jnp.where(is_o > 0.0, renewed(2, 1), renewed(2, 0))
    spread(reduced[2], qkv_g, out_g)
    spread(first, qkv_a, out_a)
    spread(first, qkv_b, out_b)
    for group, index, grad, after, short in ((0, 2, up_g, up_a, up_b), (1, 3, down_g, down_a, down_b)):
        new = renewed(group, index)
        grad[...] = reduced[group]
        after[...] = new
        short[...] = new.astype(short.dtype)

    def plain(weight, gradient, moment_old, together):
        moment = DECAY * moment_old + (1.0 - DECAY) * (gradient * gradient + square_eps)
        update = gradient * lax.rsqrt(moment)
        update_mean = jnp.mean(update * update, axis=1, keepdims=True)
        weight_mean = jnp.mean(weight * weight, axis=1, keepdims=True)
        if together is not None:
            row = lax.broadcasted_iota(jnp.int32, update_mean.shape, 0)
            number = float(weight.shape[0] - together)

            def join(mean):
                shared = jnp.sum(jnp.where(row >= together, mean, 0.0), axis=0, keepdims=True) / number
                return jnp.where(row >= together, shared, mean)

            update_mean, weight_mean = join(update_mean), join(weight_mean)
        rate_here = step_rate * jnp.sqrt(weight_mean)
        return weight - rate_here * update / jnp.maximum(1.0, jnp.sqrt(update_mean) / clip_limit), moment

    vec_g[...] = sums[0:8]
    bias_g[...] = sums[8:14]
    vec_a[...], vec_m[...] = plain(vec[...], sums[0:8], vec_moment[...], None)
    bias_a[...], bias_m[...] = plain(bias[...], sums[8:14], bias_moment[...], 2)
    spreads = jnp.sqrt(sums[14:15, 0:LANES] / (sums[14:15, 3:4] * width))
    scales = jnp.zeros((1, LANES), f32)
    lane1 = lax.broadcasted_iota(jnp.int32, (1, LANES), 1)
    for i in range(4):
        scales = scales + jnp.where(lane1 == i, scale[i : i + 1], 0.0)
    update_scale[...] = scales[:, 0:4].reshape(4)
    token_spread[...] = spreads[:, 0:3].reshape(3)
    for index, ref in ((SUB_QKV, qkvrows), (SUB_OUT, outcols), (SUB_UP, uprows), (SUB_DOWN, downcols)):
        ref[...] = sub_new[index, 0:rows]
    upcols[...] = lane_new[0]
    downrows[...] = lane_new[1]
    *cols, out_row = unpack_lanes(lane_new[2:3])
    for i in range(3):
        qkvcols[i : i + 1] = cols[i]
    outrows[...] = out_row.reshape(out_row.shape[1])
    store.wait()


def bias_rows_natural(qkv_sums, hidden_sums, n_mp, width):
    f32 = jnp.float32
    share = width // n_mp
    half = LANES // 2
    query = [qkv_sums[m : m + 1, a:b] for m in range(n_mp) for a, b in ((0, LANES), (512, 512 + half))]
    value = [qkv_sums[m : m + 1, a:b] for m in range(n_mp) for a, b in ((256, 256 + LANES), (704, 704 + half))]
    source = lax.broadcasted_iota(jnp.int32, (width, width), 0)
    target = lax.broadcasted_iota(jnp.int32, (1, width), 1)
    fan = width // share
    from_lane = target * fan
    for r in range(1, fan):
        from_lane = jnp.where(target >= r * share, (target - r * share) * fan + r, from_lane)
    move = jnp.where(source == from_lane, 1.0, 0.0).astype(jnp.bfloat16)
    moved = jnp.zeros_like(hidden_sums)
    left = hidden_sums
    for _ in range(3):
        part = left.astype(jnp.bfloat16)
        moved = moved + mm(part, move)
        left = left - part.astype(f32)
    rows = [jnp.concatenate(query, axis=1), jnp.concatenate(value, axis=1)]
    for r in range(width // share):
        rows.append(
            jnp.concatenate([moved[m : m + 1, r * share : (r + 1) * share] for m in range(n_mp)], axis=1)
        )
    return rows

class Stream:
    CUTS = 4

    def __init__(self, n_mp, src, out, send_sems, recv_sems):
        self.dp, self.mp, self.n_mp = lax.axis_index("dp"), lax.axis_index("mp"), n_mp
        self.src, self.out, self.send_sems, self.recv_sems = src, out, send_sems, recv_sems
        self.rows = out.shape[1] // self.CUTS
        self.up, self.down = jnp.minimum(self.mp + 1, n_mp - 1), jnp.maximum(self.mp - 1, 0)

    def message(self, plane, cut, way, own):
        part = pl.ds(pl.multiple_of(cut * self.rows, self.rows), self.rows)
        where = self.out.at[plane, part]
        return pltpu.make_async_remote_copy(
            src_ref=self.src.at[part] if own else where,
            dst_ref=where,
            send_sem=self.send_sems.at[way, plane, cut],
            recv_sem=self.recv_sems.at[plane, cut],
            device_id=(self.dp, self.down if way else self.up),
            device_id_type=MESH,
        )

    def step(self, s):
        distance, cut = s // self.CUTS, s % self.CUTS
        mp, last = self.mp, self.n_mp - 1

        @pl.when((distance == 0) & (mp < last))
        def _():
            self.message(mp, cut, 0, True).start()

        @pl.when((distance == 0) & (mp > 0))
        def _():
            self.message(mp, cut, 1, True).start()

        below, above = mp - distance, mp + distance

        @pl.when((distance > 0) & (below >= 0))
        def _():
            self.message(below, cut, 0, False).wait_recv()

            @pl.when(mp < last)
            def _():
                self.message(below, cut, 0, False).start()

        @pl.when((distance > 0) & (above <= last))
        def _():
            self.message(above, cut, 1, False).wait_recv()

            @pl.when(mp > 0)
            def _():
                self.message(above, cut, 1, False).start()

    STEPS = 16

    def finish(self):
        mp, last = self.mp, self.n_mp - 1

        def body(t, _):
            plane, cut = t // self.CUTS, t % self.CUTS

            @pl.when((plane <= mp) & (mp < last))
            def _():
                self.message(plane, cut, 0, False).wait_send()

            @pl.when((plane >= mp) & (mp > 0))
            def _():
                self.message(plane, cut, 1, False).wait_send()

            return 0

        lax.fori_loop(0, self.n_mp * self.CUTS, body, 0)

def layer_kernel(
    n_dp, n_mp, slots, own_rows, tokens_in, cot_in, w_qkv, w_out, w_up, w_down_t, counts, vec, biases, *rest
):
    (
        qkvrows, qkvcols, outrows, outcols, uprows, upcols, downrows, downcols,
        masters, reduced, sums_out, sub_out, lane_out, scalar_out, input_out, stream_out,
        w, tokens, cot, qkv, active, slope, mixed, proj, normed_two, normed_t, normed_two_t, turned_t, branch, d_branch, d_two,
        result, feat_q, feat_k, d_mixed, acc, d_query, bias, sums, sums_qkv, sub_prior, lane_prior,
        pair_in, halves_in, x_in, y_in, z_in, value, swap_in, early_mp, early_dp, late_mp, late_dp, last_mp, last_dp,
        credit, local_sems, g_send, g_recv, g_way, s_send, s_recv, stream_send, stream_recv, turn_send, turn_recv,
        swap_send, swap_recv, small_send, small_recv,
    ) = rest
    set_rows, width = tokens.shape
    place = Place(set_rows, own_rows)
    window, own, own_start, window_start, tiles = (
        place.window, place.own, place.own_start, place.window_start, place.tiles
    )
    low, f32 = jnp.bfloat16, jnp.float32
    dp, mp = lax.axis_index("dp"), lax.axis_index("mp")
    in_set = pl.ds(pl.multiple_of(place.set_index * set_rows, LANES), set_rows)
    token_copy = pltpu.make_async_copy(tokens_in.at[in_set], tokens, local_sems.at[0])
    in_window = pl.ds(pl.multiple_of(place.set_index * set_rows + window_start, LANES), window)
    cot_copy = pltpu.make_async_copy(cot_in.at[in_window], cot, local_sems.at[1])
    token_copy.start()
    cot_copy.start()
    net = Gather(n_mp, w, g_send, g_recv, g_way)
    back = Scatter(n_mp, w, reduced, (pair_in, halves_in, x_in, y_in, z_in), credit, s_send, s_recv)
    stream = Stream(n_mp, result, stream_out, stream_send, stream_recv)
    swaps = Doubling(value, swap_in, swap_send, swap_recv)
    exchanges = [
        Exchange(axis, size, buf, small_send.at[i], small_recv.at[i])
        for i, (axis, size, buf) in enumerate(
            (
                ("mp", n_mp, early_mp), ("dp", n_dp, early_dp), ("mp", n_mp, late_mp), ("dp", n_dp, late_dp),
                ("mp", n_mp, last_mp), ("dp", n_dp, last_dp),
            )
        )
    ]
    masters[0] = w_up[...]
    masters[1] = w_down_t[...]
    pack_first(w_qkv, w_out, masters.at[2])
    for group, source in enumerate((2, 0, 1)):
        w[group, mp, dp // 2, dp % 2] = masters[source].astype(low)
    greet(
        [((dp + away) % n_dp, mp) for away in range(1, n_dp)] + [(dp, (mp + away) % n_mp) for away in range(1, n_mp)], []
    )
    net.begin()

    def weight(group, m, lanes=None):
        block = w[group, m] if lanes is None else w[group, m, :, :, :, lanes]
        return block.reshape(width, block.shape[-1])

    pack_biases(biases, bias, n_mp, width)
    total = make_features(counts, place.set_index, slots, set_rows, feat_q, feat_k)
    token_copy.wait()
    zero_row = jnp.zeros((1, width), f32)
    normed = slope

    def norm_one(i, _):
        unit, _inv = row_stats(tokens[tile_rows(i)].astype(f32))
        per_half = own_rows // LANES
        normed[i // per_half, tile_rows(i % per_half)] = (unit * vec[0:1] + vec[1:2]).astype(low)
        return 0

    lax.fori_loop(0, set_rows // LANES, norm_one, 0)
    net.step(0)
    cot_copy.wait()

    def back_of(i):
        return cot[tile_rows(i)].astype(f32) * place.valid(i, total)

    def first_grad(i, total_row):
        db = (back_of(i) * vec[5:6]).astype(low)
        d_branch[tile_rows(i)] = db
        return total_row + place.is_own(i) * column_sum(db.astype(f32))

    branch_sum = lax.fori_loop(0, tiles, first_grad, zero_row)
    turned_t[...] = d_branch[own].T
    net.step(1)
    normed_t[...] = normed[mp % 2, 0:own_rows].T

    def project(u, _):
        net.step(u + 2)
        net.stage_d(u)
        m = net.plane(u)
        for half in range(set_rows // own_rows):
            at = pl.ds(half * own_rows, own_rows)
            qkv[m, at] = (mm(normed[half, 0:own_rows], weight(0, m)) + bias[pl.ds(m, 1)]).astype(low)
        attend(m, qkv, mixed, feat_q, feat_k, window_start, window, window // 2)
        return 0

    project(0, 0)
    lax.fori_loop(1, n_mp, project, 0)
    net.step(n_mp + 2)
    proj[...] = sum((mm(mixed[m], weight(0, m, pl.ds(MIX, 2 * LANES)), NT) for m in range(n_mp)), vec[6:7])

    def middle_of(i):
        return tokens[tile_rows(i, window_start)].astype(f32) + vec[4:5] * proj[tile_rows(i)]

    def norm_two(i, _):
        unit, _inv = row_stats(middle_of(i))
        normed_two[tile_rows(i)] = (unit * vec[2:3] + vec[3:4]).astype(low)
        return 0

    lax.fori_loop(0, tiles, norm_two, 0)
    normed_two_t[...] = normed_two[own].T

    def feed_up(u, _):
        net.stage_d(u + n_mp)
        m = net.plane(u)

        def rows(i, _):
            at = tile_rows(i)
            hidden = mm(normed_two[at], weight(1, m)) + bias[pl.ds(n_mp + m, 1)]
            act, slp = gelu_parts(hidden)
            slope[m, at] = slp.astype(low)

            @pl.when((i * LANES >= own_start) & (i * LANES < own_start + own_rows))
            def _():
                active[m, tile_rows(i - own_start // LANES)] = act.astype(low)

            return 0

        lax.fori_loop(0, tiles, rows, 0)
        net.step(u + 3 + n_mp)
        return 0

    lax.fori_loop(0, n_mp, feed_up, 0)
    half_shape = (n_dp // 2, 2, width // n_dp)

    def keep(group, m, lanes, block):
        w[group, m, :, :, :, lanes] = block.astype(low).reshape(*half_shape, block.shape[1])

    def feed_down(u, _):
        net.stage_d(u + 2 * n_mp)
        m = net.plane(u)
        part_sum = mm(active[m], weight(2, m), NT)

        @pl.when(u == 0)
        def _():
            branch[...] = part_sum

        @pl.when(u > 0)
        def _():
            branch[...] += part_sum

        def rows(i, total_row):
            at = tile_rows(i)
            dh = (mm(d_branch[at], weight(2, m)) * slope[m, at].astype(f32)).astype(low)
            slope[m, at] = dh
            return total_row + place.is_own(i) * column_sum(dh.astype(f32))

        sums[pl.ds(8 + m, 1)] = lax.fori_loop(0, tiles, rows, zero_row)
        two_sum = mm(slope[m], weight(1, m), NT)

        @pl.when(u == 0)
        def _():
            d_two[...] = two_sum

        @pl.when(u > 0)
        def _():
            d_two[...] += two_sum

        net.step(u + 3 + 2 * n_mp)

        @pl.when(u > 0)
        def _():
            for o in (2 * u - 2, 2 * u - 1):
                back.add_pair(o, *back.offered(o))

        net.finish(u + n_mp)
        net.finish(u + 2 * n_mp)
        everything = pl.ds(0, width)
        keep(2, m, everything, mm(turned_t[...], active[m]))
        back.offer(2 * u, 2, m)
        keep(1, m, everything, mm(normed_two_t[...], slope[m, own]))
        back.offer(2 * u + 1, 1, m)
        return 0

    lax.fori_loop(0, n_mp, feed_down, 0)

    def final(i, carry):
        there = own_start // LANES + i
        br = branch[tile_rows(i)] + vec[7:8]
        scaled = vec[5:6] * br
        res = middle_of(there) + scaled
        result[tile_rows(i)] = res.astype(low)
        attn = vec[4:5] * proj[tile_rows(there)]
        valid = place.valid(there, total)
        new = [column_sum(valid * v * v) for v in (res, attn, scaled)] + [column_sum(back_of(there) * br)]
        return tuple(c + n for c, n in zip(carry, new))

    *squares, back_branch = lax.fori_loop(0, own_rows // LANES, final, (zero_row,) * 4)
    own_result = pltpu.make_async_copy(result, stream_out.at[mp], local_sems.at[2])
    own_result.start()
    for cut in range(stream.CUTS):
        stream.step(cut)
    fed = 2 * n_mp
    for o in (fed - 2, fed - 1):
        back.add_pair(o, *back.offered(o))

    d_proj, d_proj_t = d_branch, turned_t

    def norm_two_back(i, carry):
        at = tile_rows(i)
        grad = d_two[at]
        dv, grad_unit = norm_grad(middle_of(i), vec[2:3], grad)
        d_mid = back_of(i) + dv
        d_two[at] = d_mid
        d_out = (d_mid * vec[4:5]).astype(low)
        d_proj[at] = d_out
        mine = place.is_own(i)
        new = (grad_unit, grad, d_mid * proj[at], d_out.astype(f32))
        return tuple(c + mine * column_sum(n) for c, n in zip(carry, new))

    gain_two, shift_two, scale_sum, proj_sum = lax.fori_loop(0, tiles, norm_two_back, (zero_row,) * 4)
    d_proj_t[...] = d_proj[own].T
    for u in range(n_mp):
        net.finish(u)
    d_normed = branch
    d_qkv = normed_two.at[pl.ds(0, own_rows)]

    def slot(k):
        back.slot(k)
        stream.step(k + stream.CUTS)

    def attention(u, _):
        m = plane_at(mp, n_mp - 1 - u)

        @pl.when(u > 0)
        def _():
            back.add_pair(fed + u - 1, 0, plane_at(mp, n_mp - u))

        dm = mm(d_proj[...], weight(0, m, pl.ds(MIX, 2 * LANES))).astype(low)
        d_mixed[:, 0:LANES] = dm[:, 0:LANES]
        d_mixed[:, LANES:] = keep_half(1, dm[:, LANES:], jnp.zeros_like(dm[:, LANES:]))
        slot(2 * u)
        attend_back(m, qkv, d_mixed, feat_q, feat_k, window_start, window, acc, d_query)
        slot(2 * u + 1)
        d_qkv[:, 0:128] = d_query[own, 0:128]
        d_qkv[:, 128:256] = acc[own, 0:128].astype(low)
        d_qkv[:, 256:384] = acc[own, 128:256].astype(low)
        d_qkv[:, 384:512] = jnp.zeros((own_rows, LANES), low)
        d_qkv[:, 512:640] = d_query[own, 128:256]
        d_qkv[:, 640:768] = acc[own, 256:384].astype(low)
        sums_qkv[pl.ds(m, 1)] = column_sum(d_qkv[...].astype(f32))
        part_sum = mm(d_qkv[...], weight(0, m), NT)

        @pl.when(u == 0)
        def _():
            d_normed[...] = part_sum

        @pl.when(u > 0)
        def _():
            d_normed[...] += part_sum

        block = mm(normed_t[...], d_qkv[...])
        extra = mm(d_proj_t[...], mixed[m, own])
        keep(0, m, pl.ds(0, MIX), block[:, 0:MIX])
        keep(0, m, pl.ds(MIX, 2 * LANES), block[:, MIX : MIX + 2 * LANES] + extra)
        keep(0, m, pl.ds(MIX + 2 * LANES, LANES), block[:, MIX + 2 * LANES :])
        back.offer(fed + u, 0, m)
        return 0

    lax.fori_loop(0, n_mp, attention, 0)
    slot(fed)
    back.add_pair(back.units - 1, 0, mp)

    input_t = normed_t

    def norm_one_back(i, carry):
        grad = d_normed[tile_rows(i)]
        rows = tokens[tile_rows(own_start // LANES + i, window_start)].astype(f32)
        dv, grad_unit = norm_grad(rows, vec[0:1], grad)
        input_t[:, tile_rows(i)] = (d_two[tile_rows(i, own_start)] + dv).astype(low).T
        return tuple(c + column_sum(n) for c, n in zip(carry, (grad_unit, grad)))

    gain_one, shift_one = lax.fori_loop(0, own_rows // LANES, norm_one_back, (zero_row, zero_row))
    share = width // n_mp

    def turn(away):
        peer = (mp + away) % n_mp
        return pltpu.make_async_remote_copy(
            src_ref=input_t.at[pl.ds(pl.multiple_of(peer * share, HD), share)],
            dst_ref=input_out.at[mp],
            send_sem=turn_send.at[away],
            recv_sem=turn_recv.at[away],
            device_id={"mp": peer},
            device_id_type=MESH,
        )

    def turned(away):
        source = (mp - away + n_mp) % n_mp
        return pltpu.make_async_remote_copy(
            src_ref=input_t.at[pl.ds(0, share)],
            dst_ref=input_out.at[source],
            send_sem=turn_send.at[away],
            recv_sem=turn_recv.at[away],
            device_id={"mp": source},
            device_id_type=MESH,
        )

    for away in range(1, n_mp):
        turn(away).start()
    own_turn = pltpu.make_async_copy(
        input_t.at[pl.ds(pl.multiple_of(mp * share, HD), share)], input_out.at[mp], local_sems.at[3]
    )
    own_turn.start()
    slot(fed + 1)

    held = jnp.clip(total - (window_start + own_start), 0, own_rows).astype(f32)
    lane_w = lax.broadcasted_iota(jnp.int32, (1, width), 1)
    scalar_row = jnp.where(lane_w == 3, held, 0.0)
    for i in range(3):
        scalar_row = scalar_row + jnp.where(lane_w == i, jnp.sum(squares[i], axis=1, keepdims=True), 0.0)
    natural = bias_rows_natural(sums_qkv[0:n_mp], sums[8 : 8 + n_mp], n_mp, width)
    vector_rows = [gain_one, shift_one, gain_two, shift_two, scale_sum, back_branch, proj_sum, branch_sum]
    for i, row in enumerate(vector_rows + natural + [scalar_row, zero_row]):
        value[0, i : i + 1] = row
    swaps.send(0)
    rows_here = qkvrows.shape[0]
    sub_prior[...] = jnp.zeros_like(sub_prior)
    for i, prior in enumerate((qkvrows, outcols, uprows, downcols)):
        sub_prior[i : i + 1, 0:rows_here] = prior[...][None, :]
    lane_prior[0:1] = upcols[...][None, :]
    lane_prior[1:2] = downrows[...][None, :]
    lane_prior[2:3] = pack_lanes([qkvcols[i : i + 1] for i in range(3)], outrows[...][None, :])
    sub_out[...] = jnp.zeros_like(sub_out)
    lane_out[...] = jnp.zeros_like(lane_out)
    factors = Factors(reduced, sub_prior, lane_prior, n_dp, exchanges)
    early, late = (0, 1), (2,)
    slot(fed + 2)
    swaps.add(0)
    swaps.send(1)
    factors.send(early, factors.early_mp, factors.early_dp)
    slot(fed + 3)
    swaps.add(1)
    swaps.send(2)
    slot(fed + 4)
    swaps.add(2)
    swaps.send(3)
    factors.collect(early, factors.early_mp, factors.early_dp, sub_out, lane_out)
    slot(fed + 5)
    factors.send(late, factors.late_mp, factors.late_dp)
    swaps.add(3)
    swaps.send(4)
    factors.collect(late, factors.late_mp, factors.late_dp, sub_out, lane_out)
    factors.finish(masters, scalar_out)
    swaps.add(4)
    sums_out[...] = value[5]
    for s in range(fed + 5 + stream.CUTS + 1, stream.STEPS):
        stream.step(s)
    for away in range(1, n_mp):
        turned(away).wait_recv()
        turn(away).wait_send()
    own_turn.wait()
    own_result.wait()
    factors.wait_sends()
    back.finish()
    stream.finish()
    swaps.finish()

def moments_of(stream):
    center = stream - jnp.mean(stream, axis=-1, keepdims=True)
    spread = jnp.mean(center * center, axis=-1, keepdims=True)
    return (center, lax.rsqrt(spread + norm_eps))


def normalize(stream, gain_row, shift_row):
    center, inverse = moments_of(stream)
    return center * inverse * gain_row + shift_row


def segment_ids(counts, set_rows):
    image_ends = jnp.cumsum(counts)
    places = jnp.arange(set_rows, dtype=jnp.int32)
    return jnp.sum((places[:, None] >= image_ends[None, :]).astype(jnp.int32), axis=1)


def scores_of(query_set, key_set, same_image, score_scale):
    raw_scores = (
        jnp.einsum("qhd,khd->hqk", query_set, key_set, preferred_element_type=jnp.float32)
        * score_scale
    )
    return jnp.where(same_image[None], raw_scores, mask_fill)


def shard_offset(shard_piece, block_index, whole_length, axis_at):
    shape_list = list(shard_piece.shape)
    shape_list[axis_at] = whole_length
    empty = jnp.zeros(tuple(shape_list), jnp.float32)
    return lax.dynamic_update_slice_in_dim(
        empty, shard_piece, block_index * shard_piece.shape[axis_at], axis_at
    )


def select_slice(whole_array, block_index, block_width, axis_at):
    return lax.dynamic_slice_in_dim(whole_array, block_index * block_width, block_width, axis_at)


def factor_step(
    gradient,
    rows_old,
    cols_old,
    rows_mine,
    cols_mine,
    rows_total,
    count_rows,
    count_cols,
    prior_total,
):
    decay_rate = 1.0 - STEP ** (-0.8)
    rows_new = decay_rate * rows_old + (1.0 - decay_rate) * (rows_mine / count_cols + square_eps)
    cols_new = decay_rate * cols_old + (1.0 - decay_rate) * (cols_mine / count_rows + square_eps)
    rows_average = (
        decay_rate * prior_total
        + (1.0 - decay_rate) * (rows_total / count_cols + count_rows * square_eps)
    ) / count_rows
    update = gradient * lax.rsqrt(rows_new[:, None] * cols_new[None, :] / rows_average)
    return (rows_new, cols_new, update, jnp.sum(update * update))


def plain_step(weight, gradient, moment_old):
    decay_rate = 1.0 - STEP ** (-0.8)
    moment = decay_rate * moment_old + (1.0 - decay_rate) * (gradient * gradient + square_eps)
    update = gradient * lax.rsqrt(moment)
    update_rms = jnp.sqrt(jnp.mean(update * update))
    rate_here = step_rate * jnp.sqrt(jnp.mean(weight * weight))
    return (weight - rate_here * update / jnp.maximum(1.0, update_rms / clip_limit), moment)


def generic(
    tokens_in,
    cotangent,
    patch_counts,
    w_qkv,
    w_out,
    w_up,
    w_down,
    layer_vector_rows,
    inner_biases,
    qkvrows_prior,
    qkvcols_prior,
    outrows_prior,
    outcols_prior,
    uprows_prior,
    upcols_prior,
    downrows_prior,
    downcols_prior,
    vector_moment,
    bias_moment,
):
    data_index = lax.axis_index("dp")
    parallel_model_index = lax.axis_index("mp")
    row_count, parallel_model_width = tokens_in.shape
    set_count, slot_count = patch_counts.shape
    set_rows = row_count // set_count
    shard_width_local = w_qkv.shape[2]
    local_hidden = w_up.shape[1]
    head_count = shard_width_local // HD
    score_scale = HD ** (-0.5)
    full_qkv, full_out, full_up, full_down = (
        lax.all_gather(w_qkv.astype(jnp.bfloat16), "dp", axis=0, tiled=True),
        lax.all_gather(w_out.astype(jnp.bfloat16), "dp", axis=1, tiled=True),
        lax.all_gather(w_up.astype(jnp.bfloat16), "dp", axis=0, tiled=True),
        lax.all_gather(w_down.astype(jnp.bfloat16), "dp", axis=1, tiled=True),
    )
    stream = tokens_in.astype(jnp.float32)
    segment = jax.vmap(lambda counts: segment_ids(counts, set_rows))(patch_counts)
    valid_rows = (segment < slot_count).astype(jnp.float32).reshape(row_count)
    centered_single, inverse_deviation_single = moments_of(stream)
    standardized_single = centered_single * inverse_deviation_single
    normalized_rows = (standardized_single * layer_vector_rows[0] + layer_vector_rows[1]).astype(
        jnp.bfloat16
    )
    bias_mine = select_slice(inner_biases, parallel_model_index, shard_width_local, 1)
    projected = jnp.einsum(
        "rd,dtc->rtc", normalized_rows, full_qkv, preferred_element_type=jnp.float32
    )
    query_rows = (projected[:, 0] + bias_mine[0]).astype(jnp.bfloat16)
    key_rows = projected[:, 1].astype(jnp.bfloat16)
    value_rows = (projected[:, 2] + bias_mine[1]).astype(jnp.bfloat16)

    def split_sets(field_in):
        return field_in.reshape(set_count, set_rows, head_count, HD)

    def attend(set_item):
        query_set, key_set, value_set, segment_set = set_item
        same_image = segment_set[:, None] == segment_set[None, :]
        raw_scores = scores_of(query_set, key_set, same_image, score_scale)
        row_top = jnp.max(raw_scores, axis=-1, keepdims=True)
        exponent = jnp.exp(raw_scores - row_top)
        row_total = jnp.sum(exponent, axis=-1, keepdims=True)
        weights = exponent / row_total
        mixed_set = jnp.einsum(
            "hqk,khd->qhd",
            weights.astype(jnp.bfloat16),
            value_set,
            preferred_element_type=jnp.float32,
        )
        return (mixed_set.astype(jnp.bfloat16), (row_top + jnp.log(row_total))[..., 0])

    mixed_heads, log_total = lax.map(
        attend, (split_sets(query_rows), split_sets(key_rows), split_sets(value_rows), segment)
    )
    mixed_heads = mixed_heads.reshape(row_count, shard_width_local)
    attn_terms = jnp.dot(mixed_heads, full_out, preferred_element_type=jnp.float32)
    proj = (
        lax.psum(attn_terms.astype(jnp.bfloat16), "mp").astype(jnp.float32) + layer_vector_rows[6]
    )
    shared_mask = shard_offset(
        jnp.ones((shard_width_local,), jnp.float32), parallel_model_index, parallel_model_width, 0
    )
    middle = stream + layer_vector_rows[4] * proj
    normed_here = normalize(middle, layer_vector_rows[2], layer_vector_rows[3]).astype(jnp.bfloat16)
    up_bias = select_slice(inner_biases[2:], parallel_model_index, shard_width_local, 1).T.reshape(
        local_hidden
    )
    hidden = jnp.dot(normed_here, full_up, preferred_element_type=jnp.float32) + up_bias
    active = jax.nn.gelu(hidden, approximate=False).astype(jnp.bfloat16)
    mlp_terms = jnp.dot(active, full_down, preferred_element_type=jnp.float32)
    branch = (
        lax.psum(mlp_terms.astype(jnp.bfloat16), "mp").astype(jnp.float32) + layer_vector_rows[7]
    )
    result = middle + layer_vector_rows[5] * branch
    result_low = result.astype(jnp.bfloat16)
    back_grad = cotangent.astype(jnp.float32) * valid_rows[:, None]
    d_branch = (back_grad * layer_vector_rows[5]).astype(jnp.bfloat16)
    down_part = jnp.einsum("rf,rd->fd", active, d_branch, preferred_element_type=jnp.float32)
    d_active = jnp.einsum("rd,fd->rf", d_branch, full_down, preferred_element_type=jnp.float32)
    gelu_out, gelu_pull = jax.vjp(lambda inputs: jax.nn.gelu(inputs, approximate=False), hidden)
    d_hidden = gelu_pull(d_active)[0].astype(jnp.bfloat16)
    up_part = jnp.einsum("rd,rf->df", normed_here, d_hidden, preferred_element_type=jnp.float32)
    mid_terms = jnp.einsum("rf,df->rd", d_hidden, full_up, preferred_element_type=jnp.float32)
    d_normed_two = lax.psum(mid_terms.astype(jnp.bfloat16), "mp").astype(jnp.float32)
    norm_out, norm_pull = jax.vjp(normalize, middle, layer_vector_rows[2], layer_vector_rows[3])
    d_through, d_gain_two, d_shift_two = norm_pull(d_normed_two)
    d_middle = back_grad + d_through
    d_proj_here = (d_middle * layer_vector_rows[4]).astype(jnp.bfloat16)
    d_middle_cols = select_slice(d_middle, parallel_model_index, shard_width_local, 1)
    out_part = jnp.einsum("rc,rd->cd", mixed_heads, d_proj_here, preferred_element_type=jnp.float32)
    d_mixed = jnp.einsum(
        "rd,cd->rc", d_proj_here, full_out, preferred_element_type=jnp.float32
    ).astype(jnp.bfloat16)

    def attend_back(set_item):
        query_set, key_set, value_set, segment_set, total_set, grad_set = set_item
        same_image = segment_set[:, None] == segment_set[None, :]
        raw_scores = scores_of(query_set, key_set, same_image, score_scale)
        weights = jnp.exp(raw_scores - total_set[..., None])
        d_value = jnp.einsum(
            "hqk,qhd->khd",
            weights.astype(jnp.bfloat16),
            grad_set,
            preferred_element_type=jnp.float32,
        )
        d_weights = jnp.einsum(
            "qhd,khd->hqk", grad_set, value_set, preferred_element_type=jnp.float32
        )
        d_scores = (
            weights * (d_weights - jnp.sum(d_weights * weights, axis=-1, keepdims=True))
        ).astype(jnp.bfloat16)
        d_query = (
            jnp.einsum("hqk,khd->qhd", d_scores, key_set, preferred_element_type=jnp.float32)
            * score_scale
        )
        d_key = (
            jnp.einsum("hqk,qhd->khd", d_scores, query_set, preferred_element_type=jnp.float32)
            * score_scale
        )
        return jnp.stack([d_query, d_key, d_value], axis=1).astype(jnp.bfloat16)

    d_projected = lax.map(
        attend_back,
        (
            split_sets(query_rows),
            split_sets(key_rows),
            split_sets(value_rows),
            segment,
            log_total,
            split_sets(d_mixed),
        ),
    )
    d_projected = d_projected.reshape(row_count, 3, shard_width_local)
    qkv_part = jnp.einsum(
        "rd,rtc->dtc", normalized_rows, d_projected, preferred_element_type=jnp.float32
    )
    normalized_gradient = lax.psum_scatter(
        jnp.einsum("rtc,dtc->rd", d_projected, full_qkv, preferred_element_type=jnp.float32).astype(
            jnp.bfloat16
        ),
        "mp",
        scatter_dimension=1,
        tiled=True,
    ).astype(jnp.float32)
    standardized_local = select_slice(
        standardized_single, parallel_model_index, shard_width_local, 1
    )
    local_gain_slice = select_slice(
        layer_vector_rows[0], parallel_model_index, shard_width_local, 0
    )
    standardized_gradient = normalized_gradient * local_gain_slice
    gradient_sum_local, product_sum_local = lax.psum(
        (
            jnp.sum(standardized_gradient, axis=1),
            jnp.sum(standardized_gradient * standardized_local, axis=1),
        ),
        "mp",
    )
    input_grad = d_middle_cols + inverse_deviation_single * (
        standardized_gradient
        - gradient_sum_local[:, None] / parallel_model_width
        - standardized_local * product_sum_local[:, None] / parallel_model_width
    )

    def mine(field_in):
        return select_slice(field_in, parallel_model_index, shard_width_local, field_in.ndim - 1)

    vector_part = jnp.stack(
        [
            shard_offset(
                jnp.sum(normalized_gradient * standardized_local, axis=0),
                parallel_model_index,
                parallel_model_width,
                0,
            ),
            shard_offset(
                jnp.sum(normalized_gradient, axis=0), parallel_model_index, parallel_model_width, 0
            ),
            d_gain_two * shared_mask,
            d_shift_two * shared_mask,
            jnp.sum(d_middle * proj, axis=0) * shared_mask,
            jnp.sum(back_grad * branch, axis=0) * shared_mask,
            shard_offset(
                jnp.sum(mine(d_proj_here).astype(jnp.float32), axis=0),
                parallel_model_index,
                parallel_model_width,
                0,
            ),
            shard_offset(
                jnp.sum(mine(d_branch).astype(jnp.float32), axis=0),
                parallel_model_index,
                parallel_model_width,
                0,
            ),
        ]
    )
    hidden_sums = (
        jnp.sum(d_hidden.astype(jnp.float32), axis=0)
        .reshape(shard_width_local, local_hidden // shard_width_local)
        .T
    )
    bias_part = jnp.concatenate(
        [
            jnp.sum(d_projected[:, 0].astype(jnp.float32), axis=0)[None],
            jnp.sum(d_projected[:, 2].astype(jnp.float32), axis=0)[None],
            hidden_sums,
        ],
        axis=0,
    )
    squares = jnp.stack(
        [
            jnp.sum(valid_rows[:, None] * shared_mask * field_in * field_in)
            for field_in in (result, layer_vector_rows[4] * proj, layer_vector_rows[5] * branch)
        ]
    )
    counted = jnp.where(parallel_model_index == 0, jnp.sum(valid_rows), 0.0)
    vector_grad, bias_grad, squares_all, counted_all = lax.psum(
        (
            vector_part,
            shard_offset(bias_part, parallel_model_index, parallel_model_width, 1),
            squares,
            counted,
        ),
        ("dp", "mp"),
    )
    token_spread = jnp.sqrt(squares_all / (counted_all * parallel_model_width))
    grad_parts = (qkv_part, out_part, up_part, down_part)
    summed = lax.psum((grad_parts[0], grad_parts[1], grad_parts[2], grad_parts[3]), "dp")
    qkv_grad = select_slice(summed[0], data_index, w_qkv.shape[0], 0)
    out_grad = select_slice(summed[1], data_index, w_out.shape[1], 1)
    up_grad = select_slice(summed[2], data_index, w_up.shape[0], 0)
    down_grad = select_slice(summed[3], data_index, w_down.shape[1], 1)
    square_qkv = qkv_grad * qkv_grad
    square_out = out_grad * out_grad
    square_up = up_grad * up_grad
    square_down = down_grad * down_grad
    scalars = jnp.stack(
        [
            jnp.sum(w_qkv * w_qkv),
            jnp.sum(w_out * w_out),
            jnp.sum(w_up * w_up),
            jnp.sum(w_down * w_down),
            jnp.where(parallel_model_index == 0, jnp.sum(qkvrows_prior), 0.0),
            jnp.where(data_index == 0, jnp.sum(outrows_prior), 0.0),
            jnp.where(parallel_model_index == 0, jnp.sum(uprows_prior), 0.0),
            jnp.where(data_index == 0, jnp.sum(downrows_prior), 0.0),
        ]
    )
    factor_totals = lax.psum(
        (
            shard_offset(jnp.sum(square_qkv, axis=(1, 2)), data_index, parallel_model_width, 0),
            shard_offset(
                jnp.sum(square_qkv, axis=0), parallel_model_index, parallel_model_width, 1
            ),
            shard_offset(
                jnp.sum(square_out, axis=1), parallel_model_index, parallel_model_width, 0
            ),
            shard_offset(jnp.sum(square_out, axis=0), data_index, parallel_model_width, 0),
            shard_offset(jnp.sum(square_up, axis=1), data_index, parallel_model_width, 0),
            shard_offset(jnp.sum(square_up, axis=0), parallel_model_index, FF, 0),
            shard_offset(jnp.sum(square_down, axis=1), parallel_model_index, FF, 0),
            shard_offset(jnp.sum(square_down, axis=0), data_index, parallel_model_width, 0),
            scalars,
        ),
        ("dp", "mp"),
    )
    (
        rows_qkv,
        cols_qkv,
        rows_out,
        cols_out,
        rows_up,
        cols_up,
        rows_down,
        cols_down,
        scalar_totals,
    ) = factor_totals
    local_rows = w_qkv.shape[0]
    local_cols = w_out.shape[1]
    qkvrows_after, qkvcols_flat, update_qkv, usq_qkv = factor_step(
        qkv_grad.reshape(local_rows, 3 * shard_width_local),
        qkvrows_prior,
        qkvcols_prior.reshape(3 * shard_width_local),
        select_slice(rows_qkv, data_index, local_rows, 0),
        select_slice(cols_qkv, parallel_model_index, shard_width_local, 1).reshape(
            3 * shard_width_local
        ),
        jnp.sum(rows_qkv),
        parallel_model_width,
        3 * parallel_model_width,
        scalar_totals[4],
    )
    outrows_after, outcols_after, update_out, usq_out = factor_step(
        out_grad,
        outrows_prior,
        outcols_prior,
        select_slice(rows_out, parallel_model_index, shard_width_local, 0),
        select_slice(cols_out, data_index, local_cols, 0),
        jnp.sum(rows_out),
        parallel_model_width,
        parallel_model_width,
        scalar_totals[5],
    )
    uprows_after, upcols_after, update_up, usq_up = factor_step(
        up_grad,
        uprows_prior,
        upcols_prior,
        select_slice(rows_up, data_index, local_rows, 0),
        select_slice(cols_up, parallel_model_index, local_hidden, 0),
        jnp.sum(rows_up),
        parallel_model_width,
        FF,
        scalar_totals[6],
    )
    downrows_after, downcols_after, update_down, usq_down = factor_step(
        down_grad,
        downrows_prior,
        downcols_prior,
        select_slice(rows_down, parallel_model_index, local_hidden, 0),
        select_slice(cols_down, data_index, local_cols, 0),
        jnp.sum(rows_down),
        FF,
        parallel_model_width,
        scalar_totals[7],
    )
    usq_totals = lax.psum(jnp.stack([usq_qkv, usq_out, usq_up, usq_down]), ("dp", "mp"))
    entry_counts = jnp.array(
        [
            3.0 * parallel_model_width * parallel_model_width,
            1.0 * parallel_model_width * parallel_model_width,
            1.0 * parallel_model_width * FF,
            1.0 * FF * parallel_model_width,
        ],
        jnp.float32,
    )
    update_scale = jnp.sqrt(usq_totals / entry_counts)
    weight_rms = jnp.sqrt(scalar_totals[:4] / entry_counts)
    limits = jnp.maximum(1.0, update_scale / clip_limit)
    qkv_after = (
        w_qkv.reshape(local_rows, 3 * shard_width_local)
        - step_rate * weight_rms[0] * update_qkv / limits[0]
    ).reshape(w_qkv.shape)
    out_after = w_out - step_rate * weight_rms[1] * update_out / limits[1]
    up_after = w_up - step_rate * weight_rms[2] * update_up / limits[2]
    down_after = w_down - step_rate * weight_rms[3] * update_down / limits[3]
    vectors_after, moment_vectors = jax.vmap(plain_step)(
        layer_vector_rows, vector_grad, vector_moment
    )
    heads_after, heads_moment = jax.vmap(plain_step)(
        inner_biases[:2], bias_grad[:2], bias_moment[:2]
    )
    upper_after, upper_moment = plain_step(
        inner_biases[2:].reshape(FF), bias_grad[2:].reshape(FF), bias_moment[2:].reshape(FF)
    )
    biases_after = jnp.concatenate(
        [heads_after, upper_after.reshape(FF // parallel_model_width, parallel_model_width)], axis=0
    )
    moment_biases = jnp.concatenate(
        [heads_moment, upper_moment.reshape(FF // parallel_model_width, parallel_model_width)],
        axis=0,
    )
    return (
        result_low,
        input_grad,
        qkv_grad,
        out_grad,
        up_grad,
        down_grad,
        qkv_after,
        out_after,
        up_after,
        down_after,
        qkv_after.astype(jnp.bfloat16),
        out_after.astype(jnp.bfloat16),
        up_after.astype(jnp.bfloat16),
        down_after.astype(jnp.bfloat16),
        qkvrows_after,
        qkvcols_flat.reshape(3, shard_width_local),
        outrows_after,
        outcols_after,
        uprows_after,
        upcols_after,
        downrows_after,
        downcols_after,
        vector_grad,
        bias_grad,
        moment_vectors,
        moment_biases,
        vectors_after,
        biases_after,
        update_scale,
        token_spread,
    )

def shards(
    tokens_in,
    cotangent,
    patch_counts,
    w_qkv,
    w_out,
    w_up,
    w_down,
    layer_vector_rows,
    inner_biases,
    qkvrows_prior,
    qkvcols_prior,
    outrows_prior,
    outcols_prior,
    uprows_prior,
    upcols_prior,
    downrows_prior,
    downcols_prior,
    vector_moment,
    bias_moment,
):
    n_dp, n_mp = lax.axis_size("dp"), lax.axis_size("mp")
    row_count, width = tokens_in.shape
    set_count, slot_count = patch_counts.shape
    set_rows = row_count // set_count
    own_rows = row_count // n_mp
    window = own_rows + HALO
    share, hidden_width, block_rows = w_qkv.shape[2], w_up.shape[1], w_up.shape[0]
    f32, low = jnp.float32, jnp.bfloat16
    vmem = pl.BlockSpec(memory_space=pltpu.VMEM)
    anywhere = pl.BlockSpec(memory_space=pl.ANY)
    scalars_in = pl.BlockSpec(memory_space=pltpu.SMEM)
    dma = pltpu.SemaphoreType.DMA
    held = pltpu.VMEM

    def shape(*dims, dtype=low):
        return jax.ShapeDtypeStruct(dims, dtype)

    masters, reduced, sums, sub_new, lane_new, scalar_rows, input_parts, stream = pl.pallas_call(
        functools.partial(layer_kernel, n_dp, n_mp, slot_count, own_rows),
        out_shape=(
            shape(GROUPS, block_rows, width, dtype=f32),
            shape(GROUPS, block_rows, width, dtype=f32),
            shape(16, width, dtype=f32),
            shape(8, LANES, dtype=f32),
            shape(8, width, dtype=f32),
            shape(8, LANES, dtype=f32),
            shape(n_mp, share, own_rows),
            shape(n_mp, own_rows, width),
        ),
        in_specs=[anywhere] * 2 + [vmem] * 4 + [scalars_in] + [vmem] * 10,
        out_specs=(vmem,) * 6 + (anywhere,) * 2,
        scratch_shapes=[
            held((GROUPS, n_mp, n_dp // 2, 2, block_rows, width), low),
            held((set_rows, width), low),
            held((window, width), low),
            held((n_mp, set_rows, width), low),
            held((n_mp, own_rows, hidden_width), low),
            held((n_mp, window, hidden_width), low),
            held((n_mp, window, 2 * LANES), low),
            held((window, width), f32),
            held((window, width), low),
            held((width, own_rows), low),
            held((width, own_rows), low),
            held((width, own_rows), low),
            held((own_rows, width), f32),
            held((window, width), low),
            held((window, width), f32),
            held((own_rows, width), low),
            held((set_rows, LANES), low),
            held((set_rows, LANES), low),
            held((window, 2 * LANES), low),
            held((window, 3 * LANES), f32),
            held((window, 2 * LANES), low),
            held((8, width), f32),
            held((16, width), f32),
            held((8, width), f32),
            held((8, LANES), f32),
            held((3, width), f32),
            held((RING, n_dp // 2, block_rows, width), low),
            held((GROUPS, n_mp, 2, block_rows // 2, width), low),
            held((GROUPS, n_mp, block_rows, width), low),
            held((GROUPS, n_mp, block_rows, width), low),
            held((GROUPS, n_mp + 1, block_rows, width), low),
            held((6, 16, width), f32),
            held((5, 16, width), f32),
            held((n_mp, 8, LANES), f32),
            held((n_dp, 2, width), f32),
            held((n_mp, 8, LANES), f32),
            held((n_dp, 1, width), f32),
            held((n_mp, 8, LANES), f32),
            held((n_dp, 8, LANES), f32),
            pltpu.SemaphoreType.REGULAR,
            dma((4,)),
            dma((GROUPS, n_mp, KINDS)),
            dma((GROUPS, n_mp, KINDS)),
            dma((GROUPS, n_mp, 2)),
            dma((GROUPS, n_mp, R_KINDS)),
            dma((GROUPS, n_mp, R_KINDS)),
            dma((2, n_mp, Stream.CUTS)),
            dma((n_mp, Stream.CUTS)),
            dma((n_mp,)),
            dma((n_mp,)),
            dma((5,)),
            dma((5,)),
            dma((6, max(n_dp, n_mp))),
            dma((6, max(n_dp, n_mp))),
        ],
        compiler_params=pltpu.CompilerParams(
            collective_id=1, has_side_effects=True, vmem_limit_bytes=63 * 2**20
        ),
    )(
        tokens_in, cotangent, w_qkv.transpose(1, 0, 2), w_out, w_up, w_down.T, patch_counts, layer_vector_rows,
        inner_biases, qkvrows_prior, qkvcols_prior, outrows_prior, outcols_prior, uprows_prior, upcols_prior,
        downrows_prior, downcols_prior,
    )

    def both(*dims):
        return (shape(*dims, dtype=f32),) * 2 + (shape(*dims),)

    kinds = [
        both(3, block_rows, share), both(share, block_rows), both(block_rows, width), both(block_rows, width)
    ]
    small = [
        (block_rows,), (3, share), (share,), (block_rows,),
        (block_rows,), (hidden_width,), (hidden_width,), (block_rows,),
    ] + [(8, width), (6, width)] * 3 + [(4,), (3,)]
    outs = pl.pallas_call(
        functools.partial(update_kernel, n_dp, n_mp),
        out_shape=(
            shape(n_mp, own_rows, width),
            shape(share, row_count, dtype=f32),
            *(kind[i] for i in range(3) for kind in kinds),
            *(shape(*dims, dtype=f32) for dims in small),
        ),
        in_specs=[vmem] * 11 + [anywhere],
        out_specs=(anywhere,) + (vmem,) * 29,
        scratch_shapes=[pltpu.VMEM((n_mp, own_rows, width), low), dma((2,))],
        compiler_params=pltpu.CompilerParams(vmem_limit_bytes=60 * 2**20),
    )(
        reduced, masters, sub_new, lane_new, scalar_rows, sums, layer_vector_rows, inner_biases, vector_moment,
        bias_moment, input_parts, stream,
    )
    weights = [
        part for i in (2, 6, 10) for part in (outs[i].transpose(1, 0, 2), outs[i + 1], outs[i + 2], outs[i + 3].T)
    ]
    return (outs[0].reshape(row_count, width), outs[1].T, *weights, *outs[14:])

def solution(mesh):
    in_specs = (
        P("dp", None),
        P("dp", None),
        P("dp", None),
        P("dp", None, "mp"),
        P("mp", "dp"),
        P("dp", "mp"),
        P("mp", "dp"),
        P(),
        P(),
        P("dp"),
        P(None, "mp"),
        P("mp"),
        P("dp"),
        P("dp"),
        P("mp"),
        P("mp"),
        P("dp"),
        P(),
        P(),
    )
    out_specs = (
        P("dp", None),
        P("dp", "mp"),
        P("dp", None, "mp"),
        P("mp", "dp"),
        P("dp", "mp"),
        P("mp", "dp"),
        P("dp", None, "mp"),
        P("mp", "dp"),
        P("dp", "mp"),
        P("mp", "dp"),
        P("dp", None, "mp"),
        P("mp", "dp"),
        P("dp", "mp"),
        P("mp", "dp"),
        P("dp"),
        P(None, "mp"),
        P("mp"),
        P("dp"),
        P("dp"),
        P("mp"),
        P("mp"),
        P("dp"),
        P(),
        P(),
        P(),
        P(),
        P(),
        P(),
        P(),
        P(),
    )
    fits = mesh.shape["dp"] == 8 and mesh.shape["mp"] == 4
    return jax.shard_map(shards if fits else generic, mesh=mesh, in_specs=in_specs, out_specs=out_specs, check_vma=False)
```

```python
import functools

import jax
import jax.numpy as jnp
from jax import lax
from jax.experimental import pallas as pl
from jax.experimental.pallas import tpu as pltpu
from jax.sharding import PartitionSpec as P

HD = 64
FF = 3072
STEP = 3


norm_eps = 1e-06
square_eps = 1e-30
clip_limit = 0.5
step_rate = 0.6
mask_fill = -1000000000.0


MESH = pl.DeviceIdType.MESH
HALO = 128
GROUPS = 3

def neighbours(dp):
    core = dp % 2
    return dp + 1 - 2 * core, dp + 2 - 4 * ((dp // 2) % 2), (dp + 4) % 8, (dp + 4) % 8 + 2 - 4 * ((dp // 2) % 2)


def flip(dp):
    return dp + 1 - 2 * (dp % 2)


def greet(devices, extra):
    barrier = pltpu.get_barrier_semaphore()
    for device in devices:
        pl.semaphore_signal(barrier, inc=1, device_id=device, device_id_type=MESH)
    for condition, device in extra:

        @pl.when(condition)
        def _():
            pl.semaphore_signal(barrier, inc=1, device_id=device, device_id_type=MESH)

    peers = len(devices)
    for condition, _ in extra:
        peers = peers + jnp.where(condition, 1, 0)
    pl.semaphore_wait(barrier, peers)


A_Z, A_X, A_Y, A_D0, A_D1, A_S, A_SX, A_SY, A_SD0, A_SD1 = range(10)
KINDS = 10
ORDERS = ((0, 1, 2, 3), (1, 0, 2, 3), (2, 3, 1, 0), (3, 2, 1, 0))


def plane_at(mp, unit):
    codes = [sum(plane * 4**i for i, plane in enumerate(order)) for order in ORDERS]
    code = jnp.where(mp == 0, codes[0], jnp.where(mp == 1, codes[1], jnp.where(mp == 2, codes[2], codes[3])))
    power = jnp.where(unit == 0, 1, jnp.where(unit == 1, 4, jnp.where(unit == 2, 16, 64)))
    return (code // power) % 4

class Gather:
    def __init__(self, n_mp, out, send_sems, recv_sems, way_sems):
        self.dp, self.mp, self.n_mp = lax.axis_index("dp"), lax.axis_index("mp"), n_mp
        self.out, self.send_sems, self.recv_sems, self.way_sems = out, send_sems, recv_sems, way_sems
        self.sib, self.xn, self.yn, self.dn = neighbours(self.dp)
        self.rows = out.shape[4]
        self.up, self.down = jnp.minimum(self.mp + 1, n_mp - 1), jnp.maximum(self.mp - 1, 0)
        self.inner = jnp.where((self.mp > 0) & (self.mp < n_mp - 1), 1, 0)
        half = self.rows // 2
        self.all, self.low, self.high = pl.ds(0, self.rows), pl.ds(0, half), pl.ds(half, half)

    def message(self, kind, group, plane, slot, part, device):
        where = self.out.at[group, plane, slot // 2, slot % 2, part]
        return pltpu.make_async_remote_copy(
            src_ref=where,
            dst_ref=where,
            send_sem=self.send_sems.at[group, plane, kind],
            recv_sem=self.recv_sems.at[group, plane, kind],
            device_id=(device, self.mp),
            device_id_type=MESH,
        )

    def along(self, group, plane, way):
        where = self.out.at[group, plane, self.dp // 2, self.dp % 2]
        return pltpu.make_async_remote_copy(
            src_ref=where,
            dst_ref=where,
            send_sem=self.way_sems.at[group, plane, way],
            recv_sem=self.recv_sems.at[group, plane, A_Z],
            device_id=(self.dp, self.down if way else self.up),
            device_id_type=MESH,
        )

    def sends(self, group, plane):
        dp, xn, yn, dn, sib = self.dp, self.xn, self.yn, self.dn, self.sib
        first = [(A_X, dp, self.all, xn), (A_Y, dp, self.all, yn), (A_S, dp, self.all, sib)]
        second = [(A_D0, xn, self.low, yn), (A_SX, xn, self.all, sib), (A_D1, yn, self.high, xn), (A_SY, yn, self.all, sib)]
        third = [(A_SD0, dn, self.low, sib), (A_SD1, dn, self.high, sib)]
        return [
            [functools.partial(self.message, kind, group, plane, *rest) for kind, *rest in part]
            for part in (first, second, third)
        ]

    def unit(self, t):
        rest = t - self.n_mp
        group = jnp.where(rest < 0, 0, 1 + t % 2)
        return group, plane_at(self.mp, jnp.where(rest < 0, t, rest // 2))

    def guarded(self, t, action):
        if isinstance(t, int):
            if 0 <= t < GROUPS * self.n_mp:
                action(*self.unit(t))
            return

        @pl.when((t >= 0) & (t < GROUPS * self.n_mp))
        def _():
            action(*self.unit(t))

    def stage_z(self, t):
        def action(group, plane):
            @pl.when(plane != self.mp)
            def _():
                self.along(group, plane, 0).wait_recv()

            @pl.when((plane <= self.mp) & (self.mp < self.n_mp - 1))
            def _():
                self.along(group, plane, 0).start()

            @pl.when((plane >= self.mp) & (self.mp > 0))
            def _():
                self.along(group, plane, 1).start()

        self.guarded(t, action)

    def stage_a(self, t):
        def action(group, plane):
            for copy in self.sends(group, plane)[0]:
                copy().start()

        self.guarded(t, action)

    def stage_b(self, t):
        def action(group, plane):
            out = self.sends(group, plane)[1]
            self.message(A_X, group, plane, self.xn, self.all, self.xn).wait_recv()
            out[0]().start()
            out[1]().start()
            self.message(A_Y, group, plane, self.yn, self.all, self.yn).wait_recv()
            out[2]().start()
            out[3]().start()

        self.guarded(t, action)

    def stage_c(self, t):
        def action(group, plane):
            out = self.sends(group, plane)[2]
            self.message(A_D0, group, plane, self.dn, self.low, self.yn).wait_recv()
            out[0]().start()
            self.message(A_D1, group, plane, self.dn, self.high, self.xn).wait_recv()
            out[1]().start()

        self.guarded(t, action)

    def stage_d(self, t):
        def action(group, plane):
            for kind, slot, part in (
                (A_S, self.sib, self.all),
                (A_SX, flip(self.xn), self.all),
                (A_SY, flip(self.yn), self.all),
                (A_SD0, flip(self.dn), self.low),
                (A_SD1, flip(self.dn), self.high),
            ):
                self.message(kind, group, plane, slot, part, self.sib).wait_recv()

        self.guarded(t, action)

    def plane(self, u):
        return plane_at(self.mp, u)

    def begin(self):
        for t in (0, 1):
            self.stage_z(t)
            self.stage_a(t)

        @pl.when(self.inner == 1)
        def _():
            self.stage_z(2)

    def step(self, s):
        self.stage_b(s)
        ahead = (2,)
        for more in ahead:
            self.stage_z(s + more + self.inner)
            self.stage_a(s + more)
        self.stage_c(s - 1)

    def finish(self, t):
        def action(group, plane):
            for part in self.sends(group, plane):
                for copy in part:
                    copy().wait_send()

            @pl.when((plane <= self.mp) & (self.mp < self.n_mp - 1))
            def _():
                self.along(group, plane, 0).wait_send()

            @pl.when((plane >= self.mp) & (self.mp > 0))
            def _():
                self.along(group, plane, 1).wait_send()

        self.guarded(t, action)

R_S, R_D0, R_D1, R_X, R_Y, R_UP, R_DOWN = range(7)
R_KINDS = 7
RING = 4


class Scatter:
    def __init__(self, n_mp, blocks, out, bufs, credit, send_sems, recv_sems):
        self.dp, self.mp, self.n_mp = lax.axis_index("dp"), lax.axis_index("mp"), n_mp
        self.blocks, self.out, self.credit = blocks, out, credit
        self.pair_in, self.halves_in, self.x_in, self.y_in, self.z_in = bufs
        self.send_sems, self.recv_sems = send_sems, recv_sems
        self.sib, self.xn, self.yn, self.dn = neighbours(self.dp)
        self.core = self.dp % 2
        self.here, self.at_x, self.at_y, self.at_d = self.dp // 2, self.xn // 2, self.yn // 2, self.dn // 2
        self.up, self.down = jnp.minimum(self.mp + 1, n_mp - 1), jnp.maximum(self.mp - 1, 0)
        rows = out.shape[1]
        self.all, self.low, self.high = pl.ds(0, rows), pl.ds(0, rows // 2), pl.ds(rows // 2, rows // 2)
        self.fed = 2 * n_mp
        self.units = GROUPS * n_mp

    def offered(self, o):
        if isinstance(o, int) and o >= self.fed:
            return 0, plane_at(self.mp, self.units - 1 - o)
        return 2 - o % 2, plane_at(self.mp, o // 2)

    def unit(self, k):
        if isinstance(k, int) and k >= self.fed:
            return 0, plane_at(self.mp, self.units - 1 - k)
        return 2 - k % 2, plane_at(self.mp, self.n_mp - 1 - k // 2)

    def remote(self, kind, group, plane, src, dst, device):
        return pltpu.make_async_remote_copy(
            src_ref=src,
            dst_ref=dst,
            send_sem=self.send_sems.at[group, plane, kind],
            recv_sem=self.recv_sems.at[group, plane, kind],
            device_id=device,
            device_id_type=MESH,
        )

    def pair(self, o, group, plane):
        return self.remote(
            R_S, group, plane, self.blocks.at[group, plane, :, 1 - self.core], self.pair_in.at[o % RING], (self.sib, self.mp)
        )

    def mine(self, group, plane, place, part=None):
        return self.blocks.at[group, plane, place, self.core, self.all if part is None else part]

    def message(self, kind, group, plane):
        mp = self.mp
        if kind == R_D0:
            src, dst = self.mine(group, plane, self.at_d, self.low), self.halves_in.at[group, plane, 0]
            device = (self.xn, mp)
        elif kind == R_D1:
            src, dst = self.mine(group, plane, self.at_d, self.high), self.halves_in.at[group, plane, 1]
            device = (self.yn, mp)
        elif kind == R_X:
            src, dst, device = self.mine(group, plane, self.at_x), self.x_in.at[group, plane], (self.xn, mp)
        elif kind == R_Y:
            src, dst, device = self.mine(group, plane, self.at_y), self.y_in.at[group, plane], (self.yn, mp)
        elif kind == R_UP:
            src, dst, device = self.mine(group, plane, self.here), self.z_in.at[group, plane], (self.dp, self.up)
        else:
            slot = jnp.where(plane == mp - 1, self.n_mp, plane)
            src, dst, device = self.mine(group, plane, self.here), self.z_in.at[group, slot], (self.dp, self.down)
        return self.remote(kind, group, plane, src, dst, device)

    def from_above(self, group, plane):
        slot = jnp.where(plane == self.mp, self.n_mp, plane)
        return slot, self.remote(
            R_DOWN, group, plane, self.mine(group, plane, self.here), self.z_in.at[group, slot], (self.dp, self.down)
        )

    def offer(self, o, group, plane):
        if isinstance(o, int):
            if o >= RING:
                pl.semaphore_wait(self.credit, 1)
        else:

            @pl.when(o >= RING)
            def _():
                pl.semaphore_wait(self.credit, 1)

        self.pair(o, group, plane).start()

    def add_pair(self, o, group, plane):
        self.pair(o, group, plane).wait_recv()
        self.blocks[group, plane, :, self.core] = self.blocks[group, plane, :, self.core] + self.pair_in[o % RING]

        @pl.when(o < self.units - RING)
        def _():
            pl.semaphore_signal(self.credit, inc=1, device_id=(self.sib, self.mp), device_id_type=MESH)

        self.message(R_D0, group, plane).start()
        self.message(R_D1, group, plane).start()

    def add_halves(self, group, plane):
        for kind, place, part, slot in ((R_D0, self.at_y, self.low, 0), (R_D1, self.at_x, self.high, 1)):
            self.message(kind, group, plane).wait_recv()
            where = self.mine(group, plane, place, part)
            where[...] = where[...] + self.halves_in[group, plane, slot]
        self.message(R_X, group, plane).start()
        self.message(R_Y, group, plane).start()

    def add_plane(self, group, plane):
        f32, mp, last = jnp.float32, self.mp, self.n_mp - 1
        self.message(R_X, group, plane).wait_recv()
        self.message(R_Y, group, plane).wait_recv()
        where = self.mine(group, plane, self.here)
        total = (
            where[...].astype(f32) + self.x_in[group, plane].astype(f32) + self.y_in[group, plane].astype(f32)
        )

        @pl.when(plane == mp)
        def _():
            self.out[(group + 2) % 3] = total

        @pl.when(plane != mp)
        def _():
            where[...] = total.astype(jnp.bfloat16)

        @pl.when((plane > mp) & (mp == 0))
        def _():
            self.message(R_UP, group, plane).start()

        @pl.when((plane < mp) & (mp == last))
        def _():
            self.message(R_DOWN, group, plane).start()

    def add_along(self, group, plane):
        f32, mp, last = jnp.float32, self.mp, self.n_mp - 1
        where = self.mine(group, plane, self.here)

        def add():
            where[...] = (where[...].astype(f32) + self.z_in[group, plane].astype(f32)).astype(jnp.bfloat16)

        @pl.when((plane > mp) & (mp > 0))
        def _():
            self.message(R_UP, group, plane).wait_recv()
            add()
            self.message(R_UP, group, plane).start()

        @pl.when((plane < mp) & (mp < last))
        def _():
            self.from_above(group, plane)[1].wait_recv()
            add()
            self.message(R_DOWN, group, plane).start()

        @pl.when((plane == mp) & (mp > 0))
        def _():
            self.message(R_UP, group, plane).wait_recv()
            self.out[(group + 2) % 3] += self.z_in[group, plane].astype(f32)

        @pl.when((plane == mp) & (mp < last))
        def _():
            slot, copy = self.from_above(group, plane)
            copy.wait_recv()
            self.out[(group + 2) % 3] += self.z_in[group, slot].astype(f32)

    def slot(self, k):
        def do(action, j):
            if isinstance(j, int):
                if 0 <= j < self.units:
                    action(*self.unit(j))
                return

            @pl.when(j >= 0)
            def _():
                action(*self.unit(j))

        do(self.add_halves, k)
        do(self.add_plane, k - 1)
        do(self.add_along, k - 2)

    def finish(self):
        def body(t, _):
            group, plane = t // self.n_mp, t % self.n_mp
            self.pair(0, group, plane).wait_send()
            for kind in (R_D0, R_D1, R_X, R_Y):
                self.message(kind, group, plane).wait_send()

            @pl.when(plane > self.mp)
            def _():
                self.message(R_UP, group, plane).wait_send()

            @pl.when(plane < self.mp)
            def _():
                self.message(R_DOWN, group, plane).wait_send()

            return 0

        lax.fori_loop(0, self.units, body, 0)

LANES = 128
NN = (((1,), (0,)), ((), ()))
NT = (((1,), (1,)), ((), ()))
BIG = 2.0**36


def mm(left, right, dims=NN):
    return lax.dot_general(left, right, dims, preferred_element_type=jnp.float32)


def gelu_parts(t):
    k = 1.0 / (1.0 + 0.2316419 * jnp.abs(t))
    series = k * (
        0.319381530 + k * (-0.356563782 + k * (1.781477937 + k * (-1.821255978 + k * 1.330274429)))
    )
    density = 0.3989422804014327 * jnp.exp(-0.5 * t * t)
    tail = density * series
    phi = jnp.where(t >= 0.0, 1.0 - tail, tail)
    return t * phi, phi + t * density


def row_stats(x):
    width = x.shape[1]
    center = x - jnp.sum(x, axis=1, keepdims=True) * (1.0 / width)
    spread = jnp.sum(center * center, axis=1, keepdims=True) * (1.0 / width)
    inverse = lax.rsqrt(spread + norm_eps)
    return center * inverse, inverse


def image_ends(counts_ref, set_index, slots):
    lane = lax.broadcasted_iota(jnp.int32, (8, LANES), 1) % (LANES // 2)
    low = jnp.zeros((8, LANES), jnp.int32)
    high = jnp.zeros((8, LANES), jnp.int32)
    edge = jnp.int32(0)
    for slot in range(slots + 1):
        after = jnp.int32(1 << 20) if slot == slots else edge + counts_ref[set_index, slot]
        low = jnp.where(lane == slot, edge, low)
        high = jnp.where(lane == slot, after, high)
        edge = after if slot < slots else edge
    return low[0:1], high[0:1], edge


def own_row(hidden_half, tile):
    lane = lax.broadcasted_iota(jnp.int32, tile.shape, 1)
    return (lane < LANES // 2) if hidden_half == 0 else (lane >= LANES // 2)


def keep_half(half, tile, other):
    return jnp.where(own_row(half, tile), tile, other)


HEAD_TILES = ((0, 128, 256, 0, 0), (0, 128, 256, 1, 1), (512, 640, 640, 0, 1))
MIX = 384


def make_features(counts_ref, set_index, slots, set_rows, feat_q, feat_k):
    low, high, total = image_ends(counts_ref, set_index, slots)
    step = 256

    def body(i, _):
        at = pl.ds(pl.multiple_of(i * step, step), step)
        row = lax.broadcasted_iota(jnp.int32, (step, LANES), 0) + i * step
        same = (row >= low) & (row < high)
        lane = lax.broadcasted_iota(jnp.int32, (step, LANES), 1) % (LANES // 2)
        feat_k[at] = jnp.where(same, 1.0, 0.0).astype(jnp.bfloat16)
        feat_q[at] = jnp.where(same | (lane > slots), 0.0, -BIG).astype(jnp.bfloat16)
        return 0

    lax.fori_loop(0, set_rows // step, body, 0)
    return total


def attend(m, qkv, mixed, feat_q, feat_k, window_start, window, step):
    keys, values = [], []
    for q_at, k_at, v_at, half, v_half in HEAD_TILES:
        keys.append(keep_half(half, qkv[m, :, k_at : k_at + LANES], feat_k[...]))
        tile = qkv[m, :, v_at : v_at + LANES]
        values.append(keep_half(v_half, tile, jnp.ones_like(tile)))

    def block(i, _):
        at = pl.ds(pl.multiple_of(window_start + i * step, LANES // 2), step)
        outs = []
        for head, (q_at, k_at, v_at, half, v_half) in enumerate(HEAD_TILES):
            query = keep_half(half, qkv[m, at, q_at : q_at + LANES], feat_q[at])
            scores = mm(query, keys[head], NT)
            top = jnp.max(scores, axis=1, keepdims=True)
            weights = jnp.exp2((scores - top) * (HD ** (-0.5) * 1.4426950408889634)).astype(jnp.bfloat16)
            out = mm(weights, values[head])
            outs.append(out / pltpu.roll(out, LANES // 2, 1))
        here = pl.ds(pl.multiple_of(i * step, LANES // 2), step)
        low = jnp.bfloat16
        mixed[m, here, 0:LANES] = keep_half(0, outs[0], outs[1]).astype(low)
        mixed[m, here, LANES : 2 * LANES] = keep_half(1, outs[2], jnp.zeros_like(outs[2])).astype(low)
        return 0

    lax.fori_loop(0, window // step, block, 0)


TN = (((0,), (0,)), ((), ()))


def norm_grad(x, gain, grad):
    width = x.shape[1]
    unit, inverse = row_stats(x)
    e = grad * gain
    mean_e = jnp.sum(e, axis=1, keepdims=True) * (1.0 / width)
    mean_eu = jnp.sum(e * unit, axis=1, keepdims=True) * (1.0 / width)
    return inverse * (e - mean_e - unit * mean_eu), grad * unit


def attend_back(m, qkv, d_mixed, feat_q, feat_k, window_start, window, acc, d_query):
    band = 3 * LANES
    acc[...] = jnp.zeros_like(acc)
    low = jnp.bfloat16
    scale = HD ** (-0.5)

    def block(b, _):
        start = jnp.clip(b - 1, 0, window // LANES - 3) * LANES
        keys_at = pl.ds(pl.multiple_of(start, LANES), band)
        keys_in = pl.ds(pl.multiple_of(window_start + start, LANES), band)
        here = pl.ds(pl.multiple_of(b * LANES, LANES), LANES)
        rows_in = pl.ds(pl.multiple_of(window_start + b * LANES, LANES), LANES)
        f_q, f_k = feat_q[rows_in], feat_k[keys_in]
        got = []
        for head, (q_at, k_at, v_at, half, v_half) in enumerate(HEAD_TILES):
            q_tile = qkv[m, rows_in, q_at : q_at + LANES]
            k_tile = qkv[m, keys_in, k_at : k_at + LANES]
            v_tile = qkv[m, keys_in, v_at : v_at + LANES]
            mix_at = 0 if head < 2 else LANES
            d_tile = d_mixed[here, mix_at : mix_at + LANES]
            d_out = keep_half(v_half, d_tile, jnp.zeros_like(d_tile))
            scores = mm(keep_half(half, k_tile, f_k), keep_half(half, q_tile, f_q), NT)
            top = jnp.max(scores, axis=0, keepdims=True)
            weights = jnp.exp((scores - top) * scale)
            weights = weights * (1.0 / jnp.sum(weights, axis=0, keepdims=True))
            d_weights = mm(v_tile, d_out, NT)
            delta = jnp.sum(d_weights * weights, axis=0, keepdims=True)
            d_scores = (weights * (d_weights - delta)).astype(low)
            d_key = mm(d_scores, keep_half(half, q_tile * scale, jnp.zeros_like(q_tile)))
            d_value = mm(weights.astype(low), d_out)
            d_q = mm(d_scores, keep_half(half, k_tile * scale, jnp.zeros_like(k_tile)), TN)
            got.append((d_q, d_key, d_value))
        acc[keys_at, 0:LANES] += got[0][1] + got[1][1]
        acc[keys_at, LANES : 2 * LANES] += got[0][2] + got[1][2]
        acc[keys_at, 2 * LANES : 3 * LANES] += got[2][1] + got[2][2]
        d_query[here, 0:LANES] = (got[0][0] + got[1][0]).astype(low)
        d_query[here, LANES : 2 * LANES] = got[2][0].astype(low)
        return 0

    lax.fori_loop(0, window // LANES, block, 0)

def tile_rows(i, first=0):
    return pl.ds(pl.multiple_of(first + i * LANES, LANES), LANES)


def column_sum(v):
    return jnp.sum(v, axis=0, keepdims=True)


class Place:
    def __init__(self, set_rows, own_rows):
        self.set_rows, self.own_rows, self.window = set_rows, own_rows, own_rows + HALO
        mp = lax.axis_index("mp")
        per_set = set_rows // own_rows
        self.set_index, part = mp // per_set, mp % per_set
        self.window_start = pl.multiple_of(part * (set_rows - self.window), LANES)
        self.own_start = pl.multiple_of(part * (self.window - own_rows), LANES)
        self.own = pl.ds(self.own_start, own_rows)
        self.own_set = pl.ds(pl.multiple_of(self.window_start + self.own_start, LANES), own_rows)
        self.tiles = self.window // LANES

    def is_own(self, i):
        first = i * LANES
        return jnp.where((first >= self.own_start) & (first < self.own_start + self.own_rows), 1.0, 0.0)

    def valid(self, i, total):
        row = lax.broadcasted_iota(jnp.int32, (LANES, 1), 0) + (self.window_start + i * LANES)
        return jnp.where(row < total, 1.0, 0.0)


def pack_first(qkv, out, packed):
    out_t = out[...].T
    for i in range(3):
        packed[:, i * LANES : (i + 1) * LANES] = qkv[i, :, 0:LANES]
    packed[:, MIX : MIX + LANES] = out_t[:, 0:LANES]
    tails = [qkv[i, :, LANES:] for i in range(3)]
    packed[:, 512:640] = jnp.concatenate([tails[0], out_t[:, LANES:]], axis=1)
    packed[:, 640:768] = jnp.concatenate([tails[1], tails[2]], axis=1)


def pack_lanes(qkv_rows, out_row):
    heads = [row[:, 0:LANES] for row in (*qkv_rows, out_row)]
    q, k, v, o = [row[:, LANES:] for row in (*qkv_rows, out_row)]
    return jnp.concatenate([*heads, q, o, k, v], axis=1)


def unpack_lanes(row):
    at = ((0, 512), (128, 640), (256, 704), (MIX, 576))
    return [jnp.concatenate([row[:, a : a + LANES], row[:, b : b + LANES // 2]], axis=1) for a, b in at]


def pack_biases(biases, packed, n_mp, width):
    f32 = jnp.float32
    share = width // n_mp
    zero = jnp.zeros((1, share), f32)
    for m in range(n_mp):
        part = [biases[r : r + 1, m * share : (m + 1) * share] for r in (0, 1)]
        packed[m : m + 1] = pack_lanes((part[0], zero, part[1]), zero)
    fan = width // share
    source = lax.broadcasted_iota(jnp.int32, (share, width), 0) * fan
    target = lax.broadcasted_iota(jnp.int32, (share, width), 1)
    total = jnp.zeros((n_mp, width), f32)
    for r in range(fan):
        rows = jnp.concatenate(
            [biases[2 + r : 3 + r, m * share : (m + 1) * share] for m in range(n_mp)], axis=0
        )
        move = jnp.where(target == source + r, 1.0, 0.0)
        total = total + lax.dot_general(rows, move, NN, precision=EXACT, preferred_element_type=f32)
    packed[n_mp : 2 * n_mp] = total

DECAY = 1.0 - STEP ** (-0.8)
EXACT = lax.Precision.HIGHEST
SUB_QKV, SUB_OUT, SUB_UP, SUB_DOWN = range(4)


class Exchange:
    def __init__(self, axis, size, bufs, send_sems, recv_sems):
        self.axis, self.size, self.bufs = axis, size, bufs
        self.send_sems, self.recv_sems = send_sems, recv_sems
        self.me = lax.axis_index(axis)

    def copy(self, away):
        peer = (self.me + away) % self.size
        return pltpu.make_async_remote_copy(
            src_ref=self.bufs.at[0],
            dst_ref=self.bufs.at[away],
            send_sem=self.send_sems.at[away],
            recv_sem=self.recv_sems.at[away],
            device_id={self.axis: peer},
            device_id_type=MESH,
        )

    def send(self, value):
        self.bufs[0] = value
        for away in range(1, self.size):
            self.copy(away).start()

    def total(self):
        for away in range(1, self.size):
            self.copy(away).wait_recv()
        total = jnp.zeros(self.bufs.shape[1:], jnp.float32)
        for index in range(self.size):
            away = (self.me - index + self.size) % self.size
            total = total + self.bufs[away]
        return total

    def wait_sends(self):
        for away in range(1, self.size):
            self.copy(away).wait_send()


class Doubling:
    def __init__(self, value, bufs, send_sems, recv_sems):
        self.value, self.bufs, self.send_sems, self.recv_sems = value, bufs, send_sems, recv_sems
        dp, mp = lax.axis_index("dp"), lax.axis_index("mp")
        sib, xn, yn, _ = neighbours(dp)
        self.peers = (
            {"dp": sib}, {"dp": xn}, {"dp": yn}, {"mp": mp + 1 - 2 * (mp % 2)}, {"mp": (mp + 2) % 4}
        )

    def copy(self, i):
        return pltpu.make_async_remote_copy(
            src_ref=self.value.at[i],
            dst_ref=self.bufs.at[i],
            send_sem=self.send_sems.at[i],
            recv_sem=self.recv_sems.at[i],
            device_id=self.peers[i],
            device_id_type=MESH,
        )

    def send(self, i):
        self.copy(i).start()

    def add(self, i):
        self.copy(i).wait_recv()
        self.value[i + 1] = self.value[i] + self.bufs[i]

    def finish(self):
        for i in range(5):
            self.copy(i).wait_send()


def lane_sums(mask, squares):
    return lax.dot_general(mask, squares, NT, precision=EXACT, preferred_element_type=jnp.float32)


def o_lanes(width):
    lane = lax.broadcasted_iota(jnp.int32, (1, width), 1)
    return jnp.where(((lane >= MIX) & (lane < MIX + 128)) | ((lane >= 576) & (lane < 640)), 1.0, 0.0)


def masks_of(width, scale_rows):
    row = lax.broadcasted_iota(jnp.int32, (8, width), 0)
    is_o = o_lanes(width)
    if not isinstance(scale_rows, list):
        scale_rows = [scale_rows[i : i + 1] for i in range(3)]
    up = jnp.where(row == SUB_UP, scale_rows[0], 0.0)
    down = jnp.where(row == SUB_DOWN, scale_rows[1], 0.0)
    first = scale_rows[2]
    mixed = jnp.where(row == SUB_QKV, first * (1.0 - is_o), jnp.where(row == SUB_OUT, first * is_o, 0.0))
    return up, down, mixed


class Factors:
    def __init__(self, reduced, sub_prior, lane_prior, n_dp, swaps):
        self.reduced, self.sub_prior, self.lane_prior = reduced, sub_prior, lane_prior
        self.rows, self.width = reduced.shape[1:]
        self.whole = float(self.rows * n_dp)
        self.early_mp, self.early_dp, self.late_mp, self.late_dp, self.last_mp, self.last_dp = swaps
        self.shares = jnp.zeros((8, self.rows), jnp.float32)
        self.totals = jnp.zeros((8, 1), jnp.float32)

    def send(self, groups, along_mp, along_dp):
        masks = masks_of(self.width, jnp.ones((3, self.width), jnp.float32))
        rows = jnp.zeros((8, self.rows), jnp.float32)
        columns = []
        for group in groups:
            squares = self.reduced[group] * self.reduced[group]
            columns.append(column_sum(squares))
            rows = rows + lane_sums(masks[group], squares)
        along_dp.send(columns[0] if len(columns) == 1 else jnp.concatenate(columns, axis=0))
        along_mp.send(jnp.concatenate([rows, jnp.zeros((8, LANES - self.rows), jnp.float32)], axis=1))
        self.totals = self.totals + jnp.sum(rows, axis=1, keepdims=True)

    def collect(self, groups, along_mp, along_dp, sub_out, lane_out):
        rows, columns = along_mp.total(), along_dp.total()
        row8 = lax.broadcasted_iota(jnp.int32, (8, LANES), 0)
        count = self.whole * jnp.where(row8 == SUB_QKV, 3.0, jnp.where(row8 == SUB_OUT, 1.0, 4.0))
        sub_new = DECAY * self.sub_prior[...] + (1.0 - DECAY) * (rows / count + square_eps)
        mine = (row8 == SUB_UP) | (row8 == SUB_DOWN)
        if 2 in groups:
            mine = (row8 == SUB_QKV) | (row8 == SUB_OUT)
        sub_out[...] = jnp.where(mine, sub_new, sub_out[...])
        scale_rows = []
        for i, group in enumerate(groups):
            new = DECAY * self.lane_prior[group : group + 1] + (1.0 - DECAY) * (
                columns[i : i + 1] / self.whole + square_eps
            )
            lane_out[group : group + 1] = new
            scale_rows.append(1.0 / new)
        if len(scale_rows) == 1:
            scale_rows = [scale_rows[0]] * 3
        masks = masks_of(self.width, scale_rows + scale_rows[:1])
        shares = jnp.zeros((8, self.rows), jnp.float32)
        for group in groups:
            shares = shares + lane_sums(masks[group], self.reduced[group] * self.reduced[group])
        self.shares = self.shares + jnp.where(mine[:, 0 : self.rows], shares / sub_new[:, 0 : self.rows], 0.0)

    def finish(self, masters, scalar_out):
        f32 = jnp.float32
        masks = masks_of(self.width, jnp.ones((3, self.width), f32))
        weights = jnp.zeros((8, 1), f32)
        for group in range(GROUPS):
            by_lane = column_sum(masters[group] * masters[group])
            weights = weights + jnp.sum(masks[group] * by_lane, axis=1, keepdims=True)
        row1 = lax.broadcasted_iota(jnp.int32, (8, 1), 0)
        lane8 = lax.broadcasted_iota(jnp.int32, (8, LANES), 1)
        sub = jnp.sum(jnp.where(lane8 < self.rows, self.sub_prior[...], 0.0), axis=1, keepdims=True)
        out = jnp.sum(self.lane_prior[2:3] * o_lanes(self.width), axis=1, keepdims=True)
        down = jnp.sum(self.lane_prior[1:2], axis=1, keepdims=True)
        prior = jnp.where(row1 == SUB_OUT, out, jnp.where(row1 == SUB_DOWN, down, sub))
        shares = jnp.sum(self.shares, axis=1, keepdims=True)
        value = jnp.where(
            lane8 == 0, shares, jnp.where(lane8 == 1, weights, jnp.where(lane8 == 2, self.totals, prior))
        )
        self.last_mp.send(value)
        self.last_dp.send(self.last_mp.total())
        scalar_out[...] = self.last_dp.total()

    def wait_sends(self):
        for swap in (self.early_mp, self.early_dp, self.late_mp, self.late_dp, self.last_mp, self.last_dp):
            swap.wait_sends()


def update_kernel(
    n_dp, n_mp, reduced, masters, sub_new, lane_new, scalars, sums, vec, bias, vec_moment, bias_moment, input_in, stream_in,
    stream_out, input_out, qkv_g, out_g, up_g, down_g, qkv_a, out_a, up_a, down_a, qkv_b, out_b, up_b, down_b,
    qkvrows, qkvcols, outrows, outcols, uprows, upcols, downrows, downcols,
    vec_g, bias_g, vec_m, bias_m, vec_a, bias_a, update_scale, token_spread, held, sems,
):
    f32 = jnp.float32
    groups, rows, width = reduced.shape
    load = pltpu.make_async_copy(stream_in, held, sems.at[0])
    load.start()
    span = input_in.shape[2]
    for i in range(n_mp):
        input_out[:, i * span : (i + 1) * span] = input_in[i].astype(f32)
    load.wait()
    store = pltpu.make_async_copy(held, stream_out, sems.at[1])
    store.start()
    whole = float(rows * n_dp)
    entries = (3.0 * whole * whole, whole * whole, 4.0 * whole * whole, 4.0 * whole * whole)
    row1 = lax.broadcasted_iota(jnp.int32, (8, 1), 0)
    size = jnp.where(row1 == 0, entries[0], jnp.where(row1 == 1, entries[1], entries[2]))
    copies = jnp.where((row1 == SUB_QKV) | (row1 == SUB_UP), float(n_mp), float(n_dp))
    length = jnp.where(row1 == SUB_DOWN, 4.0 * whole, whole)
    mean_rows = DECAY * scalars[:, 3:4] / (copies * length) + (1.0 - DECAY) * (scalars[:, 2:3] / size + square_eps)
    scale = jnp.sqrt(scalars[:, 0:1] * mean_rows / size)
    rms = jnp.sqrt(scalars[:, 1:2] / size)
    rate = step_rate * rms / jnp.maximum(1.0, scale / clip_limit)
    sub = lax.dot_general(
        jnp.where(
            lax.broadcasted_iota(jnp.int32, (rows, LANES), 0) == lax.broadcasted_iota(jnp.int32, (rows, LANES), 1), 1.0, 0.0
        ),
        sub_new[...], NT, precision=EXACT, preferred_element_type=f32,
    )
    is_o = o_lanes(width)

    def renewed(group, index):
        gradient = reduced[group]
        product = sub[:, index : index + 1] * lane_new[group : group + 1] / mean_rows[index : index + 1]
        return masters[group] - rate[index : index + 1] * (gradient * lax.rsqrt(product))

    def spread(value, qkv, out):
        q, k, v, o = unpack_lanes(value)
        for i, part in enumerate((q, k, v)):
            qkv[i] = part.astype(qkv.dtype)
        out[...] = o.T.astype(out.dtype)

    first = jnp.where(is_o > 0.0, renewed(2, 1), renewed(2, 0))
    spread(reduced[2], qkv_g, out_g)
    spread(first, qkv_a, out_a)
    spread(first, qkv_b, out_b)
    for group, index, grad, after, short in ((0, 2, up_g, up_a, up_b), (1, 3, down_g, down_a, down_b)):
        new = renewed(group, index)
        grad[...] = reduced[group]
        after[...] = new
        short[...] = new.astype(short.dtype)

    def plain(weight, gradient, moment_old, together):
        moment = DECAY * moment_old + (1.0 - DECAY) * (gradient * gradient + square_eps)
        update = gradient * lax.rsqrt(moment)
        update_mean = jnp.mean(update * update, axis=1, keepdims=True)
        weight_mean = jnp.mean(weight * weight, axis=1, keepdims=True)
        if together is not None:
            row = lax.broadcasted_iota(jnp.int32, update_mean.shape, 0)
            number = float(weight.shape[0] - together)

            def join(mean):
                shared = jnp.sum(jnp.where(row >= together, mean, 0.0), axis=0, keepdims=True) / number
                return jnp.where(row >= together, shared, mean)

            update_mean, weight_mean = join(update_mean), join(weight_mean)
        rate_here = step_rate * jnp.sqrt(weight_mean)
        return weight - rate_here * update / jnp.maximum(1.0, jnp.sqrt(update_mean) / clip_limit), moment

    vec_g[...] = sums[0:8]
    bias_g[...] = sums[8:14]
    vec_a[...], vec_m[...] = plain(vec[...], sums[0:8], vec_moment[...], None)
    bias_a[...], bias_m[...] = plain(bias[...], sums[8:14], bias_moment[...], 2)
    spreads = jnp.sqrt(sums[14:15, 0:LANES] / (sums[14:15, 3:4] * width))
    scales = jnp.zeros((1, LANES), f32)
    lane1 = lax.broadcasted_iota(jnp.int32, (1, LANES), 1)
    for i in range(4):
        scales = scales + jnp.where(lane1 == i, scale[i : i + 1], 0.0)
    update_scale[...] = scales[:, 0:4].reshape(4)
    token_spread[...] = spreads[:, 0:3].reshape(3)
    for index, ref in ((SUB_QKV, qkvrows), (SUB_OUT, outcols), (SUB_UP, uprows), (SUB_DOWN, downcols)):
        ref[...] = sub_new[index, 0:rows]
    upcols[...] = lane_new[0]
    downrows[...] = lane_new[1]
    *cols, out_row = unpack_lanes(lane_new[2:3])
    for i in range(3):
        qkvcols[i : i + 1] = cols[i]
    outrows[...] = out_row.reshape(out_row.shape[1])
    store.wait()


def bias_rows_natural(qkv_sums, hidden_sums, n_mp, width):
    f32 = jnp.float32
    share = width // n_mp
    half = LANES // 2
    query = [qkv_sums[m : m + 1, a:b] for m in range(n_mp) for a, b in ((0, LANES), (512, 512 + half))]
    value = [qkv_sums[m : m + 1, a:b] for m in range(n_mp) for a, b in ((256, 256 + LANES), (704, 704 + half))]
    source = lax.broadcasted_iota(jnp.int32, (width, width), 0)
    target = lax.broadcasted_iota(jnp.int32, (1, width), 1)
    fan = width // share
    from_lane = target * fan
    for r in range(1, fan):
        from_lane = jnp.where(target >= r * share, (target - r * share) * fan + r, from_lane)
    move = jnp.where(source == from_lane, 1.0, 0.0).astype(jnp.bfloat16)
    moved = jnp.zeros_like(hidden_sums)
    left = hidden_sums
    for _ in range(3):
        part = left.astype(jnp.bfloat16)
        moved = moved + mm(part, move)
        left = left - part.astype(f32)
    rows = [jnp.concatenate(query, axis=1), jnp.concatenate(value, axis=1)]
    for r in range(width // share):
        rows.append(
            jnp.concatenate([moved[m : m + 1, r * share : (r + 1) * share] for m in range(n_mp)], axis=1)
        )
    return rows

class Stream:
    CUTS = 4

    def __init__(self, n_mp, src, out, send_sems, recv_sems):
        self.dp, self.mp, self.n_mp = lax.axis_index("dp"), lax.axis_index("mp"), n_mp
        self.src, self.out, self.send_sems, self.recv_sems = src, out, send_sems, recv_sems
        self.rows = out.shape[1] // self.CUTS
        self.up, self.down = jnp.minimum(self.mp + 1, n_mp - 1), jnp.maximum(self.mp - 1, 0)

    def message(self, plane, cut, way, own):
        part = pl.ds(pl.multiple_of(cut * self.rows, self.rows), self.rows)
        where = self.out.at[plane, part]
        return pltpu.make_async_remote_copy(
            src_ref=self.src.at[part] if own else where,
            dst_ref=where,
            send_sem=self.send_sems.at[way, plane, cut],
            recv_sem=self.recv_sems.at[plane, cut],
            device_id=(self.dp, self.down if way else self.up),
            device_id_type=MESH,
        )

    def step(self, s):
        distance, cut = s // self.CUTS, s % self.CUTS
        mp, last = self.mp, self.n_mp - 1

        @pl.when((distance == 0) & (mp < last))
        def _():
            self.message(mp, cut, 0, True).start()

        @pl.when((distance == 0) & (mp > 0))
        def _():
            self.message(mp, cut, 1, True).start()

        below, above = mp - distance, mp + distance

        @pl.when((distance > 0) & (below >= 0))
        def _():
            self.message(below, cut, 0, False).wait_recv()

            @pl.when(mp < last)
            def _():
                self.message(below, cut, 0, False).start()

        @pl.when((distance > 0) & (above <= last))
        def _():
            self.message(above, cut, 1, False).wait_recv()

            @pl.when(mp > 0)
            def _():
                self.message(above, cut, 1, False).start()

    STEPS = 16

    def finish(self):
        mp, last = self.mp, self.n_mp - 1

        def body(t, _):
            plane, cut = t // self.CUTS, t % self.CUTS

            @pl.when((plane <= mp) & (mp < last))
            def _():
                self.message(plane, cut, 0, False).wait_send()

            @pl.when((plane >= mp) & (mp > 0))
            def _():
                self.message(plane, cut, 1, False).wait_send()

            return 0

        lax.fori_loop(0, self.n_mp * self.CUTS, body, 0)

def layer_kernel(
    n_dp, n_mp, slots, own_rows, tokens_in, cot_in, w_qkv, w_out, w_up, w_down_t, counts, vec, biases, *rest
):
    (
        qkvrows, qkvcols, outrows, outcols, uprows, upcols, downrows, downcols,
        masters, reduced, sums_out, sub_out, lane_out, scalar_out, input_out, stream_out,
        w, tokens, cot, qkv, active, slope, mixed, proj, normed_two, normed_t, normed_two_t, turned_t, branch, d_branch, d_two,
        result, feat_q, feat_k, d_mixed, acc, d_query, bias, sums, sums_qkv, sub_prior, lane_prior,
        pair_in, halves_in, x_in, y_in, z_in, value, swap_in, early_mp, early_dp, late_mp, late_dp, last_mp, last_dp,
        credit, local_sems, g_send, g_recv, g_way, s_send, s_recv, stream_send, stream_recv, turn_send, turn_recv,
        swap_send, swap_recv, small_send, small_recv,
    ) = rest
    set_rows, width = tokens.shape
    place = Place(set_rows, own_rows)
    window, own, own_start, window_start, tiles = (
        place.window, place.own, place.own_start, place.window_start, place.tiles
    )
    low, f32 = jnp.bfloat16, jnp.float32
    dp, mp = lax.axis_index("dp"), lax.axis_index("mp")
    in_set = pl.ds(pl.multiple_of(place.set_index * set_rows, LANES), set_rows)
    token_copy = pltpu.make_async_copy(tokens_in.at[in_set], tokens, local_sems.at[0])
    in_window = pl.ds(pl.multiple_of(place.set_index * set_rows + window_start, LANES), window)
    cot_copy = pltpu.make_async_copy(cot_in.at[in_window], cot, local_sems.at[1])
    token_copy.start()
    cot_copy.start()
    net = Gather(n_mp, w, g_send, g_recv, g_way)
    back = Scatter(n_mp, w, reduced, (pair_in, halves_in, x_in, y_in, z_in), credit, s_send, s_recv)
    stream = Stream(n_mp, result, stream_out, stream_send, stream_recv)
    swaps = Doubling(value, swap_in, swap_send, swap_recv)
    exchanges = [
        Exchange(axis, size, buf, small_send.at[i], small_recv.at[i])
        for i, (axis, size, buf) in enumerate(
            (
                ("mp", n_mp, early_mp), ("dp", n_dp, early_dp), ("mp", n_mp, late_mp), ("dp", n_dp, late_dp),
                ("mp", n_mp, last_mp), ("dp", n_dp, last_dp),
            )
        )
    ]
    masters[0] = w_up[...]
    masters[1] = w_down_t[...]
    pack_first(w_qkv, w_out, masters.at[2])
    for group, source in enumerate((2, 0, 1)):
        w[group, mp, dp // 2, dp % 2] = masters[source].astype(low)
    greet(
        [((dp + away) % n_dp, mp) for away in range(1, n_dp)] + [(dp, (mp + away) % n_mp) for away in range(1, n_mp)], []
    )
    net.begin()

    def weight(group, m, lanes=None):
        block = w[group, m] if lanes is None else w[group, m, :, :, :, lanes]
        return block.reshape(width, block.shape[-1])

    pack_biases(biases, bias, n_mp, width)
    total = make_features(counts, place.set_index, slots, set_rows, feat_q, feat_k)
    token_copy.wait()
    zero_row = jnp.zeros((1, width), f32)
    normed = slope

    def norm_one(i, _):
        unit, _inv = row_stats(tokens[tile_rows(i)].astype(f32))
        per_half = own_rows // LANES
        normed[i // per_half, tile_rows(i % per_half)] = (unit * vec[0:1] + vec[1:2]).astype(low)
        return 0

    lax.fori_loop(0, set_rows // LANES, norm_one, 0)
    net.step(0)
    cot_copy.wait()

    def back_of(i):
        return cot[tile_rows(i)].astype(f32) * place.valid(i, total)

    def first_grad(i, total_row):
        db = (back_of(i) * vec[5:6]).astype(low)
        d_branch[tile_rows(i)] = db
        return total_row + place.is_own(i) * column_sum(db.astype(f32))

    branch_sum = lax.fori_loop(0, tiles, first_grad, zero_row)
    turned_t[...] = d_branch[own].T
    net.step(1)
    normed_t[...] = normed[mp % 2, 0:own_rows].T

    def project(u, _):
        net.step(u + 2)
        net.stage_d(u)
        m = net.plane(u)
        for half in range(set_rows // own_rows):
            at = pl.ds(half * own_rows, own_rows)
            qkv[m, at] = (mm(normed[half, 0:own_rows], weight(0, m)) + bias[pl.ds(m, 1)]).astype(low)
        attend(m, qkv, mixed, feat_q, feat_k, window_start, window, window // 2)
        return 0

    project(0, 0)
    lax.fori_loop(1, n_mp, project, 0)
    net.step(n_mp + 2)
    proj[...] = sum((mm(mixed[m], weight(0, m, pl.ds(MIX, 2 * LANES)), NT) for m in range(n_mp)), vec[6:7])

    def middle_of(i):
        return tokens[tile_rows(i, window_start)].astype(f32) + vec[4:5] * proj[tile_rows(i)]

    def norm_two(i, _):
        unit, _inv = row_stats(middle_of(i))
        normed_two[tile_rows(i)] = (unit * vec[2:3] + vec[3:4]).astype(low)
        return 0

    lax.fori_loop(0, tiles, norm_two, 0)
    normed_two_t[...] = normed_two[own].T

    half_shape = (n_dp // 2, 2, width // n_dp)

    def keep(group, m, lanes, block):
        w[group, m, :, :, :, lanes] = block.astype(low).reshape(*half_shape, block.shape[1])

    def feed(u, _):
        first_unit = n_mp + 2 * u
        net.stage_d(first_unit)
        net.stage_d(first_unit + 1)
        m = net.plane(u)

        def rows(i, _):
            at = tile_rows(i)
            hidden = mm(normed_two[at], weight(1, m)) + bias[pl.ds(n_mp + m, 1)]
            act, slp = gelu_parts(hidden)
            slope[m, at] = slp.astype(low)

            @pl.when((i * LANES >= own_start) & (i * LANES < own_start + own_rows))
            def _():
                active[m, tile_rows(i - own_start // LANES)] = act.astype(low)

            return 0

        lax.fori_loop(0, tiles, rows, 0)
        net.step(first_unit + 3)
        part_sum = mm(active[m], weight(2, m), NT)

        @pl.when(u == 0)
        def _():
            branch[...] = part_sum

        @pl.when(u > 0)
        def _():
            branch[...] += part_sum

        def grad_rows(i, total_row):
            at = tile_rows(i)
            dh = (mm(d_branch[at], weight(2, m)) * slope[m, at].astype(f32)).astype(low)
            slope[m, at] = dh
            return total_row + place.is_own(i) * column_sum(dh.astype(f32))

        sums[pl.ds(8 + m, 1)] = lax.fori_loop(0, tiles, grad_rows, zero_row)
        net.step(first_unit + 4)
        two_sum = mm(slope[m], weight(1, m), NT)

        @pl.when(u == 0)
        def _():
            d_two[...] = two_sum

        @pl.when(u > 0)
        def _():
            d_two[...] += two_sum

        @pl.when(u > 0)
        def _():
            for o in (2 * u - 2, 2 * u - 1):
                back.add_pair(o, *back.offered(o))

        net.finish(first_unit)
        net.finish(first_unit + 1)
        everything = pl.ds(0, width)
        keep(2, m, everything, mm(turned_t[...], active[m]))
        back.offer(2 * u, 2, m)
        keep(1, m, everything, mm(normed_two_t[...], slope[m, own]))
        back.offer(2 * u + 1, 1, m)
        return 0

    lax.fori_loop(0, n_mp, feed, 0)

    def final(i, carry):
        there = own_start // LANES + i
        br = branch[tile_rows(i)] + vec[7:8]
        scaled = vec[5:6] * br
        res = middle_of(there) + scaled
        result[tile_rows(i)] = res.astype(low)
        attn = vec[4:5] * proj[tile_rows(there)]
        valid = place.valid(there, total)
        new = [column_sum(valid * v * v) for v in (res, attn, scaled)] + [column_sum(back_of(there) * br)]
        return tuple(c + n for c, n in zip(carry, new))

    *squares, back_branch = lax.fori_loop(0, own_rows // LANES, final, (zero_row,) * 4)
    own_result = pltpu.make_async_copy(result, stream_out.at[mp], local_sems.at[2])
    own_result.start()
    for cut in range(stream.CUTS):
        stream.step(cut)
    fed = 2 * n_mp
    for o in (fed - 2, fed - 1):
        back.add_pair(o, *back.offered(o))

    d_proj, d_proj_t = d_branch, turned_t

    def norm_two_back(i, carry):
        at = tile_rows(i)
        grad = d_two[at]
        dv, grad_unit = norm_grad(middle_of(i), vec[2:3], grad)
        d_mid = back_of(i) + dv
        d_two[at] = d_mid
        d_out = (d_mid * vec[4:5]).astype(low)
        d_proj[at] = d_out
        mine = place.is_own(i)
        new = (grad_unit, grad, d_mid * proj[at], d_out.astype(f32))
        return tuple(c + mine * column_sum(n) for c, n in zip(carry, new))

    gain_two, shift_two, scale_sum, proj_sum = lax.fori_loop(0, tiles, norm_two_back, (zero_row,) * 4)
    d_proj_t[...] = d_proj[own].T
    for u in range(n_mp):
        net.finish(u)
    d_normed = branch
    d_qkv = normed_two.at[pl.ds(0, own_rows)]

    def slot(k):
        back.slot(k)
        stream.step(k + stream.CUTS)

    def attention(u, _):
        m = plane_at(mp, n_mp - 1 - u)

        @pl.when(u > 0)
        def _():
            back.add_pair(fed + u - 1, 0, plane_at(mp, n_mp - u))

        dm = mm(d_proj[...], weight(0, m, pl.ds(MIX, 2 * LANES))).astype(low)
        d_mixed[:, 0:LANES] = dm[:, 0:LANES]
        d_mixed[:, LANES:] = keep_half(1, dm[:, LANES:], jnp.zeros_like(dm[:, LANES:]))
        slot(2 * u)
        attend_back(m, qkv, d_mixed, feat_q, feat_k, window_start, window, acc, d_query)
        slot(2 * u + 1)
        d_qkv[:, 0:128] = d_query[own, 0:128]
        d_qkv[:, 128:256] = acc[own, 0:128].astype(low)
        d_qkv[:, 256:384] = acc[own, 128:256].astype(low)
        d_qkv[:, 384:512] = jnp.zeros((own_rows, LANES), low)
        d_qkv[:, 512:640] = d_query[own, 128:256]
        d_qkv[:, 640:768] = acc[own, 256:384].astype(low)
        sums_qkv[pl.ds(m, 1)] = column_sum(d_qkv[...].astype(f32))
        part_sum = mm(d_qkv[...], weight(0, m), NT)

        @pl.when(u == 0)
        def _():
            d_normed[...] = part_sum

        @pl.when(u > 0)
        def _():
            d_normed[...] += part_sum

        block = mm(normed_t[...], d_qkv[...])
        extra = mm(d_proj_t[...], mixed[m, own])
        keep(0, m, pl.ds(0, MIX), block[:, 0:MIX])
        keep(0, m, pl.ds(MIX, 2 * LANES), block[:, MIX : MIX + 2 * LANES] + extra)
        keep(0, m, pl.ds(MIX + 2 * LANES, LANES), block[:, MIX + 2 * LANES :])
        back.offer(fed + u, 0, m)
        return 0

    lax.fori_loop(0, n_mp, attention, 0)
    slot(fed)
    back.add_pair(back.units - 1, 0, mp)

    input_t = normed_t

    def norm_one_back(i, carry):
        grad = d_normed[tile_rows(i)]
        rows = tokens[tile_rows(own_start // LANES + i, window_start)].astype(f32)
        dv, grad_unit = norm_grad(rows, vec[0:1], grad)
        input_t[:, tile_rows(i)] = (d_two[tile_rows(i, own_start)] + dv).astype(low).T
        return tuple(c + column_sum(n) for c, n in zip(carry, (grad_unit, grad)))

    gain_one, shift_one = lax.fori_loop(0, own_rows // LANES, norm_one_back, (zero_row, zero_row))
    share = width // n_mp

    def turn(away):
        peer = (mp + away) % n_mp
        return pltpu.make_async_remote_copy(
            src_ref=input_t.at[pl.ds(pl.multiple_of(peer * share, HD), share)],
            dst_ref=input_out.at[mp],
            send_sem=turn_send.at[away],
            recv_sem=turn_recv.at[away],
            device_id={"mp": peer},
            device_id_type=MESH,
        )

    def turned(away):
        source = (mp - away + n_mp) % n_mp
        return pltpu.make_async_remote_copy(
            src_ref=input_t.at[pl.ds(0, share)],
            dst_ref=input_out.at[source],
            send_sem=turn_send.at[away],
            recv_sem=turn_recv.at[away],
            device_id={"mp": source},
            device_id_type=MESH,
        )

    for away in range(1, n_mp):
        turn(away).start()
    own_turn = pltpu.make_async_copy(
        input_t.at[pl.ds(pl.multiple_of(mp * share, HD), share)], input_out.at[mp], local_sems.at[3]
    )
    own_turn.start()
    slot(fed + 1)

    held = jnp.clip(total - (window_start + own_start), 0, own_rows).astype(f32)
    lane_w = lax.broadcasted_iota(jnp.int32, (1, width), 1)
    scalar_row = jnp.where(lane_w == 3, held, 0.0)
    for i in range(3):
        scalar_row = scalar_row + jnp.where(lane_w == i, jnp.sum(squares[i], axis=1, keepdims=True), 0.0)
    natural = bias_rows_natural(sums_qkv[0:n_mp], sums[8 : 8 + n_mp], n_mp, width)
    vector_rows = [gain_one, shift_one, gain_two, shift_two, scale_sum, back_branch, proj_sum, branch_sum]
    for i, row in enumerate(vector_rows + natural + [scalar_row, zero_row]):
        value[0, i : i + 1] = row
    swaps.send(0)
    rows_here = qkvrows.shape[0]
    sub_prior[...] = jnp.zeros_like(sub_prior)
    for i, prior in enumerate((qkvrows, outcols, uprows, downcols)):
        sub_prior[i : i + 1, 0:rows_here] = prior[...][None, :]
    lane_prior[0:1] = upcols[...][None, :]
    lane_prior[1:2] = downrows[...][None, :]
    lane_prior[2:3] = pack_lanes([qkvcols[i : i + 1] for i in range(3)], outrows[...][None, :])
    sub_out[...] = jnp.zeros_like(sub_out)
    lane_out[...] = jnp.zeros_like(lane_out)
    factors = Factors(reduced, sub_prior, lane_prior, n_dp, exchanges)
    early, late = (0, 1), (2,)
    slot(fed + 2)
    swaps.add(0)
    swaps.send(1)
    factors.send(early, factors.early_mp, factors.early_dp)
    slot(fed + 3)
    swaps.add(1)
    swaps.send(2)
    slot(fed + 4)
    swaps.add(2)
    swaps.send(3)
    factors.collect(early, factors.early_mp, factors.early_dp, sub_out, lane_out)
    slot(fed + 5)
    factors.send(late, factors.late_mp, factors.late_dp)
    swaps.add(3)
    swaps.send(4)
    factors.collect(late, factors.late_mp, factors.late_dp, sub_out, lane_out)
    factors.finish(masters, scalar_out)
    swaps.add(4)
    sums_out[...] = value[5]
    for s in range(fed + 5 + stream.CUTS + 1, stream.STEPS):
        stream.step(s)
    for away in range(1, n_mp):
        turned(away).wait_recv()
        turn(away).wait_send()
    own_turn.wait()
    own_result.wait()
    factors.wait_sends()
    back.finish()
    stream.finish()
    swaps.finish()

def moments_of(stream):
    center = stream - jnp.mean(stream, axis=-1, keepdims=True)
    spread = jnp.mean(center * center, axis=-1, keepdims=True)
    return (center, lax.rsqrt(spread + norm_eps))


def normalize(stream, gain_row, shift_row):
    center, inverse = moments_of(stream)
    return center * inverse * gain_row + shift_row


def segment_ids(counts, set_rows):
    image_ends = jnp.cumsum(counts)
    places = jnp.arange(set_rows, dtype=jnp.int32)
    return jnp.sum((places[:, None] >= image_ends[None, :]).astype(jnp.int32), axis=1)


def scores_of(query_set, key_set, same_image, score_scale):
    raw_scores = (
        jnp.einsum("qhd,khd->hqk", query_set, key_set, preferred_element_type=jnp.float32)
        * score_scale
    )
    return jnp.where(same_image[None], raw_scores, mask_fill)


def shard_offset(shard_piece, block_index, whole_length, axis_at):
    shape_list = list(shard_piece.shape)
    shape_list[axis_at] = whole_length
    empty = jnp.zeros(tuple(shape_list), jnp.float32)
    return lax.dynamic_update_slice_in_dim(
        empty, shard_piece, block_index * shard_piece.shape[axis_at], axis_at
    )


def select_slice(whole_array, block_index, block_width, axis_at):
    return lax.dynamic_slice_in_dim(whole_array, block_index * block_width, block_width, axis_at)


def factor_step(
    gradient,
    rows_old,
    cols_old,
    rows_mine,
    cols_mine,
    rows_total,
    count_rows,
    count_cols,
    prior_total,
):
    decay_rate = 1.0 - STEP ** (-0.8)
    rows_new = decay_rate * rows_old + (1.0 - decay_rate) * (rows_mine / count_cols + square_eps)
    cols_new = decay_rate * cols_old + (1.0 - decay_rate) * (cols_mine / count_rows + square_eps)
    rows_average = (
        decay_rate * prior_total
        + (1.0 - decay_rate) * (rows_total / count_cols + count_rows * square_eps)
    ) / count_rows
    update = gradient * lax.rsqrt(rows_new[:, None] * cols_new[None, :] / rows_average)
    return (rows_new, cols_new, update, jnp.sum(update * update))


def plain_step(weight, gradient, moment_old):
    decay_rate = 1.0 - STEP ** (-0.8)
    moment = decay_rate * moment_old + (1.0 - decay_rate) * (gradient * gradient + square_eps)
    update = gradient * lax.rsqrt(moment)
    update_rms = jnp.sqrt(jnp.mean(update * update))
    rate_here = step_rate * jnp.sqrt(jnp.mean(weight * weight))
    return (weight - rate_here * update / jnp.maximum(1.0, update_rms / clip_limit), moment)


def generic(
    tokens_in,
    cotangent,
    patch_counts,
    w_qkv,
    w_out,
    w_up,
    w_down,
    layer_vector_rows,
    inner_biases,
    qkvrows_prior,
    qkvcols_prior,
    outrows_prior,
    outcols_prior,
    uprows_prior,
    upcols_prior,
    downrows_prior,
    downcols_prior,
    vector_moment,
    bias_moment,
):
    data_index = lax.axis_index("dp")
    parallel_model_index = lax.axis_index("mp")
    row_count, parallel_model_width = tokens_in.shape
    set_count, slot_count = patch_counts.shape
    set_rows = row_count // set_count
    shard_width_local = w_qkv.shape[2]
    local_hidden = w_up.shape[1]
    head_count = shard_width_local // HD
    score_scale = HD ** (-0.5)
    full_qkv, full_out, full_up, full_down = (
        lax.all_gather(w_qkv.astype(jnp.bfloat16), "dp", axis=0, tiled=True),
        lax.all_gather(w_out.astype(jnp.bfloat16), "dp", axis=1, tiled=True),
        lax.all_gather(w_up.astype(jnp.bfloat16), "dp", axis=0, tiled=True),
        lax.all_gather(w_down.astype(jnp.bfloat16), "dp", axis=1, tiled=True),
    )
    stream = tokens_in.astype(jnp.float32)
    segment = jax.vmap(lambda counts: segment_ids(counts, set_rows))(patch_counts)
    valid_rows = (segment < slot_count).astype(jnp.float32).reshape(row_count)
    centered_single, inverse_deviation_single = moments_of(stream)
    standardized_single = centered_single * inverse_deviation_single
    normalized_rows = (standardized_single * layer_vector_rows[0] + layer_vector_rows[1]).astype(
        jnp.bfloat16
    )
    bias_mine = select_slice(inner_biases, parallel_model_index, shard_width_local, 1)
    projected = jnp.einsum(
        "rd,dtc->rtc", normalized_rows, full_qkv, preferred_element_type=jnp.float32
    )
    query_rows = (projected[:, 0] + bias_mine[0]).astype(jnp.bfloat16)
    key_rows = projected[:, 1].astype(jnp.bfloat16)
    value_rows = (projected[:, 2] + bias_mine[1]).astype(jnp.bfloat16)

    def split_sets(field_in):
        return field_in.reshape(set_count, set_rows, head_count, HD)

    def attend(set_item):
        query_set, key_set, value_set, segment_set = set_item
        same_image = segment_set[:, None] == segment_set[None, :]
        raw_scores = scores_of(query_set, key_set, same_image, score_scale)
        row_top = jnp.max(raw_scores, axis=-1, keepdims=True)
        exponent = jnp.exp(raw_scores - row_top)
        row_total = jnp.sum(exponent, axis=-1, keepdims=True)
        weights = exponent / row_total
        mixed_set = jnp.einsum(
            "hqk,khd->qhd",
            weights.astype(jnp.bfloat16),
            value_set,
            preferred_element_type=jnp.float32,
        )
        return (mixed_set.astype(jnp.bfloat16), (row_top + jnp.log(row_total))[..., 0])

    mixed_heads, log_total = lax.map(
        attend, (split_sets(query_rows), split_sets(key_rows), split_sets(value_rows), segment)
    )
    mixed_heads = mixed_heads.reshape(row_count, shard_width_local)
    attn_terms = jnp.dot(mixed_heads, full_out, preferred_element_type=jnp.float32)
    proj = (
        lax.psum(attn_terms.astype(jnp.bfloat16), "mp").astype(jnp.float32) + layer_vector_rows[6]
    )
    shared_mask = shard_offset(
        jnp.ones((shard_width_local,), jnp.float32), parallel_model_index, parallel_model_width, 0
    )
    middle = stream + layer_vector_rows[4] * proj
    normed_here = normalize(middle, layer_vector_rows[2], layer_vector_rows[3]).astype(jnp.bfloat16)
    up_bias = select_slice(inner_biases[2:], parallel_model_index, shard_width_local, 1).T.reshape(
        local_hidden
    )
    hidden = jnp.dot(normed_here, full_up, preferred_element_type=jnp.float32) + up_bias
    active = jax.nn.gelu(hidden, approximate=False).astype(jnp.bfloat16)
    mlp_terms = jnp.dot(active, full_down, preferred_element_type=jnp.float32)
    branch = (
        lax.psum(mlp_terms.astype(jnp.bfloat16), "mp").astype(jnp.float32) + layer_vector_rows[7]
    )
    result = middle + layer_vector_rows[5] * branch
    result_low = result.astype(jnp.bfloat16)
    back_grad = cotangent.astype(jnp.float32) * valid_rows[:, None]
    d_branch = (back_grad * layer_vector_rows[5]).astype(jnp.bfloat16)
    down_part = jnp.einsum("rf,rd->fd", active, d_branch, preferred_element_type=jnp.float32)
    d_active = jnp.einsum("rd,fd->rf", d_branch, full_down, preferred_element_type=jnp.float32)
    gelu_out, gelu_pull = jax.vjp(lambda inputs: jax.nn.gelu(inputs, approximate=False), hidden)
    d_hidden = gelu_pull(d_active)[0].astype(jnp.bfloat16)
    up_part = jnp.einsum("rd,rf->df", normed_here, d_hidden, preferred_element_type=jnp.float32)
    mid_terms = jnp.einsum("rf,df->rd", d_hidden, full_up, preferred_element_type=jnp.float32)
    d_normed_two = lax.psum(mid_terms.astype(jnp.bfloat16), "mp").astype(jnp.float32)
    norm_out, norm_pull = jax.vjp(normalize, middle, layer_vector_rows[2], layer_vector_rows[3])
    d_through, d_gain_two, d_shift_two = norm_pull(d_normed_two)
    d_middle = back_grad + d_through
    d_proj_here = (d_middle * layer_vector_rows[4]).astype(jnp.bfloat16)
    d_middle_cols = select_slice(d_middle, parallel_model_index, shard_width_local, 1)
    out_part = jnp.einsum("rc,rd->cd", mixed_heads, d_proj_here, preferred_element_type=jnp.float32)
    d_mixed = jnp.einsum(
        "rd,cd->rc", d_proj_here, full_out, preferred_element_type=jnp.float32
    ).astype(jnp.bfloat16)

    def attend_back(set_item):
        query_set, key_set, value_set, segment_set, total_set, grad_set = set_item
        same_image = segment_set[:, None] == segment_set[None, :]
        raw_scores = scores_of(query_set, key_set, same_image, score_scale)
        weights = jnp.exp(raw_scores - total_set[..., None])
        d_value = jnp.einsum(
            "hqk,qhd->khd",
            weights.astype(jnp.bfloat16),
            grad_set,
            preferred_element_type=jnp.float32,
        )
        d_weights = jnp.einsum(
            "qhd,khd->hqk", grad_set, value_set, preferred_element_type=jnp.float32
        )
        d_scores = (
            weights * (d_weights - jnp.sum(d_weights * weights, axis=-1, keepdims=True))
        ).astype(jnp.bfloat16)
        d_query = (
            jnp.einsum("hqk,khd->qhd", d_scores, key_set, preferred_element_type=jnp.float32)
            * score_scale
        )
        d_key = (
            jnp.einsum("hqk,qhd->khd", d_scores, query_set, preferred_element_type=jnp.float32)
            * score_scale
        )
        return jnp.stack([d_query, d_key, d_value], axis=1).astype(jnp.bfloat16)

    d_projected = lax.map(
        attend_back,
        (
            split_sets(query_rows),
            split_sets(key_rows),
            split_sets(value_rows),
            segment,
            log_total,
            split_sets(d_mixed),
        ),
    )
    d_projected = d_projected.reshape(row_count, 3, shard_width_local)
    qkv_part = jnp.einsum(
        "rd,rtc->dtc", normalized_rows, d_projected, preferred_element_type=jnp.float32
    )
    normalized_gradient = lax.psum_scatter(
        jnp.einsum("rtc,dtc->rd", d_projected, full_qkv, preferred_element_type=jnp.float32).astype(
            jnp.bfloat16
        ),
        "mp",
        scatter_dimension=1,
        tiled=True,
    ).astype(jnp.float32)
    standardized_local = select_slice(
        standardized_single, parallel_model_index, shard_width_local, 1
    )
    local_gain_slice = select_slice(
        layer_vector_rows[0], parallel_model_index, shard_width_local, 0
    )
    standardized_gradient = normalized_gradient * local_gain_slice
    gradient_sum_local, product_sum_local = lax.psum(
        (
            jnp.sum(standardized_gradient, axis=1),
            jnp.sum(standardized_gradient * standardized_local, axis=1),
        ),
        "mp",
    )
    input_grad = d_middle_cols + inverse_deviation_single * (
        standardized_gradient
        - gradient_sum_local[:, None] / parallel_model_width
        - standardized_local * product_sum_local[:, None] / parallel_model_width
    )

    def mine(field_in):
        return select_slice(field_in, parallel_model_index, shard_width_local, field_in.ndim - 1)

    vector_part = jnp.stack(
        [
            shard_offset(
                jnp.sum(normalized_gradient * standardized_local, axis=0),
                parallel_model_index,
                parallel_model_width,
                0,
            ),
            shard_offset(
                jnp.sum(normalized_gradient, axis=0), parallel_model_index, parallel_model_width, 0
            ),
            d_gain_two * shared_mask,
            d_shift_two * shared_mask,
            jnp.sum(d_middle * proj, axis=0) * shared_mask,
            jnp.sum(back_grad * branch, axis=0) * shared_mask,
            shard_offset(
                jnp.sum(mine(d_proj_here).astype(jnp.float32), axis=0),
                parallel_model_index,
                parallel_model_width,
                0,
            ),
            shard_offset(
                jnp.sum(mine(d_branch).astype(jnp.float32), axis=0),
                parallel_model_index,
                parallel_model_width,
                0,
            ),
        ]
    )
    hidden_sums = (
        jnp.sum(d_hidden.astype(jnp.float32), axis=0)
        .reshape(shard_width_local, local_hidden // shard_width_local)
        .T
    )
    bias_part = jnp.concatenate(
        [
            jnp.sum(d_projected[:, 0].astype(jnp.float32), axis=0)[None],
            jnp.sum(d_projected[:, 2].astype(jnp.float32), axis=0)[None],
            hidden_sums,
        ],
        axis=0,
    )
    squares = jnp.stack(
        [
            jnp.sum(valid_rows[:, None] * shared_mask * field_in * field_in)
            for field_in in (result, layer_vector_rows[4] * proj, layer_vector_rows[5] * branch)
        ]
    )
    counted = jnp.where(parallel_model_index == 0, jnp.sum(valid_rows), 0.0)
    vector_grad, bias_grad, squares_all, counted_all = lax.psum(
        (
            vector_part,
            shard_offset(bias_part, parallel_model_index, parallel_model_width, 1),
            squares,
            counted,
        ),
        ("dp", "mp"),
    )
    token_spread = jnp.sqrt(squares_all / (counted_all * parallel_model_width))
    grad_parts = (qkv_part, out_part, up_part, down_part)
    summed = lax.psum((grad_parts[0], grad_parts[1], grad_parts[2], grad_parts[3]), "dp")
    qkv_grad = select_slice(summed[0], data_index, w_qkv.shape[0], 0)
    out_grad = select_slice(summed[1], data_index, w_out.shape[1], 1)
    up_grad = select_slice(summed[2], data_index, w_up.shape[0], 0)
    down_grad = select_slice(summed[3], data_index, w_down.shape[1], 1)
    square_qkv = qkv_grad * qkv_grad
    square_out = out_grad * out_grad
    square_up = up_grad * up_grad
    square_down = down_grad * down_grad
    scalars = jnp.stack(
        [
            jnp.sum(w_qkv * w_qkv),
            jnp.sum(w_out * w_out),
            jnp.sum(w_up * w_up),
            jnp.sum(w_down * w_down),
            jnp.where(parallel_model_index == 0, jnp.sum(qkvrows_prior), 0.0),
            jnp.where(data_index == 0, jnp.sum(outrows_prior), 0.0),
            jnp.where(parallel_model_index == 0, jnp.sum(uprows_prior), 0.0),
            jnp.where(data_index == 0, jnp.sum(downrows_prior), 0.0),
        ]
    )
    factor_totals = lax.psum(
        (
            shard_offset(jnp.sum(square_qkv, axis=(1, 2)), data_index, parallel_model_width, 0),
            shard_offset(
                jnp.sum(square_qkv, axis=0), parallel_model_index, parallel_model_width, 1
            ),
            shard_offset(
                jnp.sum(square_out, axis=1), parallel_model_index, parallel_model_width, 0
            ),
            shard_offset(jnp.sum(square_out, axis=0), data_index, parallel_model_width, 0),
            shard_offset(jnp.sum(square_up, axis=1), data_index, parallel_model_width, 0),
            shard_offset(jnp.sum(square_up, axis=0), parallel_model_index, FF, 0),
            shard_offset(jnp.sum(square_down, axis=1), parallel_model_index, FF, 0),
            shard_offset(jnp.sum(square_down, axis=0), data_index, parallel_model_width, 0),
            scalars,
        ),
        ("dp", "mp"),
    )
    (
        rows_qkv,
        cols_qkv,
        rows_out,
        cols_out,
        rows_up,
        cols_up,
        rows_down,
        cols_down,
        scalar_totals,
    ) = factor_totals
    local_rows = w_qkv.shape[0]
    local_cols = w_out.shape[1]
    qkvrows_after, qkvcols_flat, update_qkv, usq_qkv = factor_step(
        qkv_grad.reshape(local_rows, 3 * shard_width_local),
        qkvrows_prior,
        qkvcols_prior.reshape(3 * shard_width_local),
        select_slice(rows_qkv, data_index, local_rows, 0),
        select_slice(cols_qkv, parallel_model_index, shard_width_local, 1).reshape(
            3 * shard_width_local
        ),
        jnp.sum(rows_qkv),
        parallel_model_width,
        3 * parallel_model_width,
        scalar_totals[4],
    )
    outrows_after, outcols_after, update_out, usq_out = factor_step(
        out_grad,
        outrows_prior,
        outcols_prior,
        select_slice(rows_out, parallel_model_index, shard_width_local, 0),
        select_slice(cols_out, data_index, local_cols, 0),
        jnp.sum(rows_out),
        parallel_model_width,
        parallel_model_width,
        scalar_totals[5],
    )
    uprows_after, upcols_after, update_up, usq_up = factor_step(
        up_grad,
        uprows_prior,
        upcols_prior,
        select_slice(rows_up, data_index, local_rows, 0),
        select_slice(cols_up, parallel_model_index, local_hidden, 0),
        jnp.sum(rows_up),
        parallel_model_width,
        FF,
        scalar_totals[6],
    )
    downrows_after, downcols_after, update_down, usq_down = factor_step(
        down_grad,
        downrows_prior,
        downcols_prior,
        select_slice(rows_down, parallel_model_index, local_hidden, 0),
        select_slice(cols_down, data_index, local_cols, 0),
        jnp.sum(rows_down),
        FF,
        parallel_model_width,
        scalar_totals[7],
    )
    usq_totals = lax.psum(jnp.stack([usq_qkv, usq_out, usq_up, usq_down]), ("dp", "mp"))
    entry_counts = jnp.array(
        [
            3.0 * parallel_model_width * parallel_model_width,
            1.0 * parallel_model_width * parallel_model_width,
            1.0 * parallel_model_width * FF,
            1.0 * FF * parallel_model_width,
        ],
        jnp.float32,
    )
    update_scale = jnp.sqrt(usq_totals / entry_counts)
    weight_rms = jnp.sqrt(scalar_totals[:4] / entry_counts)
    limits = jnp.maximum(1.0, update_scale / clip_limit)
    qkv_after = (
        w_qkv.reshape(local_rows, 3 * shard_width_local)
        - step_rate * weight_rms[0] * update_qkv / limits[0]
    ).reshape(w_qkv.shape)
    out_after = w_out - step_rate * weight_rms[1] * update_out / limits[1]
    up_after = w_up - step_rate * weight_rms[2] * update_up / limits[2]
    down_after = w_down - step_rate * weight_rms[3] * update_down / limits[3]
    vectors_after, moment_vectors = jax.vmap(plain_step)(
        layer_vector_rows, vector_grad, vector_moment
    )
    heads_after, heads_moment = jax.vmap(plain_step)(
        inner_biases[:2], bias_grad[:2], bias_moment[:2]
    )
    upper_after, upper_moment = plain_step(
        inner_biases[2:].reshape(FF), bias_grad[2:].reshape(FF), bias_moment[2:].reshape(FF)
    )
    biases_after = jnp.concatenate(
        [heads_after, upper_after.reshape(FF // parallel_model_width, parallel_model_width)], axis=0
    )
    moment_biases = jnp.concatenate(
        [heads_moment, upper_moment.reshape(FF // parallel_model_width, parallel_model_width)],
        axis=0,
    )
    return (
        result_low,
        input_grad,
        qkv_grad,
        out_grad,
        up_grad,
        down_grad,
        qkv_after,
        out_after,
        up_after,
        down_after,
        qkv_after.astype(jnp.bfloat16),
        out_after.astype(jnp.bfloat16),
        up_after.astype(jnp.bfloat16),
        down_after.astype(jnp.bfloat16),
        qkvrows_after,
        qkvcols_flat.reshape(3, shard_width_local),
        outrows_after,
        outcols_after,
        uprows_after,
        upcols_after,
        downrows_after,
        downcols_after,
        vector_grad,
        bias_grad,
        moment_vectors,
        moment_biases,
        vectors_after,
        biases_after,
        update_scale,
        token_spread,
    )

def shards(
    tokens_in,
    cotangent,
    patch_counts,
    w_qkv,
    w_out,
    w_up,
    w_down,
    layer_vector_rows,
    inner_biases,
    qkvrows_prior,
    qkvcols_prior,
    outrows_prior,
    outcols_prior,
    uprows_prior,
    upcols_prior,
    downrows_prior,
    downcols_prior,
    vector_moment,
    bias_moment,
):
    n_dp, n_mp = lax.axis_size("dp"), lax.axis_size("mp")
    row_count, width = tokens_in.shape
    set_count, slot_count = patch_counts.shape
    set_rows = row_count // set_count
    own_rows = row_count // n_mp
    window = own_rows + HALO
    share, hidden_width, block_rows = w_qkv.shape[2], w_up.shape[1], w_up.shape[0]
    f32, low = jnp.float32, jnp.bfloat16
    vmem = pl.BlockSpec(memory_space=pltpu.VMEM)
    anywhere = pl.BlockSpec(memory_space=pl.ANY)
    scalars_in = pl.BlockSpec(memory_space=pltpu.SMEM)
    dma = pltpu.SemaphoreType.DMA
    held = pltpu.VMEM

    def shape(*dims, dtype=low):
        return jax.ShapeDtypeStruct(dims, dtype)

    masters, reduced, sums, sub_new, lane_new, scalar_rows, input_parts, stream = pl.pallas_call(
        functools.partial(layer_kernel, n_dp, n_mp, slot_count, own_rows),
        out_shape=(
            shape(GROUPS, block_rows, width, dtype=f32),
            shape(GROUPS, block_rows, width, dtype=f32),
            shape(16, width, dtype=f32),
            shape(8, LANES, dtype=f32),
            shape(8, width, dtype=f32),
            shape(8, LANES, dtype=f32),
            shape(n_mp, share, own_rows),
            shape(n_mp, own_rows, width),
        ),
        in_specs=[anywhere] * 2 + [vmem] * 4 + [scalars_in] + [vmem] * 10,
        out_specs=(vmem,) * 6 + (anywhere,) * 2,
        scratch_shapes=[
            held((GROUPS, n_mp, n_dp // 2, 2, block_rows, width), low),
            held((set_rows, width), low),
            held((window, width), low),
            held((n_mp, set_rows, width), low),
            held((n_mp, own_rows, hidden_width), low),
            held((n_mp, window, hidden_width), low),
            held((n_mp, window, 2 * LANES), low),
            held((window, width), f32),
            held((window, width), low),
            held((width, own_rows), low),
            held((width, own_rows), low),
            held((width, own_rows), low),
            held((own_rows, width), f32),
            held((window, width), low),
            held((window, width), f32),
            held((own_rows, width), low),
            held((set_rows, LANES), low),
            held((set_rows, LANES), low),
            held((window, 2 * LANES), low),
            held((window, 3 * LANES), f32),
            held((window, 2 * LANES), low),
            held((8, width), f32),
            held((16, width), f32),
            held((8, width), f32),
            held((8, LANES), f32),
            held((3, width), f32),
            held((RING, n_dp // 2, block_rows, width), low),
            held((GROUPS, n_mp, 2, block_rows // 2, width), low),
            held((GROUPS, n_mp, block_rows, width), low),
            held((GROUPS, n_mp, block_rows, width), low),
            held((GROUPS, n_mp + 1, block_rows, width), low),
            held((6, 16, width), f32),
            held((5, 16, width), f32),
            held((n_mp, 8, LANES), f32),
            held((n_dp, 2, width), f32),
            held((n_mp, 8, LANES), f32),
            held((n_dp, 1, width), f32),
            held((n_mp, 8, LANES), f32),
            held((n_dp, 8, LANES), f32),
            pltpu.SemaphoreType.REGULAR,
            dma((4,)),
            dma((GROUPS, n_mp, KINDS)),
            dma((GROUPS, n_mp, KINDS)),
            dma((GROUPS, n_mp, 2)),
            dma((GROUPS, n_mp, R_KINDS)),
            dma((GROUPS, n_mp, R_KINDS)),
            dma((2, n_mp, Stream.CUTS)),
            dma((n_mp, Stream.CUTS)),
            dma((n_mp,)),
            dma((n_mp,)),
            dma((5,)),
            dma((5,)),
            dma((6, max(n_dp, n_mp))),
            dma((6, max(n_dp, n_mp))),
        ],
        compiler_params=pltpu.CompilerParams(
            collective_id=1, has_side_effects=True, vmem_limit_bytes=63 * 2**20
        ),
    )(
        tokens_in, cotangent, w_qkv.transpose(1, 0, 2), w_out, w_up, w_down.T, patch_counts, layer_vector_rows,
        inner_biases, qkvrows_prior, qkvcols_prior, outrows_prior, outcols_prior, uprows_prior, upcols_prior,
        downrows_prior, downcols_prior,
    )

    def both(*dims):
        return (shape(*dims, dtype=f32),) * 2 + (shape(*dims),)

    kinds = [
        both(3, block_rows, share), both(share, block_rows), both(block_rows, width), both(block_rows, width)
    ]
    small = [
        (block_rows,), (3, share), (share,), (block_rows,),
        (block_rows,), (hidden_width,), (hidden_width,), (block_rows,),
    ] + [(8, width), (6, width)] * 3 + [(4,), (3,)]
    outs = pl.pallas_call(
        functools.partial(update_kernel, n_dp, n_mp),
        out_shape=(
            shape(n_mp, own_rows, width),
            shape(share, row_count, dtype=f32),
            *(kind[i] for i in range(3) for kind in kinds),
            *(shape(*dims, dtype=f32) for dims in small),
        ),
        in_specs=[vmem] * 11 + [anywhere],
        out_specs=(anywhere,) + (vmem,) * 29,
        scratch_shapes=[pltpu.VMEM((n_mp, own_rows, width), low), dma((2,))],
        compiler_params=pltpu.CompilerParams(vmem_limit_bytes=60 * 2**20),
    )(
        reduced, masters, sub_new, lane_new, scalar_rows, sums, layer_vector_rows, inner_biases, vector_moment,
        bias_moment, input_parts, stream,
    )
    weights = [
        part for i in (2, 6, 10) for part in (outs[i].transpose(1, 0, 2), outs[i + 1], outs[i + 2], outs[i + 3].T)
    ]
    return (outs[0].reshape(row_count, width), outs[1].T, *weights, *outs[14:])

def solution(mesh):
    in_specs = (
        P("dp", None),
        P("dp", None),
        P("dp", None),
        P("dp", None, "mp"),
        P("mp", "dp"),
        P("dp", "mp"),
        P("mp", "dp"),
        P(),
        P(),
        P("dp"),
        P(None, "mp"),
        P("mp"),
        P("dp"),
        P("dp"),
        P("mp"),
        P("mp"),
        P("dp"),
        P(),
        P(),
    )
    out_specs = (
        P("dp", None),
        P("dp", "mp"),
        P("dp", None, "mp"),
        P("mp", "dp"),
        P("dp", "mp"),
        P("mp", "dp"),
        P("dp", None, "mp"),
        P("mp", "dp"),
        P("dp", "mp"),
        P("mp", "dp"),
        P("dp", None, "mp"),
        P("mp", "dp"),
        P("dp", "mp"),
        P("mp", "dp"),
        P("dp"),
        P(None, "mp"),
        P("mp"),
        P("dp"),
        P("dp"),
        P("mp"),
        P("mp"),
        P("dp"),
        P(),
        P(),
        P(),
        P(),
        P(),
        P(),
        P(),
        P(),
    )
    fits = mesh.shape["dp"] == 8 and mesh.shape["mp"] == 4
    return jax.shard_map(shards if fits else generic, mesh=mesh, in_specs=in_specs, out_specs=out_specs, check_vma=False)
```

```python
import functools

import jax
import jax.numpy as jnp
from jax import lax
from jax.experimental import pallas as pl
from jax.experimental.pallas import tpu as pltpu
from jax.sharding import PartitionSpec as P

HD = 64
FF = 3072
STEP = 3


norm_eps = 1e-06
square_eps = 1e-30
clip_limit = 0.5
step_rate = 0.6
mask_fill = -1000000000.0


MESH = pl.DeviceIdType.MESH
HALO = 128
GROUPS = 3

def neighbours(dp):
    core = dp % 2
    return dp + 1 - 2 * core, dp + 2 - 4 * ((dp // 2) % 2), (dp + 4) % 8, (dp + 4) % 8 + 2 - 4 * ((dp // 2) % 2)


def flip(dp):
    return dp + 1 - 2 * (dp % 2)


def greet(devices, extra):
    barrier = pltpu.get_barrier_semaphore()
    for device in devices:
        pl.semaphore_signal(barrier, inc=1, device_id=device, device_id_type=MESH)
    for condition, device in extra:

        @pl.when(condition)
        def _():
            pl.semaphore_signal(barrier, inc=1, device_id=device, device_id_type=MESH)

    peers = len(devices)
    for condition, _ in extra:
        peers = peers + jnp.where(condition, 1, 0)
    pl.semaphore_wait(barrier, peers)


A_Z, A_X, A_Y, A_D0, A_D1, A_S, A_SX, A_SY, A_SD0, A_SD1 = range(10)
KINDS = 10
ORDERS = ((0, 1, 2, 3), (1, 0, 2, 3), (2, 3, 1, 0), (3, 2, 1, 0))


def plane_at(mp, unit):
    codes = [sum(plane * 4**i for i, plane in enumerate(order)) for order in ORDERS]
    code = jnp.where(mp == 0, codes[0], jnp.where(mp == 1, codes[1], jnp.where(mp == 2, codes[2], codes[3])))
    power = jnp.where(unit == 0, 1, jnp.where(unit == 1, 4, jnp.where(unit == 2, 16, 64)))
    return (code // power) % 4

class Gather:
    def __init__(self, n_mp, out, send_sems, recv_sems, way_sems):
        self.dp, self.mp, self.n_mp = lax.axis_index("dp"), lax.axis_index("mp"), n_mp
        self.out, self.send_sems, self.recv_sems, self.way_sems = out, send_sems, recv_sems, way_sems
        self.sib, self.xn, self.yn, self.dn = neighbours(self.dp)
        self.rows = out.shape[4]
        self.up, self.down = jnp.minimum(self.mp + 1, n_mp - 1), jnp.maximum(self.mp - 1, 0)
        self.inner = jnp.where((self.mp > 0) & (self.mp < n_mp - 1), 1, 0)
        half = self.rows // 2
        self.all, self.low, self.high = pl.ds(0, self.rows), pl.ds(0, half), pl.ds(half, half)

    def message(self, kind, group, plane, slot, part, device):
        where = self.out.at[group, plane, slot // 2, slot % 2, part]
        return pltpu.make_async_remote_copy(
            src_ref=where,
            dst_ref=where,
            send_sem=self.send_sems.at[group, plane, kind],
            recv_sem=self.recv_sems.at[group, plane, kind],
            device_id=(device, self.mp),
            device_id_type=MESH,
        )

    def along(self, group, plane, way):
        where = self.out.at[group, plane, self.dp // 2, self.dp % 2]
        return pltpu.make_async_remote_copy(
            src_ref=where,
            dst_ref=where,
            send_sem=self.way_sems.at[group, plane, way],
            recv_sem=self.recv_sems.at[group, plane, A_Z],
            device_id=(self.dp, self.down if way else self.up),
            device_id_type=MESH,
        )

    def sends(self, group, plane):
        dp, xn, yn, dn, sib = self.dp, self.xn, self.yn, self.dn, self.sib
        first = [(A_X, dp, self.all, xn), (A_Y, dp, self.all, yn), (A_S, dp, self.all, sib)]
        second = [(A_D0, xn, self.low, yn), (A_SX, xn, self.all, sib), (A_D1, yn, self.high, xn), (A_SY, yn, self.all, sib)]
        third = [(A_SD0, dn, self.low, sib), (A_SD1, dn, self.high, sib)]
        return [
            [functools.partial(self.message, kind, group, plane, *rest) for kind, *rest in part]
            for part in (first, second, third)
        ]

    def unit(self, t):
        rest = t - self.n_mp
        group = jnp.where(rest < 0, 0, 1 + t % 2)
        return group, plane_at(self.mp, jnp.where(rest < 0, t, rest // 2))

    def guarded(self, t, action):
        if isinstance(t, int):
            if 0 <= t < GROUPS * self.n_mp:
                action(*self.unit(t))
            return

        @pl.when((t >= 0) & (t < GROUPS * self.n_mp))
        def _():
            action(*self.unit(t))

    def stage_z(self, t):
        def action(group, plane):
            @pl.when(plane != self.mp)
            def _():
                self.along(group, plane, 0).wait_recv()

            @pl.when((plane <= self.mp) & (self.mp < self.n_mp - 1))
            def _():
                self.along(group, plane, 0).start()

            @pl.when((plane >= self.mp) & (self.mp > 0))
            def _():
                self.along(group, plane, 1).start()

        self.guarded(t, action)

    def stage_a(self, t):
        def action(group, plane):
            for copy in self.sends(group, plane)[0]:
                copy().start()

        self.guarded(t, action)

    def stage_b(self, t):
        def action(group, plane):
            out = self.sends(group, plane)[1]
            self.message(A_X, group, plane, self.xn, self.all, self.xn).wait_recv()
            out[0]().start()
            out[1]().start()
            self.message(A_Y, group, plane, self.yn, self.all, self.yn).wait_recv()
            out[2]().start()
            out[3]().start()

        self.guarded(t, action)

    def stage_c(self, t):
        def action(group, plane):
            out = self.sends(group, plane)[2]
            self.message(A_D0, group, plane, self.dn, self.low, self.yn).wait_recv()
            out[0]().start()
            self.message(A_D1, group, plane, self.dn, self.high, self.xn).wait_recv()
            out[1]().start()

        self.guarded(t, action)

    def stage_d(self, t):
        def action(group, plane):
            for kind, slot, part in (
                (A_S, self.sib, self.all),
                (A_SX, flip(self.xn), self.all),
                (A_SY, flip(self.yn), self.all),
                (A_SD0, flip(self.dn), self.low),
                (A_SD1, flip(self.dn), self.high),
            ):
                self.message(kind, group, plane, slot, part, self.sib).wait_recv()

        self.guarded(t, action)

    def plane(self, u):
        return plane_at(self.mp, u)

    def begin(self):
        for t in (0, 1):
            self.stage_z(t)
            self.stage_a(t)

        @pl.when(self.inner == 1)
        def _():
            self.stage_z(2)

    def step(self, s):
        self.stage_b(s)
        ahead = (2,)
        for more in ahead:
            self.stage_z(s + more + self.inner)
            self.stage_a(s + more)
        self.stage_c(s - 1)

    def finish(self, t):
        def action(group, plane):
            for part in self.sends(group, plane):
                for copy in part:
                    copy().wait_send()

            @pl.when((plane <= self.mp) & (self.mp < self.n_mp - 1))
            def _():
                self.along(group, plane, 0).wait_send()

            @pl.when((plane >= self.mp) & (self.mp > 0))
            def _():
                self.along(group, plane, 1).wait_send()

        self.guarded(t, action)

R_S, R_D0, R_D1, R_X, R_Y, R_UP, R_DOWN = range(7)
R_KINDS = 7
RING = 4


class Scatter:
    def __init__(self, n_mp, blocks, out, bufs, credit, send_sems, recv_sems):
        self.dp, self.mp, self.n_mp = lax.axis_index("dp"), lax.axis_index("mp"), n_mp
        self.blocks, self.out, self.credit = blocks, out, credit
        self.pair_in, self.halves_in, self.x_in, self.y_in, self.z_in = bufs
        self.send_sems, self.recv_sems = send_sems, recv_sems
        self.sib, self.xn, self.yn, self.dn = neighbours(self.dp)
        self.core = self.dp % 2
        self.here, self.at_x, self.at_y, self.at_d = self.dp // 2, self.xn // 2, self.yn // 2, self.dn // 2
        self.up, self.down = jnp.minimum(self.mp + 1, n_mp - 1), jnp.maximum(self.mp - 1, 0)
        rows = out.shape[1]
        self.all, self.low, self.high = pl.ds(0, rows), pl.ds(0, rows // 2), pl.ds(rows // 2, rows // 2)
        self.fed = 2 * n_mp
        self.units = GROUPS * n_mp

    def offered(self, o):
        if isinstance(o, int) and o >= self.fed:
            return 0, plane_at(self.mp, self.units - 1 - o)
        return 2 - o % 2, plane_at(self.mp, o // 2)

    def unit(self, k):
        if isinstance(k, int) and k >= self.fed:
            return 0, plane_at(self.mp, self.units - 1 - k)
        return 2 - k % 2, plane_at(self.mp, self.n_mp - 1 - k // 2)

    def remote(self, kind, group, plane, src, dst, device):
        return pltpu.make_async_remote_copy(
            src_ref=src,
            dst_ref=dst,
            send_sem=self.send_sems.at[group, plane, kind],
            recv_sem=self.recv_sems.at[group, plane, kind],
            device_id=device,
            device_id_type=MESH,
        )

    def pair(self, o, group, plane):
        return self.remote(
            R_S, group, plane, self.blocks.at[group, plane, :, 1 - self.core], self.pair_in.at[o % RING], (self.sib, self.mp)
        )

    def mine(self, group, plane, place, part=None):
        return self.blocks.at[group, plane, place, self.core, self.all if part is None else part]

    def message(self, kind, group, plane):
        mp = self.mp
        if kind == R_D0:
            src, dst = self.mine(group, plane, self.at_d, self.low), self.halves_in.at[group, plane, 0]
            device = (self.xn, mp)
        elif kind == R_D1:
            src, dst = self.mine(group, plane, self.at_d, self.high), self.halves_in.at[group, plane, 1]
            device = (self.yn, mp)
        elif kind == R_X:
            src, dst, device = self.mine(group, plane, self.at_x), self.x_in.at[group, plane], (self.xn, mp)
        elif kind == R_Y:
            src, dst, device = self.mine(group, plane, self.at_y), self.y_in.at[group, plane], (self.yn, mp)
        elif kind == R_UP:
            src, dst, device = self.mine(group, plane, self.here), self.z_in.at[group, plane], (self.dp, self.up)
        else:
            slot = jnp.where(plane == mp - 1, self.n_mp, plane)
            src, dst, device = self.mine(group, plane, self.here), self.z_in.at[group, slot], (self.dp, self.down)
        return self.remote(kind, group, plane, src, dst, device)

    def from_above(self, group, plane):
        slot = jnp.where(plane == self.mp, self.n_mp, plane)
        return slot, self.remote(
            R_DOWN, group, plane, self.mine(group, plane, self.here), self.z_in.at[group, slot], (self.dp, self.down)
        )

    def offer(self, o, group, plane):
        if isinstance(o, int):
            if o >= RING:
                pl.semaphore_wait(self.credit, 1)
        else:

            @pl.when(o >= RING)
            def _():
                pl.semaphore_wait(self.credit, 1)

        self.pair(o, group, plane).start()

    def add_pair(self, o, group, plane):
        self.pair(o, group, plane).wait_recv()
        self.blocks[group, plane, :, self.core] = self.blocks[group, plane, :, self.core] + self.pair_in[o % RING]

        @pl.when(o < self.units - RING)
        def _():
            pl.semaphore_signal(self.credit, inc=1, device_id=(self.sib, self.mp), device_id_type=MESH)

        self.message(R_D0, group, plane).start()
        self.message(R_D1, group, plane).start()

    def add_halves(self, group, plane):
        for kind, place, part, slot in ((R_D0, self.at_y, self.low, 0), (R_D1, self.at_x, self.high, 1)):
            self.message(kind, group, plane).wait_recv()
            where = self.mine(group, plane, place, part)
            where[...] = where[...] + self.halves_in[group, plane, slot]
        self.message(R_X, group, plane).start()
        self.message(R_Y, group, plane).start()

    def add_plane(self, group, plane):
        f32, mp, last = jnp.float32, self.mp, self.n_mp - 1
        self.message(R_X, group, plane).wait_recv()
        self.message(R_Y, group, plane).wait_recv()
        where = self.mine(group, plane, self.here)
        total = (
            where[...].astype(f32) + self.x_in[group, plane].astype(f32) + self.y_in[group, plane].astype(f32)
        )

        @pl.when(plane == mp)
        def _():
            self.out[(group + 2) % 3] = total

        @pl.when(plane != mp)
        def _():
            where[...] = total.astype(jnp.bfloat16)

        @pl.when((plane > mp) & (mp == 0))
        def _():
            self.message(R_UP, group, plane).start()

        @pl.when((plane < mp) & (mp == last))
        def _():
            self.message(R_DOWN, group, plane).start()

    def add_along(self, group, plane):
        f32, mp, last = jnp.float32, self.mp, self.n_mp - 1
        where = self.mine(group, plane, self.here)

        def add():
            where[...] = (where[...].astype(f32) + self.z_in[group, plane].astype(f32)).astype(jnp.bfloat16)

        @pl.when((plane > mp) & (mp > 0))
        def _():
            self.message(R_UP, group, plane).wait_recv()
            add()
            self.message(R_UP, group, plane).start()

        @pl.when((plane < mp) & (mp < last))
        def _():
            self.from_above(group, plane)[1].wait_recv()
            add()
            self.message(R_DOWN, group, plane).start()

        @pl.when((plane == mp) & (mp > 0))
        def _():
            self.message(R_UP, group, plane).wait_recv()
            self.out[(group + 2) % 3] += self.z_in[group, plane].astype(f32)

        @pl.when((plane == mp) & (mp < last))
        def _():
            slot, copy = self.from_above(group, plane)
            copy.wait_recv()
            self.out[(group + 2) % 3] += self.z_in[group, slot].astype(f32)

    def slot(self, k):
        def do(action, j):
            if isinstance(j, int):
                if 0 <= j < self.units:
                    action(*self.unit(j))
                return

            @pl.when(j >= 0)
            def _():
                action(*self.unit(j))

        do(self.add_halves, k)
        do(self.add_plane, k - 1)
        do(self.add_along, k - 2)

    def finish(self):
        def body(t, _):
            group, plane = t // self.n_mp, t % self.n_mp
            self.pair(0, group, plane).wait_send()
            for kind in (R_D0, R_D1, R_X, R_Y):
                self.message(kind, group, plane).wait_send()

            @pl.when(plane > self.mp)
            def _():
                self.message(R_UP, group, plane).wait_send()

            @pl.when(plane < self.mp)
            def _():
                self.message(R_DOWN, group, plane).wait_send()

            return 0

        lax.fori_loop(0, self.units, body, 0)

LANES = 128
NN = (((1,), (0,)), ((), ()))
NT = (((1,), (1,)), ((), ()))
BIG = 2.0**36


def mm(left, right, dims=NN):
    return lax.dot_general(left, right, dims, preferred_element_type=jnp.float32)


def gelu_parts(t):
    k = 1.0 / (1.0 + 0.2316419 * jnp.abs(t))
    series = k * (
        0.319381530 + k * (-0.356563782 + k * (1.781477937 + k * (-1.821255978 + k * 1.330274429)))
    )
    density = 0.3989422804014327 * jnp.exp(-0.5 * t * t)
    tail = density * series
    phi = jnp.where(t >= 0.0, 1.0 - tail, tail)
    return t * phi, phi + t * density


def row_stats(x):
    width = x.shape[1]
    center = x - jnp.sum(x, axis=1, keepdims=True) * (1.0 / width)
    spread = jnp.sum(center * center, axis=1, keepdims=True) * (1.0 / width)
    inverse = lax.rsqrt(spread + norm_eps)
    return center * inverse, inverse


def image_ends(counts_ref, set_index, slots):
    lane = lax.broadcasted_iota(jnp.int32, (8, LANES), 1) % (LANES // 2)
    low = jnp.zeros((8, LANES), jnp.int32)
    high = jnp.zeros((8, LANES), jnp.int32)
    edge = jnp.int32(0)
    for slot in range(slots + 1):
        after = jnp.int32(1 << 20) if slot == slots else edge + counts_ref[set_index, slot]
        low = jnp.where(lane == slot, edge, low)
        high = jnp.where(lane == slot, after, high)
        edge = after if slot < slots else edge
    return low[0:1], high[0:1], edge


def own_row(hidden_half, tile):
    lane = lax.broadcasted_iota(jnp.int32, tile.shape, 1)
    return (lane < LANES // 2) if hidden_half == 0 else (lane >= LANES // 2)


def keep_half(half, tile, other):
    return jnp.where(own_row(half, tile), tile, other)


HEAD_TILES = ((0, 128, 256, 0, 0), (0, 128, 256, 1, 1), (512, 640, 640, 0, 1))
MIX = 384


def make_features(counts_ref, set_index, slots, set_rows, feat_q, feat_k):
    low, high, total = image_ends(counts_ref, set_index, slots)
    step = 256

    def body(i, _):
        at = pl.ds(pl.multiple_of(i * step, step), step)
        row = lax.broadcasted_iota(jnp.int32, (step, LANES), 0) + i * step
        same = (row >= low) & (row < high)
        lane = lax.broadcasted_iota(jnp.int32, (step, LANES), 1) % (LANES // 2)
        feat_k[at] = jnp.where(same, 1.0, 0.0).astype(jnp.bfloat16)
        feat_q[at] = jnp.where(same | (lane > slots), 0.0, -BIG).astype(jnp.bfloat16)
        return 0

    lax.fori_loop(0, set_rows // step, body, 0)
    return total


def attend(m, qkv, mixed, feat_q, feat_k, window_start, window, step):
    keys, values = [], []
    for q_at, k_at, v_at, half, v_half in HEAD_TILES:
        keys.append(keep_half(half, qkv[m, :, k_at : k_at + LANES], feat_k[...]))
        tile = qkv[m, :, v_at : v_at + LANES]
        values.append(keep_half(v_half, tile, jnp.ones_like(tile)))

    def block(i, _):
        at = pl.ds(pl.multiple_of(window_start + i * step, LANES // 2), step)
        outs = []
        for head, (q_at, k_at, v_at, half, v_half) in enumerate(HEAD_TILES):
            query = keep_half(half, qkv[m, at, q_at : q_at + LANES], feat_q[at])
            scores = mm(query, keys[head], NT)
            top = jnp.max(scores, axis=1, keepdims=True)
            weights = jnp.exp2((scores - top) * (HD ** (-0.5) * 1.4426950408889634)).astype(jnp.bfloat16)
            out = mm(weights, values[head])
            outs.append(out / pltpu.roll(out, LANES // 2, 1))
        here = pl.ds(pl.multiple_of(i * step, LANES // 2), step)
        low = jnp.bfloat16
        mixed[m, here, 0:LANES] = keep_half(0, outs[0], outs[1]).astype(low)
        mixed[m, here, LANES : 2 * LANES] = keep_half(1, outs[2], jnp.zeros_like(outs[2])).astype(low)
        return 0

    lax.fori_loop(0, window // step, block, 0)


TN = (((0,), (0,)), ((), ()))


def norm_grad(x, gain, grad):
    width = x.shape[1]
    unit, inverse = row_stats(x)
    e = grad * gain
    mean_e = jnp.sum(e, axis=1, keepdims=True) * (1.0 / width)
    mean_eu = jnp.sum(e * unit, axis=1, keepdims=True) * (1.0 / width)
    return inverse * (e - mean_e - unit * mean_eu), grad * unit


def attend_back(m, qkv, d_mixed, feat_q, feat_k, window_start, window, acc, d_query):
    band = 3 * LANES
    acc[...] = jnp.zeros_like(acc)
    low = jnp.bfloat16
    scale = HD ** (-0.5)

    def block(b, _):
        start = jnp.clip(b - 1, 0, window // LANES - 3) * LANES
        keys_at = pl.ds(pl.multiple_of(start, LANES), band)
        keys_in = pl.ds(pl.multiple_of(window_start + start, LANES), band)
        here = pl.ds(pl.multiple_of(b * LANES, LANES), LANES)
        rows_in = pl.ds(pl.multiple_of(window_start + b * LANES, LANES), LANES)
        f_q, f_k = feat_q[rows_in], feat_k[keys_in]
        got = []
        for head, (q_at, k_at, v_at, half, v_half) in enumerate(HEAD_TILES):
            q_tile = qkv[m, rows_in, q_at : q_at + LANES]
            k_tile = qkv[m, keys_in, k_at : k_at + LANES]
            v_tile = qkv[m, keys_in, v_at : v_at + LANES]
            mix_at = 0 if head < 2 else LANES
            d_tile = d_mixed[here, mix_at : mix_at + LANES]
            d_out = keep_half(v_half, d_tile, jnp.zeros_like(d_tile))
            scores = mm(keep_half(half, k_tile, f_k), keep_half(half, q_tile, f_q), NT)
            top = jnp.max(scores, axis=0, keepdims=True)
            weights = jnp.exp((scores - top) * scale)
            weights = weights * (1.0 / jnp.sum(weights, axis=0, keepdims=True))
            d_weights = mm(v_tile, d_out, NT)
            delta = jnp.sum(d_weights * weights, axis=0, keepdims=True)
            d_scores = (weights * (d_weights - delta)).astype(low)
            d_key = mm(d_scores, keep_half(half, q_tile * scale, jnp.zeros_like(q_tile)))
            d_value = mm(weights.astype(low), d_out)
            d_q = mm(d_scores, keep_half(half, k_tile * scale, jnp.zeros_like(k_tile)), TN)
            got.append((d_q, d_key, d_value))
        acc[keys_at, 0:LANES] += got[0][1] + got[1][1]
        acc[keys_at, LANES : 2 * LANES] += got[0][2] + got[1][2]
        acc[keys_at, 2 * LANES : 3 * LANES] += got[2][1] + got[2][2]
        d_query[here, 0:LANES] = (got[0][0] + got[1][0]).astype(low)
        d_query[here, LANES : 2 * LANES] = got[2][0].astype(low)
        return 0

    lax.fori_loop(0, window // LANES, block, 0, unroll=True)

def tile_rows(i, first=0):
    return pl.ds(pl.multiple_of(first + i * LANES, LANES), LANES)


def column_sum(v):
    return jnp.sum(v, axis=0, keepdims=True)


class Place:
    def __init__(self, set_rows, own_rows):
        self.set_rows, self.own_rows, self.window = set_rows, own_rows, own_rows + HALO
        mp = lax.axis_index("mp")
        per_set = set_rows // own_rows
        self.set_index, part = mp // per_set, mp % per_set
        self.window_start = pl.multiple_of(part * (set_rows - self.window), LANES)
        self.own_start = pl.multiple_of(part * (self.window - own_rows), LANES)
        self.own = pl.ds(self.own_start, own_rows)
        self.own_set = pl.ds(pl.multiple_of(self.window_start + self.own_start, LANES), own_rows)
        self.tiles = self.window // LANES

    def is_own(self, i):
        first = i * LANES
        return jnp.where((first >= self.own_start) & (first < self.own_start + self.own_rows), 1.0, 0.0)

    def valid(self, i, total):
        row = lax.broadcasted_iota(jnp.int32, (LANES, 1), 0) + (self.window_start + i * LANES)
        return jnp.where(row < total, 1.0, 0.0)


def pack_first(qkv, out, packed):
    out_t = out[...].T
    for i in range(3):
        packed[:, i * LANES : (i + 1) * LANES] = qkv[i, :, 0:LANES]
    packed[:, MIX : MIX + LANES] = out_t[:, 0:LANES]
    tails = [qkv[i, :, LANES:] for i in range(3)]
    packed[:, 512:640] = jnp.concatenate([tails[0], out_t[:, LANES:]], axis=1)
    packed[:, 640:768] = jnp.concatenate([tails[1], tails[2]], axis=1)


def pack_lanes(qkv_rows, out_row):
    heads = [row[:, 0:LANES] for row in (*qkv_rows, out_row)]
    q, k, v, o = [row[:, LANES:] for row in (*qkv_rows, out_row)]
    return jnp.concatenate([*heads, q, o, k, v], axis=1)


def unpack_lanes(row):
    at = ((0, 512), (128, 640), (256, 704), (MIX, 576))
    return [jnp.concatenate([row[:, a : a + LANES], row[:, b : b + LANES // 2]], axis=1) for a, b in at]


def pack_biases(biases, packed, n_mp, width):
    f32 = jnp.float32
    share = width // n_mp
    zero = jnp.zeros((1, share), f32)
    for m in range(n_mp):
        part = [biases[r : r + 1, m * share : (m + 1) * share] for r in (0, 1)]
        packed[m : m + 1] = pack_lanes((part[0], zero, part[1]), zero)
    fan = width // share
    source = lax.broadcasted_iota(jnp.int32, (share, width), 0) * fan
    target = lax.broadcasted_iota(jnp.int32, (share, width), 1)
    total = jnp.zeros((n_mp, width), f32)
    for r in range(fan):
        rows = jnp.concatenate(
            [biases[2 + r : 3 + r, m * share : (m + 1) * share] for m in range(n_mp)], axis=0
        )
        move = jnp.where(target == source + r, 1.0, 0.0)
        total = total + lax.dot_general(rows, move, NN, precision=EXACT, preferred_element_type=f32)
    packed[n_mp : 2 * n_mp] = total

DECAY = 1.0 - STEP ** (-0.8)
EXACT = lax.Precision.HIGHEST
SUB_QKV, SUB_OUT, SUB_UP, SUB_DOWN = range(4)


class Exchange:
    def __init__(self, axis, size, bufs, send_sems, recv_sems):
        self.axis, self.size, self.bufs = axis, size, bufs
        self.send_sems, self.recv_sems = send_sems, recv_sems
        self.me = lax.axis_index(axis)

    def copy(self, away):
        peer = (self.me + away) % self.size
        return pltpu.make_async_remote_copy(
            src_ref=self.bufs.at[0],
            dst_ref=self.bufs.at[away],
            send_sem=self.send_sems.at[away],
            recv_sem=self.recv_sems.at[away],
            device_id={self.axis: peer},
            device_id_type=MESH,
        )

    def send(self, value):
        self.bufs[0] = value
        for away in range(1, self.size):
            self.copy(away).start()

    def total(self):
        for away in range(1, self.size):
            self.copy(away).wait_recv()
        total = jnp.zeros(self.bufs.shape[1:], jnp.float32)
        for index in range(self.size):
            away = (self.me - index + self.size) % self.size
            total = total + self.bufs[away]
        return total

    def wait_sends(self):
        for away in range(1, self.size):
            self.copy(away).wait_send()


class Doubling:
    def __init__(self, value, bufs, send_sems, recv_sems):
        self.value, self.bufs, self.send_sems, self.recv_sems = value, bufs, send_sems, recv_sems
        dp, mp = lax.axis_index("dp"), lax.axis_index("mp")
        sib, xn, yn, _ = neighbours(dp)
        self.peers = (
            {"dp": sib}, {"dp": xn}, {"dp": yn}, {"mp": mp + 1 - 2 * (mp % 2)}, {"mp": (mp + 2) % 4}
        )

    def copy(self, i):
        return pltpu.make_async_remote_copy(
            src_ref=self.value.at[i],
            dst_ref=self.bufs.at[i],
            send_sem=self.send_sems.at[i],
            recv_sem=self.recv_sems.at[i],
            device_id=self.peers[i],
            device_id_type=MESH,
        )

    def send(self, i):
        self.copy(i).start()

    def add(self, i):
        self.copy(i).wait_recv()
        self.value[i + 1] = self.value[i] + self.bufs[i]

    def finish(self):
        for i in range(5):
            self.copy(i).wait_send()


def lane_sums(mask, squares):
    return lax.dot_general(mask, squares, NT, precision=EXACT, preferred_element_type=jnp.float32)


def o_lanes(width):
    lane = lax.broadcasted_iota(jnp.int32, (1, width), 1)
    return jnp.where(((lane >= MIX) & (lane < MIX + 128)) | ((lane >= 576) & (lane < 640)), 1.0, 0.0)


def masks_of(width, scale_rows):
    row = lax.broadcasted_iota(jnp.int32, (8, width), 0)
    is_o = o_lanes(width)
    if not isinstance(scale_rows, list):
        scale_rows = [scale_rows[i : i + 1] for i in range(3)]
    up = jnp.where(row == SUB_UP, scale_rows[0], 0.0)
    down = jnp.where(row == SUB_DOWN, scale_rows[1], 0.0)
    first = scale_rows[2]
    mixed = jnp.where(row == SUB_QKV, first * (1.0 - is_o), jnp.where(row == SUB_OUT, first * is_o, 0.0))
    return up, down, mixed


class Factors:
    def __init__(self, reduced, sub_prior, lane_prior, n_dp, swaps):
        self.reduced, self.sub_prior, self.lane_prior = reduced, sub_prior, lane_prior
        self.rows, self.width = reduced.shape[1:]
        self.whole = float(self.rows * n_dp)
        self.early_mp, self.early_dp, self.late_mp, self.late_dp, self.last_mp, self.last_dp = swaps
        self.shares = jnp.zeros((8, self.rows), jnp.float32)
        self.totals = jnp.zeros((8, 1), jnp.float32)

    def send(self, groups, along_mp, along_dp):
        masks = masks_of(self.width, jnp.ones((3, self.width), jnp.float32))
        rows = jnp.zeros((8, self.rows), jnp.float32)
        columns = []
        for group in groups:
            squares = self.reduced[group] * self.reduced[group]
            columns.append(column_sum(squares))
            rows = rows + lane_sums(masks[group], squares)
        along_dp.send(columns[0] if len(columns) == 1 else jnp.concatenate(columns, axis=0))
        along_mp.send(jnp.concatenate([rows, jnp.zeros((8, LANES - self.rows), jnp.float32)], axis=1))
        self.totals = self.totals + jnp.sum(rows, axis=1, keepdims=True)

    def collect(self, groups, along_mp, along_dp, sub_out, lane_out):
        rows, columns = along_mp.total(), along_dp.total()
        row8 = lax.broadcasted_iota(jnp.int32, (8, LANES), 0)
        count = self.whole * jnp.where(row8 == SUB_QKV, 3.0, jnp.where(row8 == SUB_OUT, 1.0, 4.0))
        sub_new = DECAY * self.sub_prior[...] + (1.0 - DECAY) * (rows / count + square_eps)
        mine = (row8 == SUB_UP) | (row8 == SUB_DOWN)
        if 2 in groups:
            mine = (row8 == SUB_QKV) | (row8 == SUB_OUT)
        sub_out[...] = jnp.where(mine, sub_new, sub_out[...])
        scale_rows = []
        for i, group in enumerate(groups):
            new = DECAY * self.lane_prior[group : group + 1] + (1.0 - DECAY) * (
                columns[i : i + 1] / self.whole + square_eps
            )
            lane_out[group : group + 1] = new
            scale_rows.append(1.0 / new)
        if len(scale_rows) == 1:
            scale_rows = [scale_rows[0]] * 3
        masks = masks_of(self.width, scale_rows + scale_rows[:1])
        shares = jnp.zeros((8, self.rows), jnp.float32)
        for group in groups:
            shares = shares + lane_sums(masks[group], self.reduced[group] * self.reduced[group])
        self.shares = self.shares + jnp.where(mine[:, 0 : self.rows], shares / sub_new[:, 0 : self.rows], 0.0)

    def finish(self, masters, scalar_out):
        f32 = jnp.float32
        masks = masks_of(self.width, jnp.ones((3, self.width), f32))
        weights = jnp.zeros((8, 1), f32)
        for group in range(GROUPS):
            by_lane = column_sum(masters[group] * masters[group])
            weights = weights + jnp.sum(masks[group] * by_lane, axis=1, keepdims=True)
        row1 = lax.broadcasted_iota(jnp.int32, (8, 1), 0)
        lane8 = lax.broadcasted_iota(jnp.int32, (8, LANES), 1)
        sub = jnp.sum(jnp.where(lane8 < self.rows, self.sub_prior[...], 0.0), axis=1, keepdims=True)
        out = jnp.sum(self.lane_prior[2:3] * o_lanes(self.width), axis=1, keepdims=True)
        down = jnp.sum(self.lane_prior[1:2], axis=1, keepdims=True)
        prior = jnp.where(row1 == SUB_OUT, out, jnp.where(row1 == SUB_DOWN, down, sub))
        shares = jnp.sum(self.shares, axis=1, keepdims=True)
        value = jnp.where(
            lane8 == 0, shares, jnp.where(lane8 == 1, weights, jnp.where(lane8 == 2, self.totals, prior))
        )
        self.last_mp.send(value)
        self.last_dp.send(self.last_mp.total())
        scalar_out[...] = self.last_dp.total()

    def wait_sends(self):
        for swap in (self.early_mp, self.early_dp, self.late_mp, self.late_dp, self.last_mp, self.last_dp):
            swap.wait_sends()


def update_kernel(
    n_dp, n_mp, reduced, masters, sub_new, lane_new, scalars, sums, vec, bias, vec_moment, bias_moment, input_in, stream_in,
    stream_out, input_out, qkv_g, out_g, up_g, down_g, qkv_a, out_a, up_a, down_a, qkv_b, out_b, up_b, down_b,
    qkvrows, qkvcols, outrows, outcols, uprows, upcols, downrows, downcols,
    vec_g, bias_g, vec_m, bias_m, vec_a, bias_a, update_scale, token_spread, held, sems,
):
    f32 = jnp.float32
    groups, rows, width = reduced.shape
    load = pltpu.make_async_copy(stream_in, held, sems.at[0])
    load.start()
    span = input_in.shape[2]
    for i in range(n_mp):
        input_out[:, i * span : (i + 1) * span] = input_in[i].astype(f32)
    load.wait()
    store = pltpu.make_async_copy(held, stream_out, sems.at[1])
    store.start()
    whole = float(rows * n_dp)
    entries = (3.0 * whole * whole, whole * whole, 4.0 * whole * whole, 4.0 * whole * whole)
    row1 = lax.broadcasted_iota(jnp.int32, (8, 1), 0)
    size = jnp.where(row1 == 0, entries[0], jnp.where(row1 == 1, entries[1], entries[2]))
    copies = jnp.where((row1 == SUB_QKV) | (row1 == SUB_UP), float(n_mp), float(n_dp))
    length = jnp.where(row1 == SUB_DOWN, 4.0 * whole, whole)
    mean_rows = DECAY * scalars[:, 3:4] / (copies * length) + (1.0 - DECAY) * (scalars[:, 2:3] / size + square_eps)
    scale = jnp.sqrt(scalars[:, 0:1] * mean_rows / size)
    rms = jnp.sqrt(scalars[:, 1:2] / size)
    rate = step_rate * rms / jnp.maximum(1.0, scale / clip_limit)
    sub = lax.dot_general(
        jnp.where(
            lax.broadcasted_iota(jnp.int32, (rows, LANES), 0) == lax.broadcasted_iota(jnp.int32, (rows, LANES), 1), 1.0, 0.0
        ),
        sub_new[...], NT, precision=EXACT, preferred_element_type=f32,
    )
    is_o = o_lanes(width)

    def renewed(group, index):
        gradient = reduced[group]
        product = sub[:, index : index + 1] * lane_new[group : group + 1] / mean_rows[index : index + 1]
        return masters[group] - rate[index : index + 1] * (gradient * lax.rsqrt(product))

    def spread(value, qkv, out):
        q, k, v, o = unpack_lanes(value)
        for i, part in enumerate((q, k, v)):
            qkv[i] = part.astype(qkv.dtype)
        out[...] = o.T.astype(out.dtype)

    first = jnp.where(is_o > 0.0, renewed(2, 1), renewed(2, 0))
    spread(reduced[2], qkv_g, out_g)
    spread(first, qkv_a, out_a)
    spread(first, qkv_b, out_b)
    for group, index, grad, after, short in ((0, 2, up_g, up_a, up_b), (1, 3, down_g, down_a, down_b)):
        new = renewed(group, index)
        grad[...] = reduced[group]
        after[...] = new
        short[...] = new.astype(short.dtype)

    def plain(weight, gradient, moment_old, together):
        moment = DECAY * moment_old + (1.0 - DECAY) * (gradient * gradient + square_eps)
        update = gradient * lax.rsqrt(moment)
        update_mean = jnp.mean(update * update, axis=1, keepdims=True)
        weight_mean = jnp.mean(weight * weight, axis=1, keepdims=True)
        if together is not None:
            row = lax.broadcasted_iota(jnp.int32, update_mean.shape, 0)
            number = float(weight.shape[0] - together)

            def join(mean):
                shared = jnp.sum(jnp.where(row >= together, mean, 0.0), axis=0, keepdims=True) / number
                return jnp.where(row >= together, shared, mean)

            update_mean, weight_mean = join(update_mean), join(weight_mean)
        rate_here = step_rate * jnp.sqrt(weight_mean)
        return weight - rate_here * update / jnp.maximum(1.0, jnp.sqrt(update_mean) / clip_limit), moment

    vec_g[...] = sums[0:8]
    bias_g[...] = sums[8:14]
    vec_a[...], vec_m[...] = plain(vec[...], sums[0:8], vec_moment[...], None)
    bias_a[...], bias_m[...] = plain(bias[...], sums[8:14], bias_moment[...], 2)
    spreads = jnp.sqrt(sums[14:15, 0:LANES] / (sums[14:15, 3:4] * width))
    scales = jnp.zeros((1, LANES), f32)
    lane1 = lax.broadcasted_iota(jnp.int32, (1, LANES), 1)
    for i in range(4):
        scales = scales + jnp.where(lane1 == i, scale[i : i + 1], 0.0)
    update_scale[...] = scales[:, 0:4].reshape(4)
    token_spread[...] = spreads[:, 0:3].reshape(3)
    for index, ref in ((SUB_QKV, qkvrows), (SUB_OUT, outcols), (SUB_UP, uprows), (SUB_DOWN, downcols)):
        ref[...] = sub_new[index, 0:rows]
    upcols[...] = lane_new[0]
    downrows[...] = lane_new[1]
    *cols, out_row = unpack_lanes(lane_new[2:3])
    for i in range(3):
        qkvcols[i : i + 1] = cols[i]
    outrows[...] = out_row.reshape(out_row.shape[1])
    store.wait()


def bias_rows_natural(qkv_sums, hidden_sums, n_mp, width):
    f32 = jnp.float32
    share = width // n_mp
    half = LANES // 2
    query = [qkv_sums[m : m + 1, a:b] for m in range(n_mp) for a, b in ((0, LANES), (512, 512 + half))]
    value = [qkv_sums[m : m + 1, a:b] for m in range(n_mp) for a, b in ((256, 256 + LANES), (704, 704 + half))]
    source = lax.broadcasted_iota(jnp.int32, (width, width), 0)
    target = lax.broadcasted_iota(jnp.int32, (1, width), 1)
    fan = width // share
    from_lane = target * fan
    for r in range(1, fan):
        from_lane = jnp.where(target >= r * share, (target - r * share) * fan + r, from_lane)
    move = jnp.where(source == from_lane, 1.0, 0.0).astype(jnp.bfloat16)
    moved = jnp.zeros_like(hidden_sums)
    left = hidden_sums
    for _ in range(3):
        part = left.astype(jnp.bfloat16)
        moved = moved + mm(part, move)
        left = left - part.astype(f32)
    rows = [jnp.concatenate(query, axis=1), jnp.concatenate(value, axis=1)]
    for r in range(width // share):
        rows.append(
            jnp.concatenate([moved[m : m + 1, r * share : (r + 1) * share] for m in range(n_mp)], axis=1)
        )
    return rows

class Stream:
    CUTS = 4

    def __init__(self, n_mp, src, out, send_sems, recv_sems):
        self.dp, self.mp, self.n_mp = lax.axis_index("dp"), lax.axis_index("mp"), n_mp
        self.src, self.out, self.send_sems, self.recv_sems = src, out, send_sems, recv_sems
        self.rows = out.shape[1] // self.CUTS
        self.up, self.down = jnp.minimum(self.mp + 1, n_mp - 1), jnp.maximum(self.mp - 1, 0)

    def message(self, plane, cut, way, own):
        part = pl.ds(pl.multiple_of(cut * self.rows, self.rows), self.rows)
        where = self.out.at[plane, part]
        return pltpu.make_async_remote_copy(
            src_ref=self.src.at[part] if own else where,
            dst_ref=where,
            send_sem=self.send_sems.at[way, plane, cut],
            recv_sem=self.recv_sems.at[plane, cut],
            device_id=(self.dp, self.down if way else self.up),
            device_id_type=MESH,
        )

    def step(self, s):
        distance, cut = s // self.CUTS, s % self.CUTS
        mp, last = self.mp, self.n_mp - 1

        @pl.when((distance == 0) & (mp < last))
        def _():
            self.message(mp, cut, 0, True).start()

        @pl.when((distance == 0) & (mp > 0))
        def _():
            self.message(mp, cut, 1, True).start()

        below, above = mp - distance, mp + distance

        @pl.when((distance > 0) & (below >= 0))
        def _():
            self.message(below, cut, 0, False).wait_recv()

            @pl.when(mp < last)
            def _():
                self.message(below, cut, 0, False).start()

        @pl.when((distance > 0) & (above <= last))
        def _():
            self.message(above, cut, 1, False).wait_recv()

            @pl.when(mp > 0)
            def _():
                self.message(above, cut, 1, False).start()

    STEPS = 16

    def finish(self):
        mp, last = self.mp, self.n_mp - 1

        def body(t, _):
            plane, cut = t // self.CUTS, t % self.CUTS

            @pl.when((plane <= mp) & (mp < last))
            def _():
                self.message(plane, cut, 0, False).wait_send()

            @pl.when((plane >= mp) & (mp > 0))
            def _():
                self.message(plane, cut, 1, False).wait_send()

            return 0

        lax.fori_loop(0, self.n_mp * self.CUTS, body, 0)

def layer_kernel(
    n_dp, n_mp, slots, own_rows, tokens_in, cot_in, w_qkv, w_out, w_up, w_down_t, counts, vec, biases, *rest
):
    (
        qkvrows, qkvcols, outrows, outcols, uprows, upcols, downrows, downcols,
        masters, reduced, sums_out, sub_out, lane_out, scalar_out, input_out, stream_out,
        w, tokens, cot, qkv, active, slope, mixed, proj, normed_two, normed_t, normed_two_t, turned_t, branch, d_branch, d_two,
        result, feat_q, feat_k, d_mixed, acc, d_query, bias, sums, sums_qkv, sub_prior, lane_prior,
        pair_in, halves_in, x_in, y_in, z_in, value, swap_in, early_mp, early_dp, late_mp, late_dp, last_mp, last_dp,
        credit, local_sems, g_send, g_recv, g_way, s_send, s_recv, stream_send, stream_recv, turn_send, turn_recv,
        swap_send, swap_recv, small_send, small_recv,
    ) = rest
    set_rows, width = tokens.shape
    place = Place(set_rows, own_rows)
    window, own, own_start, window_start, tiles = (
        place.window, place.own, place.own_start, place.window_start, place.tiles
    )
    low, f32 = jnp.bfloat16, jnp.float32
    dp, mp = lax.axis_index("dp"), lax.axis_index("mp")
    in_set = pl.ds(pl.multiple_of(place.set_index * set_rows, LANES), set_rows)
    token_copy = pltpu.make_async_copy(tokens_in.at[in_set], tokens, local_sems.at[0])
    in_window = pl.ds(pl.multiple_of(place.set_index * set_rows + window_start, LANES), window)
    cot_copy = pltpu.make_async_copy(cot_in.at[in_window], cot, local_sems.at[1])
    token_copy.start()
    cot_copy.start()
    net = Gather(n_mp, w, g_send, g_recv, g_way)
    back = Scatter(n_mp, w, reduced, (pair_in, halves_in, x_in, y_in, z_in), credit, s_send, s_recv)
    stream = Stream(n_mp, result, stream_out, stream_send, stream_recv)
    swaps = Doubling(value, swap_in, swap_send, swap_recv)
    exchanges = [
        Exchange(axis, size, buf, small_send.at[i], small_recv.at[i])
        for i, (axis, size, buf) in enumerate(
            (
                ("mp", n_mp, early_mp), ("dp", n_dp, early_dp), ("mp", n_mp, late_mp), ("dp", n_dp, late_dp),
                ("mp", n_mp, last_mp), ("dp", n_dp, last_dp),
            )
        )
    ]
    masters[0] = w_up[...]
    masters[1] = w_down_t[...]
    pack_first(w_qkv, w_out, masters.at[2])
    for group, source in enumerate((2, 0, 1)):
        w[group, mp, dp // 2, dp % 2] = masters[source].astype(low)
    greet(
        [((dp + away) % n_dp, mp) for away in range(1, n_dp)] + [(dp, (mp + away) % n_mp) for away in range(1, n_mp)], []
    )
    net.begin()

    def weight(group, m, lanes=None):
        block = w[group, m] if lanes is None else w[group, m, :, :, :, lanes]
        return block.reshape(width, block.shape[-1])

    pack_biases(biases, bias, n_mp, width)
    total = make_features(counts, place.set_index, slots, set_rows, feat_q, feat_k)
    token_copy.wait()
    zero_row = jnp.zeros((1, width), f32)
    normed = slope

    def norm_one(i, _):
        unit, _inv = row_stats(tokens[tile_rows(i)].astype(f32))
        per_half = own_rows // LANES
        normed[i // per_half, tile_rows(i % per_half)] = (unit * vec[0:1] + vec[1:2]).astype(low)
        return 0

    lax.fori_loop(0, set_rows // LANES, norm_one, 0)
    net.step(0)
    cot_copy.wait()

    def back_of(i):
        return cot[tile_rows(i)].astype(f32) * place.valid(i, total)

    def first_grad(i, total_row):
        db = (back_of(i) * vec[5:6]).astype(low)
        d_branch[tile_rows(i)] = db
        return total_row + place.is_own(i) * column_sum(db.astype(f32))

    branch_sum = lax.fori_loop(0, tiles, first_grad, zero_row)
    turned_t[...] = d_branch[own].T
    net.step(1)
    normed_t[...] = normed[mp % 2, 0:own_rows].T

    def project(u, _):
        net.step(u + 2)
        net.stage_d(u)
        m = net.plane(u)
        for half in range(set_rows // own_rows):
            at = pl.ds(half * own_rows, own_rows)
            qkv[m, at] = (mm(normed[half, 0:own_rows], weight(0, m)) + bias[pl.ds(m, 1)]).astype(low)
        attend(m, qkv, mixed, feat_q, feat_k, window_start, window, window)
        return 0

    lax.fori_loop(0, n_mp, project, 0)
    net.step(n_mp + 2)
    proj[...] = sum((mm(mixed[m], weight(0, m, pl.ds(MIX, 2 * LANES)), NT) for m in range(n_mp)), vec[6:7])

    def middle_of(i):
        return tokens[tile_rows(i, window_start)].astype(f32) + vec[4:5] * proj[tile_rows(i)]

    def norm_two(i, _):
        unit, _inv = row_stats(middle_of(i))
        normed_two[tile_rows(i)] = (unit * vec[2:3] + vec[3:4]).astype(low)
        return 0

    lax.fori_loop(0, tiles, norm_two, 0)
    normed_two_t[...] = normed_two[own].T

    half_shape = (n_dp // 2, 2, width // n_dp)

    def keep(group, m, lanes, block):
        w[group, m, :, :, :, lanes] = block.astype(low).reshape(*half_shape, block.shape[1])

    piece = window // 1

    def feed(u, _):
        first_unit = n_mp + 2 * u
        net.stage_d(first_unit)
        net.stage_d(first_unit + 1)
        m = net.plane(u)

        def rows(i, _):
            at = pl.ds(pl.multiple_of(i * piece, LANES // 2), piece)
            hidden = mm(normed_two[at], weight(1, m)) + bias[pl.ds(n_mp + m, 1)]
            act, slp = gelu_parts(hidden)
            active[m, at] = act.astype(low)
            slope[m, at] = slp.astype(low)
            return 0

        lax.fori_loop(0, window // piece, rows, 0)
        net.step(first_unit + 3)
        part_sum = mm(active[m, own], weight(2, m), NT)

        @pl.when(u == 0)
        def _():
            branch[...] = part_sum

        @pl.when(u > 0)
        def _():
            branch[...] += part_sum

        def grad_rows(i, total_row):
            at = pl.ds(pl.multiple_of(i * piece, LANES // 2), piece)
            row = lax.broadcasted_iota(jnp.int32, (piece, 1), 0) + i * piece
            mine = jnp.where((row >= own_start) & (row < own_start + own_rows), 1.0, 0.0)
            dh = (mm(d_branch[at], weight(2, m)) * slope[m, at].astype(f32)).astype(low)
            slope[m, at] = dh
            return total_row + column_sum(mine * dh.astype(f32))

        sums[pl.ds(8 + m, 1)] = lax.fori_loop(0, window // piece, grad_rows, zero_row)
        net.step(first_unit + 4)
        two_sum = mm(slope[m], weight(1, m), NT)

        @pl.when(u == 0)
        def _():
            d_two[...] = two_sum

        @pl.when(u > 0)
        def _():
            d_two[...] += two_sum

        @pl.when(u > 0)
        def _():
            for o in (2 * u - 2, 2 * u - 1):
                back.add_pair(o, *back.offered(o))

        net.finish(first_unit)
        net.finish(first_unit + 1)
        everything = pl.ds(0, width)
        keep(2, m, everything, mm(turned_t[...], active[m, own]))
        back.offer(2 * u, 2, m)
        keep(1, m, everything, mm(normed_two_t[...], slope[m, own]))
        back.offer(2 * u + 1, 1, m)
        return 0

    lax.fori_loop(0, n_mp, feed, 0)

    def final(i, carry):
        there = own_start // LANES + i
        br = branch[tile_rows(i)] + vec[7:8]
        scaled = vec[5:6] * br
        res = middle_of(there) + scaled
        result[tile_rows(i)] = res.astype(low)
        attn = vec[4:5] * proj[tile_rows(there)]
        valid = place.valid(there, total)
        new = [column_sum(valid * v * v) for v in (res, attn, scaled)] + [column_sum(back_of(there) * br)]
        return tuple(c + n for c, n in zip(carry, new))

    *squares, back_branch = lax.fori_loop(0, own_rows // LANES, final, (zero_row,) * 4)
    own_result = pltpu.make_async_copy(result, stream_out.at[mp], local_sems.at[2])
    own_result.start()
    for cut in range(stream.CUTS):
        stream.step(cut)
    fed = 2 * n_mp
    for o in (fed - 2, fed - 1):
        back.add_pair(o, *back.offered(o))

    d_proj, d_proj_t = d_branch, turned_t

    def norm_two_back(i, carry):
        at = tile_rows(i)
        grad = d_two[at]
        dv, grad_unit = norm_grad(middle_of(i), vec[2:3], grad)
        d_mid = back_of(i) + dv
        d_two[at] = d_mid
        d_out = (d_mid * vec[4:5]).astype(low)
        d_proj[at] = d_out
        mine = place.is_own(i)
        new = (grad_unit, grad, d_mid * proj[at], d_out.astype(f32))
        return tuple(c + mine * column_sum(n) for c, n in zip(carry, new))

    gain_two, shift_two, scale_sum, proj_sum = lax.fori_loop(0, tiles, norm_two_back, (zero_row,) * 4)
    d_proj_t[...] = d_proj[own].T

    def sent(u, _):
        net.finish(u)
        return 0

    lax.fori_loop(0, n_mp, sent, 0)
    d_normed = branch
    d_qkv = normed_two.at[pl.ds(0, own_rows)]

    def slot(k):
        back.slot(k)
        stream.step(k + stream.CUTS)

    def attention(u, _):
        m = plane_at(mp, n_mp - 1 - u)

        @pl.when(u > 0)
        def _():
            back.add_pair(fed + u - 1, 0, plane_at(mp, n_mp - u))

        dm = mm(d_proj[...], weight(0, m, pl.ds(MIX, 2 * LANES))).astype(low)
        d_mixed[:, 0:LANES] = dm[:, 0:LANES]
        d_mixed[:, LANES:] = keep_half(1, dm[:, LANES:], jnp.zeros_like(dm[:, LANES:]))
        slot(2 * u)
        attend_back(m, qkv, d_mixed, feat_q, feat_k, window_start, window, acc, d_query)
        slot(2 * u + 1)
        d_qkv[:, 0:128] = d_query[own, 0:128]
        d_qkv[:, 128:256] = acc[own, 0:128].astype(low)
        d_qkv[:, 256:384] = acc[own, 128:256].astype(low)
        d_qkv[:, 384:512] = jnp.zeros((own_rows, LANES), low)
        d_qkv[:, 512:640] = d_query[own, 128:256]
        d_qkv[:, 640:768] = acc[own, 256:384].astype(low)
        sums_qkv[pl.ds(m, 1)] = column_sum(d_qkv[...].astype(f32))
        part_sum = mm(d_qkv[...], weight(0, m), NT)

        @pl.when(u == 0)
        def _():
            d_normed[...] = part_sum

        @pl.when(u > 0)
        def _():
            d_normed[...] += part_sum

        block = mm(normed_t[...], d_qkv[...])
        extra = mm(d_proj_t[...], mixed[m, own])
        keep(0, m, pl.ds(0, MIX), block[:, 0:MIX])
        keep(0, m, pl.ds(MIX, 2 * LANES), block[:, MIX : MIX + 2 * LANES] + extra)
        keep(0, m, pl.ds(MIX + 2 * LANES, LANES), block[:, MIX + 2 * LANES :])
        back.offer(fed + u, 0, m)
        return 0

    lax.fori_loop(0, n_mp, attention, 0)
    slot(fed)
    back.add_pair(back.units - 1, 0, mp)

    input_t = normed_t

    def norm_one_back(i, carry):
        grad = d_normed[tile_rows(i)]
        rows = tokens[tile_rows(own_start // LANES + i, window_start)].astype(f32)
        dv, grad_unit = norm_grad(rows, vec[0:1], grad)
        input_t[:, tile_rows(i)] = (d_two[tile_rows(i, own_start)] + dv).astype(low).T
        return tuple(c + column_sum(n) for c, n in zip(carry, (grad_unit, grad)))

    gain_one, shift_one = lax.fori_loop(0, own_rows // LANES, norm_one_back, (zero_row, zero_row))
    share = width // n_mp

    def turn(away):
        peer = (mp + away) % n_mp
        return pltpu.make_async_remote_copy(
            src_ref=input_t.at[pl.ds(pl.multiple_of(peer * share, HD), share)],
            dst_ref=input_out.at[mp],
            send_sem=turn_send.at[away],
            recv_sem=turn_recv.at[away],
            device_id={"mp": peer},
            device_id_type=MESH,
        )

    def turned(away):
        source = (mp - away + n_mp) % n_mp
        return pltpu.make_async_remote_copy(
            src_ref=input_t.at[pl.ds(0, share)],
            dst_ref=input_out.at[source],
            send_sem=turn_send.at[away],
            recv_sem=turn_recv.at[away],
            device_id={"mp": source},
            device_id_type=MESH,
        )

    for away in range(1, n_mp):
        turn(away).start()
    own_turn = pltpu.make_async_copy(
        input_t.at[pl.ds(pl.multiple_of(mp * share, HD), share)], input_out.at[mp], local_sems.at[3]
    )
    own_turn.start()
    slot(fed + 1)

    held = jnp.clip(total - (window_start + own_start), 0, own_rows).astype(f32)
    lane_w = lax.broadcasted_iota(jnp.int32, (1, width), 1)
    scalar_row = jnp.where(lane_w == 3, held, 0.0)
    for i in range(3):
        scalar_row = scalar_row + jnp.where(lane_w == i, jnp.sum(squares[i], axis=1, keepdims=True), 0.0)
    natural = bias_rows_natural(sums_qkv[0:n_mp], sums[8 : 8 + n_mp], n_mp, width)
    vector_rows = [gain_one, shift_one, gain_two, shift_two, scale_sum, back_branch, proj_sum, branch_sum]
    for i, row in enumerate(vector_rows + natural + [scalar_row, zero_row]):
        value[0, i : i + 1] = row
    swaps.send(0)
    rows_here = qkvrows.shape[0]
    sub_prior[...] = jnp.zeros_like(sub_prior)
    for i, prior in enumerate((qkvrows, outcols, uprows, downcols)):
        sub_prior[i : i + 1, 0:rows_here] = prior[...][None, :]
    lane_prior[0:1] = upcols[...][None, :]
    lane_prior[1:2] = downrows[...][None, :]
    lane_prior[2:3] = pack_lanes([qkvcols[i : i + 1] for i in range(3)], outrows[...][None, :])
    sub_out[...] = jnp.zeros_like(sub_out)
    lane_out[...] = jnp.zeros_like(lane_out)
    factors = Factors(reduced, sub_prior, lane_prior, n_dp, exchanges)
    early, late = (0, 1), (2,)
    slot(fed + 2)
    swaps.add(0)
    swaps.send(1)
    factors.send(early, factors.early_mp, factors.early_dp)
    slot(fed + 3)
    swaps.add(1)
    swaps.send(2)
    slot(fed + 4)
    swaps.add(2)
    swaps.send(3)
    factors.collect(early, factors.early_mp, factors.early_dp, sub_out, lane_out)
    slot(fed + 5)
    factors.send(late, factors.late_mp, factors.late_dp)
    swaps.add(3)
    swaps.send(4)
    factors.collect(late, factors.late_mp, factors.late_dp, sub_out, lane_out)
    factors.finish(masters, scalar_out)
    swaps.add(4)
    sums_out[...] = value[5]
    for s in range(fed + 5 + stream.CUTS + 1, stream.STEPS):
        stream.step(s)
    for away in range(1, n_mp):
        turned(away).wait_recv()
        turn(away).wait_send()
    own_turn.wait()
    own_result.wait()
    factors.wait_sends()
    back.finish()
    stream.finish()
    swaps.finish()

def moments_of(stream):
    center = stream - jnp.mean(stream, axis=-1, keepdims=True)
    spread = jnp.mean(center * center, axis=-1, keepdims=True)
    return (center, lax.rsqrt(spread + norm_eps))


def normalize(stream, gain_row, shift_row):
    center, inverse = moments_of(stream)
    return center * inverse * gain_row + shift_row


def segment_ids(counts, set_rows):
    image_ends = jnp.cumsum(counts)
    places = jnp.arange(set_rows, dtype=jnp.int32)
    return jnp.sum((places[:, None] >= image_ends[None, :]).astype(jnp.int32), axis=1)


def scores_of(query_set, key_set, same_image, score_scale):
    raw_scores = (
        jnp.einsum("qhd,khd->hqk", query_set, key_set, preferred_element_type=jnp.float32)
        * score_scale
    )
    return jnp.where(same_image[None], raw_scores, mask_fill)


def shard_offset(shard_piece, block_index, whole_length, axis_at):
    shape_list = list(shard_piece.shape)
    shape_list[axis_at] = whole_length
    empty = jnp.zeros(tuple(shape_list), jnp.float32)
    return lax.dynamic_update_slice_in_dim(
        empty, shard_piece, block_index * shard_piece.shape[axis_at], axis_at
    )


def select_slice(whole_array, block_index, block_width, axis_at):
    return lax.dynamic_slice_in_dim(whole_array, block_index * block_width, block_width, axis_at)


def factor_step(
    gradient,
    rows_old,
    cols_old,
    rows_mine,
    cols_mine,
    rows_total,
    count_rows,
    count_cols,
    prior_total,
):
    decay_rate = 1.0 - STEP ** (-0.8)
    rows_new = decay_rate * rows_old + (1.0 - decay_rate) * (rows_mine / count_cols + square_eps)
    cols_new = decay_rate * cols_old + (1.0 - decay_rate) * (cols_mine / count_rows + square_eps)
    rows_average = (
        decay_rate * prior_total
        + (1.0 - decay_rate) * (rows_total / count_cols + count_rows * square_eps)
    ) / count_rows
    update = gradient * lax.rsqrt(rows_new[:, None] * cols_new[None, :] / rows_average)
    return (rows_new, cols_new, update, jnp.sum(update * update))


def plain_step(weight, gradient, moment_old):
    decay_rate = 1.0 - STEP ** (-0.8)
    moment = decay_rate * moment_old + (1.0 - decay_rate) * (gradient * gradient + square_eps)
    update = gradient * lax.rsqrt(moment)
    update_rms = jnp.sqrt(jnp.mean(update * update))
    rate_here = step_rate * jnp.sqrt(jnp.mean(weight * weight))
    return (weight - rate_here * update / jnp.maximum(1.0, update_rms / clip_limit), moment)


def generic(
    tokens_in,
    cotangent,
    patch_counts,
    w_qkv,
    w_out,
    w_up,
    w_down,
    layer_vector_rows,
    inner_biases,
    qkvrows_prior,
    qkvcols_prior,
    outrows_prior,
    outcols_prior,
    uprows_prior,
    upcols_prior,
    downrows_prior,
    downcols_prior,
    vector_moment,
    bias_moment,
):
    data_index = lax.axis_index("dp")
    parallel_model_index = lax.axis_index("mp")
    row_count, parallel_model_width = tokens_in.shape
    set_count, slot_count = patch_counts.shape
    set_rows = row_count // set_count
    shard_width_local = w_qkv.shape[2]
    local_hidden = w_up.shape[1]
    head_count = shard_width_local // HD
    score_scale = HD ** (-0.5)
    full_qkv, full_out, full_up, full_down = (
        lax.all_gather(w_qkv.astype(jnp.bfloat16), "dp", axis=0, tiled=True),
        lax.all_gather(w_out.astype(jnp.bfloat16), "dp", axis=1, tiled=True),
        lax.all_gather(w_up.astype(jnp.bfloat16), "dp", axis=0, tiled=True),
        lax.all_gather(w_down.astype(jnp.bfloat16), "dp", axis=1, tiled=True),
    )
    stream = tokens_in.astype(jnp.float32)
    segment = jax.vmap(lambda counts: segment_ids(counts, set_rows))(patch_counts)
    valid_rows = (segment < slot_count).astype(jnp.float32).reshape(row_count)
    centered_single, inverse_deviation_single = moments_of(stream)
    standardized_single = centered_single * inverse_deviation_single
    normalized_rows = (standardized_single * layer_vector_rows[0] + layer_vector_rows[1]).astype(
        jnp.bfloat16
    )
    bias_mine = select_slice(inner_biases, parallel_model_index, shard_width_local, 1)
    projected = jnp.einsum(
        "rd,dtc->rtc", normalized_rows, full_qkv, preferred_element_type=jnp.float32
    )
    query_rows = (projected[:, 0] + bias_mine[0]).astype(jnp.bfloat16)
    key_rows = projected[:, 1].astype(jnp.bfloat16)
    value_rows = (projected[:, 2] + bias_mine[1]).astype(jnp.bfloat16)

    def split_sets(field_in):
        return field_in.reshape(set_count, set_rows, head_count, HD)

    def attend(set_item):
        query_set, key_set, value_set, segment_set = set_item
        same_image = segment_set[:, None] == segment_set[None, :]
        raw_scores = scores_of(query_set, key_set, same_image, score_scale)
        row_top = jnp.max(raw_scores, axis=-1, keepdims=True)
        exponent = jnp.exp(raw_scores - row_top)
        row_total = jnp.sum(exponent, axis=-1, keepdims=True)
        weights = exponent / row_total
        mixed_set = jnp.einsum(
            "hqk,khd->qhd",
            weights.astype(jnp.bfloat16),
            value_set,
            preferred_element_type=jnp.float32,
        )
        return (mixed_set.astype(jnp.bfloat16), (row_top + jnp.log(row_total))[..., 0])

    mixed_heads, log_total = lax.map(
        attend, (split_sets(query_rows), split_sets(key_rows), split_sets(value_rows), segment)
    )
    mixed_heads = mixed_heads.reshape(row_count, shard_width_local)
    attn_terms = jnp.dot(mixed_heads, full_out, preferred_element_type=jnp.float32)
    proj = (
        lax.psum(attn_terms.astype(jnp.bfloat16), "mp").astype(jnp.float32) + layer_vector_rows[6]
    )
    shared_mask = shard_offset(
        jnp.ones((shard_width_local,), jnp.float32), parallel_model_index, parallel_model_width, 0
    )
    middle = stream + layer_vector_rows[4] * proj
    normed_here = normalize(middle, layer_vector_rows[2], layer_vector_rows[3]).astype(jnp.bfloat16)
    up_bias = select_slice(inner_biases[2:], parallel_model_index, shard_width_local, 1).T.reshape(
        local_hidden
    )
    hidden = jnp.dot(normed_here, full_up, preferred_element_type=jnp.float32) + up_bias
    active = jax.nn.gelu(hidden, approximate=False).astype(jnp.bfloat16)
    mlp_terms = jnp.dot(active, full_down, preferred_element_type=jnp.float32)
    branch = (
        lax.psum(mlp_terms.astype(jnp.bfloat16), "mp").astype(jnp.float32) + layer_vector_rows[7]
    )
    result = middle + layer_vector_rows[5] * branch
    result_low = result.astype(jnp.bfloat16)
    back_grad = cotangent.astype(jnp.float32) * valid_rows[:, None]
    d_branch = (back_grad * layer_vector_rows[5]).astype(jnp.bfloat16)
    down_part = jnp.einsum("rf,rd->fd", active, d_branch, preferred_element_type=jnp.float32)
    d_active = jnp.einsum("rd,fd->rf", d_branch, full_down, preferred_element_type=jnp.float32)
    gelu_out, gelu_pull = jax.vjp(lambda inputs: jax.nn.gelu(inputs, approximate=False), hidden)
    d_hidden = gelu_pull(d_active)[0].astype(jnp.bfloat16)
    up_part = jnp.einsum("rd,rf->df", normed_here, d_hidden, preferred_element_type=jnp.float32)
    mid_terms = jnp.einsum("rf,df->rd", d_hidden, full_up, preferred_element_type=jnp.float32)
    d_normed_two = lax.psum(mid_terms.astype(jnp.bfloat16), "mp").astype(jnp.float32)
    norm_out, norm_pull = jax.vjp(normalize, middle, layer_vector_rows[2], layer_vector_rows[3])
    d_through, d_gain_two, d_shift_two = norm_pull(d_normed_two)
    d_middle = back_grad + d_through
    d_proj_here = (d_middle * layer_vector_rows[4]).astype(jnp.bfloat16)
    d_middle_cols = select_slice(d_middle, parallel_model_index, shard_width_local, 1)
    out_part = jnp.einsum("rc,rd->cd", mixed_heads, d_proj_here, preferred_element_type=jnp.float32)
    d_mixed = jnp.einsum(
        "rd,cd->rc", d_proj_here, full_out, preferred_element_type=jnp.float32
    ).astype(jnp.bfloat16)

    def attend_back(set_item):
        query_set, key_set, value_set, segment_set, total_set, grad_set = set_item
        same_image = segment_set[:, None] == segment_set[None, :]
        raw_scores = scores_of(query_set, key_set, same_image, score_scale)
        weights = jnp.exp(raw_scores - total_set[..., None])
        d_value = jnp.einsum(
            "hqk,qhd->khd",
            weights.astype(jnp.bfloat16),
            grad_set,
            preferred_element_type=jnp.float32,
        )
        d_weights = jnp.einsum(
            "qhd,khd->hqk", grad_set, value_set, preferred_element_type=jnp.float32
        )
        d_scores = (
            weights * (d_weights - jnp.sum(d_weights * weights, axis=-1, keepdims=True))
        ).astype(jnp.bfloat16)
        d_query = (
            jnp.einsum("hqk,khd->qhd", d_scores, key_set, preferred_element_type=jnp.float32)
            * score_scale
        )
        d_key = (
            jnp.einsum("hqk,qhd->khd", d_scores, query_set, preferred_element_type=jnp.float32)
            * score_scale
        )
        return jnp.stack([d_query, d_key, d_value], axis=1).astype(jnp.bfloat16)

    d_projected = lax.map(
        attend_back,
        (
            split_sets(query_rows),
            split_sets(key_rows),
            split_sets(value_rows),
            segment,
            log_total,
            split_sets(d_mixed),
        ),
    )
    d_projected = d_projected.reshape(row_count, 3, shard_width_local)
    qkv_part = jnp.einsum(
        "rd,rtc->dtc", normalized_rows, d_projected, preferred_element_type=jnp.float32
    )
    normalized_gradient = lax.psum_scatter(
        jnp.einsum("rtc,dtc->rd", d_projected, full_qkv, preferred_element_type=jnp.float32).astype(
            jnp.bfloat16
        ),
        "mp",
        scatter_dimension=1,
        tiled=True,
    ).astype(jnp.float32)
    standardized_local = select_slice(
        standardized_single, parallel_model_index, shard_width_local, 1
    )
    local_gain_slice = select_slice(
        layer_vector_rows[0], parallel_model_index, shard_width_local, 0
    )
    standardized_gradient = normalized_gradient * local_gain_slice
    gradient_sum_local, product_sum_local = lax.psum(
        (
            jnp.sum(standardized_gradient, axis=1),
            jnp.sum(standardized_gradient * standardized_local, axis=1),
        ),
        "mp",
    )
    input_grad = d_middle_cols + inverse_deviation_single * (
        standardized_gradient
        - gradient_sum_local[:, None] / parallel_model_width
        - standardized_local * product_sum_local[:, None] / parallel_model_width
    )

    def mine(field_in):
        return select_slice(field_in, parallel_model_index, shard_width_local, field_in.ndim - 1)

    vector_part = jnp.stack(
        [
            shard_offset(
                jnp.sum(normalized_gradient * standardized_local, axis=0),
                parallel_model_index,
                parallel_model_width,
                0,
            ),
            shard_offset(
                jnp.sum(normalized_gradient, axis=0), parallel_model_index, parallel_model_width, 0
            ),
            d_gain_two * shared_mask,
            d_shift_two * shared_mask,
            jnp.sum(d_middle * proj, axis=0) * shared_mask,
            jnp.sum(back_grad * branch, axis=0) * shared_mask,
            shard_offset(
                jnp.sum(mine(d_proj_here).astype(jnp.float32), axis=0),
                parallel_model_index,
                parallel_model_width,
                0,
            ),
            shard_offset(
                jnp.sum(mine(d_branch).astype(jnp.float32), axis=0),
                parallel_model_index,
                parallel_model_width,
                0,
            ),
        ]
    )
    hidden_sums = (
        jnp.sum(d_hidden.astype(jnp.float32), axis=0)
        .reshape(shard_width_local, local_hidden // shard_width_local)
        .T
    )
    bias_part = jnp.concatenate(
        [
            jnp.sum(d_projected[:, 0].astype(jnp.float32), axis=0)[None],
            jnp.sum(d_projected[:, 2].astype(jnp.float32), axis=0)[None],
            hidden_sums,
        ],
        axis=0,
    )
    squares = jnp.stack(
        [
            jnp.sum(valid_rows[:, None] * shared_mask * field_in * field_in)
            for field_in in (result, layer_vector_rows[4] * proj, layer_vector_rows[5] * branch)
        ]
    )
    counted = jnp.where(parallel_model_index == 0, jnp.sum(valid_rows), 0.0)
    vector_grad, bias_grad, squares_all, counted_all = lax.psum(
        (
            vector_part,
            shard_offset(bias_part, parallel_model_index, parallel_model_width, 1),
            squares,
            counted,
        ),
        ("dp", "mp"),
    )
    token_spread = jnp.sqrt(squares_all / (counted_all * parallel_model_width))
    grad_parts = (qkv_part, out_part, up_part, down_part)
    summed = lax.psum((grad_parts[0], grad_parts[1], grad_parts[2], grad_parts[3]), "dp")
    qkv_grad = select_slice(summed[0], data_index, w_qkv.shape[0], 0)
    out_grad = select_slice(summed[1], data_index, w_out.shape[1], 1)
    up_grad = select_slice(summed[2], data_index, w_up.shape[0], 0)
    down_grad = select_slice(summed[3], data_index, w_down.shape[1], 1)
    square_qkv = qkv_grad * qkv_grad
    square_out = out_grad * out_grad
    square_up = up_grad * up_grad
    square_down = down_grad * down_grad
    scalars = jnp.stack(
        [
            jnp.sum(w_qkv * w_qkv),
            jnp.sum(w_out * w_out),
            jnp.sum(w_up * w_up),
            jnp.sum(w_down * w_down),
            jnp.where(parallel_model_index == 0, jnp.sum(qkvrows_prior), 0.0),
            jnp.where(data_index == 0, jnp.sum(outrows_prior), 0.0),
            jnp.where(parallel_model_index == 0, jnp.sum(uprows_prior), 0.0),
            jnp.where(data_index == 0, jnp.sum(downrows_prior), 0.0),
        ]
    )
    factor_totals = lax.psum(
        (
            shard_offset(jnp.sum(square_qkv, axis=(1, 2)), data_index, parallel_model_width, 0),
            shard_offset(
                jnp.sum(square_qkv, axis=0), parallel_model_index, parallel_model_width, 1
            ),
            shard_offset(
                jnp.sum(square_out, axis=1), parallel_model_index, parallel_model_width, 0
            ),
            shard_offset(jnp.sum(square_out, axis=0), data_index, parallel_model_width, 0),
            shard_offset(jnp.sum(square_up, axis=1), data_index, parallel_model_width, 0),
            shard_offset(jnp.sum(square_up, axis=0), parallel_model_index, FF, 0),
            shard_offset(jnp.sum(square_down, axis=1), parallel_model_index, FF, 0),
            shard_offset(jnp.sum(square_down, axis=0), data_index, parallel_model_width, 0),
            scalars,
        ),
        ("dp", "mp"),
    )
    (
        rows_qkv,
        cols_qkv,
        rows_out,
        cols_out,
        rows_up,
        cols_up,
        rows_down,
        cols_down,
        scalar_totals,
    ) = factor_totals
    local_rows = w_qkv.shape[0]
    local_cols = w_out.shape[1]
    qkvrows_after, qkvcols_flat, update_qkv, usq_qkv = factor_step(
        qkv_grad.reshape(local_rows, 3 * shard_width_local),
        qkvrows_prior,
        qkvcols_prior.reshape(3 * shard_width_local),
        select_slice(rows_qkv, data_index, local_rows, 0),
        select_slice(cols_qkv, parallel_model_index, shard_width_local, 1).reshape(
            3 * shard_width_local
        ),
        jnp.sum(rows_qkv),
        parallel_model_width,
        3 * parallel_model_width,
        scalar_totals[4],
    )
    outrows_after, outcols_after, update_out, usq_out = factor_step(
        out_grad,
        outrows_prior,
        outcols_prior,
        select_slice(rows_out, parallel_model_index, shard_width_local, 0),
        select_slice(cols_out, data_index, local_cols, 0),
        jnp.sum(rows_out),
        parallel_model_width,
        parallel_model_width,
        scalar_totals[5],
    )
    uprows_after, upcols_after, update_up, usq_up = factor_step(
        up_grad,
        uprows_prior,
        upcols_prior,
        select_slice(rows_up, data_index, local_rows, 0),
        select_slice(cols_up, parallel_model_index, local_hidden, 0),
        jnp.sum(rows_up),
        parallel_model_width,
        FF,
        scalar_totals[6],
    )
    downrows_after, downcols_after, update_down, usq_down = factor_step(
        down_grad,
        downrows_prior,
        downcols_prior,
        select_slice(rows_down, parallel_model_index, local_hidden, 0),
        select_slice(cols_down, data_index, local_cols, 0),
        jnp.sum(rows_down),
        FF,
        parallel_model_width,
        scalar_totals[7],
    )
    usq_totals = lax.psum(jnp.stack([usq_qkv, usq_out, usq_up, usq_down]), ("dp", "mp"))
    entry_counts = jnp.array(
        [
            3.0 * parallel_model_width * parallel_model_width,
            1.0 * parallel_model_width * parallel_model_width,
            1.0 * parallel_model_width * FF,
            1.0 * FF * parallel_model_width,
        ],
        jnp.float32,
    )
    update_scale = jnp.sqrt(usq_totals / entry_counts)
    weight_rms = jnp.sqrt(scalar_totals[:4] / entry_counts)
    limits = jnp.maximum(1.0, update_scale / clip_limit)
    qkv_after = (
        w_qkv.reshape(local_rows, 3 * shard_width_local)
        - step_rate * weight_rms[0] * update_qkv / limits[0]
    ).reshape(w_qkv.shape)
    out_after = w_out - step_rate * weight_rms[1] * update_out / limits[1]
    up_after = w_up - step_rate * weight_rms[2] * update_up / limits[2]
    down_after = w_down - step_rate * weight_rms[3] * update_down / limits[3]
    vectors_after, moment_vectors = jax.vmap(plain_step)(
        layer_vector_rows, vector_grad, vector_moment
    )
    heads_after, heads_moment = jax.vmap(plain_step)(
        inner_biases[:2], bias_grad[:2], bias_moment[:2]
    )
    upper_after, upper_moment = plain_step(
        inner_biases[2:].reshape(FF), bias_grad[2:].reshape(FF), bias_moment[2:].reshape(FF)
    )
    biases_after = jnp.concatenate(
        [heads_after, upper_after.reshape(FF // parallel_model_width, parallel_model_width)], axis=0
    )
    moment_biases = jnp.concatenate(
        [heads_moment, upper_moment.reshape(FF // parallel_model_width, parallel_model_width)],
        axis=0,
    )
    return (
        result_low,
        input_grad,
        qkv_grad,
        out_grad,
        up_grad,
        down_grad,
        qkv_after,
        out_after,
        up_after,
        down_after,
        qkv_after.astype(jnp.bfloat16),
        out_after.astype(jnp.bfloat16),
        up_after.astype(jnp.bfloat16),
        down_after.astype(jnp.bfloat16),
        qkvrows_after,
        qkvcols_flat.reshape(3, shard_width_local),
        outrows_after,
        outcols_after,
        uprows_after,
        upcols_after,
        downrows_after,
        downcols_after,
        vector_grad,
        bias_grad,
        moment_vectors,
        moment_biases,
        vectors_after,
        biases_after,
        update_scale,
        token_spread,
    )

def shards(
    tokens_in,
    cotangent,
    patch_counts,
    w_qkv,
    w_out,
    w_up,
    w_down,
    layer_vector_rows,
    inner_biases,
    qkvrows_prior,
    qkvcols_prior,
    outrows_prior,
    outcols_prior,
    uprows_prior,
    upcols_prior,
    downrows_prior,
    downcols_prior,
    vector_moment,
    bias_moment,
):
    n_dp, n_mp = lax.axis_size("dp"), lax.axis_size("mp")
    row_count, width = tokens_in.shape
    set_count, slot_count = patch_counts.shape
    set_rows = row_count // set_count
    own_rows = row_count // n_mp
    window = own_rows + HALO
    share, hidden_width, block_rows = w_qkv.shape[2], w_up.shape[1], w_up.shape[0]
    f32, low = jnp.float32, jnp.bfloat16
    vmem = pl.BlockSpec(memory_space=pltpu.VMEM)
    anywhere = pl.BlockSpec(memory_space=pl.ANY)
    scalars_in = pl.BlockSpec(memory_space=pltpu.SMEM)
    dma = pltpu.SemaphoreType.DMA
    held = pltpu.VMEM

    def shape(*dims, dtype=low):
        return jax.ShapeDtypeStruct(dims, dtype)

    masters, reduced, sums, sub_new, lane_new, scalar_rows, input_parts, stream = pl.pallas_call(
        functools.partial(layer_kernel, n_dp, n_mp, slot_count, own_rows),
        out_shape=(
            shape(GROUPS, block_rows, width, dtype=f32),
            shape(GROUPS, block_rows, width, dtype=f32),
            shape(16, width, dtype=f32),
            shape(8, LANES, dtype=f32),
            shape(8, width, dtype=f32),
            shape(8, LANES, dtype=f32),
            shape(n_mp, share, own_rows),
            shape(n_mp, own_rows, width),
        ),
        in_specs=[anywhere] * 2 + [vmem] * 4 + [scalars_in] + [vmem] * 10,
        out_specs=(vmem,) * 6 + (anywhere,) * 2,
        scratch_shapes=[
            held((GROUPS, n_mp, n_dp // 2, 2, block_rows, width), low),
            held((set_rows, width), low),
            held((window, width), low),
            held((n_mp, set_rows, width), low),
            held((n_mp, window, hidden_width), low),
            held((n_mp, window, hidden_width), low),
            held((n_mp, window, 2 * LANES), low),
            held((window, width), f32),
            held((window, width), low),
            held((width, own_rows), low),
            held((width, own_rows), low),
            held((width, own_rows), low),
            held((own_rows, width), f32),
            held((window, width), low),
            held((window, width), f32),
            held((own_rows, width), low),
            held((set_rows, LANES), low),
            held((set_rows, LANES), low),
            held((window, 2 * LANES), low),
            held((window, 3 * LANES), f32),
            held((window, 2 * LANES), low),
            held((8, width), f32),
            held((16, width), f32),
            held((8, width), f32),
            held((8, LANES), f32),
            held((3, width), f32),
            held((RING, n_dp // 2, block_rows, width), low),
            held((GROUPS, n_mp, 2, block_rows // 2, width), low),
            held((GROUPS, n_mp, block_rows, width), low),
            held((GROUPS, n_mp, block_rows, width), low),
            held((GROUPS, n_mp + 1, block_rows, width), low),
            held((6, 16, width), f32),
            held((5, 16, width), f32),
            held((n_mp, 8, LANES), f32),
            held((n_dp, 2, width), f32),
            held((n_mp, 8, LANES), f32),
            held((n_dp, 1, width), f32),
            held((n_mp, 8, LANES), f32),
            held((n_dp, 8, LANES), f32),
            pltpu.SemaphoreType.REGULAR,
            dma((4,)),
            dma((GROUPS, n_mp, KINDS)),
            dma((GROUPS, n_mp, KINDS)),
            dma((GROUPS, n_mp, 2)),
            dma((GROUPS, n_mp, R_KINDS)),
            dma((GROUPS, n_mp, R_KINDS)),
            dma((2, n_mp, Stream.CUTS)),
            dma((n_mp, Stream.CUTS)),
            dma((n_mp,)),
            dma((n_mp,)),
            dma((5,)),
            dma((5,)),
            dma((6, max(n_dp, n_mp))),
            dma((6, max(n_dp, n_mp))),
        ],
        compiler_params=pltpu.CompilerParams(
            collective_id=1, has_side_effects=True, vmem_limit_bytes=63 * 2**20
        ),
    )(
        tokens_in, cotangent, w_qkv.transpose(1, 0, 2), w_out, w_up, w_down.T, patch_counts, layer_vector_rows,
        inner_biases, qkvrows_prior, qkvcols_prior, outrows_prior, outcols_prior, uprows_prior, upcols_prior,
        downrows_prior, downcols_prior,
    )

    def both(*dims):
        return (shape(*dims, dtype=f32),) * 2 + (shape(*dims),)

    kinds = [
        both(3, block_rows, share), both(share, block_rows), both(block_rows, width), both(block_rows, width)
    ]
    small = [
        (block_rows,), (3, share), (share,), (block_rows,),
        (block_rows,), (hidden_width,), (hidden_width,), (block_rows,),
    ] + [(8, width), (6, width)] * 3 + [(4,), (3,)]
    outs = pl.pallas_call(
        functools.partial(update_kernel, n_dp, n_mp),
        out_shape=(
            shape(n_mp, own_rows, width),
            shape(share, row_count, dtype=f32),
            *(kind[i] for i in range(3) for kind in kinds),
            *(shape(*dims, dtype=f32) for dims in small),
        ),
        in_specs=[vmem] * 11 + [anywhere],
        out_specs=(anywhere,) + (vmem,) * 29,
        scratch_shapes=[pltpu.VMEM((n_mp, own_rows, width), low), dma((2,))],
        compiler_params=pltpu.CompilerParams(vmem_limit_bytes=60 * 2**20),
    )(
        reduced, masters, sub_new, lane_new, scalar_rows, sums, layer_vector_rows, inner_biases, vector_moment,
        bias_moment, input_parts, stream,
    )
    weights = [
        part for i in (2, 6, 10) for part in (outs[i].transpose(1, 0, 2), outs[i + 1], outs[i + 2], outs[i + 3].T)
    ]
    return (outs[0].reshape(row_count, width), outs[1].T, *weights, *outs[14:])

def solution(mesh):
    in_specs = (
        P("dp", None),
        P("dp", None),
        P("dp", None),
        P("dp", None, "mp"),
        P("mp", "dp"),
        P("dp", "mp"),
        P("mp", "dp"),
        P(),
        P(),
        P("dp"),
        P(None, "mp"),
        P("mp"),
        P("dp"),
        P("dp"),
        P("mp"),
        P("mp"),
        P("dp"),
        P(),
        P(),
    )
    out_specs = (
        P("dp", None),
        P("dp", "mp"),
        P("dp", None, "mp"),
        P("mp", "dp"),
        P("dp", "mp"),
        P("mp", "dp"),
        P("dp", None, "mp"),
        P("mp", "dp"),
        P("dp", "mp"),
        P("mp", "dp"),
        P("dp", None, "mp"),
        P("mp", "dp"),
        P("dp", "mp"),
        P("mp", "dp"),
        P("dp"),
        P(None, "mp"),
        P("mp"),
        P("dp"),
        P("dp"),
        P("mp"),
        P("mp"),
        P("dp"),
        P(),
        P(),
        P(),
        P(),
        P(),
        P(),
        P(),
        P(),
    )
    fits = mesh.shape["dp"] == 8 and mesh.shape["mp"] == 4
    return jax.shard_map(shards if fits else generic, mesh=mesh, in_specs=in_specs, out_specs=out_specs, check_vma=False)
```
